32 devices in a mesh: dp: 8 (over z, y), stream: 4 (over x, core).
Axes of the slice: x: 2, y: 2, z: 4, core: 2. Of those that a mesh axis runs over, the one named last changes fastest.
Arguments:
- text_input: bfloat16 [2, 128, 40, 768], P(None, ('dp', 'stream')), may hold values from -6 to 6
- patch_input: bfloat16 [2, 32, 145, 1024], P(None, ('dp', 'stream')), may hold values from -6 to 6
- text_lengths: int32 [2, 128], P(None, ('dp', 'stream')), may hold values from 6 to 40, as said below
- image_of_row: int32 [2, 128], P(None, ('dp', 'stream')), may hold values from 0 to 3, as said below
- cotangent: bfloat16 [2, 128, 40, 768], P(None, ('dp', 'stream')), may hold values from -6 to 6
- self_qkv: bfloat16 [3, 768, 768], P(None, 'dp'), may hold values from -0.21875 to 0.21875
- self_out: bfloat16 [768, 768], P('dp'), may hold values from -0.4375 to 0.4375
- cross_q: bfloat16 [768, 768], P('dp'), may hold values from -0.21875 to 0.21875
- cross_kv: bfloat16 [2, 1024, 768], P(None, 'dp'), may hold values from -0.1875 to 0.1875
- cross_out: bfloat16 [768, 768], P('dp'), may hold values from -0.75 to 0.75
- ffn_in: bfloat16 [768, 3072], P('dp'), may hold values from -0.21875 to 0.21875
- ffn_out: bfloat16 [3072, 768], P('dp'), may hold values from -0.109375 to 0.109375
- biases: bfloat16 [10, 768], P(None, 'dp'), may hold values from -1 to 1
- norm_gains: bfloat16 [3, 768], P(None, 'dp'), may hold values from 0.25 to 1.75
- ffn_bias: bfloat16 [3072], P('dp'), may hold values from -1 to 1
Outputs:
- layer_out: bfloat16 [2, 128, 40, 768], P(None, ('dp', 'stream'))
- text_grad: bfloat16 [2, 128, 40, 768], P(None, ('dp', 'stream'))
- patch_grad: bfloat16 [2, 32, 145, 1024], P(None, ('dp', 'stream'))
- grad_self_qkv: float32 [3, 768, 768], P(None, 'dp')
- grad_self_out: float32 [768, 768], P('dp')
- grad_cross_q: float32 [768, 768], P('dp')
- grad_cross_kv: float32 [2, 1024, 768], P(None, 'dp')
- grad_cross_out: float32 [768, 768], P('dp')
- grad_ffn_in: float32 [768, 3072], P('dp')
- grad_ffn_out: float32 [3072, 768], P('dp')
- grad_biases: float32 [10, 768], P(None, 'dp')
- grad_norm_gains: float32 [3, 768], P(None, 'dp')
- grad_ffn_bias: float32 [3072], P('dp')
The draws below stay inside these ranges and needn't reach their ends.
Inputs may be any that keep to these rules, and one draw needn't show every extreme that they name: `text_lengths`: valid tokens of each row, counted from the row's start. `image_of_row`: each row names one of the 4 images of its group.
All inputs are finite; a program needn't handle non-finite values.
Results may differ from the reference program's by a relative error of at most 0.02.
Values may be sent and summed in bfloat16 or wider, within the bound.
No kernel may reach another device: no remote copies, remote signals or barrier semaphores. Data moves between devices by JAX's collectives and lax.ppermute only.
A program may use at most 512 MiB of HBM per device.

```python
import math
import jax
import jax.numpy as jnp
from jax import lax

D = 768
HEADS = 12
HEAD = 64
FF = 3072
DV = 1024
PATCHES = 145
SEQ_LEN = 40
MICRO = 2
ROWS_DEV = 4
IMG_DEV = 1
GROUP_ROWS = 16
GROUP_IMAGES = 4
ROWS = 128
IMAGES = 32


def draw_text_lengths(key, part):
    key = jax.random.fold_in(key, 11)
    shortest = min(6, SEQ_LEN)
    blocks = ROWS // ROWS_DEV
    values_drawn = jax.random.randint(key, (MICRO, blocks, ROWS_DEV), shortest, SEQ_LEN + 1, dtype=jnp.int32)
    values_drawn = values_drawn.at[:, :, 0].set(SEQ_LEN)
    values_drawn = values_drawn.at[:, :, 1].set(shortest)
    return values_drawn.reshape(MICRO, ROWS)


def draw_image_of_row(key, part):
    key = jax.random.fold_in(key, 23)
    key_rows, key_slots, key_order = jax.random.split(key, 3)
    blocks = ROWS // ROWS_DEV
    streams = GROUP_IMAGES // IMG_DEV
    values_drawn = jax.random.randint(key_rows, (MICRO, blocks, ROWS_DEV), 0, GROUP_IMAGES, dtype=jnp.int32)
    within = jax.random.randint(key_slots, (MICRO, blocks, streams), 0, IMG_DEV, dtype=jnp.int32)
    order_scores = jax.random.randint(key_order, (MICRO, blocks, streams), 0, 1048576, dtype=jnp.int32) * streams + jnp.arange(streams, dtype=jnp.int32)[None, None, :]
    order = jnp.argsort(order_scores, axis=-1, stable=True).astype(jnp.int32)
    forced = order * IMG_DEV + within
    values_drawn = values_drawn.at[:, :, :streams].set(forced)
    return values_drawn.reshape(MICRO, ROWS)


def with_spikes(array, key, source, target, shards_of, factor):
    def block_of(position):
        return (jnp.arange(array.shape[position]) // (array.shape[position] // shards_of)).reshape((-1,) + (1,) * (array.ndim - 1 - position))

    near = jax.random.permutation(key, shards_of)[block_of(target)]
    far = (block_of(target) + shards_of // 2) % shards_of
    return jnp.where((block_of(source) == near) | (block_of(source) == far), factor * array, array)


def levels(own_key, shape, pieces, smallest, top_value):
    gain = 1.0
    for axis_at, blocks in pieces:
        steps = jax.random.uniform(jax.random.fold_in(jax.random.fold_in(own_key, 6), axis_at), (blocks,), jnp.float32, smallest / len(pieces), top_value / len(pieces))
        gain = gain * jnp.repeat(jnp.exp(steps), shape[axis_at] // blocks).reshape((-1,) + (1,) * (len(shape) - 1 - axis_at))
    return gain


def gaussian(key, extent, width, bound, shards=(), kind=jnp.bfloat16):
    level = levels(key, extent, shards, -0.22, 0.18) if shards else 1.0
    drawn = jax.random.normal(key, extent, jnp.float32) * width * level
    return jnp.minimum(jnp.maximum(drawn, -bound), bound).astype(kind)


def heavy_noise(rng, extent, scale, reach, shards, heavy, kind=jnp.bfloat16):
    drawn = scale * jax.random.normal(rng, extent, jnp.float32)
    if shards:
        drawn = drawn * levels(rng, extent, shards, -0.22, 0.18)
    return jnp.clip(with_spikes(drawn, jax.random.fold_in(rng, 3), *heavy), -reach, reach).astype(kind)


def setup_inputs(seed: int = 0) -> dict:
    key_list = jax.random.split(jax.random.key(seed), 16)
    text_input = gaussian(key_list[0], (MICRO, ROWS, SEQ_LEN, D), 1.0, 6.0, ((1, 32),))
    patch_input = gaussian(key_list[1], (MICRO, IMAGES, PATCHES, DV), 1.0, 6.0, ((1, 32),))
    text_lengths = draw_text_lengths(jax.random.fold_in(key_list[15], 71), 0)
    image_of_row = draw_image_of_row(jax.random.fold_in(key_list[15], 71), 0)
    cotangent = heavy_noise(key_list[4], (MICRO, ROWS, SEQ_LEN, D), 1.0, 6.0, ((1, 32),), (1, 3, 32, 2.75))
    self_qkv = gaussian(key_list[5], (3, D, D), D ** -0.5, 0.21875, ((1, 8),))
    self_out = gaussian(key_list[6], (D, D), (D // 4) ** -0.5, 0.4375, ((0, 8),))
    cross_q = gaussian(key_list[7], (D, D), D ** -0.5, 0.21875, ((0, 8),))
    cross_kv = gaussian(key_list[8], (2, DV, D), DV ** -0.5, 0.1875, ((1, 8),))
    cross_out = gaussian(key_list[9], (D, D), (D // 12) ** -0.5, 0.75, ((0, 8),))
    ffn_in = gaussian(key_list[10], (D, FF), D ** -0.5, 0.21875, ((0, 8),))
    ffn_out = gaussian(key_list[11], (FF, D), FF ** -0.5, 0.109375, ((0, 8),))
    biases = gaussian(key_list[12], (10, D), 0.2, 1.0, ((1, 8),))
    norm_gains = jnp.clip(1.0 + 0.15 * jax.random.normal(key_list[13], (3, D), jnp.float32), 0.25, 1.75).astype(jnp.bfloat16)
    ffn_bias = gaussian(key_list[14], (FF,), 0.2, 1.0, ((0, 8),))
    return dict(text_input=text_input, patch_input=patch_input, text_lengths=text_lengths, image_of_row=image_of_row, cotangent=cotangent, self_qkv=self_qkv, self_out=self_out, cross_q=cross_q, cross_kv=cross_kv, cross_out=cross_out, ffn_in=ffn_in, ffn_out=ffn_out, biases=biases, norm_gains=norm_gains, ffn_bias=ffn_bias)


@jax.custom_vjp
def low(v):
    return lax.optimization_barrier(v.astype(jnp.bfloat16)).astype(jnp.float32)

@jax.custom_vjp
def low_back(v):
    return v

def low_keep(v):
    return (low(v), None)

def low_pass(kept, grad):
    return (grad,)

def back_keep(v):
    return (v, None)

def back_low(kept, grad):
    return (low(grad),)
low.defvjp(low_keep, low_pass)
low_back.defvjp(back_keep, back_low)
HIGHEST = lax.Precision.HIGHEST
EPSILON = 1e-06
ROOT_HALF = 0.7071067811865476

def both_ways(value):
    return low_back(low(value))

def layer_norm(summed, gain_row, shift_row):
    center = summed - lax.optimization_barrier(jnp.mean(summed, axis=-1, keepdims=True))
    variance = lax.optimization_barrier(jnp.mean(center * center, axis=-1, keepdims=True))
    return center * lax.rsqrt(variance + EPSILON) * gain_row + shift_row

def softmax_rows(scores):
    row_peak = lax.optimization_barrier(jnp.max(scores, axis=-1, keepdims=True))
    raised = jnp.exp(scores - row_peak)
    return raised / lax.optimization_barrier(jnp.sum(raised, axis=-1, keepdims=True))

def split_heads(values):
    return values.reshape(values.shape[:-1] + (HEADS, HEAD))

def forward(params, word_rows, pixels, lengths, images):
    self_qkv, self_out, cross_q, cross_kv, cross_out, ffn_in, ffn_out, biases, norm_gains, ffn_bias = params
    score_scale = 1.0 / math.sqrt(HEAD)
    projected = jnp.einsum('rld,jde->jrle', word_rows, self_qkv, precision=HIGHEST)
    queries = both_ways(projected[0] + biases[0])
    keys_self = both_ways(projected[1])
    values_self = both_ways(projected[2] + biases[1])
    scores = low_back(jnp.einsum('rqhc,rkhc->rhqk', split_heads(queries), split_heads(keys_self), precision=HIGHEST) * score_scale)
    key_valid = jnp.arange(SEQ_LEN, dtype=jnp.int32)[None, :] < lengths[:, None]
    attention = softmax_rows(jnp.where(key_valid[:, None, None, :], scores, -jnp.inf))
    attended = both_ways(jnp.einsum('rhqk,rkhc->rqhc', low(attention), split_heads(values_self), precision=HIGHEST).reshape(word_rows.shape))
    branch = low_back(jnp.einsum('rld,de->rle', attended, self_out, precision=HIGHEST) + biases[2])
    first_norm = layer_norm(word_rows + branch, norm_gains[0], biases[3])
    cross_query = both_ways(jnp.einsum('rld,de->rle', low(first_norm), cross_q, precision=HIGHEST) + biases[4])
    image_kv = jnp.einsum('ipv,jvd->jipd', pixels, cross_kv, precision=HIGHEST)
    image_keys = both_ways(image_kv[0])
    image_values = both_ways(image_kv[1] + biases[5])
    row_keys = jnp.take(image_keys, images, axis=0)
    row_values = jnp.take(image_values, images, axis=0)
    cross_scores = low_back(jnp.einsum('rqhc,rkhc->rhqk', split_heads(cross_query), split_heads(row_keys), precision=HIGHEST) * score_scale)
    cross_attention = softmax_rows(cross_scores)
    cross_heads = both_ways(jnp.einsum('rhqk,rkhc->rqhc', low(cross_attention), split_heads(row_values), precision=HIGHEST).reshape(word_rows.shape))
    cross_branch = low_back(jnp.einsum('rld,de->rle', cross_heads, cross_out, precision=HIGHEST) + biases[6])
    second_norm = layer_norm(first_norm + cross_branch, norm_gains[1], biases[7])
    hidden_pre = low_back(jnp.einsum('rld,df->rlf', low(second_norm), ffn_in, precision=HIGHEST) + ffn_bias)
    active = low(0.5 * hidden_pre * (1.0 + lax.erf(hidden_pre * ROOT_HALF)))
    lowered = low_back(jnp.einsum('rlf,fd->rld', active, ffn_out, precision=HIGHEST) + biases[8])
    return layer_norm(second_norm + lowered, norm_gains[2], biases[9])

def reference(text_input, patch_input, text_lengths, image_of_row, cotangent, self_qkv, self_out, cross_q, cross_kv, cross_out, ffn_in, ffn_out, biases, norm_gains, ffn_bias):
    params = tuple((weight.astype(jnp.float32) for weight in (self_qkv, self_out, cross_q, cross_kv, cross_out, ffn_in, ffn_out, biases, norm_gains, ffn_bias)))
    groups = ROWS // GROUP_ROWS
    totals = tuple((jnp.zeros(weight.shape, jnp.float32) for weight in params))
    positions = jnp.arange(SEQ_LEN, dtype=jnp.int32)

    def group_step(running, group_block):
        word_rows, pixels, lengths, images, upstream = group_block

        def run_block(weights, word_part, pixel_part):
            return forward(weights, word_part, pixel_part, lengths, images)
        output_rows, pullback = jax.vjp(run_block, params, word_rows, pixels)
        token_mask = (positions[None, :] < lengths[:, None]).astype(jnp.float32)
        grad_params, grad_words, grad_pixels = pullback(upstream * token_mask[:, :, None])
        running = tuple((left + right for left, right in zip(running, grad_params)))
        return (running, (output_rows.astype(jnp.bfloat16), grad_words.astype(jnp.bfloat16), grad_pixels.astype(jnp.bfloat16)))
    output_list = []
    text_list = []
    patch_list = []
    for micro_step in range(MICRO):
        group_blocks = (text_input[micro_step].astype(jnp.float32).reshape(groups, GROUP_ROWS, SEQ_LEN, D), patch_input[micro_step].astype(jnp.float32).reshape(groups, GROUP_IMAGES, PATCHES, DV), text_lengths[micro_step].reshape(groups, GROUP_ROWS), image_of_row[micro_step].reshape(groups, GROUP_ROWS), cotangent[micro_step].astype(jnp.float32).reshape(groups, GROUP_ROWS, SEQ_LEN, D))
        totals, (output_part, text_part, patch_part) = lax.scan(group_step, totals, group_blocks)
        output_list.append(output_part.reshape(ROWS, SEQ_LEN, D))
        text_list.append(text_part.reshape(ROWS, SEQ_LEN, D))
        patch_list.append(patch_part.reshape(IMAGES, PATCHES, DV))
    return (jnp.stack(output_list), jnp.stack(text_list), jnp.stack(patch_list), totals[0], totals[1], totals[2], totals[3], totals[4], totals[5], totals[6], totals[7], totals[8], totals[9])
```

```python
import functools
import math

import jax
import jax.numpy as jnp
from jax import lax
from jax.experimental import pallas as pl
from jax.experimental.pallas import tpu as pltpu
from jax.sharding import PartitionSpec as P

HEADS = 12
LANES = 384

CORE = ((0, 1), (1, 0), (2, 3), (3, 2))
ACROSS = ((0, 2), (2, 0), (1, 3), (3, 1))
BESIDE = ((0, 1), (1, 0), (2, 3), (3, 2), (4, 5), (5, 4), (6, 7), (7, 6))
PAIR = ((0, 2), (2, 0), (1, 3), (3, 1), (4, 6), (6, 4), (5, 7), (7, 5))
MIDDLE = ((2, 4), (4, 2), (3, 5), (5, 3))
OUTWARD = ((2, 0), (3, 1), (4, 6), (5, 7))
INWARD = ((0, 2), (1, 3), (6, 4), (7, 5))


def pick(array, index, axis=0):
    return lax.dynamic_index_in_dim(array, index, axis, keepdims=False)


def place():
    dp_at, stream_at = lax.axis_index("dp"), lax.axis_index("stream")
    return dp_at // 2, dp_at % 2, stream_at // 2, stream_at % 2


def pack_shard(shard, units):
    if shard.ndim == 2:
        rows, columns = shard.shape
        split = shard.reshape(2, rows // 2, 2, units, LANES).transpose(2, 0, 3, 1, 4)
    else:
        _, rows, columns = shard.shape
        split = shard.reshape(units, 2, rows // 2, 2, LANES).transpose(3, 1, 0, 2, 4)
    return split.reshape(2, 2, units * rows // 2, LANES)


def gather_pieces(own_both):
    _, _, x_at, core_at = place()
    z_at = lax.axis_index("dp") // 2
    own = pick(own_both, core_at)
    mate = lax.ppermute(own, "dp", PAIR)
    pair = jnp.stack((own, mate))
    middle = lax.ppermute(pair, "dp", MIDDLE)
    outer = lax.ppermute(middle, "dp", OUTWARD)
    inside = (z_at == 1) | (z_at == 2)
    other = jnp.where(inside, middle, outer)
    near = lax.ppermute(pick(pair, x_at, 1), "dp", BESIDE)
    far = lax.ppermute(pick(other, x_at, 1), "dp", BESIDE)
    near_x = lax.ppermute(near, "stream", ACROSS)
    far_x = lax.ppermute(far, "stream", ACROSS)
    mine = (mate, other, near, far, near_x, far_x)
    theirs = tuple(lax.ppermute(piece, "stream", CORE) for piece in mine)
    return (own_both, *mine, *theirs)


def assemble_kernel(units, *refs):
    n_out = len(units)
    own_both, mate, other, near, far, near_x, far_x, *theirs = refs[:13]
    outs = refs[13 : 13 + n_out]
    sems = refs[13 + n_out]
    dp_at, stream_at = lax.axis_index("dp"), lax.axis_index("stream")
    z_at, y_at = dp_at // 2, dp_at % 2
    x_at, core_at = stream_at // 2, stream_at % 2
    copies = []

    def whole(piece, z_from, y_from, x_from, core_from):
        row = 0
        for (count, depth), out in zip(units, outs):
            start = (z_from * 2 + y_from) * (2 * depth) + x_from * depth
            for unit in range(count):
                copies.append(
                    pltpu.make_async_copy(
                        piece.at[pl.ds(row, depth)],
                        out.at[core_from, unit, pl.ds(pl.multiple_of(start, 16), depth)],
                        sems.at[len(copies)],
                    )
                )
                copies[-1].start()
                row += depth

    for core_from in range(2):
        for x_from in range(2):
            whole(own_both.at[core_from, x_from], z_at, y_at, x_from, core_from)
    base = 2 - (z_at // 2) * 2
    others = (jnp.where(z_at < 2, 2, 1), jnp.where(z_at < 2, 3, 0))
    pair_z = (z_at, z_at + 1 - 2 * (z_at % 2))
    for group, core_from in (((mate, other, near, far, near_x, far_x), core_at), (theirs, 1 - core_at)):
        g_mate, g_other, g_near, g_far, g_near_x, g_far_x = group
        for x_from in range(2):
            whole(g_mate.at[x_from], pair_z[1], y_at, x_from, core_from)
            for j in range(2):
                whole(g_other.at[j, x_from], others[j], y_at, x_from, core_from)
        for j in range(2):
            whole(g_near.at[j], pair_z[j], 1 - y_at, x_at, core_from)
            whole(g_far.at[j], others[j], 1 - y_at, x_at, core_from)
            whole(g_near_x.at[j], pair_z[j], 1 - y_at, 1 - x_at, core_from)
            whole(g_far_x.at[j], others[j], 1 - y_at, 1 - x_at, core_from)
    for copy in copies:
        copy.wait()


def gather_group(shards, units):
    packed = [
        shard if shard.ndim == 4 else pack_shard(shard, count)
        for shard, (count, _) in zip(shards, units)
    ]
    own_both = jnp.concatenate(packed, axis=2)
    dp = lax.axis_size("dp")
    if dp != 8 or lax.axis_size("stream") != 4:
        whole = lax.all_gather(own_both, "dp", axis=0, tiled=False)
        results = []
        row = 0
        for count, depth in units:
            part = whole[:, :, :, row : row + count * depth]
            part = part.reshape(dp, 2, 2, count, depth, LANES).transpose(1, 3, 0, 2, 4, 5)
            results.append(part.reshape(2, count, dp * 2 * depth, LANES))
            row += count * depth
        return results
    pieces = gather_pieces(own_both)
    total = sum(count for count, _ in units)
    return pl.pallas_call(
        functools.partial(assemble_kernel, units),
        out_shape=[
            jax.ShapeDtypeStruct((2, count, dp * 2 * depth, LANES), own_both.dtype)
            for count, depth in units
        ],
        in_specs=[pl.BlockSpec(memory_space=pl.ANY)] * 13,
        out_specs=[pl.BlockSpec(memory_space=pltpu.VMEM)] * len(units),
        scratch_shapes=[pltpu.SemaphoreType.DMA((32 * total,))],
        compiler_params=pltpu.CompilerParams(vmem_limit_bytes=40 * 2**20),
        name="assemble",
    )(*pieces)


def low(value):
    return value.astype(jnp.bfloat16)


def wide(value):
    return value.astype(jnp.float32)


def reduce_group(mine, sibling):
    z_at, y_at, x_at, core_at = place()
    came = lax.ppermute(sibling, "stream", CORE)
    mine_y, came_y = pick(mine, 1 - y_at, 1), pick(came, 1 - y_at, 1)
    hop = low(wide(pick(mine_y, 1 - x_at, 1)) + wide(pick(came_y, 1 - x_at, 1)))
    from_x = lax.ppermute(hop, "stream", ACROSS)
    hop = low(wide(pick(mine_y, x_at, 1)) + wide(pick(came_y, x_at, 1)) + wide(from_x))
    from_y = lax.ppermute(hop, "dp", BESIDE)
    here = jnp.arange(2)[None, :, None, None] == x_at
    held = low(
        wide(pick(mine, y_at, 1))
        + wide(pick(came, y_at, 1))
        + jnp.where(here, wide(from_y)[:, None], 0.0)
    )
    side = z_at // 2
    halves = held.reshape(2, 2, *held.shape[1:])
    hop = pick(halves, 1 - side)
    first = lax.ppermute(hop, "dp", INWARD)
    second = lax.ppermute(low(wide(hop) + wide(first)), "dp", MIDDLE)
    kept = pick(halves, side)
    spot = z_at % 2
    hop = low(wide(pick(kept, 1 - spot)) + wide(pick(second, 1 - spot)))
    third = lax.ppermute(hop, "dp", PAIR)
    total = low(wide(pick(kept, spot)) + wide(pick(second, spot)) + wide(third))
    from_x = lax.ppermute(total, "stream", ACROSS)
    total = low(wide(total) + wide(from_x))
    total = lax.optimization_barrier(total)
    other = lax.ppermute(total, "stream", CORE)
    first_half = jnp.where(core_at == 0, total, other)
    second_half = jnp.where(core_at == 0, other, total)
    return jnp.stack((first_half, second_half))


def reduce_any(both):
    dp = lax.axis_size("dp")
    if dp != 8 or lax.axis_size("stream") != 4:
        own = lax.psum_scatter(both, "dp", scatter_dimension=1, tiled=True)[:, 0]
        return lax.psum(own, "stream")
    core_at = lax.axis_index("stream") % 2
    both = both.reshape(2, 4, 2, *both.shape[2:])
    return reduce_group(pick(both, core_at), pick(both, 1 - core_at))


def pack_grad(grad, units):
    dp = lax.axis_size("dp")
    if grad.ndim == 2:
        depth = grad.shape[0] // (2 * dp)
        split = grad.reshape(dp, 2, depth, 2, units, LANES).transpose(3, 0, 1, 4, 2, 5)
    else:
        depth = grad.shape[1] // (2 * dp)
        split = grad.reshape(units, dp, 2, depth, 2, LANES).transpose(4, 1, 2, 0, 3, 5)
    return low(split).reshape(2, dp, 2, units * depth, LANES)


def unpack_shard(packed, units, depth, flat):
    split = packed.reshape(2, 2, units, depth, LANES)
    if flat:
        return wide(split.transpose(1, 3, 0, 2, 4).reshape(2 * depth, 2 * units * LANES))
    return wide(split.transpose(2, 1, 3, 0, 4).reshape(units, 2 * depth, 2 * LANES))


EPSILON = 1e-06
ROOT_HALF = 0.7071067811865476
INV_ROOT_TAU = 0.3989422804014327
HIGHEST = lax.Precision.HIGHEST


def product(left, right):
    return jnp.dot(left, right, preferred_element_type=jnp.float32)


def contract_rows(left, right):
    return lax.dot_general(
        left, right, (((0,), (0,)), ((), ())), preferred_element_type=jnp.float32
    )


def contract_last(left, right):
    return lax.dot_general(
        left, right, (((1,), (1,)), ((), ())), preferred_element_type=jnp.float32
    )


def column_sum(matrix):
    return jnp.sum(matrix.astype(jnp.float32), axis=0)


def norm_forward(summed, gain_row, shift_row):
    center = summed - jnp.mean(summed, axis=-1, keepdims=True)
    inverse = lax.rsqrt(jnp.mean(center * center, axis=-1, keepdims=True) + EPSILON)
    normed = center * inverse
    return (normed * gain_row + shift_row, normed, inverse)


def norm_backward(upstream, normed, inverse, gain_row):
    scaled = upstream * gain_row
    grad_input = inverse * (
        scaled
        - jnp.mean(scaled, axis=-1, keepdims=True)
        - normed * jnp.mean(scaled * normed, axis=-1, keepdims=True)
    )
    return (grad_input, jnp.sum(upstream * normed, axis=0), jnp.sum(upstream, axis=0))


def softmax_rows(scores):
    row_peak = jnp.max(scores, axis=-1, keepdims=True)
    raised = jnp.exp(scores - row_peak)
    return raised / jnp.sum(raised, axis=-1, keepdims=True)


def gelu_value(hidden_pre):
    return 0.5 * hidden_pre * (1.0 + lax.erf(hidden_pre * ROOT_HALF))


def gelu_slope(hidden_pre):
    return 0.5 * (1.0 + lax.erf(hidden_pre * ROOT_HALF)) + hidden_pre * INV_ROOT_TAU * jnp.exp(
        -0.5 * hidden_pre * hidden_pre
    )


def micro_batch(weights, word_rows, pixels, lengths, images, micro_of_row, upstream_rows):
    (
        self_qkv,
        self_out,
        cross_q,
        cross_kv,
        cross_out,
        ffn_in,
        ffn_out,
        biases,
        norm_gains,
        ffn_bias,
    ) = weights
    bias_rows = biases.astype(jnp.float32)
    gain_rows = norm_gains.astype(jnp.float32)
    ffn_shift = ffn_bias.astype(jnp.float32)
    row_count, seq_len, width_all = word_rows.shape
    head_size = width_all // HEADS
    patch_count = pixels.shape[1]
    score_scale = 1.0 / math.sqrt(head_size)
    tokens = row_count * seq_len
    flat_tokens = word_rows.reshape(tokens, width_all)
    position = jnp.arange(tokens, dtype=jnp.int32)
    segment = position // seq_len
    key_ok = position % seq_len < jnp.repeat(lengths, seq_len, total_repeat_length=tokens)
    allowed = (segment[:, None] == segment[None, :]) & key_ok[None, :]
    projected = jnp.einsum("nd,jde->jne", flat_tokens, self_qkv, preferred_element_type=jnp.float32)
    queries = (projected[0] + bias_rows[0]).astype(jnp.bfloat16).reshape(tokens, HEADS, head_size)
    keys_self = projected[1].astype(jnp.bfloat16).reshape(tokens, HEADS, head_size)
    values_self = (
        (projected[2] + bias_rows[1]).astype(jnp.bfloat16).reshape(tokens, HEADS, head_size)
    )
    scores = (
        jnp.einsum("qhc,khc->hqk", queries, keys_self, preferred_element_type=jnp.float32)
        * score_scale
    )
    attention = softmax_rows(jnp.where(allowed[None], scores, -jnp.inf))
    attention_low = attention.astype(jnp.bfloat16)
    attended = (
        jnp.einsum("hqk,khc->qhc", attention_low, values_self, preferred_element_type=jnp.float32)
        .reshape(tokens, width_all)
        .astype(jnp.bfloat16)
    )
    branch = product(attended, self_out) + bias_rows[2]
    first_norm, first_normed, first_inverse = norm_forward(
        flat_tokens.astype(jnp.float32) + branch, gain_rows[0], bias_rows[3]
    )
    first_low = first_norm.astype(jnp.bfloat16)
    cross_query = (product(first_low, cross_q) + bias_rows[4]).astype(jnp.bfloat16)
    cross_query_heads = cross_query.reshape(row_count, seq_len, HEADS, head_size)
    image_kv = jnp.einsum("ipv,jvd->jipd", pixels, cross_kv, preferred_element_type=jnp.float32)
    own_kv = jnp.stack((image_kv[0], image_kv[1] + bias_rows[5])).astype(jnp.bfloat16)
    beside_kv = lax.ppermute(own_kv, "stream", CORE)
    across_kv = lax.ppermute(jnp.stack((own_kv, beside_kv)), "stream", ACROSS)
    group_kv = jnp.concatenate((own_kv[None], beside_kv[None], across_kv))
    group_count = group_kv.shape[0]
    row_kv = jnp.stack(tuple(group_kv[images, j, micro_of_row] for j in range(2)))
    row_keys = row_kv[0].reshape(row_count, patch_count, HEADS, head_size)
    row_values = row_kv[1].reshape(row_count, patch_count, HEADS, head_size)
    cross_scores = (
        jnp.einsum(
            "rqhc,rkhc->rhqk", cross_query_heads, row_keys, preferred_element_type=jnp.float32
        )
        * score_scale
    )
    cross_attention = softmax_rows(cross_scores)
    cross_low = cross_attention.astype(jnp.bfloat16)
    cross_heads = (
        jnp.einsum("rhqk,rkhc->rqhc", cross_low, row_values, preferred_element_type=jnp.float32)
        .reshape(tokens, width_all)
        .astype(jnp.bfloat16)
    )
    cross_branch = product(cross_heads, cross_out) + bias_rows[6]
    second_norm, second_normed, second_inverse = norm_forward(
        first_norm + cross_branch, gain_rows[1], bias_rows[7]
    )
    second_low = second_norm.astype(jnp.bfloat16)
    hidden_pre = product(second_low, ffn_in) + ffn_shift
    active = gelu_value(hidden_pre).astype(jnp.bfloat16)
    lowered = product(active, ffn_out) + bias_rows[8]
    output_rows, third_normed, third_inverse = norm_forward(
        second_norm + lowered, gain_rows[2], bias_rows[9]
    )
    upstream = (
        upstream_rows.reshape(tokens, width_all).astype(jnp.float32)
        * key_ok.astype(jnp.float32)[:, None]
    )
    grad_third, third_gain, third_shift = norm_backward(
        upstream, third_normed, third_inverse, gain_rows[2]
    )
    grad_lowered = grad_third.astype(jnp.bfloat16)
    grad_ffn_out = contract_rows(active, grad_lowered)
    grad_hidden = (contract_last(grad_lowered, ffn_out) * gelu_slope(hidden_pre)).astype(
        jnp.bfloat16
    )
    grad_ffn_in = contract_rows(second_low, grad_hidden)
    grad_second_total = grad_third + contract_last(grad_hidden, ffn_in)
    grad_second, second_gain, second_shift = norm_backward(
        grad_second_total, second_normed, second_inverse, gain_rows[1]
    )
    grad_cross_branch = grad_second.astype(jnp.bfloat16)
    grad_cross_out = contract_rows(cross_heads, grad_cross_branch)
    grad_cross_heads = (
        contract_last(grad_cross_branch, cross_out)
        .astype(jnp.bfloat16)
        .reshape(row_count, seq_len, HEADS, head_size)
    )
    grad_cross_attention = jnp.einsum(
        "rqhc,rkhc->rhqk", grad_cross_heads, row_values, preferred_element_type=jnp.float32
    )
    grad_row_values = jnp.einsum(
        "rhqk,rqhc->rkhc", cross_low, grad_cross_heads, preferred_element_type=jnp.float32
    )
    grad_cross_scores = (
        cross_attention
        * (
            grad_cross_attention
            - jnp.sum(grad_cross_attention * cross_attention, axis=-1, keepdims=True)
        )
    ).astype(jnp.bfloat16)
    grad_cross_query = (
        (
            jnp.einsum(
                "rhqk,rkhc->rqhc", grad_cross_scores, row_keys, preferred_element_type=jnp.float32
            )
            * score_scale
        )
        .astype(jnp.bfloat16)
        .reshape(tokens, width_all)
    )
    grad_row_keys = (
        jnp.einsum(
            "rhqk,rqhc->rkhc",
            grad_cross_scores,
            cross_query_heads,
            preferred_element_type=jnp.float32,
        )
        * score_scale
    )
    grad_rows_kv = jnp.stack(
        (
            grad_row_keys.reshape(row_count, patch_count, width_all),
            grad_row_values.reshape(row_count, patch_count, width_all),
        )
    )
    selector = (
        (images[:, None, None] == jnp.arange(group_count, dtype=jnp.int32)[None, :, None])
        & (micro_of_row[:, None, None] == jnp.arange(pixels.shape[0])[None, None, :])
    ).astype(jnp.float32)
    grad_group_kv = jnp.einsum("rim,jrpd->ijmpd", selector, grad_rows_kv, precision=HIGHEST)
    from_x = lax.ppermute(low(grad_group_kv[2:]), "stream", ACROSS)
    grad_pair = grad_group_kv[:2] + wide(from_x)
    grad_own_kv = low(grad_pair[0] + wide(lax.ppermute(low(grad_pair[1]), "stream", CORE)))
    grad_cross_kv = jnp.einsum(
        "ipv,jipd->jvd", pixels, grad_own_kv, preferred_element_type=jnp.float32
    )
    value_bias = jnp.sum(grad_own_kv[1].astype(jnp.float32), axis=(0, 1))
    grad_pixels = jnp.einsum(
        "jipd,jvd->ipv", grad_own_kv, cross_kv, preferred_element_type=jnp.float32
    ).astype(jnp.bfloat16)
    grad_cross_q = contract_rows(first_low, grad_cross_query)
    grad_first_total = grad_second + contract_last(grad_cross_query, cross_q)
    grad_first, first_gain, first_shift = norm_backward(
        grad_first_total, first_normed, first_inverse, gain_rows[0]
    )
    grad_branch = grad_first.astype(jnp.bfloat16)
    grad_self_out = contract_rows(attended, grad_branch)
    grad_attended = (
        contract_last(grad_branch, self_out).astype(jnp.bfloat16).reshape(tokens, HEADS, head_size)
    )
    grad_attention = jnp.einsum(
        "qhc,khc->hqk", grad_attended, values_self, preferred_element_type=jnp.float32
    )
    grad_values = jnp.einsum(
        "hqk,qhc->khc", attention_low, grad_attended, preferred_element_type=jnp.float32
    )
    grad_scores = (
        attention * (grad_attention - jnp.sum(grad_attention * attention, axis=-1, keepdims=True))
    ).astype(jnp.bfloat16)
    grad_queries = (
        jnp.einsum("hqk,khc->qhc", grad_scores, keys_self, preferred_element_type=jnp.float32)
        * score_scale
    )
    grad_keys = (
        jnp.einsum("hqk,qhc->khc", grad_scores, queries, preferred_element_type=jnp.float32)
        * score_scale
    )
    grad_qkv_low = (
        jnp.stack((grad_queries, grad_keys, grad_values))
        .astype(jnp.bfloat16)
        .reshape(3, tokens, width_all)
    )
    grad_self_qkv = jnp.einsum(
        "nd,jne->jde", flat_tokens, grad_qkv_low, preferred_element_type=jnp.float32
    )
    grad_text = grad_first + jnp.einsum(
        "jne,jde->nd", grad_qkv_low, self_qkv, preferred_element_type=jnp.float32
    )
    grad_biases = jnp.stack(
        (
            column_sum(grad_qkv_low[0]),
            column_sum(grad_qkv_low[2]),
            column_sum(grad_branch),
            first_shift,
            column_sum(grad_cross_query),
            value_bias,
            column_sum(grad_cross_branch),
            second_shift,
            column_sum(grad_lowered),
            third_shift,
        )
    )
    grad_gains = jnp.stack((first_gain, second_gain, third_gain))
    grads = (
        grad_self_qkv,
        grad_self_out,
        grad_cross_q,
        grad_cross_kv,
        grad_cross_out,
        grad_ffn_in,
        grad_ffn_out,
        grad_biases,
        grad_gains,
        column_sum(grad_hidden),
    )
    return (
        output_rows.astype(jnp.bfloat16).reshape(row_count, seq_len, width_all),
        grad_text.astype(jnp.bfloat16).reshape(row_count, seq_len, width_all),
        grad_pixels,
        grads,
    )


def on_device(
    text_input,
    patch_input,
    text_lengths,
    image_of_row,
    cotangent,
    self_qkv,
    self_out,
    cross_q,
    cross_kv,
    cross_out,
    ffn_in,
    ffn_out,
    biases,
    norm_gains,
    ffn_bias,
):
    dp = lax.axis_size("dp")
    micros, row_count, seq_len, width = text_input.shape
    part = biases.shape[1]
    small = jnp.concatenate((biases, norm_gains, ffn_bias.reshape(-1, part)))
    small_rows = small.shape[0]
    wide_rows = biases.shape[0] + norm_gains.shape[0]
    small = jnp.pad(small, ((0, 32 - small_rows), (0, LANES - part)))
    small = jnp.broadcast_to(small.reshape(2, 16, LANES), (2, 2, 16, LANES))
    half = width // dp // 2
    half_v = cross_kv.shape[1] // 2
    half_f = ffn_out.shape[0] // 2
    in_units = ffn_in.shape[1] // (2 * LANES)
    w_qkv, w_small = gather_group((self_qkv, small), ((3, half), (1, 16)))
    small = w_small[0, 0].reshape(dp, 32, LANES)[:, :small_rows, :part]
    rows_all = small[:, :wide_rows].transpose(1, 0, 2).reshape(wide_rows, width)
    bias_all, gain_all = rows_all[: biases.shape[0]], rows_all[biases.shape[0] :]
    ffn_bias_all = small[:, wide_rows:].reshape(-1)

    w_kv, w_so, w_cq = gather_group((cross_kv, self_out, cross_q), ((2, half_v), (1, half), (1, half)))
    w_co, w_in = gather_group((cross_out, ffn_in), ((1, half), (in_units, half)))
    (w_out,) = gather_group((ffn_out,), ((1, half_f),))

    def columns(whole):
        return whole.transpose(2, 0, 1, 3).reshape(whole.shape[2], -1)

    def stacked(whole):
        return whole.transpose(1, 2, 0, 3).reshape(whole.shape[1], whole.shape[2], -1)

    weights = (
        stacked(w_qkv), columns(w_so), columns(w_cq), stacked(w_kv), columns(w_co), columns(w_in),
        columns(w_out), bias_all, gain_all, ffn_bias_all,
    )
    micro_of_row = jnp.repeat(jnp.arange(micros, dtype=jnp.int32), row_count)
    slots = image_of_row.reshape(-1) ^ lax.axis_index("stream")
    out_rows, text_rows, patch_rows, grads = micro_batch(
        weights,
        text_input.reshape(micros * row_count, seq_len, width),
        patch_input.reshape(-1, *patch_input.shape[2:]),
        text_lengths.reshape(-1),
        slots,
        micro_of_row,
        cotangent.reshape(micros * row_count, seq_len, width),
    )
    g_qkv, g_so, g_cq, g_kv, g_co, g_in, g_out, g_biases, g_gains, g_ffn_bias = grads
    r_out = reduce_any(pack_grad(g_out, 1))
    r_in = reduce_any(pack_grad(g_in, in_units))
    mid = jnp.concatenate((pack_grad(g_co, 1), pack_grad(g_kv, 2), pack_grad(g_cq, 1), pack_grad(g_so, 1)), axis=3)
    r_mid = reduce_any(mid)
    g_small = jnp.concatenate(
        (
            jnp.concatenate((g_biases, g_gains)).reshape(wide_rows, dp, part).transpose(1, 0, 2),
            g_ffn_bias.reshape(dp, -1, part),
        ),
        axis=1,
    )
    g_small = jnp.pad(low(g_small), ((0, 0), (0, 32 - small_rows), (0, LANES - part)))
    g_small = g_small.reshape(1, dp, 2, 16, LANES)
    g_small = jnp.concatenate((g_small, jnp.zeros_like(g_small)))
    r_qkv = reduce_any(jnp.concatenate((pack_grad(g_qkv, 3), g_small), axis=3))
    at = 0
    mids = []
    for units, depth, flat in ((1, half, True), (2, half_v, False), (1, half, True), (1, half, True)):
        mids.append(unpack_shard(r_mid[:, :, at : at + units * depth], units, depth, flat))
        at += units * depth
    s_co, s_kv, s_cq, s_so = mids
    g_small = wide(r_qkv[0, :, 3 * half :, :part].reshape(32, part)[:small_rows])
    return (
        out_rows.reshape(text_input.shape),
        text_rows.reshape(text_input.shape),
        patch_rows.reshape(patch_input.shape),
        unpack_shard(r_qkv[:, :, : 3 * half], 3, half, False),
        s_so,
        s_cq,
        s_kv,
        s_co,
        unpack_shard(r_in, in_units, half, True),
        unpack_shard(r_out, 1, half_f, True),
        g_small[: biases.shape[0]],
        g_small[biases.shape[0] : wide_rows],
        g_small[wide_rows:].reshape(-1),
    )


def solution(mesh):
    placed = (
        P(None, ("dp", "stream"), None, None),
        P(None, ("dp", "stream"), None, None),
        P(None, ("dp", "stream")),
        P(None, ("dp", "stream")),
        P(None, ("dp", "stream"), None, None),
        P(None, "dp", None),
        P("dp", None),
        P("dp", None),
        P(None, "dp", None),
        P("dp", None),
        P("dp", None),
        P("dp", None),
        P(None, "dp"),
        P(None, "dp"),
        P("dp"),
    )
    return jax.shard_map(
        on_device,
        mesh=mesh,
        in_specs=placed,
        out_specs=(
            P(None, ("dp", "stream"), None, None),
            P(None, ("dp", "stream"), None, None),
            P(None, ("dp", "stream"), None, None),
            P(None, "dp", None),
            P("dp", None),
            P("dp", None),
            P(None, "dp", None),
            P("dp", None),
            P("dp", None),
            P("dp", None),
            P(None, "dp"),
            P(None, "dp"),
            P("dp"),
        ),
        check_vma=False,
    )
```

```python
import functools

import jax
import jax.numpy as jnp
from jax import lax
from jax.experimental import pallas as pl
from jax.experimental.pallas import tpu as pltpu
from jax.sharding import PartitionSpec as P

HEADS = 12
LANES = 384
PAD_ROWS = 16
MIB = 2**20

EPSILON = 1e-06
ROOT_HALF = 0.7071067811865476
INV_ROOT_TAU = 0.3989422804014327

CORE = ((0, 1), (1, 0), (2, 3), (3, 2))
ACROSS = ((0, 2), (2, 0), (1, 3), (3, 1))
BESIDE = ((0, 1), (1, 0), (2, 3), (3, 2), (4, 5), (5, 4), (6, 7), (7, 6))
PAIR = ((0, 2), (2, 0), (1, 3), (3, 1), (4, 6), (6, 4), (5, 7), (7, 5))
HALFWAY = ((0, 4), (4, 0), (1, 5), (5, 1), (2, 6), (6, 2), (3, 7), (7, 3))
MIRROR = ((0, 6), (6, 0), (1, 7), (7, 1), (2, 4), (4, 2), (3, 5), (5, 3))

B_Q, B_V, B_SO, B_N1, B_CQ, B_CV, B_CO, B_N2, B_FO, B_N3, G_1, G_2, G_3 = range(13)


def low(value):
    return value.astype(jnp.bfloat16)


def wide(value):
    return value.astype(jnp.float32)


def dot(left, right):
    return jnp.dot(left, right, preferred_element_type=jnp.float32)


def dot_last(left, right):
    return lax.dot_general(
        left, right, (((1,), (1,)), ((), ())), preferred_element_type=jnp.float32
    )


def dot_first(left, right):
    return lax.dot_general(
        left, right, (((0,), (0,)), ((), ())), preferred_element_type=jnp.float32
    )


def pick(array, index, axis=0):
    return lax.dynamic_index_in_dim(array, index, axis, keepdims=False)


def place():
    dp_at, stream_at = lax.axis_index("dp"), lax.axis_index("stream")
    return dp_at // 2, dp_at % 2, stream_at // 2, stream_at % 2


class Clock:
    def __init__(self):
        self.before = []
        self.waiting = {}

    def step(self, moving=(), compute=()):
        asked = []
        for mover in moving:
            if mover.done:
                continue
            asked.append((mover, mover.requests))
        operands = [[operand for operand, _, _ in requests] for _, requests in asked]
        operands, self.before = lax.optimization_barrier((operands, self.before))
        after = []
        for (mover, requests), arrays in zip(asked, operands):
            came = [
                lax.ppermute(array, axis, hops)
                for array, (_, axis, hops) in zip(arrays, requests)
            ]
            mover.give(came)
            after += came
        for work in compute:
            after += jax.tree.leaves(work(self.tie))
        self.before = after

    def tie(self, array):
        return lax.optimization_barrier((array, self.before))[0]


class Mover:
    def __init__(self, steps):
        self.steps = steps
        self.done = False
        self.result = None
        self.requests = next(steps)

    def give(self, came):
        try:
            self.requests = self.steps.send(came)
        except StopIteration as stop:
            self.done, self.result = True, stop.value


def special_mesh():
    return lax.axis_size("dp") == 8 and lax.axis_size("stream") == 4


VMEM = pl.BlockSpec(memory_space=pltpu.VMEM)
SMEM = pl.BlockSpec(memory_space=pltpu.SMEM)
ANY = pl.BlockSpec(memory_space=pl.ANY)


def call(kernel, out_shape, in_specs, scratch=(), mib=48, flops=0, out_specs=None, **more):
    return pl.pallas_call(
        kernel,
        out_shape=out_shape,
        in_specs=in_specs,
        out_specs=jax.tree.map(lambda _: VMEM, out_shape) if out_specs is None else out_specs,
        scratch_shapes=list(scratch),
        compiler_params=pltpu.CompilerParams(vmem_limit_bytes=mib * MIB),
        cost_estimate=pl.CostEstimate(flops=flops, bytes_accessed=4 * MIB, transcendentals=0),
        **more,
    )


def shape(dims, dtype=jnp.bfloat16):
    return jax.ShapeDtypeStruct(tuple(dims), dtype)


F32 = jnp.float32


def pack_shard(shard, units):
    if shard.ndim == 2:
        rows, _ = shard.shape
        split = shard.reshape(2, rows // 2, 2, units, LANES).transpose(2, 0, 3, 1, 4)
    else:
        _, rows, _ = shard.shape
        split = shard.reshape(units, 2, rows // 2, 2, LANES).transpose(3, 1, 0, 2, 4)
    return split.reshape(2, 2, units * rows // 2, LANES)


def gather_steps(own_both):
    _, _, x_at, core_at = place()
    own = pick(own_both, core_at)
    own_x = pick(own, x_at)
    mate, half_z, mirror_z, beside = yield [
        (own, "dp", PAIR),
        (own_x, "dp", HALFWAY),
        (own_x, "dp", MIRROR),
        (own, "dp", BESIDE),
    ]
    others = jnp.stack((pick(mate, x_at), half_z, mirror_z))
    beside_others, half_x, mirror_x, *core_a = yield [
        (others, "dp", BESIDE),
        (half_z, "stream", ACROSS),
        (mirror_z, "stream", ACROSS),
        (mate, "stream", CORE),
        (half_z, "stream", CORE),
        (mirror_z, "stream", CORE),
        (beside, "stream", CORE),
    ]
    beside_x, *core_b = yield [
        (beside_others, "stream", ACROSS),
        (half_x, "stream", CORE),
        (mirror_x, "stream", CORE),
        (beside_others, "stream", CORE),
    ]
    core_c = yield [(beside_x, "stream", CORE)]
    mine = (mate, half_z, mirror_z, beside, half_x, mirror_x, beside_others, beside_x)
    return (own_both, *mine, *core_a, *core_b, *core_c)


def assemble_kernel(units, *refs):
    n_out = len(units)
    own_both, *pieces = refs[:17]
    outs = refs[17 : 17 + n_out]
    sems = refs[17 + n_out]
    z_at, y_at, x_at, core_at = place()
    copies = []

    def whole(piece, z_from, y_from, x_from, core_from):
        row = 0
        for (count, depth), out in zip(units, outs):
            start = (z_from * 2 + y_from) * (2 * depth) + x_from * depth
            copies.append(
                pltpu.make_async_copy(
                    piece.at[pl.ds(row, count * depth)].reshape(count, depth, LANES),
                    out.at[core_from, :, pl.ds(pl.multiple_of(start, 16), depth)],
                    sems.at[len(copies)],
                )
            )
            copies[-1].start()
            row += count * depth

    for core_from in range(2):
        for x_from in range(2):
            whole(own_both.at[core_from, x_from], z_at, y_at, x_from, core_from)
    _, z_mate, z_half, z_mirror = shard_slots(z_at)
    for group, core_from in ((pieces[:8], core_at), (pieces[8:], 1 - core_at)):
        mate, half_z, mirror_z, beside, half_x, mirror_x, beside_others, beside_x = group
        for x_from in range(2):
            whole(mate.at[x_from], z_mate, y_at, x_from, core_from)
            whole(beside.at[x_from], z_at, 1 - y_at, x_from, core_from)
        whole(half_z, z_half, y_at, x_at, core_from)
        whole(mirror_z, z_mirror, y_at, x_at, core_from)
        whole(half_x, z_half, y_at, 1 - x_at, core_from)
        whole(mirror_x, z_mirror, y_at, 1 - x_at, core_from)
        for j, z_from in enumerate((z_mate, z_half, z_mirror)):
            whole(beside_others.at[j], z_from, 1 - y_at, x_at, core_from)
            whole(beside_x.at[j], z_from, 1 - y_at, 1 - x_at, core_from)
    for copy in copies:
        copy.wait()


def pack_group(shards, units):
    packed = [
        shard if shard.ndim == 4 else pack_shard(shard, count)
        for shard, (count, _) in zip(shards, units)
    ]
    return jnp.concatenate(packed, axis=2)


def gather_plain(shards, units):
    whole = lax.all_gather(pack_group(shards, units), "dp", axis=0, tiled=False)
    results = []
    row = 0
    for count, depth in units:
        part = whole[:, :, :, row : row + count * depth]
        part = part.reshape(-1, 2, 2, count, depth, LANES).transpose(1, 3, 0, 2, 4, 5)
        results.append(part.reshape(2, count, -1, LANES))
        row += count * depth
    return results


def assemble(pieces, units):
    return call(
        functools.partial(assemble_kernel, units),
        [shape((2, count, 16 * depth, LANES)) for count, depth in units],
        [ANY] * 17,
        [pltpu.SemaphoreType.DMA((32 * len(units),))],
        mib=32,
        name="assemble",
    )(*pieces)


def shard_slots(z_at):
    return z_at, z_at + 1 - 2 * (z_at % 2), (z_at + 2) % 4, 3 - z_at


def sibling_grad_kernel(jobs, *refs):
    operands, out = refs[:-1], refs[-1]
    core_at = lax.axis_index("stream") % 2
    for left_at, right_at, lead, first, units, row, depth in jobs:
        left, right = operands[left_at], operands[right_at]
        right = right if lead is None else right.at[lead]
        for unit in range(units):
            start = (1 - core_at) * (units * LANES) + unit * LANES
            columns = right[:, pl.ds(pl.multiple_of(start, 128), LANES)]
            product = low(dot_first(left[...], columns))
            at = row + unit * depth
            out[:, :, at : at + depth] = product.reshape(8, 2, depth, LANES)


TO_X = ((2, False, False), (3, False, False), (2, True, False), (3, True, False))
TO_Y_A = ((0, False, True), (0, False, False), (1, False, True), (1, False, False))
TO_Y_B = ((2, False, True), (3, False, True))
TO_Z_A = ((1, True, True), (1, True, False))
TO_Z_B = ((2, True, True), (3, True, True))
OWN = ((0, True, True), (0, True, False))
PARTS = (TO_X, TO_Y_A, TO_Y_B, TO_Z_A, TO_Z_B, OWN)


def part_at(part):
    z_at, y_at, x_at, _ = place()
    slot, own_y, own_x = part
    return (
        shard_slots(z_at)[slot] * 2 + (y_at if own_y else 1 - y_at),
        x_at if own_x else 1 - x_at,
    )


def own_grad_kernel(jobs, *refs):
    outs, work = refs[-1 - len(PARTS) : -1], refs[-1]
    *operands, came = refs[: -1 - len(PARTS)]
    core_at = lax.axis_index("stream") % 2
    for left_at, right_at, lead, first, units, row, depth in jobs:
        left, right = operands[left_at], operands[right_at]
        right = right if lead is None else right.at[lead]
        for unit in range(units):
            start = core_at * (units * LANES) + unit * LANES
            columns = right[:, pl.ds(pl.multiple_of(start, 128), LANES)]
            at = row + unit * depth
            rows = slice(at, at + depth)
            product = dot_first(left[...], columns).reshape(8, 2, depth, LANES)
            work[:, :, :depth] = product + wide(came[:, :, rows])
            for out, parts in zip(outs, PARTS):
                for j, part in enumerate(parts):
                    dp_from, x_from = part_at(part)
                    out[j, rows] = low(work[dp_from, x_from, :depth])


def reduce_steps(to_x, to_y_a, to_y_b, to_z_a, to_z_b, own):
    from_x, from_y_a = yield [(to_x, "stream", ACROSS), (to_y_a, "dp", BESIDE)]
    from_y_b, mate = yield [
        (low(wide(to_y_b) + wide(from_x[:2])), "dp", BESIDE),
        (low(wide(to_z_a) + wide(from_y_a[2:])), "dp", PAIR),
    ]
    to_z = low(wide(to_z_b) + wide(from_x[2:]) + wide(from_y_b))
    half_z, mirror_z = yield [(to_z[0], "dp", HALFWAY), (to_z[1], "dp", MIRROR)]
    total = wide(own) + wide(from_y_a[:2]) + wide(mate)
    total = low(jnp.stack((total[0] + wide(half_z) + wide(mirror_z), total[1])))
    (from_x,) = yield [(total, "stream", ACROSS)]
    total = low(wide(total) + wide(from_x[::-1]))
    (other,) = yield [(total, "stream", CORE)]
    return total, other


def unpack_kernel(jobs, mine, other, *outs):
    _, _, x_at, core_at = place()
    for source, core_from in ((mine, core_at), (other, 1 - core_at)):
        for j in range(2):
            x_from = x_at if j == 0 else 1 - x_at
            for out_at, lead, units, row, depth in jobs:
                out = outs[out_at] if lead is None else outs[out_at].at[lead]
                for unit in range(units):
                    at = row + unit * depth
                    start = core_from * (units * LANES) + unit * LANES
                    out[
                        pl.ds(pl.multiple_of(x_from * depth, 8), depth),
                        pl.ds(pl.multiple_of(start, 128), LANES),
                    ] = wide(source[j, at : at + depth])


def reduce_plain(parts):
    shards = []
    for left, right in parts:
        if right.ndim == 2:
            whole = low(dot_first(left, right))
            own = lax.psum_scatter(whole, "dp", scatter_dimension=0, tiled=True)
        else:
            whole = low(jnp.stack([dot_first(left, r) for r in right]))
            own = lax.psum_scatter(whole, "dp", scatter_dimension=1, tiled=True)
        shards.append(wide(lax.psum(own, "stream")))
    return shards


class Group:
    def __init__(self, parts):
        self.operands, self.jobs, self.out_jobs, self.out_shapes = [], [], [], []
        self.rows, self.flops = 0, 0
        for left, right in parts:
            left_at, right_at = len(self.operands), len(self.operands) + 1
            self.operands += [left, right]
            depth = left.shape[1] // 16
            units = right.shape[-1] // (2 * LANES)
            for lead in [None] if right.ndim == 2 else range(right.shape[0]):
                self.jobs.append((left_at, right_at, lead, 0, units, self.rows, depth))
                self.out_jobs.append((len(self.out_shapes), lead, units, self.rows, depth))
                self.rows += units * depth
            self.out_shapes.append(
                shape((*right.shape[:-2], 2 * depth, right.shape[-1]), F32)
            )
            self.flops += left.shape[0] * left.shape[1] * right.size // right.shape[-2]

    def sibling(self, tie):
        self.sent = call(
            functools.partial(sibling_grad_kernel, self.jobs),
            shape((8, 2, self.rows, LANES)),
            [VMEM] * len(self.operands),
            flops=self.flops,
            name="sibling_grad",
        )(tie(self.operands[0]), *self.operands[1:])
        return self.sent

    def core_steps(self):
        (self.came,) = yield [(self.sent, "stream", CORE)]

    def own(self, tie, small=None):
        deepest = max(job[-1] for job in self.jobs)
        self.parts = call(
            functools.partial(own_grad_kernel, self.jobs),
            [shape((len(parts), self.rows, LANES)) for parts in PARTS],
            [VMEM] * (len(self.operands) + 1),
            [pltpu.VMEM((8, 2, deepest, LANES), F32)],
            flops=self.flops,
            name="own_grad",
        )(tie(self.operands[0]), *self.operands[1:], self.came)
        if small is not None:
            _, small_rows, part = small.shape
            both = jnp.pad(low(small), ((0, 0), (0, 2 * PAD_ROWS - small_rows), (0, LANES - part)))
            both = both.reshape(8, 2, PAD_ROWS, LANES)
            self.parts = [
                jnp.concatenate(
                    (made, jnp.stack([both[part_at(part)] for part in parts])), axis=1
                )
                for made, parts in zip(self.parts, PARTS)
            ]
        return self.parts

    def unpack(self, moved):
        return call(
            functools.partial(unpack_kernel, self.out_jobs),
            self.out_shapes,
            [VMEM, VMEM],
            name="unpack",
        )(*moved)

    def unpack_small(self, moved, small_rows, part):
        x_at = lax.axis_index("stream") // 2
        pieces = wide(moved[0][:, self.rows :]) + wide(moved[1][:, self.rows :])
        pieces = jnp.where(x_at == 0, pieces, pieces[::-1]).reshape(2 * PAD_ROWS, LANES)
        return pieces[:small_rows, :part]


def norm_parts(summed):
    center = summed - jnp.mean(summed, axis=-1, keepdims=True)
    inverse = lax.rsqrt(jnp.mean(center * center, axis=-1, keepdims=True) + EPSILON)
    return center * inverse, inverse


def norm_back(upstream, normed, inverse, gain):
    scaled = upstream * gain
    return inverse * (
        scaled
        - jnp.mean(scaled, axis=-1, keepdims=True)
        - normed * jnp.mean(scaled * normed, axis=-1, keepdims=True)
    )


def head_pair(two):
    first = lax.broadcasted_iota(jnp.int32, two.shape, 1) < 64
    return low(jnp.concatenate((jnp.where(first, two, 0.0), jnp.where(first, 0.0, two)), axis=0))


def join_pair(stacked):
    rows = stacked.shape[0] // 2
    first = lax.broadcasted_iota(jnp.int32, (rows, stacked.shape[1]), 1) < 64
    return jnp.where(first, stacked[:rows], stacked[rows:])


def softmax(scores):
    raised = jnp.exp(scores - jnp.max(scores, axis=-1, keepdims=True))
    return raised * (1.0 / jnp.sum(raised, axis=-1, keepdims=True))


def row_sum(value):
    return jnp.sum(value, axis=0, keepdims=True)


def self_kernel(seq, lengths, x_ref, w_ref, vec, qkv_ref, out_ref, q, k, v, o):
    tokens = x_ref.shape[0]
    for j, (scratch, bias) in enumerate(((q, B_Q), (k, None), (v, B_V))):
        for c in range(2):
            columns = slice(c * LANES, (c + 1) * LANES)
            made = dot(x_ref[...], w_ref[c, j])
            if bias is not None:
                made = made + vec[bias : bias + 1, columns]
            made = low(made)
            qkv_ref[j, :, columns] = made
            scratch[:, columns] = wide(made)

    def step(r, _):
        rows = pl.ds(pl.multiple_of(r * seq, 8), seq)
        valid = lax.broadcasted_iota(jnp.int32, (2 * seq, seq), 1) < lengths[r]
        for pair in range(HEADS // 2):
            columns = slice(pair * 128, (pair + 1) * 128)
            asked = head_pair(q[rows, columns] * 0.125)
            scores = dot_last(asked, low(k[rows, columns]))
            weight = softmax(jnp.where(valid, scores, -jnp.inf))
            o[rows, columns] = join_pair(dot(low(weight), low(v[rows, columns])))
        return 0

    lax.fori_loop(0, tokens // seq, step, 0)
    out_ref[...] = low(o[...])


def first_norm_kernel(seq, o_ref, x_ref, wso, wcq, vec, normed, inverse, h_low, qc, z):
    for c in range(2):
        columns = slice(c * LANES, (c + 1) * LANES)
        z[:, columns] = (
            dot(o_ref[...], wso[c, 0])
            + vec[B_SO : B_SO + 1, columns]
            + wide(x_ref[:, columns])
        )
    made, scale = norm_parts(z[...])
    normed[...] = made
    inverse[...] = scale
    h_low[...] = low(made * vec[G_1 : G_1 + 1] + vec[B_N1 : B_N1 + 1])
    for c in range(2):
        columns = slice(c * LANES, (c + 1) * LANES)
        qc[:, columns] = low(dot(h_low[...], wcq[c, 0]) + vec[B_CQ : B_CQ + 1, columns])


def image_kernel(y_ref, w_ref, vec, kv_ref):
    for m in range(y_ref.shape[0]):
        for c in range(2):
            columns = slice(c * LANES, (c + 1) * LANES)
            kv_ref[0, m, :, columns] = low(dot(y_ref[m], w_ref[c, 0]))
            kv_ref[1, m, :, columns] = low(
                dot(y_ref[m], w_ref[c, 1]) + vec[B_CV : B_CV + 1, columns]
            )


def fetch_images(held, kv, sems):
    copies = [
        pltpu.make_async_copy(image, kv.at[j], sems.at[j]) for j, image in enumerate(held)
    ]
    for copy in copies:
        copy.start()
    return copies


def cross_kernel(
    seq, patches, micro_rows, slots, qc, own, beside, across, apart, n1, wco, vec,
    oc, n2, inverse, h_low, kv, q, o, sems,
):
    copies = fetch_images((own, beside, across, apart), kv, sems)
    q[...] = wide(qc[...]) * 0.125
    for copy in copies:
        copy.wait()
    tokens = qc.shape[0]
    padded = kv.shape[3]
    there = lax.broadcasted_iota(jnp.int32, (2 * seq, padded), 1) < patches

    def step(r, _):
        rows = pl.ds(pl.multiple_of(r * seq, 8), seq)
        slot, m = slots[r], r // micro_rows
        for pair in range(HEADS // 2):
            columns = slice(pair * 128, (pair + 1) * 128)
            scores = dot_last(head_pair(q[rows, columns]), kv[slot, 0, m, :, columns])
            weight = softmax(jnp.where(there, scores, -jnp.inf))
            o[rows, columns] = join_pair(dot(low(weight), kv[slot, 1, m, :, columns]))
        return 0

    lax.fori_loop(0, tokens // seq, step, 0)
    oc[...] = low(o[...])
    for c in range(2):
        columns = slice(c * LANES, (c + 1) * LANES)
        first = n1[:, columns] * vec[G_1 : G_1 + 1, columns] + vec[B_N1 : B_N1 + 1, columns]
        o[:, columns] = first + dot(oc[...], wco[c, 0]) + vec[B_CO : B_CO + 1, columns]
    made, scale = norm_parts(o[...])
    n2[...] = made
    inverse[...] = scale
    h_low[...] = low(made * vec[G_2 : G_2 + 1] + vec[B_N2 : B_N2 + 1])


def hidden_kernel(h_low, w_ref, bias, active, slope):
    i = pl.program_id(0)
    pre = dot(h_low[...], w_ref[0, 0]) + bias[pl.ds(i, 1), :]
    cumulative = 0.5 * (1.0 + lax.erf(pre * ROOT_HALF))
    active[...] = low(pre * cumulative)
    slope[...] = low(cumulative + pre * INV_ROOT_TAU * jnp.exp(-0.5 * pre * pre))


def last_norm_kernel(
    seq, lengths, g_ref, w_ref, n2, cot, vec, out, dz, df, rows_out, total
):
    i = pl.program_id(0)

    @pl.when(i == 0)
    def _():
        total[...] = jnp.zeros_like(total)

    for c in range(2):
        columns = slice(c * LANES, (c + 1) * LANES)
        total[:, columns] += dot(g_ref[...], w_ref[c, 0])

    @pl.when(i == pl.num_programs(0) - 1)
    def _():
        def step(r, sums):
            rows = pl.ds(pl.multiple_of(r * seq, 8), seq)
            second = n2[rows, :] * vec[G_2 : G_2 + 1] + vec[B_N2 : B_N2 + 1]
            made, scale = norm_parts(second + total[rows, :] + vec[B_FO : B_FO + 1])
            out[r] = low(made * vec[G_3 : G_3 + 1] + vec[B_N3 : B_N3 + 1])
            valid = lax.broadcasted_iota(jnp.int32, made.shape, 0) < lengths[r]
            upstream = jnp.where(valid, wide(cot[r]), 0.0)
            back = norm_back(upstream, made, scale, vec[G_3 : G_3 + 1])
            dz[rows, :] = back
            gain, shift, lowered = sums
            return (
                gain + row_sum(upstream * made),
                shift + row_sum(upstream),
                lowered + row_sum(wide(low(back))),
            )

        zero = jnp.zeros((1, total.shape[1]), F32)
        gain, shift, lowered = lax.fori_loop(0, out.shape[0], step, (zero, zero, zero))
        df[...] = low(dz[...])
        rows_out[0:1] = gain
        rows_out[1:2] = shift
        rows_out[2:3] = lowered
        rows_out[3:8] = jnp.zeros((5, total.shape[1]), F32)


def norm_back_rows(total, dz_ref, normed, inverse, gain, dz, low_ref, rows_out, step_rows):
    def step(r, sums):
        rows = pl.ds(pl.multiple_of(r * step_rows, 8), step_rows)
        upstream = total[rows, :] + dz_ref[rows, :]
        made = normed[rows, :]
        back = norm_back(upstream, made, inverse[rows, :], gain)
        dz[rows, :] = back
        return (
            sums[0] + row_sum(upstream * made),
            sums[1] + row_sum(upstream),
            sums[2] + row_sum(wide(low(back))),
        )

    zero = jnp.zeros((1, total.shape[1]), F32)
    sums = lax.fori_loop(0, total.shape[0] // step_rows, step, (zero, zero, zero))
    low_ref[...] = low(dz[...])
    for j in range(3):
        rows_out[j : j + 1] = sums[j]
    rows_out[3:8] = jnp.zeros((5, total.shape[1]), F32)


def hidden_back_kernel(
    seq, df, wout, win, slope, dz3, n2, inverse, vec, du, bias_out, dz2, dac, rows_out, total
):
    i = pl.program_id(0)

    @pl.when(i == 0)
    def _():
        total[...] = jnp.zeros_like(total)

    raw = dot_last(df[:, :LANES], wout[0, 0]) + dot_last(df[:, LANES:], wout[1, 0])
    made = low(raw * wide(slope[...]))
    du[...] = made
    bias_out[pl.ds(i, 1), :] = row_sum(wide(made))
    total[...] += dot_last(made, win[0, 0])

    @pl.when(i == pl.num_programs(0) - 1)
    def _():
        norm_back_rows(
            total, dz3, n2, inverse, vec[G_2 : G_2 + 1], dz2, dac, rows_out, seq
        )


def cross_back_kernel(
    seq, patches, micro_rows, slots, dac, qc, own, beside, across, apart, wco,
    dqc, dkv_out, kv, dkv, q, do, dq, sems,
):
    copies = fetch_images((own, beside, across, apart), kv, sems)
    q[...] = wide(qc[...]) * 0.125
    do[...] = wide(
        low(dot_last(dac[:, :LANES], wco[0, 0]) + dot_last(dac[:, LANES:], wco[1, 0]))
    )
    dkv[...] = jnp.zeros_like(dkv)
    for copy in copies:
        copy.wait()
    tokens = qc.shape[0]
    padded = kv.shape[3]
    there = lax.broadcasted_iota(jnp.int32, (2 * seq, padded), 1) < patches

    def step(r, _):
        rows = pl.ds(pl.multiple_of(r * seq, 8), seq)
        slot, m = slots[r], r // micro_rows
        for pair in range(HEADS // 2):
            columns = slice(pair * 128, (pair + 1) * 128)
            asked, came = head_pair(q[rows, columns]), head_pair(do[rows, columns])
            keys, values = kv[slot, 0, m, :, columns], kv[slot, 1, m, :, columns]
            weight = softmax(jnp.where(there, dot_last(asked, keys), -jnp.inf))
            back = dot_last(came, values)
            back = low(weight * (back - jnp.sum(back * weight, axis=-1, keepdims=True)))
            dq[rows, columns] = join_pair(dot(back, keys)) * 0.125
            dkv[slot, 0, m, :, columns] += dot_first(back, asked)
            dkv[slot, 1, m, :, columns] += dot_first(low(weight), came)
        return 0

    lax.fori_loop(0, tokens // seq, step, 0)
    dqc[...] = low(dq[...])
    dkv_out[...] = low(dkv[...])


def first_back_kernel(seq, dqc, wcq, dz2, n1, inverse, vec, dz1, da, rows_out, total):
    total[...] = dot_last(dqc[:, :LANES], wcq[0, 0]) + dot_last(dqc[:, LANES:], wcq[1, 0])
    norm_back_rows(total, dz2, n1, inverse, vec[G_1 : G_1 + 1], dz1, da, rows_out, seq)
    rows_out[3:4] = row_sum(wide(dqc[...]))


def self_back_kernel(seq, lengths, da, qkv, wso, dqkv, rows_out, q, k, v, do, dq, dk, dv):
    q[...] = wide(qkv[0]) * 0.125
    k[...] = wide(qkv[1])
    v[...] = wide(qkv[2])
    do[...] = wide(low(dot_last(da[:, :LANES], wso[0, 0]) + dot_last(da[:, LANES:], wso[1, 0])))
    tokens = da.shape[0]

    def step(r, _):
        rows = pl.ds(pl.multiple_of(r * seq, 8), seq)
        valid = lax.broadcasted_iota(jnp.int32, (2 * seq, seq), 1) < lengths[r]
        for pair in range(HEADS // 2):
            columns = slice(pair * 128, (pair + 1) * 128)
            asked, came = head_pair(q[rows, columns]), head_pair(do[rows, columns])
            keys, values = low(k[rows, columns]), low(v[rows, columns])
            weight = softmax(jnp.where(valid, dot_last(asked, keys), -jnp.inf))
            back = dot_last(came, values)
            back = low(weight * (back - jnp.sum(back * weight, axis=-1, keepdims=True)))
            dq[rows, columns] = join_pair(dot(back, keys)) * 0.125
            dk[rows, columns] = dot_first(back, asked)
            dv[rows, columns] = dot_first(low(weight), came)
        return 0

    lax.fori_loop(0, tokens // seq, step, 0)
    for j, made in enumerate((dq, dk, dv)):
        dqkv[j] = low(made[...])
    rows_out[0:1] = row_sum(wide(dqkv[0]))
    rows_out[1:2] = row_sum(wide(dqkv[2]))
    rows_out[2:8] = jnp.zeros((6, q.shape[1]), F32)


def text_grad_kernel(dz1, dqkv, w_ref, out, total):
    total[...] = dz1[...]
    for j in range(3):
        for c in range(2):
            total[...] += dot_last(dqkv[j, :, c * LANES : (c + 1) * LANES], w_ref[c, j])
    seq = out.shape[1]
    for r in range(out.shape[0]):
        out[r] = low(total[r * seq : (r + 1) * seq, :])


def patch_grad_kernel(mine, came, w_ref, dkv, out, rows_out):
    padded = mine.shape[2]
    images = mine.shape[1]
    for j in range(2):
        for m in range(images):
            dkv[j, m * padded : (m + 1) * padded] = low(wide(mine[j, m]) + wide(came[j, m]))
    for m in range(images):
        rows = slice(m * padded, (m + 1) * padded)
        made = None
        for j in range(2):
            for c in range(2):
                term = dot_last(dkv[j, rows, c * LANES : (c + 1) * LANES], w_ref[c, j])
                made = term if made is None else made + term
        out[m] = low(made)[: out.shape[1]]
    rows_out[0:1] = row_sum(wide(dkv[1]))
    rows_out[1:8] = jnp.zeros((7, rows_out.shape[1]), F32)


def on_device(
    text_input,
    patch_input,
    text_lengths,
    image_of_row,
    cotangent,
    self_qkv,
    self_out,
    cross_q,
    cross_kv,
    cross_out,
    ffn_in,
    ffn_out,
    biases,
    norm_gains,
    ffn_bias,
):
    dp = lax.axis_size("dp")
    micros, row_count, seq, width = text_input.shape
    patches, patch_width = patch_input.shape[2:]
    rows_all = micros * row_count
    tokens = rows_all * seq
    hidden = ffn_in.shape[1]
    padded = -(-patches // 16) * 16
    images = micros * patch_input.shape[1]

    part = biases.shape[1]
    small = jnp.concatenate((biases, norm_gains, ffn_bias.reshape(-1, part)))
    small_rows = small.shape[0]
    wide_rows = biases.shape[0] + norm_gains.shape[0]
    small = jnp.pad(small, ((0, 2 * PAD_ROWS - small_rows), (0, LANES - part)))
    small = jnp.broadcast_to(small.reshape(2, PAD_ROWS, LANES), (2, 2, PAD_ROWS, LANES))

    half = width // dp // 2
    half_v = cross_kv.shape[1] // 2
    half_f = ffn_out.shape[0] // 2
    in_units = hidden // (2 * LANES)
    weight_groups = (
        ((cross_kv, small), ((2, half_v), (1, PAD_ROWS))),
        ((self_qkv, self_out, cross_q), ((3, half), (1, half), (1, half))),
        ((cross_out, ffn_in), ((1, half), (in_units, half))),
        ((ffn_out,), ((1, half_f),)),
    )

    text = text_input.reshape(tokens, width)
    pixels = jnp.pad(
        patch_input.reshape(images, patches, patch_width), ((0, 0), (0, padded - patches), (0, 0))
    )
    lengths = text_lengths.reshape(-1)
    slots = image_of_row.reshape(-1) ^ lax.axis_index("stream")
    flat = (tokens, width)
    full = pltpu.VMEM(flat, F32)
    flops = 2 * tokens * width * width
    steps = hidden // LANES
    chunks = hidden // width
    kv_all = pltpu.VMEM((4, 2, images, padded, width), jnp.bfloat16)
    v = {}

    def small_parts(whole):
        values = wide(whole[0, 0].reshape(dp, 2 * PAD_ROWS, LANES)[:, :small_rows, :part])
        vec = values[:, :wide_rows].transpose(1, 0, 2).reshape(wide_rows, width)
        v["vec"] = jnp.pad(vec, ((0, 16 - wide_rows), (0, 0)))
        v["hidden_bias"] = values[:, wide_rows:].reshape(-1, LANES)

    def run_image(tie):
        v["own_kv"] = call(
            image_kernel,
            shape((2, images, padded, width)),
            [VMEM] * 3,
            flops=4 * flops,
            name="image_kv",
        )(tie(pixels), v["w_kv"], v["vec"])
        return v["own_kv"]

    def image_steps():
        v["beside_kv"], v["across_kv"] = yield [
            (v["own_kv"], "stream", CORE),
            (v["own_kv"], "stream", ACROSS),
        ]
        (v["apart_kv"],) = yield [(v["across_kv"], "stream", CORE)]

    def run_self(tie):
        v["qkv"], v["attended"] = call(
            functools.partial(self_kernel, seq),
            [shape((3, *flat)), shape(flat)],
            [SMEM, VMEM, VMEM, VMEM],
            [full] * 4,
            flops=4 * flops,
            name="self_attention",
        )(lengths, tie(text), v["w_qkv"], v["vec"])
        return v["attended"]

    def run_first(tie):
        v["n1"], v["inverse1"], v["h1"], v["qc"] = call(
            functools.partial(first_norm_kernel, seq),
            [shape(flat, F32), shape((tokens, 1), F32), shape(flat), shape(flat)],
            [VMEM] * 5,
            [full],
            flops=2 * flops,
            name="first_norm",
        )(v["attended"], tie(text), v["w_so"], v["w_cq"], v["vec"])
        return v["qc"]

    def held_images():
        return v["own_kv"], v["beside_kv"], v["across_kv"], v["apart_kv"]

    def run_cross(tie):
        v["oc"], v["n2"], v["inverse2"], v["h2"] = call(
            functools.partial(cross_kernel, seq, patches, row_count),
            [shape(flat), shape(flat, F32), shape((tokens, 1), F32), shape(flat)],
            [SMEM, VMEM, ANY, ANY, ANY, ANY, VMEM, VMEM, VMEM],
            [kv_all, full, full, pltpu.SemaphoreType.DMA((4,))],
            flops=2 * flops,
            name="cross_attention",
        )(slots, tie(v["qc"]), *held_images(), v["n1"], v["w_co"], v["vec"])
        return v["h2"]

    def run_hidden(tie):
        v["active"], v["slope"] = call(
            hidden_kernel,
            [shape((tokens, hidden)), shape((tokens, hidden))],
            [
                VMEM,
                pl.BlockSpec((1, 1, width, LANES), lambda i: (i // in_units, i % in_units, 0, 0)),
                VMEM,
            ],
            out_specs=[pl.BlockSpec((tokens, LANES), lambda i: (0, i))] * 2,
            grid=(steps,),
            flops=4 * flops,
            name="hidden",
        )(tie(v["h2"]), v["w_in"], v["hidden_bias"])
        return v["active"]

    def run_last(tie):
        v["out_rows"], v["dz3"], v["df"], v["sums3"] = call(
            functools.partial(last_norm_kernel, seq),
            [shape((rows_all, seq, width)), shape(flat, F32), shape(flat), shape((8, width), F32)],
            [
                SMEM,
                pl.BlockSpec((tokens, width), lambda i: (0, i)),
                pl.BlockSpec((2, 1, width, LANES), lambda i: (0, 0, i, 0)),
                VMEM,
                VMEM,
                VMEM,
            ],
            [full],
            grid=(chunks,),
            flops=4 * flops,
            name="last_norm",
        )(
            lengths, tie(v["active"]), v["w_out"], v["n2"],
            cotangent.reshape(rows_all, seq, width), v["vec"],
        )
        return v["df"]

    def run_hidden_back(tie):
        v["du"], v["hidden_bias_grad"], v["dz2"], v["dac"], v["sums2"] = call(
            functools.partial(hidden_back_kernel, seq),
            [
                shape((tokens, hidden)),
                shape((steps, LANES), F32),
                shape(flat, F32),
                shape(flat),
                shape((8, width), F32),
            ],
            [
                VMEM,
                pl.BlockSpec((2, 1, LANES, LANES), lambda i: (0, 0, i, 0)),
                pl.BlockSpec((1, 1, width, LANES), lambda i: (i // in_units, i % in_units, 0, 0)),
                pl.BlockSpec((tokens, LANES), lambda i: (0, i)),
                VMEM,
                VMEM,
                VMEM,
                VMEM,
            ],
            [full],
            out_specs=[pl.BlockSpec((tokens, LANES), lambda i: (0, i)), VMEM, VMEM, VMEM, VMEM],
            grid=(steps,),
            flops=8 * flops,
            name="hidden_back",
        )(
            tie(v["df"]), v["w_out"], v["w_in"], v["slope"], v["dz3"], v["n2"], v["inverse2"],
            v["vec"],
        )
        return v["dac"]

    def run_cross_back(tie):
        v["dqc"], v["dkv_all"] = call(
            functools.partial(cross_back_kernel, seq, patches, row_count),
            [shape(flat), shape((4, 2, images, padded, width))],
            [SMEM, VMEM, VMEM, ANY, ANY, ANY, ANY, VMEM],
            [
                kv_all,
                pltpu.VMEM((4, 2, images, padded, width), F32),
                full,
                full,
                full,
                pltpu.SemaphoreType.DMA((4,)),
            ],
            flops=4 * flops,
            mib=56,
            name="cross_back",
        )(slots, tie(v["dac"]), v["qc"], *held_images(), v["w_co"])
        return v["dqc"]

    def image_back_steps():
        dkv = v["dkv_all"]
        near, far = yield [(dkv[1], "stream", CORE), (dkv[3], "stream", CORE)]
        (across,) = yield [(low(wide(dkv[2]) + wide(far)), "stream", ACROSS)]
        v["mine_kv"] = low(wide(dkv[0]) + wide(near))
        v["came_kv"] = across

    def run_first_back(tie):
        v["dz1"], v["da"], v["sums1"] = call(
            functools.partial(first_back_kernel, seq),
            [shape(flat, F32), shape(flat), shape((8, width), F32)],
            [VMEM] * 6,
            [full],
            flops=flops,
            name="first_back",
        )(tie(v["dqc"]), v["w_cq"], v["dz2"], v["n1"], v["inverse1"], v["vec"])
        return v["da"]

    def run_self_back(tie):
        v["dqkv"], v["sums0"] = call(
            functools.partial(self_back_kernel, seq),
            [shape((3, *flat)), shape((8, width), F32)],
            [SMEM, VMEM, VMEM, VMEM],
            [full] * 7,
            flops=4 * flops,
            name="self_back",
        )(lengths, tie(v["da"]), v["qkv"], v["w_so"])
        return v["dqkv"]

    def run_patch_grad(tie):
        v["dkv"], v["patch_rows"], v["sums_kv"] = call(
            patch_grad_kernel,
            [
                shape((2, images * padded, width)),
                shape((images, patches, patch_width)),
                shape((8, width), F32),
            ],
            [VMEM] * 3,
            flops=4 * flops,
            name="patch_grad",
        )(tie(v["mine_kv"]), v["came_kv"], v["w_kv"])
        return v["dkv"]

    def run_text_grad(tie):
        v["text_rows"] = call(
            text_grad_kernel,
            shape((rows_all, seq, width)),
            [VMEM] * 3,
            [full],
            flops=3 * flops,
            name="text_grad",
        )(tie(v["dz1"]), v["dqkv"], v["w_qkv"])
        return v["text_rows"]

    def small_grads():
        sums0, sums1, sums2, sums3, sums_kv = (
            v[name] for name in ("sums0", "sums1", "sums2", "sums3", "sums_kv")
        )
        grads = jnp.concatenate(
            (
                sums0[0:2], sums1[2:3], sums1[1:2], sums1[3:4], sums_kv[0:1], sums2[2:3],
                sums2[1:2], sums3[2:3], sums3[1:2], sums1[0:1], sums2[0:1], sums3[0:1],
            )
        )
        return jnp.concatenate(
            (
                grads.reshape(wide_rows, dp, part).transpose(1, 0, 2),
                v["hidden_bias_grad"].reshape(dp, -1, part),
            ),
            axis=1,
        )

    def run_all(moves):
        mover = Mover(moves)
        while not mover.done:
            mover.give([lax.ppermute(array, axis, hops) for array, axis, hops in mover.requests])

    pixels_flat = pixels.reshape(images * padded, patch_width)
    if not special_mesh():
        def free(array):
            return array

        (v["w_kv"], w_small), (v["w_qkv"], v["w_so"], v["w_cq"]), (v["w_co"], v["w_in"]), (v["w_out"],) = [
            gather_plain(shards, units) for shards, units in weight_groups
        ]
        small_parts(w_small)
        run_image(free)
        run_all(image_steps())
        for work in (
            run_self, run_first, run_cross, run_hidden, run_last, run_hidden_back, run_cross_back
        ):
            work(free)
        run_all(image_back_steps())
        for work in (run_first_back, run_self_back, run_patch_grad, run_text_grad):
            work(free)
        s_out, s_in, s_co, s_cq, s_so, s_kv, s_qkv = reduce_plain(
            (
                (v["active"], v["df"]), (v["h2"], v["du"]), (v["oc"], v["dac"]), (v["h1"], v["dqc"]),
                (v["attended"], v["da"]), (pixels_flat, v["dkv"]), (text, v["dqkv"]),
            )
        )
        s_small = lax.psum_scatter(low(small_grads()), "dp", scatter_dimension=0, tiled=True)
        s_small = wide(lax.psum(s_small, "stream"))[0]
    else:
        clock = Clock()
        movers = [Mover(gather_steps(pack_group(*group))) for group in weight_groups]
        g_a, g_b, g_c, g_d = movers

        def build(index, names):
            def work(tie):
                pieces, units = movers[index].result, weight_groups[index][1]
                made = assemble((tie(pieces[0]), *pieces[1:]), units)
                v.update(zip(names, made))
                return made[0]
            return work

        clock.step([g_a])
        clock.step([g_a, g_b])
        clock.step([g_a, g_b, g_c])
        clock.step([g_a, g_b, g_c, g_d])
        def first_images(tie):
            made = build(0, ("w_kv", "w_small"))(tie)
            small_parts(v["w_small"])
            return run_image(tie)
        clock.step([g_b, g_c, g_d], [first_images])
        images_move = Mover(image_steps())
        clock.step([images_move, g_c, g_d], [build(1, ("w_qkv", "w_so", "w_cq")), run_self])
        clock.step([images_move, g_d], [run_first, build(2, ("w_co", "w_in"))])
        clock.step([], [run_cross, build(3, ("w_out",))])
        clock.step([], [run_hidden])
        clock.step([], [run_last])

        group_out = Group(((v["active"], v["df"]),))
        clock.step([], [group_out.sibling])
        core_out = Mover(group_out.core_steps())
        clock.step([core_out], [run_hidden_back])
        group_in = Group(((v["h2"], v["du"]),))
        clock.step([], [group_out.own, group_in.sibling])
        move_out, core_in = Mover(reduce_steps(*group_out.parts)), Mover(group_in.core_steps())
        clock.step([move_out, core_in], [run_cross_back])
        images_back = Mover(image_back_steps())
        clock.step([move_out, images_back], [group_in.own, run_first_back])
        group_mid = Group(
            ((v["oc"], v["dac"]), (v["h1"], v["dqc"]), (v["attended"], v["da"]))
        )
        move_in = Mover(reduce_steps(*group_in.parts))
        clock.step([move_out, images_back, move_in], [group_mid.sibling])
        core_mid = Mover(group_mid.core_steps())
        clock.step([move_out, move_in, core_mid], [run_patch_grad, run_self_back])
        group_kv = Group(((pixels_flat, v["dkv"]),))
        group_qkv = Group(((text, v["dqkv"]),))
        clock.step([move_out, move_in], [group_mid.own, group_qkv.sibling, group_kv.sibling])
        move_mid = Mover(reduce_steps(*group_mid.parts))
        core_qkv, core_kv = Mover(group_qkv.core_steps()), Mover(group_kv.core_steps())
        clock.step([move_in, move_mid, core_qkv, core_kv])
        clock.step(
            [move_in, move_mid],
            [lambda tie: group_qkv.own(tie, small_grads()), group_kv.own],
        )
        move_qkv, move_kv = Mover(reduce_steps(*group_qkv.parts)), Mover(reduce_steps(*group_kv.parts))
        last = [move_mid, move_kv, move_qkv]
        clock.step(last, [run_text_grad])
        while not all(mover.done for mover in last):
            clock.step(last)
        (s_out,) = group_out.unpack(move_out.result)
        (s_in,) = group_in.unpack(move_in.result)
        s_co, s_cq, s_so = group_mid.unpack(move_mid.result)
        (s_kv,) = group_kv.unpack(move_kv.result)
        (s_qkv,) = group_qkv.unpack(move_qkv.result)
        s_small = group_qkv.unpack_small(move_qkv.result, small_rows, part)
    return (
        v["out_rows"].reshape(text_input.shape),
        v["text_rows"].reshape(text_input.shape),
        v["patch_rows"].reshape(patch_input.shape),
        s_qkv,
        s_so,
        s_cq,
        s_kv,
        s_co,
        s_in,
        s_out,
        s_small[: biases.shape[0]],
        s_small[biases.shape[0] : wide_rows],
        s_small[wide_rows:].reshape(-1),
    )


def solution(mesh):
    placed = (
        P(None, ("dp", "stream"), None, None),
        P(None, ("dp", "stream"), None, None),
        P(None, ("dp", "stream")),
        P(None, ("dp", "stream")),
        P(None, ("dp", "stream"), None, None),
        P(None, "dp", None),
        P("dp", None),
        P("dp", None),
        P(None, "dp", None),
        P("dp", None),
        P("dp", None),
        P("dp", None),
        P(None, "dp"),
        P(None, "dp"),
        P("dp"),
    )
    return jax.shard_map(
        on_device,
        mesh=mesh,
        in_specs=placed,
        out_specs=(
            P(None, ("dp", "stream"), None, None),
            P(None, ("dp", "stream"), None, None),
            P(None, ("dp", "stream"), None, None),
            P(None, "dp", None),
            P("dp", None),
            P("dp", None),
            P(None, "dp", None),
            P("dp", None),
            P("dp", None),
            P("dp", None),
            P(None, "dp"),
            P(None, "dp"),
            P("dp"),
        ),
        check_vma=False,
    )
```

```python
import functools
import types

import jax
import jax.numpy as jnp
from jax import lax
from jax.experimental import pallas as pl
from jax.experimental.pallas import tpu as pltpu
from jax.sharding import PartitionSpec as P

HEADS = 12
LANES = 384
PAD_ROWS = 16
MIB = 2**20
DP, STREAM = "dp", "stream"

EPSILON = 1e-06
ROOT_HALF = 0.7071067811865476
INV_ROOT_TAU = 0.3989422804014327

CORE = ((0, 1), (1, 0), (2, 3), (3, 2))
ACROSS = ((0, 2), (2, 0), (1, 3), (3, 1))
BESIDE = ((0, 1), (1, 0), (2, 3), (3, 2), (4, 5), (5, 4), (6, 7), (7, 6))
PAIR = ((0, 2), (2, 0), (1, 3), (3, 1), (4, 6), (6, 4), (5, 7), (7, 5))
HALFWAY = ((0, 4), (4, 0), (1, 5), (5, 1), (2, 6), (6, 2), (3, 7), (7, 3))
MIRROR = ((0, 6), (6, 0), (1, 7), (7, 1), (2, 4), (4, 2), (3, 5), (5, 3))

B_Q, B_V, B_SO, B_N1, B_CQ, B_CV, B_CO, B_N2, B_FO, B_N3, G_1, G_2, G_3 = range(13)


def low(value):
    return value.astype(jnp.bfloat16)


def wide(value):
    return value.astype(jnp.float32)


def dot(left, right):
    return jnp.dot(left, right, preferred_element_type=jnp.float32)


def dot_last(left, right):
    return lax.dot_general(
        left, right, (((1,), (1,)), ((), ())), preferred_element_type=jnp.float32
    )


def dot_first(left, right):
    return lax.dot_general(
        left, right, (((0,), (0,)), ((), ())), preferred_element_type=jnp.float32
    )


def pick(array, index, axis=0):
    return lax.dynamic_index_in_dim(array, index, axis, keepdims=False)


def place():
    dp_at, stream_at = lax.axis_index(DP), lax.axis_index(STREAM)
    return dp_at // 2, dp_at % 2, stream_at // 2, stream_at % 2


class Clock:
    def __init__(self):
        self.before = []
        self.waiting = {}

    def step(self, moving=(), compute=()):
        asked = []
        for mover in moving:
            if mover.done:
                continue
            asked.append((mover, mover.requests))
        operands = [[operand for operand, _, _ in requests] for _, requests in asked]
        operands, self.before = lax.optimization_barrier((operands, self.before))
        after = []
        for (mover, requests), arrays in zip(asked, operands):
            came = [
                lax.ppermute(array, axis, hops)
                for array, (_, axis, hops) in zip(arrays, requests)
            ]
            mover.give(came)
            after += came
        for work in compute:
            after += jax.tree.leaves(work(self.tie))
        self.before = after

    def tie(self, array):
        return lax.optimization_barrier((array, self.before))[0]


class Mover:
    def __init__(self, steps):
        self.steps = steps
        self.done = False
        self.result = None
        self.requests = next(steps)

    def give(self, came):
        try:
            self.requests = self.steps.send(came)
        except StopIteration as stop:
            self.done, self.result = True, stop.value


def special_mesh():
    return lax.axis_size(DP) == 8 and lax.axis_size(STREAM) == 4


VMEM = pl.BlockSpec(memory_space=pltpu.VMEM)
SMEM = pl.BlockSpec(memory_space=pltpu.SMEM)
ANY = pl.BlockSpec(memory_space=pl.ANY)


def call(kernel, out_shape, in_specs, scratch=(), mib=24, flops=0, out_specs=None, **more):
    return pl.pallas_call(
        kernel,
        out_shape=out_shape,
        in_specs=in_specs,
        out_specs=jax.tree.map(lambda _: VMEM, out_shape) if out_specs is None else out_specs,
        scratch_shapes=list(scratch),
        compiler_params=pltpu.CompilerParams(vmem_limit_bytes=mib * MIB),
        cost_estimate=pl.CostEstimate(flops=flops, bytes_accessed=4 * MIB, transcendentals=0),
        **more,
    )


def shape(dims, dtype=jnp.bfloat16):
    return jax.ShapeDtypeStruct(tuple(dims), dtype)


F32 = jnp.float32


def pack_shard(shard, units):
    if shard.ndim == 2:
        rows, _ = shard.shape
        split = shard.reshape(2, rows // 2, 2, units, LANES).transpose(2, 0, 3, 1, 4)
    else:
        _, rows, _ = shard.shape
        split = shard.reshape(units, 2, rows // 2, 2, LANES).transpose(3, 1, 0, 2, 4)
    return split.reshape(2, 2, units * rows // 2, LANES)


def pack_kernel(units, *refs):
    _, _, x_at, core_at = place()
    shards, (both, own, own_x) = refs[: len(units)], refs[len(units) :]
    row = 0
    for shard, (count, depth) in zip(shards, units):
        if len(shard.shape) == 4:
            both[:, :, row : row + depth] = shard[...]
            row += depth
            continue
        for unit in range(count):
            rows = slice(row, row + depth)
            for x in range(2):
                for c in range(2):
                    if len(shard.shape) == 3:
                        block = shard[unit, x * depth : (x + 1) * depth, c * LANES : (c + 1) * LANES]
                    else:
                        start = (c * count + unit) * LANES
                        block = shard[x * depth : (x + 1) * depth, start : start + LANES]
                    both[c, x, rows] = block
            row += depth
    own[...] = both[core_at]
    own_x[...] = both[core_at, x_at]


def pack_own_kernel(units, *refs):
    _, _, x_at, core_at = place()
    shards, out = refs[:-1], refs[-1]
    row = 0
    for shard, (count, depth) in zip(shards, units):
        for unit in range(count):
            start = (core_at * count + unit) * LANES
            out[row : row + depth] = shard[
                pl.ds(pl.multiple_of(x_at * depth, 16), depth),
                pl.ds(pl.multiple_of(start, 128), LANES),
            ]
            row += depth


def pack_group(shards, units):
    rows = sum(count * depth for count, depth in units)
    return call(
        functools.partial(pack_kernel, units),
        [shape((2, 2, rows, LANES)), shape((2, rows, LANES)), shape((rows, LANES))],
        [VMEM] * len(shards),
    )(*shards)


def pack_own(shards, units):
    rows = sum(count * depth for count, depth in units)
    return call(
        functools.partial(pack_own_kernel, units), shape((rows, LANES)), [VMEM] * len(shards)
    )(*shards)


def gather_steps(own_both, own, own_x):
    x_at = lax.axis_index(STREAM) // 2
    mate, half_z, mirror_z, beside = yield [
        (own, DP, PAIR),
        (own_x, DP, HALFWAY),
        (own_x, DP, MIRROR),
        (own, DP, BESIDE),
    ]
    others = jnp.stack((pick(mate, x_at), half_z, mirror_z))
    beside_others, half_x, mirror_x, *core_a = yield [
        (others, DP, BESIDE),
        (half_z, STREAM, ACROSS),
        (mirror_z, STREAM, ACROSS),
        (mate, STREAM, CORE),
        (half_z, STREAM, CORE),
        (mirror_z, STREAM, CORE),
        (beside, STREAM, CORE),
    ]
    beside_x, *core_b = yield [
        (beside_others, STREAM, ACROSS),
        (half_x, STREAM, CORE),
        (mirror_x, STREAM, CORE),
        (beside_others, STREAM, CORE),
    ]
    core_c = yield [(beside_x, STREAM, CORE)]
    mine = (mate, half_z, mirror_z, beside, half_x, mirror_x, beside_others, beside_x)
    return (own_both, *mine, *core_a, *core_b, *core_c)


def assemble_kernel(units, *refs):
    n_out = len(units)
    own_both, *pieces = refs[:17]
    outs = refs[17 : 17 + n_out]
    sems = refs[17 + n_out]
    z_at, y_at, x_at, core_at = place()
    copies = []

    def whole(piece, z_from, y_from, x_from, core_from):
        row = 0
        for (count, depth), out in zip(units, outs):
            start = (z_from * 2 + y_from) * (2 * depth) + x_from * depth
            copies.append(
                pltpu.make_async_copy(
                    piece.at[pl.ds(row, count * depth)].reshape(count, depth, LANES),
                    out.at[core_from, :, pl.ds(pl.multiple_of(start, 16), depth)],
                    sems.at[len(copies)],
                )
            )
            copies[-1].start()
            row += count * depth

    for core_from in range(2):
        for x_from in range(2):
            whole(own_both.at[core_from, x_from], z_at, y_at, x_from, core_from)
    _, z_mate, z_half, z_mirror = shard_slots(z_at)
    for group, core_from in ((pieces[:8], core_at), (pieces[8:], 1 - core_at)):
        mate, half_z, mirror_z, beside, half_x, mirror_x, beside_others, beside_x = group
        for x_from in range(2):
            whole(mate.at[x_from], z_mate, y_at, x_from, core_from)
            whole(beside.at[x_from], z_at, 1 - y_at, x_from, core_from)
        whole(half_z, z_half, y_at, x_at, core_from)
        whole(mirror_z, z_mirror, y_at, x_at, core_from)
        whole(half_x, z_half, y_at, 1 - x_at, core_from)
        whole(mirror_x, z_mirror, y_at, 1 - x_at, core_from)
        for j, z_from in enumerate((z_mate, z_half, z_mirror)):
            whole(beside_others.at[j], z_from, 1 - y_at, x_at, core_from)
            whole(beside_x.at[j], z_from, 1 - y_at, 1 - x_at, core_from)
    for copy in copies:
        copy.wait()


def gather_plain(shards, units):
    packed = [
        shard if shard.ndim == 4 else pack_shard(shard, count)
        for shard, (count, _) in zip(shards, units)
    ]
    whole = lax.all_gather(jnp.concatenate(packed, axis=2), DP, axis=0, tiled=False)
    results = []
    row = 0
    for count, depth in units:
        part = whole[:, :, :, row : row + count * depth]
        part = part.reshape(-1, 2, 2, count, depth, LANES).transpose(1, 3, 0, 2, 4, 5)
        results.append(part.reshape(2, count, -1, LANES))
        row += count * depth
    return results


def assemble(pieces, units):
    return call(
        functools.partial(assemble_kernel, units),
        [shape((2, count, 16 * depth, LANES)) for count, depth in units],
        [ANY] * 17,
        [pltpu.SemaphoreType.DMA((32 * len(units),))],
        mib=24,
    )(*pieces)


def shard_slots(z_at):
    return z_at, z_at + 1 - 2 * (z_at % 2), (z_at + 2) % 4, 3 - z_at


def grad_columns(right, core, units):
    blocks = []
    for lead in [None] if len(right.shape) == 2 else range(right.shape[0]):
        of_lead = right if lead is None else right.at[lead]
        start = pl.multiple_of(core * (units * LANES), 128)
        blocks.append(of_lead[:, pl.ds(start, units * LANES)])
    return blocks[0] if len(blocks) == 1 else jnp.concatenate(blocks, axis=1)


def sibling_grad_kernel(jobs, *refs):
    operands, out = refs[:-1], refs[-1]
    core_at = lax.axis_index(STREAM) % 2
    row = 0
    for at, (units, blocks, depth) in enumerate(jobs):
        left, right = operands[2 * at], operands[2 * at + 1]
        product = low(dot_first(left[...], grad_columns(right, 1 - core_at, units)))
        for block in range(blocks):
            columns = product[:, block * LANES : (block + 1) * LANES]
            out[:, :, row : row + depth] = columns.reshape(8, 2, depth, LANES)
            row += depth


TO_X = ((2, False, False), (3, False, False), (3, True, False))
TO_Y_A = ((0, False, True), (0, False, False), (1, False, True), (1, False, False))
TO_Y_B = ((2, False, True), (3, False, True))
TO_Z_A = ((1, True, True), (1, True, False))
TO_Z_B = ((2, True, False),)
TO_Z_C = ((2, True, True), (3, True, True))
OWN = ((0, True, True), (0, True, False))
PARTS = (TO_X, TO_Y_A, TO_Y_B, TO_Z_A, TO_Z_B, TO_Z_C, OWN)


def part_at(part):
    z_at, y_at, x_at, _ = place()
    slot, own_y, own_x = part
    return (
        shard_slots(z_at)[slot] * 2 + (y_at if own_y else 1 - y_at),
        x_at if own_x else 1 - x_at,
    )


def own_grad_kernel(jobs, sent, *refs):
    outs, work = refs[-1 - len(PARTS) : -1], refs[-1]
    operands, came = refs[: 2 * len(jobs)], refs[2 * len(jobs) : -1 - len(PARTS)]
    core_at = lax.axis_index(STREAM) % 2
    row = 0
    for at, (units, blocks, depth) in enumerate(jobs):
        left, right = operands[2 * at], operands[2 * at + 1]
        product = dot_first(left[...], grad_columns(right, core_at, units))
        array, came_row = sent[at]
        for block in range(blocks):
            columns = product[:, block * LANES : (block + 1) * LANES]
            rows = slice(row, row + depth)
            work[:, :, :depth] = columns.reshape(8, 2, depth, LANES) + wide(
                came[array][:, :, came_row : came_row + depth]
            )
            for out, parts in zip(outs, PARTS):
                for j, part in enumerate(parts):
                    dp_from, x_from = part_at(part)
                    out[j, rows] = low(work[dp_from, x_from, :depth])
            row += depth
            came_row += depth


def reduce_steps(to_x, to_y_a, to_y_b, to_z_a, to_z_b, to_z_c, own):
    from_y_a, from_x, half_other = yield [
        (to_y_a, DP, BESIDE),
        (to_x, STREAM, ACROSS),
        (to_z_b, DP, HALFWAY),
    ]
    from_y_b, mate = yield [
        (low(wide(to_y_b) + wide(from_x[:2])), DP, BESIDE),
        (low(wide(to_z_a) + wide(from_y_a[2:])), DP, PAIR),
    ]
    half, mirror = yield [
        (low(wide(to_z_c[0]) + wide(from_y_b[0])), DP, HALFWAY),
        (low(wide(to_z_c[1]) + wide(from_x[2]) + wide(from_y_b[1])), DP, MIRROR),
    ]
    total = wide(own) + wide(from_y_a[:2]) + wide(mate)
    total = low(
        jnp.stack((total[0] + wide(half) + wide(mirror), total[1] + wide(half_other[0])))
    )
    (from_x,) = yield [(total, STREAM, ACROSS)]
    total = low(wide(total) + wide(from_x[::-1]))
    (other,) = yield [(total, STREAM, CORE)]
    return total, other


def unpack_kernel(jobs, mine, other, *outs):
    _, _, x_at, core_at = place()
    for source, core_from in ((mine, core_at), (other, 1 - core_at)):
        for j in range(2):
            x_from = x_at if j == 0 else 1 - x_at
            for out_at, lead, units, row, depth in jobs:
                out = outs[out_at] if lead is None else outs[out_at].at[lead]
                for unit in range(units):
                    at = row + unit * depth
                    start = core_from * (units * LANES) + unit * LANES
                    out[
                        pl.ds(pl.multiple_of(x_from * depth, 8), depth),
                        pl.ds(pl.multiple_of(start, 128), LANES),
                    ] = wide(source[j, at : at + depth])


def reduce_plain(parts):
    shards = []
    for left, right in parts:
        if right.ndim == 2:
            whole = low(dot_first(left, right))
            own = lax.psum_scatter(whole, DP, scatter_dimension=0, tiled=True)
        else:
            whole = low(jnp.stack([dot_first(left, r) for r in right]))
            own = lax.psum_scatter(whole, DP, scatter_dimension=1, tiled=True)
        shards.append(wide(lax.psum(own, STREAM)))
    return shards


class Group:
    def __init__(self):
        self.operands, self.jobs, self.out_jobs, self.out_shapes = [], [], [], []
        self.rows, self.flops, self.sent, self.came, self.from_sent = 0, 0, [], [], []

    def sibling(self, tie, *parts):
        jobs, operands, rows, flops = [], [], 0, 0
        for left, right in parts:
            operands += [left, right]
            depth = left.shape[1] // 16
            units = right.shape[-1] // (2 * LANES)
            leads = [None] if right.ndim == 2 else range(right.shape[0])
            jobs.append((units, units * len(leads), depth))
            self.from_sent.append((len(self.sent), rows))
            for lead in leads:
                self.out_jobs.append(
                    (len(self.out_shapes), lead, units, self.rows + rows, depth)
                )
                rows += units * depth
            self.out_shapes.append(
                shape((*right.shape[:-2], 2 * depth, right.shape[-1]), F32)
            )
            flops += left.shape[0] * left.shape[1] * right.size // right.shape[-2]
        self.sent.append(
            call(
                functools.partial(sibling_grad_kernel, jobs),
                shape((8, 2, rows, LANES)),
                [VMEM] * len(operands),
                flops=flops,
            )(tie(operands[0]), *operands[1:])
        )
        self.jobs += jobs
        self.operands += operands
        self.rows += rows
        self.flops += flops
        return self.sent[-1]

    def core_move(self):
        def steps(sent):
            (came,) = yield [(sent, STREAM, CORE)]
            self.came.append(came)

        return Mover(steps(self.sent[-1]))

    def own(self, tie, small=None):
        deepest = max(job[-1] for job in self.jobs)
        self.parts = call(
            functools.partial(own_grad_kernel, self.jobs, self.from_sent),
            [shape((len(parts), self.rows, LANES)) for parts in PARTS],
            [VMEM] * (len(self.operands) + len(self.came)),
            [pltpu.VMEM((8, 2, deepest, LANES), F32)],
            flops=self.flops,
        )(tie(self.operands[0]), *self.operands[1:], *self.came)
        if small is not None:
            _, small_rows, part = small.shape
            both = jnp.pad(low(small), ((0, 0), (0, 2 * PAD_ROWS - small_rows), (0, LANES - part)))
            both = both.reshape(8, 2, PAD_ROWS, LANES)
            self.parts = [
                jnp.concatenate(
                    (made, jnp.stack([both[part_at(part)] for part in parts])), axis=1
                )
                for made, parts in zip(self.parts, PARTS)
            ]
        return self.parts

    def move(self):
        return Mover(reduce_steps(*self.parts))

    def unpack(self, moved):
        return call(
            functools.partial(unpack_kernel, self.out_jobs),
            self.out_shapes,
            [VMEM, VMEM],
        )(*moved)

    def unpack_small(self, moved, small_rows, part):
        x_at = lax.axis_index(STREAM) // 2
        pieces = wide(moved[0][:, self.rows :]) + wide(moved[1][:, self.rows :])
        pieces = jnp.where(x_at == 0, pieces, pieces[::-1]).reshape(2 * PAD_ROWS, LANES)
        return pieces[:small_rows, :part]


def norm_parts(summed):
    center = summed - jnp.mean(summed, axis=-1, keepdims=True)
    inverse = lax.rsqrt(jnp.mean(center * center, axis=-1, keepdims=True) + EPSILON)
    return center * inverse, inverse


def norm_back(upstream, normed, inverse, gain):
    scaled = upstream * gain
    return inverse * (
        scaled
        - jnp.mean(scaled, axis=-1, keepdims=True)
        - normed * jnp.mean(scaled * normed, axis=-1, keepdims=True)
    )


def heads_apart(four):
    head = lax.broadcasted_iota(jnp.int32, four.shape, 1) // 64
    return low(jnp.concatenate([jnp.where(head == j, four, 0.0) for j in range(4)], axis=0))


def heads_joined(stacked):
    rows = stacked.shape[0] // 4
    head = lax.broadcasted_iota(jnp.int32, (rows, stacked.shape[1]), 1) // 64
    made = stacked[:rows]
    for j in range(1, 4):
        made = jnp.where(head == j, stacked[j * rows : (j + 1) * rows], made)
    return made


def quads():
    return [slice(j * 256, (j + 1) * 256) for j in range(HEADS // 4)]


def softmax(scores):
    raised = jnp.exp(scores - jnp.max(scores, axis=-1, keepdims=True))
    return raised * (1.0 / jnp.sum(raised, axis=-1, keepdims=True))


def score_back(weight, back):
    return low(weight * (back - jnp.sum(back * weight, axis=-1, keepdims=True)))


def row_sum(value):
    return jnp.sum(value, axis=0, keepdims=True)


def self_kernel(seq, lengths, x_ref, w_ref, vec, qkv_ref, out_ref, q, k, v, o):
    tokens = x_ref.shape[0]
    for j, (scratch, bias) in enumerate(((q, B_Q), (k, None), (v, B_V))):
        for c in range(2):
            columns = slice(c * LANES, (c + 1) * LANES)
            made = dot(x_ref[...], w_ref[c, j])
            if bias is not None:
                made = made + vec[bias : bias + 1, columns]
            made = low(made)
            qkv_ref[j, :, columns] = made
            scratch[:, columns] = wide(made)

    def step(r, _):
        rows = pl.ds(pl.multiple_of(r * seq, 8), seq)
        valid = lax.broadcasted_iota(jnp.int32, (4 * seq, seq), 1) < lengths[r]
        asked = [heads_apart(q[rows, c] * 0.125) for c in quads()]
        scores = [dot_last(a, low(k[rows, c])) for a, c in zip(asked, quads())]
        weights = [softmax(jnp.where(valid, score, -jnp.inf)) for score in scores]
        made = [dot(low(w), low(v[rows, c])) for w, c in zip(weights, quads())]
        for part, c in zip(made, quads()):
            o[rows, c] = heads_joined(part)
        return 0

    lax.fori_loop(0, tokens // seq, step, 0, unroll=2)
    out_ref[...] = low(o[...])


def first_norm_kernel(seq, o_ref, x_ref, wso, wcq, vec, normed, inverse, h_low, qc, z):
    for c in range(2):
        columns = slice(c * LANES, (c + 1) * LANES)
        z[:, columns] = (
            dot(o_ref[...], wso[c, 0])
            + vec[B_SO : B_SO + 1, columns]
            + wide(x_ref[:, columns])
        )
    made, scale = norm_parts(z[...])
    normed[...] = made
    inverse[...] = scale
    h_low[...] = low(made * vec[G_1 : G_1 + 1] + vec[B_N1 : B_N1 + 1])
    for c in range(2):
        columns = slice(c * LANES, (c + 1) * LANES)
        qc[:, columns] = low(dot(h_low[...], wcq[c, 0]) + vec[B_CQ : B_CQ + 1, columns])


def image_kernel(y_ref, w_ref, vec, kv_ref):
    slots, _, images, padded, _ = kv_ref.shape
    rows = images * padded
    for slot in range(slots):
        pixels = y_ref[slot * rows : (slot + 1) * rows]
        for c in range(2):
            columns = slice(c * LANES, (c + 1) * LANES)
            for j in range(2):
                made = dot(pixels, w_ref[c, j])
                if j == 1:
                    made = made + vec[B_CV : B_CV + 1, columns]
                kv_ref[slot, j, :, :, columns] = low(made).reshape(images, padded, LANES)


def cross_kernel(
    seq, patches, micro_rows, slots, qc, kv, n1, wco, vec, oc, n2, inverse, h_low, q, o
):
    q[...] = wide(qc[...]) * 0.125
    tokens = qc.shape[0]
    padded = kv.shape[3]
    there = lax.broadcasted_iota(jnp.int32, (4 * seq, padded), 1) < patches

    def step(r, _):
        rows = pl.ds(pl.multiple_of(r * seq, 8), seq)
        slot, m = slots[r], r // micro_rows
        asked = [heads_apart(q[rows, c]) for c in quads()]
        scores = [dot_last(a, kv[slot, 0, m, :, c]) for a, c in zip(asked, quads())]
        weights = [softmax(jnp.where(there, score, -jnp.inf)) for score in scores]
        made = [dot(low(w), kv[slot, 1, m, :, c]) for w, c in zip(weights, quads())]
        for part, c in zip(made, quads()):
            o[rows, c] = heads_joined(part)
        return 0

    lax.fori_loop(0, tokens // seq, step, 0, unroll=2)
    oc[...] = low(o[...])
    for c in range(2):
        columns = slice(c * LANES, (c + 1) * LANES)
        first = n1[:, columns] * vec[G_1 : G_1 + 1, columns] + vec[B_N1 : B_N1 + 1, columns]
        o[:, columns] = first + dot(oc[...], wco[c, 0]) + vec[B_CO : B_CO + 1, columns]
    made, scale = norm_parts(o[...])
    n2[...] = made
    inverse[...] = scale
    h_low[...] = low(made * vec[G_2 : G_2 + 1] + vec[B_N2 : B_N2 + 1])


def hidden_kernel(h_low, w_ref, bias, active, slope):
    i = pl.program_id(0)
    weights = w_ref[:, :, 0].reshape(-1, LANES)
    pre = dot(h_low[...], weights) + bias[pl.ds(i, 1), :]
    cumulative = 0.5 * (1.0 + lax.erf(pre * ROOT_HALF))
    active[...] = low(pre * cumulative)
    slope[...] = low(cumulative + pre * INV_ROOT_TAU * jnp.exp(-0.5 * pre * pre))


def last_norm_kernel(
    seq, lengths, g_ref, w_ref, n2, cot, vec, out, dz, df, rows_out, total
):
    i = pl.program_id(0)

    @pl.when(i == 0)
    def _():
        total[...] = jnp.zeros_like(total)

    for c in range(2):
        columns = slice(c * LANES, (c + 1) * LANES)
        total[:, columns] += dot(g_ref[...], w_ref[:, :, c].reshape(-1, LANES))

    @pl.when(i == pl.num_programs(0) - 1)
    def _():
        def step(r, sums):
            rows = pl.ds(pl.multiple_of(r * seq, 8), seq)
            second = n2[rows, :] * vec[G_2 : G_2 + 1] + vec[B_N2 : B_N2 + 1]
            made, scale = norm_parts(second + total[rows, :] + vec[B_FO : B_FO + 1])
            out[r] = low(made * vec[G_3 : G_3 + 1] + vec[B_N3 : B_N3 + 1])
            valid = lax.broadcasted_iota(jnp.int32, made.shape, 0) < lengths[r]
            upstream = jnp.where(valid, wide(cot[r]), 0.0)
            back = norm_back(upstream, made, scale, vec[G_3 : G_3 + 1])
            dz[rows, :] = back
            gain, shift, lowered = sums
            return (
                gain + row_sum(upstream * made),
                shift + row_sum(upstream),
                lowered + row_sum(wide(low(back))),
            )

        zero = jnp.zeros((1, total.shape[1]), F32)
        gain, shift, lowered = lax.fori_loop(0, out.shape[0], step, (zero, zero, zero))
        df[...] = low(dz[...])
        rows_out[0:1] = gain
        rows_out[1:2] = shift
        rows_out[2:3] = lowered
        rows_out[3:8] = jnp.zeros((5, total.shape[1]), F32)


def norm_back_rows(total, dz_ref, normed, inverse, gain, dz, low_ref, rows_out, step_rows):
    def step(r, sums):
        rows = pl.ds(pl.multiple_of(r * step_rows, 8), step_rows)
        upstream = total[rows, :] + dz_ref[rows, :]
        made = normed[rows, :]
        back = norm_back(upstream, made, inverse[rows, :], gain)
        dz[rows, :] = back
        return (
            sums[0] + row_sum(upstream * made),
            sums[1] + row_sum(upstream),
            sums[2] + row_sum(wide(low(back))),
        )

    zero = jnp.zeros((1, total.shape[1]), F32)
    sums = lax.fori_loop(0, total.shape[0] // step_rows, step, (zero, zero, zero))
    low_ref[...] = low(dz[...])
    for j in range(3):
        rows_out[j : j + 1] = sums[j]
    rows_out[3:8] = jnp.zeros((5, total.shape[1]), F32)


def hidden_back_kernel(
    seq, df, wout, win, slope, dz3, n2, inverse, vec, du, bias_out, dz2, dac, rows_out, total
):
    i = pl.program_id(0)

    @pl.when(i == 0)
    def _():
        total[...] = jnp.zeros_like(total)

    raw = dot_last(df[:, :LANES], wout[0, :, 0].reshape(-1, LANES))
    raw = raw + dot_last(df[:, LANES:], wout[0, :, 1].reshape(-1, LANES))
    made = low(raw * wide(slope[...]))
    du[...] = made
    bias_out[pl.ds(i, 1), :] = row_sum(wide(made))
    total[...] += dot_last(made, win[:, :, 0].reshape(-1, LANES))

    @pl.when(i == pl.num_programs(0) - 1)
    def _():
        norm_back_rows(
            total, dz3, n2, inverse, vec[G_2 : G_2 + 1], dz2, dac, rows_out, seq
        )


def cross_back_kernel(
    seq, patches, micro_rows, slots, dac, qc, kv, wco, dqc, dkv_out, dkv, q, do, dq
):
    q[...] = wide(qc[...]) * 0.125
    do[...] = wide(
        low(dot_last(dac[:, :LANES], wco[0, 0]) + dot_last(dac[:, LANES:], wco[1, 0]))
    )
    dkv[...] = jnp.zeros_like(dkv)
    tokens = qc.shape[0]
    padded = kv.shape[3]
    there = lax.broadcasted_iota(jnp.int32, (4 * seq, padded), 1) < patches

    def step(r, _):
        rows = pl.ds(pl.multiple_of(r * seq, 8), seq)
        slot, m = slots[r], r // micro_rows
        asked = [heads_apart(q[rows, c]) for c in quads()]
        came = [heads_apart(do[rows, c]) for c in quads()]
        keys = [kv[slot, 0, m, :, c] for c in quads()]
        values = [kv[slot, 1, m, :, c] for c in quads()]
        scores = [dot_last(a, key) for a, key in zip(asked, keys)]
        backs = [dot_last(d, value) for d, value in zip(came, values)]
        weights = [softmax(jnp.where(there, score, -jnp.inf)) for score in scores]
        backs = [score_back(w, b) for w, b in zip(weights, backs)]
        queries = [heads_joined(dot(b, key)) for b, key in zip(backs, keys)]
        key_parts = [dot_first(b, a) for b, a in zip(backs, asked)]
        value_parts = [dot_first(low(w), d) for w, d in zip(weights, came)]
        for j, c in enumerate(quads()):
            dq[rows, c] = queries[j] * 0.125
            dkv[0, slot, m, :, c] += key_parts[j]
            dkv[1, slot, m, :, c] += value_parts[j]
        return 0

    lax.fori_loop(0, tokens // seq, step, 0, unroll=2)
    dqc[...] = low(dq[...])
    dkv_out[...] = low(dkv[...])


def first_back_kernel(seq, dqc, wcq, dz2, n1, inverse, vec, dz1, da, rows_out, total):
    total[...] = dot_last(dqc[:, :LANES], wcq[0, 0]) + dot_last(dqc[:, LANES:], wcq[1, 0])
    norm_back_rows(total, dz2, n1, inverse, vec[G_1 : G_1 + 1], dz1, da, rows_out, seq)
    rows_out[3:4] = row_sum(wide(dqc[...]))


def self_back_kernel(seq, lengths, da, qkv, wso, dqkv, rows_out, q, k, v, do, dq, dk, dv):
    q[...] = wide(qkv[0]) * 0.125
    k[...] = wide(qkv[1])
    v[...] = wide(qkv[2])
    do[...] = wide(low(dot_last(da[:, :LANES], wso[0, 0]) + dot_last(da[:, LANES:], wso[1, 0])))
    tokens = da.shape[0]

    def step(r, _):
        rows = pl.ds(pl.multiple_of(r * seq, 8), seq)
        valid = lax.broadcasted_iota(jnp.int32, (4 * seq, seq), 1) < lengths[r]
        asked = [heads_apart(q[rows, c]) for c in quads()]
        came = [heads_apart(do[rows, c]) for c in quads()]
        keys = [low(k[rows, c]) for c in quads()]
        values = [low(v[rows, c]) for c in quads()]
        scores = [dot_last(a, key) for a, key in zip(asked, keys)]
        backs = [dot_last(d, value) for d, value in zip(came, values)]
        weights = [softmax(jnp.where(valid, score, -jnp.inf)) for score in scores]
        backs = [score_back(w, b) for w, b in zip(weights, backs)]
        queries = [heads_joined(dot(b, key)) for b, key in zip(backs, keys)]
        key_parts = [dot_first(b, a) for b, a in zip(backs, asked)]
        value_parts = [dot_first(low(w), d) for w, d in zip(weights, came)]
        for j, c in enumerate(quads()):
            dq[rows, c] = queries[j] * 0.125
            dk[rows, c] = key_parts[j]
            dv[rows, c] = value_parts[j]
        return 0

    lax.fori_loop(0, tokens // seq, step, 0, unroll=2)
    for j, made in enumerate((dq, dk, dv)):
        dqkv[j] = low(made[...])
    rows_out[0:1] = row_sum(wide(dqkv[0]))
    rows_out[1:2] = row_sum(wide(dqkv[2]))
    rows_out[2:8] = jnp.zeros((6, q.shape[1]), F32)


def text_grad_kernel(dz1, dqkv, w_ref, out, total):
    total[...] = dz1[...]
    for j in range(3):
        for c in range(2):
            total[...] += dot_last(dqkv[j, :, c * LANES : (c + 1) * LANES], w_ref[c, j])
    seq = out.shape[1]
    for r in range(out.shape[0]):
        out[r] = low(total[r * seq : (r + 1) * seq, :])


def patch_grad_kernel(dkv, w_ref, out, rows_out):
    _, slots, images, padded, width = dkv.shape
    rows = images * padded
    total = jnp.zeros((1, width), F32)
    for slot in range(slots):
        made = None
        for j in range(2):
            grad = dkv[j, slot].reshape(rows, width)
            for c in range(2):
                term = dot_last(grad[:, c * LANES : (c + 1) * LANES], w_ref[c, j])
                made = term if made is None else made + term
        out[slot] = low(made).reshape(images, padded, w_ref.shape[2])
        total = total + row_sum(wide(grad))
    rows_out[0:1] = total
    rows_out[1:8] = jnp.zeros((7, width), F32)


def on_device(
    text_input,
    patch_input,
    text_lengths,
    image_of_row,
    cotangent,
    self_qkv,
    self_out,
    cross_q,
    cross_kv,
    cross_out,
    ffn_in,
    ffn_out,
    biases,
    norm_gains,
    ffn_bias,
):
    dp = lax.axis_size(DP)
    micros, row_count, seq, width = text_input.shape
    patches, patch_width = patch_input.shape[2:]
    rows_all = micros * row_count
    tokens = rows_all * seq
    hidden = ffn_in.shape[1]
    padded = -(-patches // 16) * 16
    images = micros * patch_input.shape[1]

    part = biases.shape[1]
    small = jnp.concatenate((biases, norm_gains, ffn_bias.reshape(-1, part)))
    small_rows = small.shape[0]
    wide_rows = biases.shape[0] + norm_gains.shape[0]
    small = jnp.pad(small, ((0, 2 * PAD_ROWS - small_rows), (0, LANES - part)))
    small = jnp.broadcast_to(small.reshape(2, PAD_ROWS, LANES), (2, 2, PAD_ROWS, LANES))

    half = width // dp // 2
    half_v = cross_kv.shape[1] // 2
    in_units = hidden // (2 * LANES)
    group_a = ((cross_kv, small), ((2, half_v), (1, PAD_ROWS)))
    group_b = (
        (self_qkv, self_out, cross_q, cross_out),
        ((3, half), (1, half), (1, half), (1, half)),
    )
    hidden_rows = width * in_units // 16
    hidden_units = ((in_units, width // 16), (1, hidden // 16))

    text = text_input.reshape(tokens, width)
    pixels = jnp.pad(
        patch_input.reshape(images, patches, patch_width), ((0, 0), (0, padded - patches), (0, 0))
    )
    lengths = text_lengths.reshape(-1)
    slots = image_of_row.reshape(-1) ^ lax.axis_index(STREAM)
    flat = (tokens, width)
    full = pltpu.VMEM(flat, F32)
    flops = 2 * tokens * width * width
    steps = hidden // LANES
    chunks = hidden // width
    kv_shape = (4, 2, images, padded, width)
    in_block = pl.BlockSpec(
        (8, 2, 1, width // 16, LANES), lambda i: (0, 0, i // in_units, i % in_units, 0)
    )
    v = types.SimpleNamespace()

    def small_parts(whole):
        values = wide(whole[0, 0].reshape(dp, 2 * PAD_ROWS, LANES)[:, :small_rows, :part])
        vec = values[:, :wide_rows].transpose(1, 0, 2).reshape(wide_rows, width)
        v.vec = jnp.pad(vec, ((0, 16 - wide_rows), (0, 0)))
        v.hidden_bias = values[:, wide_rows:].reshape(-1, LANES)

    def pixel_steps():
        beside, across = yield [(pixels, STREAM, CORE), (pixels, STREAM, ACROSS)]
        (apart,) = yield [(across, STREAM, CORE)]
        v.pixels_all = jnp.stack((pixels, beside, across, apart)).reshape(-1, patch_width)

    def run_image(tie):
        v.kv = call(
            image_kernel,
            shape(kv_shape),
            [VMEM] * 3,
            flops=16 * flops,
        )(tie(v.pixels_all), v.w_kv, v.vec)
        return v.kv

    def run_self(tie):
        v.qkv, v.attended = call(
            functools.partial(self_kernel, seq),
            [shape((3, *flat)), shape(flat)],
            [SMEM, VMEM, VMEM, VMEM],
            [full] * 4,
            flops=4 * flops,
        )(lengths, tie(text), v.w_qkv, v.vec)
        return v.attended

    def run_first(tie):
        v.n1, v.inverse1, v.h1, v.qc = call(
            functools.partial(first_norm_kernel, seq),
            [shape(flat, F32), shape((tokens, 1), F32), shape(flat), shape(flat)],
            [VMEM] * 5,
            [full],
            flops=2 * flops,
        )(v.attended, tie(text), v.w_so, v.w_cq, v.vec)
        return v.qc

    def run_cross(tie):
        v.oc, v.n2, v.inverse2, v.h2 = call(
            functools.partial(cross_kernel, seq, patches, row_count),
            [shape(flat), shape(flat, F32), shape((tokens, 1), F32), shape(flat)],
            [SMEM, VMEM, VMEM, VMEM, VMEM, VMEM],
            [full, full],
            flops=2 * flops,
        )(slots, tie(v.qc), v.kv, v.n1, v.w_co, v.vec)
        return v.h2

    def run_hidden(tie):
        v.active, v.slope = call(
            hidden_kernel,
            [shape((tokens, hidden)), shape((tokens, hidden))],
            [
                VMEM,
                in_block,
                VMEM,
            ],
            out_specs=[pl.BlockSpec((tokens, LANES), lambda i: (0, i))] * 2,
            grid=(steps,),
            flops=4 * flops,
        )(tie(v.h2), v.w_hidden, v.hidden_bias)
        return v.active

    def run_last(tie):
        v.out_rows, v.dz3, v.df, v.sums3 = call(
            functools.partial(last_norm_kernel, seq),
            [shape((rows_all, seq, width)), shape(flat, F32), shape(flat), shape((8, width), F32)],
            [
                SMEM,
                pl.BlockSpec((tokens, width), lambda i: (0, i)),
                pl.BlockSpec((8 // chunks, 2, 2, hidden // 16, LANES), lambda i: (i, 0, 0, 1, 0)),
                VMEM,
                VMEM,
                VMEM,
            ],
            [full],
            grid=(chunks,),
            flops=4 * flops,
        )(
            lengths, tie(v.active), v.w_hidden, v.n2,
            cotangent.reshape(rows_all, seq, width), v.vec,
        )
        return v.df

    def run_hidden_back(tie):
        v.du, v.hidden_bias_grad, v.dz2, v.dac, v.sums2 = call(
            functools.partial(hidden_back_kernel, seq),
            [
                shape((tokens, hidden)),
                shape((steps, LANES), F32),
                shape(flat, F32),
                shape(flat),
                shape((8, width), F32),
            ],
            [
                VMEM,
                pl.BlockSpec((1, 2, 2, hidden // 16, LANES), lambda i: (i, 0, 0, 1, 0)),
                in_block,
                pl.BlockSpec((tokens, LANES), lambda i: (0, i)),
                VMEM,
                VMEM,
                VMEM,
                VMEM,
            ],
            [full],
            out_specs=[pl.BlockSpec((tokens, LANES), lambda i: (0, i)), VMEM, VMEM, VMEM, VMEM],
            grid=(steps,),
            flops=8 * flops,
        )(
            tie(v.df), v.w_hidden, v.w_hidden, v.slope, v.dz3, v.n2, v.inverse2,
            v.vec,
        )
        return v.dac

    def run_cross_back(tie):
        v.dqc, v.dkv_all = call(
            functools.partial(cross_back_kernel, seq, patches, row_count),
            [shape(flat), shape((2, 4, images, padded, width))],
            [SMEM, VMEM, VMEM, VMEM, VMEM],
            [pltpu.VMEM((2, 4, images, padded, width), F32), full, full, full],
            flops=4 * flops,
        )(slots, tie(v.dac), v.qc, v.kv, v.w_co)
        return v.dqc

    def patch_steps():
        made = v.patch_parts
        near, far = yield [(made[1], STREAM, CORE), (made[3], STREAM, CORE)]
        (across,) = yield [(low(wide(made[2]) + wide(far)), STREAM, ACROSS)]
        v.patch_rows = low(wide(made[0]) + wide(near) + wide(across))[:, :patches]

    def run_first_back(tie):
        v.dz1, v.da, v.sums1 = call(
            functools.partial(first_back_kernel, seq),
            [shape(flat, F32), shape(flat), shape((8, width), F32)],
            [VMEM] * 6,
            [full],
            flops=flops,
        )(tie(v.dqc), v.w_cq, v.dz2, v.n1, v.inverse1, v.vec)
        return v.da

    def run_self_back(tie):
        v.dqkv, v.sums0 = call(
            functools.partial(self_back_kernel, seq),
            [shape((3, *flat)), shape((8, width), F32)],
            [SMEM, VMEM, VMEM, VMEM],
            [full] * 7,
            flops=4 * flops,
        )(lengths, tie(v.da), v.qkv, v.w_so)
        return v.dqkv

    def run_patch_grad(tie):
        v.patch_parts, v.sums_kv = call(
            patch_grad_kernel,
            [shape((4, images, padded, patch_width)), shape((8, width), F32)],
            [VMEM] * 2,
            flops=16 * flops,
        )(tie(v.dkv_all), v.w_kv)
        return v.patch_parts

    def run_text_grad(tie):
        v.text_rows = call(
            text_grad_kernel,
            shape((rows_all, seq, width)),
            [VMEM] * 3,
            [full],
            flops=3 * flops,
        )(tie(v.dz1), v.dqkv, v.w_qkv)
        return v.text_rows

    def small_grads():
        sums0, sums1, sums2, sums3, sums_kv = v.sums0, v.sums1, v.sums2, v.sums3, v.sums_kv
        grads = jnp.concatenate(
            (
                sums0[0:2], sums1[2:3], sums1[1:2], sums1[3:4], sums_kv[0:1], sums2[2:3],
                sums2[1:2], sums3[2:3], sums3[1:2], sums1[0:1], sums2[0:1], sums3[0:1],
            )
        )
        return jnp.concatenate(
            (
                grads.reshape(wide_rows, dp, part).transpose(1, 0, 2),
                v.hidden_bias_grad.reshape(dp, -1, part),
            ),
            axis=1,
        )

    def run_all(moves):
        mover = Mover(moves)
        while not mover.done:
            mover.give([lax.ppermute(array, axis, hops) for array, axis, hops in mover.requests])

    if not special_mesh():
        def free(array):
            return array

        v.w_kv, w_small = gather_plain(*group_a)
        v.w_qkv, v.w_so, v.w_cq, v.w_co = gather_plain(*group_b)
        w_in = lax.all_gather(ffn_in, DP, axis=0, tiled=True)
        w_out = lax.all_gather(ffn_out, DP, axis=0, tiled=True)
        w_in = w_in.reshape(8, 2, width // 16, 2, in_units, LANES).transpose(0, 1, 3, 4, 2, 5)
        w_out = w_out.reshape(8, 2, hidden // 16, 2, LANES).transpose(0, 1, 3, 2, 4)
        v.w_hidden = jnp.concatenate((w_in.reshape(8, 2, 2, hidden_rows, LANES), w_out), axis=3)
        small_parts(w_small)
        run_all(pixel_steps())
        for work in (
            run_image, run_self, run_first, run_cross, run_hidden, run_last, run_hidden_back,
            run_cross_back, run_patch_grad,
        ):
            work(free)
        run_all(patch_steps())
        for work in (run_first_back, run_self_back, run_text_grad):
            work(free)
        s_out, s_in, s_co, s_cq, s_so, s_kv, s_qkv = reduce_plain(
            (
                (v.active, v.df), (v.h2, v.du), (v.oc, v.dac), (v.h1, v.dqc),
                (v.attended, v.da), (v.pixels_all, v.dkv_all.reshape(2, -1, width)), (text, v.dqkv),
            )
        )
        s_small = lax.psum_scatter(low(small_grads()), DP, scatter_dimension=0, tiled=True)
        s_small = wide(lax.psum(s_small, STREAM))[0]
    else:
        clock = Clock()
        v.w_hidden = lax.all_gather(pack_own((ffn_in, ffn_out), hidden_units), (DP, STREAM), axis=0)
        v.w_hidden = v.w_hidden.reshape(8, 2, 2, -1, LANES)
        move_a = Mover(gather_steps(*pack_group(*group_a)))
        move_b = Mover(gather_steps(*pack_group(*group_b)))
        move_pixels = Mover(pixel_steps())

        def build_a(tie):
            v.w_kv, whole = assemble((tie(move_a.result[0]), *move_a.result[1:]), group_a[1])
            small_parts(whole)
            return v.w_kv

        def build_b(tie):
            v.w_qkv, v.w_so, v.w_cq, v.w_co = assemble(
                (tie(move_b.result[0]), *move_b.result[1:]), group_b[1]
            )
            return v.w_qkv

        clock.step([move_a, move_pixels])
        clock.step([move_a, move_b, move_pixels])
        clock.step([move_a, move_b])
        clock.step([move_a, move_b])
        clock.step([move_b], [build_a, run_image])
        clock.step([], [build_b, run_self, run_first, run_cross, run_hidden, run_last])

        hidden_group, mid_group, last_group = Group(), Group(), Group()
        clock.step([], [lambda tie: hidden_group.sibling(tie, (v.active, v.df))])
        clock.step([hidden_group.core_move()], [run_hidden_back])
        clock.step([], [lambda tie: hidden_group.sibling(tie, (v.h2, v.du))])
        clock.step([hidden_group.core_move()])
        clock.step([], [hidden_group.own])
        move_hidden = hidden_group.move()
        clock.step([move_hidden], [run_cross_back, run_first_back])
        clock.step(
            [move_hidden],
            [
                lambda tie: mid_group.sibling(
                    tie,
                    (v.oc, v.dac),
                    (v.h1, v.dqc),
                    (v.pixels_all, v.dkv_all.reshape(2, -1, width)),
                ),
                run_self_back,
            ],
        )
        clock.step(
            [move_hidden, mid_group.core_move()],
            [
                lambda tie: last_group.sibling(tie, (v.attended, v.da), (text, v.dqkv)),
                run_patch_grad,
            ],
        )
        move_patch = Mover(patch_steps())
        clock.step(
            [last_group.core_move(), move_patch],
            [mid_group.own, lambda tie: last_group.own(tie, small_grads())],
        )
        move_mid, move_last = mid_group.move(), last_group.move()
        movers = [move_hidden, move_mid, move_last, move_patch]
        clock.step(movers, [run_text_grad])
        while not all(mover.done for mover in movers):
            clock.step(movers)
        s_out, s_in = hidden_group.unpack(move_hidden.result)
        s_co, s_cq, s_kv = mid_group.unpack(move_mid.result)
        s_so, s_qkv = last_group.unpack(move_last.result)
        s_small = last_group.unpack_small(move_last.result, small_rows, part)
    return (
        v.out_rows.reshape(text_input.shape),
        v.text_rows.reshape(text_input.shape),
        v.patch_rows.reshape(patch_input.shape),
        s_qkv,
        s_so,
        s_cq,
        s_kv,
        s_co,
        s_in,
        s_out,
        s_small[: biases.shape[0]],
        s_small[biases.shape[0] : wide_rows],
        s_small[wide_rows:].reshape(-1),
    )


def solution(mesh):
    placed = (
        P(None, (DP, STREAM), None, None),
        P(None, (DP, STREAM), None, None),
        P(None, (DP, STREAM)),
        P(None, (DP, STREAM)),
        P(None, (DP, STREAM), None, None),
        P(None, DP, None),
        P(DP, None),
        P(DP, None),
        P(None, DP, None),
        P(DP, None),
        P(DP, None),
        P(DP, None),
        P(None, DP),
        P(None, DP),
        P(DP),
    )
    return jax.shard_map(
        on_device,
        mesh=mesh,
        in_specs=placed,
        out_specs=(
            P(None, (DP, STREAM), None, None),
            P(None, (DP, STREAM), None, None),
            P(None, (DP, STREAM), None, None),
            P(None, DP, None),
            P(DP, None),
            P(DP, None),
            P(None, DP, None),
            P(DP, None),
            P(DP, None),
            P(DP, None),
            P(None, DP),
            P(None, DP),
            P(DP),
        ),
        check_vma=False,
    )
```

```python
import functools
import types

import jax
import jax.numpy as jnp
from jax import lax
from jax.experimental import pallas as pl
from jax.experimental.pallas import tpu as pltpu
from jax.sharding import PartitionSpec as P

HEADS = 12
LANES = 384
PAD_ROWS = 16
MIB = 2**20
DP, STREAM = "dp", "stream"

EPSILON = 1e-06
ROOT_HALF = 0.7071067811865476
INV_ROOT_TAU = 0.3989422804014327

CORE = ((0, 1), (1, 0), (2, 3), (3, 2))
ACROSS = ((0, 2), (2, 0), (1, 3), (3, 1))
BESIDE = ((0, 1), (1, 0), (2, 3), (3, 2), (4, 5), (5, 4), (6, 7), (7, 6))
PAIR = ((0, 2), (2, 0), (1, 3), (3, 1), (4, 6), (6, 4), (5, 7), (7, 5))
HALFWAY = ((0, 4), (4, 0), (1, 5), (5, 1), (2, 6), (6, 2), (3, 7), (7, 3))
MIRROR = ((0, 6), (6, 0), (1, 7), (7, 1), (2, 4), (4, 2), (3, 5), (5, 3))

B_Q, B_V, B_SO, B_N1, B_CQ, B_CV, B_CO, B_N2, B_FO, B_N3, G_1, G_2, G_3 = range(13)


def low(value):
    return value.astype(jnp.bfloat16)


def wide(value):
    return value.astype(jnp.float32)


def dot(left, right):
    return jnp.dot(left, right, preferred_element_type=jnp.float32)


def dot_last(left, right):
    return lax.dot_general(
        left, right, (((1,), (1,)), ((), ())), preferred_element_type=jnp.float32
    )


def dot_first(left, right):
    return lax.dot_general(
        left, right, (((0,), (0,)), ((), ())), preferred_element_type=jnp.float32
    )


def pick(array, index, axis=0):
    return lax.dynamic_index_in_dim(array, index, axis, keepdims=False)


def place():
    dp_at, stream_at = lax.axis_index(DP), lax.axis_index(STREAM)
    return dp_at // 2, dp_at % 2, stream_at // 2, stream_at % 2


class Clock:
    def __init__(self):
        self.before = []
        self.came = []

    def take(self, arrays):
        given = {}
        for array, (_, sends) in zip(arrays, self.came):
            row = 0
            for mover, at, sent in sends:
                part = array
                if len(sends) > 1:
                    rows = sent.size // LANES
                    part = array[row : row + rows].reshape(sent.shape)
                    row += rows
                given.setdefault(mover, {})[at] = part
        self.came = []
        for mover, parts in given.items():
            mover.give([parts[at] for at in range(len(parts))])

    def step(self, moving=(), compute=(), eager=False):
        arrays = [array for array, _ in self.came]
        arrays, self.before = lax.optimization_barrier((arrays, self.before + arrays[:1]))
        self.take(arrays)
        ways = {}
        for mover in moving:
            if mover.done:
                continue
            for at, (array, axis, hops) in enumerate(mover.requests):
                alone = hops is CORE or array.shape[-1] != LANES
                key = (axis, hops, (mover, at) if alone else None)
                ways.setdefault(key, []).append((mover, at, array))
        joined = [
            sends[0][2]
            if len(sends) == 1
            else jnp.concatenate([array.reshape(-1, LANES) for _, _, array in sends])
            for sends in ways.values()
        ]
        joined, self.before = lax.optimization_barrier((joined, self.before))
        self.came = [
            (lax.ppermute(array, axis, hops), sends)
            for array, ((axis, hops, _), sends) in zip(joined, ways.items())
        ]
        after = []
        if eager:
            movers = [mover for sends in ways.values() for mover, _, _ in sends]
            self.take([array for array, _ in self.came])
            for mover in dict.fromkeys(movers):
                if mover.done:
                    after += jax.tree.leaves(mover.result)
                else:
                    after += [array for array, _, _ in mover.requests]
        for work in compute() if callable(compute) else compute:
            after += jax.tree.leaves(work(self.tie))
        if after:
            self.before = after

    def tie(self, array):
        return lax.optimization_barrier((array, self.before))[0]


class Mover:
    def __init__(self, steps):
        self.steps = steps
        self.done = False
        self.result = None
        self.requests = next(steps)

    def give(self, came):
        try:
            self.requests = self.steps.send(came)
        except StopIteration as stop:
            self.done, self.result = True, stop.value


def special_mesh():
    return lax.axis_size(DP) == 8 and lax.axis_size(STREAM) == 4


VMEM = pl.BlockSpec(memory_space=pltpu.VMEM)
SMEM = pl.BlockSpec(memory_space=pltpu.SMEM)
ANY = pl.BlockSpec(memory_space=pl.ANY)


def call(kernel, out_shape, in_specs, scratch=(), mib=24, flops=0, out_specs=None, **more):
    return pl.pallas_call(
        kernel,
        out_shape=out_shape,
        in_specs=in_specs,
        out_specs=jax.tree.map(lambda _: VMEM, out_shape) if out_specs is None else out_specs,
        scratch_shapes=list(scratch),
        compiler_params=pltpu.CompilerParams(vmem_limit_bytes=mib * MIB),
        cost_estimate=pl.CostEstimate(flops=flops, bytes_accessed=4 * MIB, transcendentals=0),
        **more,
    )


def shape(dims, dtype=jnp.bfloat16):
    return jax.ShapeDtypeStruct(tuple(dims), dtype)


F32 = jnp.float32


def pack_shard(shard, units):
    if shard.ndim == 2:
        rows, _ = shard.shape
        split = shard.reshape(2, rows // 2, 2, units, LANES).transpose(2, 0, 3, 1, 4)
    else:
        _, rows, _ = shard.shape
        split = shard.reshape(units, 2, rows // 2, 2, LANES).transpose(3, 1, 0, 2, 4)
    return split.reshape(2, 2, units * rows // 2, LANES)


def pack_kernel(units, *refs):
    _, _, x_at, core_at = place()
    shards, (both, own, own_x) = refs[: len(units)], refs[len(units) :]
    row = 0
    for shard, (count, depth) in zip(shards, units):
        if len(shard.shape) == 4:
            both[:, :, row : row + depth] = shard[...]
            row += depth
            continue
        for unit in range(count):
            rows = slice(row, row + depth)
            for x in range(2):
                for c in range(2):
                    if len(shard.shape) == 3:
                        block = shard[unit, x * depth : (x + 1) * depth, c * LANES : (c + 1) * LANES]
                    else:
                        start = (c * count + unit) * LANES
                        block = shard[x * depth : (x + 1) * depth, start : start + LANES]
                    both[c, x, rows] = block
            row += depth
    own[...] = both[core_at]
    own_x[...] = both[core_at, x_at]


def pack_own_kernel(units, *refs):
    _, _, x_at, core_at = place()
    shards, out = refs[:-1], refs[-1]
    row = 0
    for shard, (count, depth) in zip(shards, units):
        for unit in range(count):
            start = (core_at * count + unit) * LANES
            out[row : row + depth] = shard[
                pl.ds(pl.multiple_of(x_at * depth, 16), depth),
                pl.ds(pl.multiple_of(start, 128), LANES),
            ]
            row += depth


def pack_group(shards, units):
    rows = sum(count * depth for count, depth in units)
    return call(
        functools.partial(pack_kernel, units),
        [shape((2, 2, rows, LANES)), shape((2, rows, LANES)), shape((rows, LANES))],
        [VMEM] * len(shards),
    )(*shards)


def pack_own(shards, units):
    rows = sum(count * depth for count, depth in units)
    return call(
        functools.partial(pack_own_kernel, units), shape((rows, LANES)), [VMEM] * len(shards)
    )(*shards)


def gather_steps(own_both, own, own_x):
    x_at = lax.axis_index(STREAM) // 2
    mate, half_z, mirror_z, beside = yield [
        (own, DP, PAIR),
        (own_x, DP, HALFWAY),
        (own_x, DP, MIRROR),
        (own, DP, BESIDE),
    ]
    others = jnp.stack((pick(mate, x_at), half_z, mirror_z))
    beside_others, half_x, mirror_x = yield [
        (others, DP, BESIDE),
        (half_z, STREAM, ACROSS),
        (mirror_z, STREAM, ACROSS),
    ]
    early = (mate, beside, half_z, mirror_z, half_x, mirror_x, beside_others)
    core_early = [lax.ppermute(piece, STREAM, CORE) for piece in early]
    late = yield [
        (beside_others[1:], STREAM, ACROSS),
        (pick(mate, 1 - x_at), DP, BESIDE),
    ]
    core_late = [lax.ppermute(piece, STREAM, CORE) for piece in late]
    return (own_both, *early, *late, *core_early, *core_late)


def piece_places(sources):
    own_both, *pieces = sources
    z_at, y_at, x_at, core_at = place()
    _, z_mate, z_half, z_mirror = shard_slots(z_at)
    parts = [
        (own_both.at[core_from, x_from], z_at, y_at, x_from, core_from)
        for core_from in range(2)
        for x_from in range(2)
    ]
    for group, core_from in ((pieces[:9], core_at), (pieces[9:], 1 - core_at)):
        mate, beside, half_z, mirror_z, half_x, mirror_x, others, others_x, mate_x = group
        for x_from in range(2):
            parts.append((mate.at[x_from], z_mate, y_at, x_from, core_from))
            parts.append((beside.at[x_from], z_at, 1 - y_at, x_from, core_from))
        parts += [
            (half_z, z_half, y_at, x_at, core_from),
            (mirror_z, z_mirror, y_at, x_at, core_from),
            (half_x, z_half, y_at, 1 - x_at, core_from),
            (mirror_x, z_mirror, y_at, 1 - x_at, core_from),
            (others.at[0], z_mate, 1 - y_at, x_at, core_from),
            (others.at[1], z_half, 1 - y_at, x_at, core_from),
            (others.at[2], z_mirror, 1 - y_at, x_at, core_from),
            (mate_x, z_mate, 1 - y_at, 1 - x_at, core_from),
            (others_x.at[0], z_half, 1 - y_at, 1 - x_at, core_from),
            (others_x.at[1], z_mirror, 1 - y_at, 1 - x_at, core_from),
        ]
    return parts


def piece_copies(units, sources, wholes, sems):
    parts = piece_places(sources)
    copies, row, sem = [], 0, 0
    for (count, depth), whole in zip(units, wholes):
        of_weight = []
        for piece, z_from, y_from, x_from, core_from in parts:
            start = (z_from * 2 + y_from) * (2 * depth) + x_from * depth
            of_weight.append(
                pltpu.make_async_copy(
                    piece.at[pl.ds(row, count * depth)].reshape(count, depth, LANES),
                    whole.at[core_from, :, pl.ds(pl.multiple_of(start, 16), depth)],
                    sems.at[sem],
                )
            )
            sem += 1
        copies.append(of_weight)
        row += count * depth
    return copies


def gather_plain(shards, units):
    packed = [
        shard if shard.ndim == 4 else pack_shard(shard, count)
        for shard, (count, _) in zip(shards, units)
    ]
    whole = lax.all_gather(jnp.concatenate(packed, axis=2), DP, axis=0, tiled=False)
    results = []
    row = 0
    for count, depth in units:
        part = whole[:, :, :, row : row + count * depth]
        part = part.reshape(-1, 2, 2, count, depth, LANES).transpose(1, 3, 0, 2, 4, 5)
        results.append(part.reshape(2, count, -1, LANES))
        row += count * depth
    return results


def shard_slots(z_at):
    return z_at, z_at + 1 - 2 * (z_at % 2), (z_at + 2) % 4, 3 - z_at


def grad_columns(right, core, units):
    blocks = []
    for lead in [None] if len(right.shape) == 2 else range(right.shape[0]):
        of_lead = right if lead is None else right.at[lead]
        start = pl.multiple_of(core * (units * LANES), 128)
        blocks.append(of_lead[:, pl.ds(start, units * LANES)])
    return blocks[0] if len(blocks) == 1 else jnp.concatenate(blocks, axis=1)


def sibling_grad_kernel(jobs, *refs):
    operands, out = refs[:-1], refs[-1]
    core_at = lax.axis_index(STREAM) % 2
    row = 0
    for at, (units, blocks, depth) in enumerate(jobs):
        left, right = operands[2 * at], operands[2 * at + 1]
        product = low(dot_first(left[...], grad_columns(right, 1 - core_at, units)))
        for block in range(blocks):
            columns = product[:, block * LANES : (block + 1) * LANES]
            out[:, :, row : row + depth] = columns.reshape(8, 2, depth, LANES)
            row += depth


TO_X = ((2, False, False), (3, False, False), (2, True, False), (3, True, False))
TO_Y_A = ((0, False, True), (0, False, False), (1, False, True), (1, False, False))
TO_Y_B = ((2, False, True), (3, False, True))
TO_Z_A = ((1, True, True), (1, True, False))
TO_Z_B = ((2, True, True), (3, True, True))
OWN = ((0, True, True), (0, True, False))
PARTS = (TO_X, TO_Y_A, TO_Y_B, TO_Z_A, TO_Z_B, OWN)


def part_at(part):
    z_at, y_at, x_at, _ = place()
    slot, own_y, own_x = part
    return (
        shard_slots(z_at)[slot] * 2 + (y_at if own_y else 1 - y_at),
        x_at if own_x else 1 - x_at,
    )


def small_grad_rows(sums, hidden_bias, work):
    sums0, sums1, sums2, sums3, sums_kv = sums
    rows = (
        (sums0, 0), (sums0, 1), (sums1, 2), (sums1, 1), (sums1, 3), (sums_kv, 0), (sums2, 2),
        (sums2, 1), (sums3, 2), (sums3, 1), (sums1, 0), (sums2, 0), (sums3, 0),
    )
    part = sums0.shape[1] // 8
    work[...] = jnp.zeros_like(work)
    for dp_to in range(8):
        columns = slice(dp_to * part, (dp_to + 1) * part)
        for row, (array, at) in enumerate(rows):
            work[dp_to, row : row + 1, :part] = array[at : at + 1, columns]
        for j in range(hidden_bias.shape[1] // part):
            at = len(rows) + j
            work[dp_to, at : at + 1, :part] = hidden_bias[
                dp_to : dp_to + 1, j * part : (j + 1) * part
            ]


def own_grad_kernel(jobs, sent, small, *refs):
    inputs = 2 * len(jobs) + len(sent)
    operands, came = refs[: 2 * len(jobs)], refs[2 * len(jobs) : inputs]
    extra = refs[inputs : inputs + 6 * small]
    outs = refs[inputs + 6 * small : inputs + 6 * small + len(PARTS)]
    work, *small_work = refs[inputs + 6 * small + len(PARTS) :]
    core_at = lax.axis_index(STREAM) % 2
    row = 0
    for at, (units, blocks, depth) in enumerate(jobs):
        left, right = operands[2 * at], operands[2 * at + 1]
        product = dot_first(left[...], grad_columns(right, core_at, units))
        array, came_row = sent[at]
        for block in range(blocks):
            columns = product[:, block * LANES : (block + 1) * LANES]
            rows = slice(row, row + depth)
            work[:, :, :depth] = columns.reshape(8, 2, depth, LANES) + wide(
                came[array][:, :, came_row : came_row + depth]
            )
            for out, parts in zip(outs, PARTS):
                for j, part in enumerate(parts):
                    dp_from, x_from = part_at(part)
                    out[j, rows] = low(work[dp_from, x_from, :depth])
            row += depth
            came_row += depth
    if small:
        small_grad_rows(extra[:5], extra[5], small_work[0])
        for out, parts in zip(outs, PARTS):
            for j, part in enumerate(parts):
                dp_from, x_from = part_at(part)
                rows = pl.ds(pl.multiple_of(x_from * PAD_ROWS, PAD_ROWS), PAD_ROWS)
                out[j, row : row + PAD_ROWS] = low(small_work[0][dp_from, rows])


def reduce_steps(to_x, to_y_a, to_y_b, to_z_a, to_z_b, own):
    from_y_a, from_x = yield [(to_y_a, DP, BESIDE), (to_x, STREAM, ACROSS)]
    from_y_b, mate = yield [
        (low(wide(to_y_b) + wide(from_x[:2])), DP, BESIDE),
        (low(wide(to_z_a) + wide(from_y_a[2:])), DP, PAIR),
    ]
    far = wide(to_z_b) + wide(from_x[2:]) + wide(from_y_b)
    (by_mate,) = yield [(low(far[1]), DP, PAIR)]
    (half,) = yield [(low(far[0] + wide(by_mate)), DP, HALFWAY)]
    total = wide(own) + wide(from_y_a[:2]) + wide(mate)
    total = low(jnp.stack((total[0] + wide(half), total[1])))
    (from_x,) = yield [(total, STREAM, ACROSS)]
    total = low(wide(total) + wide(from_x[::-1]))
    return total, lax.ppermute(total, STREAM, CORE)


def unpack_kernel(jobs, small, mine, other, *outs):
    _, _, x_at, core_at = place()
    for source, core_from in ((mine, core_at), (other, 1 - core_at)):
        for j in range(2):
            x_from = x_at if j == 0 else 1 - x_at
            for out_at, lead, units, row, depth in jobs:
                out = outs[out_at] if lead is None else outs[out_at].at[lead]
                for unit in range(units):
                    at = row + unit * depth
                    start = core_from * (units * LANES) + unit * LANES
                    out[
                        pl.ds(pl.multiple_of(x_from * depth, 8), depth),
                        pl.ds(pl.multiple_of(start, 128), LANES),
                    ] = wide(source[j, at : at + depth])
    if small is not None:
        biases, gains, hidden_bias, work = outs[-4:]
        for j in range(2):
            x_from = x_at if j == 0 else 1 - x_at
            rows = slice(small, small + PAD_ROWS)
            work[pl.ds(pl.multiple_of(x_from * PAD_ROWS, 8), PAD_ROWS)] = wide(
                mine[j, rows]
            ) + wide(other[j, rows])
        part = biases.shape[1]
        biases[...] = work[:G_1, :part]
        gains[...] = work[G_1 : G_3 + 1, :part]
        hidden_bias[...] = work[G_3 + 1 : G_3 + 1 + hidden_bias.shape[0], :part]


def reduce_plain(parts):
    shards = []
    for left, right in parts:
        if right.ndim == 2:
            whole = low(dot_first(left, right))
            own = lax.psum_scatter(whole, DP, scatter_dimension=0, tiled=True)
        else:
            whole = low(jnp.stack([dot_first(left, r) for r in right]))
            own = lax.psum_scatter(whole, DP, scatter_dimension=1, tiled=True)
        shards.append(wide(lax.psum(own, STREAM)))
    return shards


class Group:
    def __init__(self):
        self.operands, self.jobs, self.out_jobs, self.out_shapes = [], [], [], []
        self.rows, self.flops, self.sent, self.came, self.from_sent = 0, 0, [], [], []

    def sibling(self, tie, *parts):
        jobs, operands, rows, flops = [], [], 0, 0
        for left, right in parts:
            operands += [left, right]
            depth = left.shape[1] // 16
            units = right.shape[-1] // (2 * LANES)
            leads = [None] if right.ndim == 2 else range(right.shape[0])
            jobs.append((units, units * len(leads), depth))
            self.from_sent.append((len(self.sent), rows))
            for lead in leads:
                self.out_jobs.append(
                    (len(self.out_shapes), lead, units, self.rows + rows, depth)
                )
                rows += units * depth
            self.out_shapes.append(
                shape((*right.shape[:-2], 2 * depth, right.shape[-1]), F32)
            )
            flops += left.shape[0] * left.shape[1] * right.size // right.shape[-2]
        self.sent.append(
            call(
                functools.partial(sibling_grad_kernel, jobs),
                shape((8, 2, rows, LANES)),
                [VMEM] * len(operands),
                flops=flops,
            )(tie(operands[0]), *operands[1:])
        )
        self.jobs += jobs
        self.operands += operands
        self.rows += rows
        self.flops += flops
        return self.sent[-1]

    def core_move(self):
        def steps(sent):
            (came,) = yield [(sent, STREAM, CORE)]
            self.came.append(came)

        return Mover(steps(self.sent[-1]))

    def own(self, tie, small=()):
        deepest = max(job[-1] for job in self.jobs)
        scratch = [pltpu.VMEM((8, 2, deepest, LANES), F32)]
        if small:
            scratch.append(pltpu.VMEM((8, 2 * PAD_ROWS, LANES), F32))
        rows = self.rows + PAD_ROWS * bool(small)
        came = [self.came[array] for array, _ in self.from_sent]
        self.parts = call(
            functools.partial(
                own_grad_kernel,
                self.jobs,
                [(at, row) for at, (_, row) in enumerate(self.from_sent)],
                bool(small),
            ),
            [shape((len(parts), rows, LANES)) for parts in PARTS],
            [VMEM] * (len(self.operands) + len(came) + len(small)),
            scratch,
            flops=self.flops,
        )(tie(self.operands[0]), *self.operands[1:], *came, *small)
        return self.parts

    def move(self):
        return Mover(reduce_steps(*self.parts))

    def unpack(self, moved, small=()):
        return call(
            functools.partial(unpack_kernel, self.out_jobs, self.rows if small else None),
            [*self.out_shapes, *small],
            [VMEM, VMEM],
            [pltpu.VMEM((2 * PAD_ROWS, LANES), F32)] * bool(small),
        )(*moved)


def norm_parts(summed):
    center = summed - jnp.mean(summed, axis=-1, keepdims=True)
    inverse = lax.rsqrt(jnp.mean(center * center, axis=-1, keepdims=True) + EPSILON)
    return center * inverse, inverse


def norm_back(upstream, normed, inverse, gain):
    scaled = upstream * gain
    return inverse * (
        scaled
        - jnp.mean(scaled, axis=-1, keepdims=True)
        - normed * jnp.mean(scaled * normed, axis=-1, keepdims=True)
    )


def heads_apart(four):
    head = lax.broadcasted_iota(jnp.int32, four.shape, 1) // 64
    return low(jnp.concatenate([jnp.where(head == j, four, 0.0) for j in range(4)], axis=0))


def heads_joined(stacked):
    rows = stacked.shape[0] // 4
    head = lax.broadcasted_iota(jnp.int32, (rows, stacked.shape[1]), 1) // 64
    made = stacked[:rows]
    for j in range(1, 4):
        made = jnp.where(head == j, stacked[j * rows : (j + 1) * rows], made)
    return made


def quads():
    return [slice(j * 256, (j + 1) * 256) for j in range(HEADS // 4)]


def softmax(scores):
    raised = jnp.exp(scores - jnp.max(scores, axis=-1, keepdims=True))
    return raised * (1.0 / jnp.sum(raised, axis=-1, keepdims=True))


def score_back(weight, back):
    return low(weight * (back - jnp.sum(back * weight, axis=-1, keepdims=True)))


def row_sum(value):
    return jnp.sum(value, axis=0, keepdims=True)


def self_kernel(seq, lengths, x_ref, w_ref, vec, qkv_ref, out_ref, q, k, v, o):
    tokens = x_ref.shape[0]
    for j, (scratch, bias) in enumerate(((q, B_Q), (k, None), (v, B_V))):
        for c in range(2):
            columns = slice(c * LANES, (c + 1) * LANES)
            made = dot(x_ref[...], w_ref[c, j])
            if bias is not None:
                made = made + vec[bias : bias + 1, columns]
            made = low(made)
            qkv_ref[j, :, columns] = made
            scratch[:, columns] = wide(made)

    def step(r, _):
        rows = pl.ds(pl.multiple_of(r * seq, 8), seq)
        valid = lax.broadcasted_iota(jnp.int32, (4 * seq, seq), 1) < lengths[r]
        asked = [heads_apart(q[rows, c] * 0.125) for c in quads()]
        scores = [dot_last(a, low(k[rows, c])) for a, c in zip(asked, quads())]
        weights = [softmax(jnp.where(valid, score, -jnp.inf)) for score in scores]
        made = [dot(low(w), low(v[rows, c])) for w, c in zip(weights, quads())]
        for part, c in zip(made, quads()):
            o[rows, c] = heads_joined(part)
        return 0

    lax.fori_loop(0, tokens // seq, step, 0, unroll=2)
    out_ref[...] = low(o[...])


def first_norm_kernel(seq, o_ref, x_ref, wso, wcq, vec, normed, inverse, h_low, qc, z):
    for c in range(2):
        columns = slice(c * LANES, (c + 1) * LANES)
        z[:, columns] = (
            dot(o_ref[...], wso[c, 0])
            + vec[B_SO : B_SO + 1, columns]
            + wide(x_ref[:, columns])
        )
    made, scale = norm_parts(z[...])
    normed[...] = made
    inverse[...] = scale
    h_low[...] = low(made * vec[G_1 : G_1 + 1] + vec[B_N1 : B_N1 + 1])
    for c in range(2):
        columns = slice(c * LANES, (c + 1) * LANES)
        qc[:, columns] = low(dot(h_low[...], wcq[c, 0]) + vec[B_CQ : B_CQ + 1, columns])


def pixel_kernel(patch_ref, out_ref):
    images, patches, _ = patch_ref.shape
    out_ref[:, :patches] = patch_ref[...]
    out_ref[:, patches:] = jnp.zeros_like(out_ref[:, patches:])


def image_kernel(pixels, w_ref, vec, kv_ref):
    slots, _, images, padded, _ = kv_ref.shape
    for slot in range(slots):
        for c in range(2):
            columns = slice(c * LANES, (c + 1) * LANES)
            for j in range(2):
                made = dot(pixels[slot].reshape(images * padded, -1), w_ref[c, j])
                if j == 1:
                    made = made + vec[B_CV : B_CV + 1, columns]
                kv_ref[slot, j, :, :, columns] = low(made).reshape(images, padded, LANES)


def cross_kernel(
    seq, patches, micro_rows, slots, qc, kv, n1, wco, vec, oc, n2, inverse, h_low, q, o
):
    q[...] = wide(qc[...]) * 0.125
    tokens = qc.shape[0]
    padded = kv.shape[3]
    there = lax.broadcasted_iota(jnp.int32, (4 * seq, padded), 1) < patches

    def step(r, _):
        rows = pl.ds(pl.multiple_of(r * seq, 8), seq)
        slot, m = slots[r], r // micro_rows
        asked = [heads_apart(q[rows, c]) for c in quads()]
        scores = [dot_last(a, kv[slot, 0, m, :, c]) for a, c in zip(asked, quads())]
        weights = [softmax(jnp.where(there, score, -jnp.inf)) for score in scores]
        made = [dot(low(w), kv[slot, 1, m, :, c]) for w, c in zip(weights, quads())]
        for part, c in zip(made, quads()):
            o[rows, c] = heads_joined(part)
        return 0

    lax.fori_loop(0, tokens // seq, step, 0, unroll=2)
    oc[...] = low(o[...])
    for c in range(2):
        columns = slice(c * LANES, (c + 1) * LANES)
        first = n1[:, columns] * vec[G_1 : G_1 + 1, columns] + vec[B_N1 : B_N1 + 1, columns]
        o[:, columns] = first + dot(oc[...], wco[c, 0]) + vec[B_CO : B_CO + 1, columns]
    made, scale = norm_parts(o[...])
    n2[...] = made
    inverse[...] = scale
    h_low[...] = low(made * vec[G_2 : G_2 + 1] + vec[B_N2 : B_N2 + 1])


def small_rows_kernel(shards, vec, hidden_bias, part):
    wide_rows = G_3 + 1
    vec[...] = jnp.zeros_like(vec)
    for dp_from in range(8):
        rows = wide(shards[dp_from * 2 * PAD_ROWS : (dp_from + 1) * 2 * PAD_ROWS])
        vec[:wide_rows, dp_from * part : (dp_from + 1) * part] = rows[:wide_rows, :part]
        for j in range(LANES // part):
            hidden_bias[dp_from : dp_from + 1, j * part : (j + 1) * part] = rows[
                wide_rows + j : wide_rows + j + 1, :part
            ]


def take_weights(units, sources, wholes, outs, in_sems, out_sems, kept):
    if len(sources) == len(units):
        copies = [
            [pltpu.make_async_copy(source, whole, in_sems.at[at])]
            for at, (source, whole) in enumerate(zip(sources, wholes))
        ]
    else:
        copies = piece_copies(units, sources, wholes, in_sems)
    for of_weight in copies:
        for copy in of_weight:
            copy.start()

    def take(at):
        for copy in copies[at]:
            copy.wait()
        if outs[at] is not None:
            send(wholes[at], outs[at])

    def send(source, target):
        kept.append(pltpu.make_async_copy(source, target, out_sems.at[len(kept)]))
        kept[-1].start()

    return take, send


def text_kernel(units, gathered, seq, lengths, text, *refs):
    sources, refs = refs[:gathered], refs[gathered:]
    if gathered == len(units):
        small, refs = refs[:2], refs[2:]
    outs, refs = refs[:11], refs[11:]
    vec, hidden_bias, attended, n1, inverse1, h1, qc, qkv_out, *w_outs = outs
    wholes, (qkv, q, k, v, o, in_sems, out_sems) = refs[:4], refs[4:]
    w_small, w_qkv, w_so, w_cq = wholes
    kept = []
    take, send = take_weights(units, sources, wholes, (None, *w_outs), in_sems, out_sems, kept)
    take(0)
    if gathered == len(units):
        vec[...], hidden_bias[...] = small[0][...], small[1][...]
    else:
        small_rows_kernel(w_small.at[0, 0], vec, hidden_bias, text.shape[1] // 8)
    take(1)
    self_kernel(seq, lengths, text, w_qkv, vec, qkv, attended, q, k, v, o)
    send(qkv, qkv_out)
    take(2)
    take(3)
    first_norm_kernel(seq, attended, text, w_so, w_cq, vec, n1, inverse1, h1, qc, o)
    for copy in kept:
        copy.wait()


def patch_kernel(units, gathered, seq, patches, micro_rows, slots, qc, n1, vec, *refs):
    sources, held, refs = refs[:gathered], refs[gathered : gathered + 4], refs[gathered + 4 :]
    (oc, n2, inverse2, h2, kv_out, pixels_out, *w_outs), refs = refs[:8], refs[8:]
    wholes, (kv, pixels, q, o, in_sems, pixel_sems, out_sems) = refs[:2], refs[2:]
    w_kv, w_co = wholes
    pixel_copies = [
        pltpu.make_async_copy(image, pixels.at[at], pixel_sems.at[at])
        for at, image in enumerate(held)
    ]
    for copy in pixel_copies:
        copy.start()
    kept = []
    take, send = take_weights(units, sources, wholes, w_outs, in_sems, out_sems, kept)
    for copy in pixel_copies:
        copy.wait()
    send(pixels, pixels_out)
    take(0)
    image_kernel(pixels, w_kv, vec, kv)
    send(kv, kv_out)
    take(1)
    cross_kernel(
        seq, patches, micro_rows, slots, qc, kv, n1, w_co, vec, oc, n2, inverse2, h2, q, o
    )
    for copy in kept:
        copy.wait()


def hidden_weights(w, block, in_units):
    core, unit = divmod(block, in_units)
    depth = w.shape[3] // 2 // in_units
    return w[:, :, core, unit * depth : (unit + 1) * depth].reshape(-1, LANES)


def ffn_kernel(
    gathered, in_units, seq, lengths, h2, bias, n2, cot, vec, *refs
):
    sources, refs = refs[:gathered], refs[gathered:]
    out, dz, df, rows_out, active, slope, w_out, w, total, in_sems, out_sem = refs
    if gathered == 1:
        copies = [pltpu.make_async_copy(sources[0], w, in_sems.at[0])]
    else:
        copies = [
            pltpu.make_async_copy(
                piece, w.at[z_from * 2 + y_from, x_from, core_from], in_sems.at[at]
            )
            for at, (piece, z_from, y_from, x_from, core_from) in enumerate(piece_places(sources))
        ]
    for copy in copies:
        copy.start()
    for copy in copies:
        copy.wait()
    keep = pltpu.make_async_copy(w, w_out, out_sem.at[0])
    keep.start()
    for block in range(2 * in_units):
        columns = slice(block * LANES, (block + 1) * LANES)
        pre = dot(h2[...], hidden_weights(w, block, in_units)) + bias[block : block + 1]
        cumulative = 0.5 * (1.0 + lax.erf(pre * ROOT_HALF))
        active[:, columns] = low(pre * cumulative)
        slope[:, columns] = low(cumulative + pre * INV_ROOT_TAU * jnp.exp(-0.5 * pre * pre))
    half_rows = w.shape[3] // 2
    for c in range(2):
        columns = slice(c * LANES, (c + 1) * LANES)
        made = None
        for part in range(4):
            weights = w[2 * part : 2 * part + 2, :, c, half_rows:].reshape(-1, LANES)
            depth = weights.shape[0]
            term = dot(active[:, part * depth : (part + 1) * depth], weights)
            made = term if made is None else made + term
        total[:, columns] = made

    def step(r, sums):
        rows = pl.ds(pl.multiple_of(r * seq, 8), seq)
        second = n2[rows, :] * vec[G_2 : G_2 + 1] + vec[B_N2 : B_N2 + 1]
        made, scale = norm_parts(second + total[rows, :] + vec[B_FO : B_FO + 1])
        out[r] = low(made * vec[G_3 : G_3 + 1] + vec[B_N3 : B_N3 + 1])
        valid = lax.broadcasted_iota(jnp.int32, made.shape, 0) < lengths[r]
        upstream = jnp.where(valid, wide(cot[r]), 0.0)
        back = norm_back(upstream, made, scale, vec[G_3 : G_3 + 1])
        dz[rows, :] = back
        gain, shift, lowered = sums
        return (
            gain + row_sum(upstream * made),
            shift + row_sum(upstream),
            lowered + row_sum(wide(low(back))),
        )

    zero = jnp.zeros((1, total.shape[1]), F32)
    sums = lax.fori_loop(0, out.shape[0], step, (zero, zero, zero), unroll=2)
    df[...] = low(dz[...])
    for j in range(3):
        rows_out[j : j + 1] = sums[j]
    rows_out[3:8] = jnp.zeros((5, total.shape[1]), F32)
    keep.wait()


def norm_back_rows(total, dz_ref, normed, inverse, gain, dz, low_ref, rows_out, step_rows):
    def step(r, sums):
        rows = pl.ds(pl.multiple_of(r * step_rows, 8), step_rows)
        upstream = total[rows, :] + dz_ref[rows, :]
        made = normed[rows, :]
        back = norm_back(upstream, made, inverse[rows, :], gain)
        dz[rows, :] = back
        return (
            sums[0] + row_sum(upstream * made),
            sums[1] + row_sum(upstream),
            sums[2] + row_sum(wide(low(back))),
        )

    zero = jnp.zeros((1, total.shape[1]), F32)
    sums = lax.fori_loop(0, total.shape[0] // step_rows, step, (zero, zero, zero))
    low_ref[...] = low(dz[...])
    for j in range(3):
        rows_out[j : j + 1] = sums[j]
    rows_out[3:8] = jnp.zeros((5, total.shape[1]), F32)


def hidden_back_kernel(
    seq, df, wout, win, slope, dz3, n2, inverse, vec, du, bias_out, dz2, dac, rows_out, total
):
    i = pl.program_id(0)

    @pl.when(i == 0)
    def _():
        total[...] = jnp.zeros_like(total)

    raw = dot_last(df[:, :LANES], wout[0, :, 0].reshape(-1, LANES))
    raw = raw + dot_last(df[:, LANES:], wout[0, :, 1].reshape(-1, LANES))
    made = low(raw * wide(slope[...]))
    du[...] = made
    bias_out[pl.ds(i, 1), :] = row_sum(wide(made))
    total[...] += dot_last(made, win[:, :, 0].reshape(-1, LANES))

    @pl.when(i == pl.num_programs(0) - 1)
    def _():
        norm_back_rows(
            total, dz3, n2, inverse, vec[G_2 : G_2 + 1], dz2, dac, rows_out, seq
        )


def cross_back_kernel(
    seq, patches, micro_rows, slots, dac, qc, kv, wco, dqc, dkv_out, dkv, q, do, dq
):
    q[...] = wide(qc[...]) * 0.125
    do[...] = wide(
        low(dot_last(dac[:, :LANES], wco[0, 0]) + dot_last(dac[:, LANES:], wco[1, 0]))
    )
    dkv[...] = jnp.zeros_like(dkv)
    tokens = qc.shape[0]
    padded = kv.shape[3]
    there = lax.broadcasted_iota(jnp.int32, (4 * seq, padded), 1) < patches

    def step(r, _):
        rows = pl.ds(pl.multiple_of(r * seq, 8), seq)
        slot, m = slots[r], r // micro_rows
        asked = [heads_apart(q[rows, c]) for c in quads()]
        came = [heads_apart(do[rows, c]) for c in quads()]
        keys = [kv[slot, 0, m, :, c] for c in quads()]
        values = [kv[slot, 1, m, :, c] for c in quads()]
        scores = [dot_last(a, key) for a, key in zip(asked, keys)]
        backs = [dot_last(d, value) for d, value in zip(came, values)]
        weights = [softmax(jnp.where(there, score, -jnp.inf)) for score in scores]
        backs = [score_back(w, b) for w, b in zip(weights, backs)]
        queries = [heads_joined(dot(b, key)) for b, key in zip(backs, keys)]
        key_parts = [dot_first(b, a) for b, a in zip(backs, asked)]
        value_parts = [dot_first(low(w), d) for w, d in zip(weights, came)]
        for j, c in enumerate(quads()):
            dq[rows, c] = queries[j] * 0.125
            dkv[0, slot, m, :, c] += key_parts[j]
            dkv[1, slot, m, :, c] += value_parts[j]
        return 0

    lax.fori_loop(0, tokens // seq, step, 0, unroll=2)
    dqc[...] = low(dq[...])
    dkv_out[...] = low(dkv[...])


def first_back_kernel(seq, dqc, wcq, dz2, n1, inverse, vec, dz1, da, rows_out, total):
    total[...] = dot_last(dqc[:, :LANES], wcq[0, 0]) + dot_last(dqc[:, LANES:], wcq[1, 0])
    norm_back_rows(total, dz2, n1, inverse, vec[G_1 : G_1 + 1], dz1, da, rows_out, seq)
    rows_out[3:4] = row_sum(wide(dqc[...]))


def self_back_kernel(seq, lengths, da, qkv, wso, dqkv, rows_out, q, k, v, do, dq, dk, dv):
    q[...] = wide(qkv[0]) * 0.125
    k[...] = wide(qkv[1])
    v[...] = wide(qkv[2])
    do[...] = wide(low(dot_last(da[:, :LANES], wso[0, 0]) + dot_last(da[:, LANES:], wso[1, 0])))
    tokens = da.shape[0]

    def step(r, _):
        rows = pl.ds(pl.multiple_of(r * seq, 8), seq)
        valid = lax.broadcasted_iota(jnp.int32, (4 * seq, seq), 1) < lengths[r]
        asked = [heads_apart(q[rows, c]) for c in quads()]
        came = [heads_apart(do[rows, c]) for c in quads()]
        keys = [low(k[rows, c]) for c in quads()]
        values = [low(v[rows, c]) for c in quads()]
        scores = [dot_last(a, key) for a, key in zip(asked, keys)]
        backs = [dot_last(d, value) for d, value in zip(came, values)]
        weights = [softmax(jnp.where(valid, score, -jnp.inf)) for score in scores]
        backs = [score_back(w, b) for w, b in zip(weights, backs)]
        queries = [heads_joined(dot(b, key)) for b, key in zip(backs, keys)]
        key_parts = [dot_first(b, a) for b, a in zip(backs, asked)]
        value_parts = [dot_first(low(w), d) for w, d in zip(weights, came)]
        for j, c in enumerate(quads()):
            dq[rows, c] = queries[j] * 0.125
            dk[rows, c] = key_parts[j]
            dv[rows, c] = value_parts[j]
        return 0

    lax.fori_loop(0, tokens // seq, step, 0, unroll=2)
    for j, made in enumerate((dq, dk, dv)):
        dqkv[j] = low(made[...])
    rows_out[0:1] = row_sum(wide(dqkv[0]))
    rows_out[1:2] = row_sum(wide(dqkv[2]))
    rows_out[2:8] = jnp.zeros((6, q.shape[1]), F32)


def text_grad_kernel(dz1, dqkv, w_ref, out, total):
    total[...] = dz1[...]
    for j in range(3):
        for c in range(2):
            total[...] += dot_last(dqkv[j, :, c * LANES : (c + 1) * LANES], w_ref[c, j])
    seq = out.shape[1]
    for r in range(out.shape[0]):
        out[r] = low(total[r * seq : (r + 1) * seq, :])


def patch_grad_kernel(dkv, w_ref, kept, sent, rows_out):
    _, slots, images, padded, width = dkv.shape
    rows = images * padded
    total = jnp.zeros((1, width), F32)
    for slot in range(slots):
        made = None
        for j in range(2):
            grad = dkv[j, slot].reshape(rows, width)
            for c in range(2):
                term = dot_last(grad[:, c * LANES : (c + 1) * LANES], w_ref[c, j])
                made = term if made is None else made + term
        out = sent if slot % 2 else kept
        out[slot // 2] = low(made).reshape(images, padded, w_ref.shape[2])
        total = total + row_sum(wide(grad))
    rows_out[0:1] = total
    rows_out[1:8] = jnp.zeros((7, width), F32)


def on_device(
    text_input,
    patch_input,
    text_lengths,
    image_of_row,
    cotangent,
    self_qkv,
    self_out,
    cross_q,
    cross_kv,
    cross_out,
    ffn_in,
    ffn_out,
    biases,
    norm_gains,
    ffn_bias,
):
    dp = lax.axis_size(DP)
    micros, row_count, seq, width = text_input.shape
    patches, patch_width = patch_input.shape[2:]
    rows_all = micros * row_count
    tokens = rows_all * seq
    hidden = ffn_in.shape[1]
    padded = -(-patches // 16) * 16
    images = micros * patch_input.shape[1]

    part = biases.shape[1]
    small = jnp.concatenate((biases, norm_gains, ffn_bias.reshape(-1, part)))
    small_rows = small.shape[0]
    wide_rows = biases.shape[0] + norm_gains.shape[0]
    small = jnp.pad(small, ((0, 2 * PAD_ROWS - small_rows), (0, LANES - part)))
    small = jnp.broadcast_to(small.reshape(2, PAD_ROWS, LANES), (2, 2, PAD_ROWS, LANES))

    half = width // dp // 2
    half_v = cross_kv.shape[1] // 2
    in_units = hidden // (2 * LANES)
    text_group = (
        (small, self_qkv, self_out, cross_q),
        ((1, PAD_ROWS), (3, half), (1, half), (1, half)),
    )
    patch_group = ((cross_kv, cross_out), ((2, half_v), (1, half)))
    hidden_group = ((ffn_in, ffn_out), ((in_units, half), (1, ffn_out.shape[0] // 2)))

    text = text_input.reshape(tokens, width)
    pixels = call(pixel_kernel, shape((images, padded, patch_width)), [VMEM])(
        patch_input.reshape(images, patches, patch_width)
    )
    lengths = text_lengths.reshape(-1)
    slots = image_of_row.reshape(-1) ^ lax.axis_index(STREAM)
    flat = (tokens, width)
    full = pltpu.VMEM(flat, F32)
    flops = 2 * tokens * width * width
    steps = hidden // LANES
    chunks = hidden // width
    kv_shape = (4, 2, images, padded, width)
    in_block = pl.BlockSpec(
        (8, 2, 1, width // 16, LANES), lambda i: (0, 0, i // in_units, i % in_units, 0)
    )
    v = types.SimpleNamespace()

    bf16 = jnp.bfloat16

    def move_pixels(tied):
        v.across = lax.ppermute(tied, STREAM, ACROSS)
        v.beside = lax.ppermute(tied, STREAM, CORE)
        v.apart = lax.ppermute(v.across, STREAM, CORE)

    def run_text(tie, sources, small_inputs=()):
        units = text_group[1]
        wholes = [(2, 1, 16 * PAD_ROWS, LANES)]
        wholes += [(2, count, depth * 2 * dp, LANES) for count, depth in units[1:]]
        outs = [
            shape((16, width), F32), shape((steps, LANES), F32), shape(flat), shape(flat, F32),
            shape((tokens, 1), F32), shape(flat), shape(flat), shape((3, *flat)),
            *[shape(dims) for dims in wholes[1:]],
        ]
        (
            v.vec, v.hidden_bias, v.attended, v.n1, v.inverse1, v.h1, v.qc, v.qkv,
            v.w_qkv, v.w_so, v.w_cq,
        ) = call(
            functools.partial(text_kernel, units, len(sources), seq),
            outs,
            [SMEM, VMEM] + [ANY] * len(sources) + [VMEM] * len(small_inputs),
            [
                *[pltpu.VMEM(dims, bf16) for dims in wholes],
                pltpu.VMEM((3, *flat), bf16), full, full, full, full,
                pltpu.SemaphoreType.DMA((32 * len(units),)), pltpu.SemaphoreType.DMA((4,)),
            ],
            out_specs=[VMEM] * 7 + [ANY] * 4,
            mib=60,
            flops=8 * flops,
        )(lengths, tie(text), *sources, *small_inputs)
        return v.qc

    def run_patch(tie, sources):
        units = patch_group[1]
        wholes = [(2, count, depth * 2 * dp, LANES) for count, depth in units]
        pixels_shape = (4, images, padded, patch_width)
        outs = [
            shape(flat), shape(flat, F32), shape((tokens, 1), F32), shape(flat),
            shape(kv_shape), shape(pixels_shape), *[shape(dims) for dims in wholes],
        ]
        v.oc, v.n2, v.inverse2, v.h2, v.kv, pixels_all, v.w_kv, v.w_co = call(
            functools.partial(patch_kernel, units, len(sources), seq, patches, row_count),
            outs,
            [SMEM, VMEM, VMEM, VMEM] + [ANY] * (len(sources) + 4),
            [
                *[pltpu.VMEM(dims, bf16) for dims in wholes],
                pltpu.VMEM(kv_shape, bf16), pltpu.VMEM(pixels_shape, bf16), full, full,
                pltpu.SemaphoreType.DMA((32 * len(units),)), pltpu.SemaphoreType.DMA((4,)),
                pltpu.SemaphoreType.DMA((4,)),
            ],
            out_specs=[VMEM] * 4 + [ANY] * 4,
            mib=60,
            flops=18 * flops,
        )(slots, tie(v.qc), v.n1, v.vec, *sources, pixels, v.beside, v.across, v.apart)
        v.pixels_all = pixels_all.reshape(-1, patch_width)
        return v.h2

    def run_ffn(tie, sources):
        w_shape = (8, 2, 2, hidden // 8, LANES)
        v.out_rows, v.dz3, v.df, v.sums3, v.active, v.slope, v.w_hidden = call(
            functools.partial(ffn_kernel, len(sources), in_units, seq),
            [
                shape((rows_all, seq, width)), shape(flat, F32), shape(flat),
                shape((8, width), F32), shape((tokens, hidden)), shape((tokens, hidden)),
                shape(w_shape),
            ],
            [SMEM] + [VMEM] * 5 + [ANY] * len(sources),
            [
                pltpu.VMEM(w_shape, bf16), full, pltpu.SemaphoreType.DMA((32,)),
                pltpu.SemaphoreType.DMA((1,)),
            ],
            out_specs=[VMEM] * 6 + [ANY],
            flops=8 * flops,
        )(
            lengths, tie(v.h2), v.hidden_bias, v.n2,
            cotangent.reshape(rows_all, seq, width), v.vec, *sources,
        )
        return v.df

    def run_hidden_back(tie):
        v.du, v.hidden_bias_grad, v.dz2, v.dac, v.sums2 = call(
            functools.partial(hidden_back_kernel, seq),
            [
                shape((tokens, hidden)),
                shape((steps, LANES), F32),
                shape(flat, F32),
                shape(flat),
                shape((8, width), F32),
            ],
            [
                VMEM,
                pl.BlockSpec((1, 2, 2, hidden // 16, LANES), lambda i: (i, 0, 0, 1, 0)),
                in_block,
                pl.BlockSpec((tokens, LANES), lambda i: (0, i)),
                VMEM,
                VMEM,
                VMEM,
                VMEM,
            ],
            [full],
            out_specs=[pl.BlockSpec((tokens, LANES), lambda i: (0, i)), VMEM, VMEM, VMEM, VMEM],
            grid=(steps,),
            flops=8 * flops,
        )(
            tie(v.df), v.w_hidden, v.w_hidden, v.slope, v.dz3, v.n2, v.inverse2,
            v.vec,
        )
        return v.dac

    def run_cross_back(tie):
        v.dqc, v.dkv_all = call(
            functools.partial(cross_back_kernel, seq, patches, row_count),
            [shape(flat), shape((2, 4, images, padded, width))],
            [SMEM, VMEM, VMEM, VMEM, VMEM],
            [pltpu.VMEM((2, 4, images, padded, width), F32), full, full, full],
            flops=4 * flops,
        )(slots, tie(v.dac), v.qc, v.kv, v.w_co)
        return v.dqc

    def patch_steps():
        (came,) = yield [(v.patch_sent, STREAM, CORE)]
        made = wide(v.patch_kept) + wide(came)
        (across,) = yield [(low(made[1]), STREAM, ACROSS)]
        v.patch_rows = low(made[0] + wide(across))[:, :patches].reshape(patch_input.shape)

    def run_first_back(tie):
        v.dz1, v.da, v.sums1 = call(
            functools.partial(first_back_kernel, seq),
            [shape(flat, F32), shape(flat), shape((8, width), F32)],
            [VMEM] * 6,
            [full],
            flops=flops,
        )(tie(v.dqc), v.w_cq, v.dz2, v.n1, v.inverse1, v.vec)
        return v.da

    def run_self_back(tie):
        v.dqkv, v.sums0 = call(
            functools.partial(self_back_kernel, seq),
            [shape((3, *flat)), shape((8, width), F32)],
            [SMEM, VMEM, VMEM, VMEM],
            [full] * 7,
            flops=4 * flops,
        )(lengths, tie(v.da), v.qkv, v.w_so)
        return v.dqkv

    def run_patch_grad(tie):
        v.patch_kept, v.patch_sent, v.sums_kv = call(
            patch_grad_kernel,
            [shape((2, images, padded, patch_width))] * 2 + [shape((8, width), F32)],
            [VMEM] * 2,
            flops=16 * flops,
        )(tie(v.dkv_all), v.w_kv)
        return v.patch_sent

    def run_text_grad(tie):
        v.text_rows = call(
            text_grad_kernel,
            shape((rows_all, seq, width)),
            [VMEM] * 3,
            [full],
            flops=3 * flops,
        )(tie(v.dz1), v.dqkv, v.w_qkv)
        return v.text_rows

    def small_grads():
        sums0, sums1, sums2, sums3, sums_kv = v.sums0, v.sums1, v.sums2, v.sums3, v.sums_kv
        grads = jnp.concatenate(
            (
                sums0[0:2], sums1[2:3], sums1[1:2], sums1[3:4], sums_kv[0:1], sums2[2:3],
                sums2[1:2], sums3[2:3], sums3[1:2], sums1[0:1], sums2[0:1], sums3[0:1],
            )
        )
        return jnp.concatenate(
            (
                grads.reshape(wide_rows, dp, part).transpose(1, 0, 2),
                v.hidden_bias_grad.reshape(dp, -1, part),
            ),
            axis=1,
        )

    def run_all(moves):
        mover = Mover(moves)
        while not mover.done:
            mover.give([lax.ppermute(array, axis, hops) for array, axis, hops in mover.requests])

    if not special_mesh():
        def free(array):
            return array

        w_small, *wholes = gather_plain(*text_group)
        patch_wholes = gather_plain(*patch_group)
        values = wide(w_small[0, 0].reshape(dp, 2 * PAD_ROWS, LANES)[:, :small_rows, :part])
        vec = values[:, :wide_rows].transpose(1, 0, 2).reshape(wide_rows, width)
        vec = jnp.pad(vec, ((0, 16 - wide_rows), (0, 0)))
        hidden_bias = values[:, wide_rows:].reshape(-1, LANES)
        w_small = w_small[:, :, : 16 * PAD_ROWS]
        w_in = lax.all_gather(ffn_in, DP, axis=0, tiled=True)
        w_out = lax.all_gather(ffn_out, DP, axis=0, tiled=True)
        w_in = w_in.reshape(8, 2, width // 16, 2, in_units, LANES).transpose(0, 1, 3, 4, 2, 5)
        w_in = w_in.reshape(8, 2, 2, -1, LANES)
        w_out = w_out.reshape(8, 2, hidden // 16, 2, LANES).transpose(0, 1, 3, 2, 4)
        w_hidden = jnp.concatenate((w_in, w_out), axis=3)
        move_pixels(pixels)
        run_text(free, (w_small, *wholes), (vec, hidden_bias))
        run_patch(free, patch_wholes)
        run_ffn(free, (w_hidden,))
        for work in (run_hidden_back, run_cross_back, run_patch_grad):
            work(free)
        run_all(patch_steps())
        for work in (run_first_back, run_self_back, run_text_grad):
            work(free)
        s_out, s_in, s_co, s_cq, s_so, s_kv, s_qkv = reduce_plain(
            (
                (v.active, v.df), (v.h2, v.du), (v.oc, v.dac), (v.h1, v.dqc),
                (v.attended, v.da), (v.pixels_all, v.dkv_all.reshape(2, -1, width)), (text, v.dqkv),
            )
        )
        s_small = lax.psum_scatter(low(small_grads()), DP, scatter_dimension=0, tiled=True)
        s_small = wide(lax.psum(s_small, STREAM))[0]
        s_biases = s_small[: biases.shape[0]]
        s_gains = s_small[biases.shape[0] : wide_rows]
        s_hidden_bias = s_small[wide_rows:]
    else:
        clock = Clock()
        gather_text, gather_patch, gather_hidden = (
            Mover(gather_steps(*pack_group(*group)))
            for group in (text_group, patch_group, hidden_group)
        )
        move_pixels(pixels)
        clock.step([gather_text])
        clock.step([gather_text, gather_patch])
        clock.step([gather_hidden, gather_text, gather_patch])
        clock.step(
            [gather_hidden, gather_patch], [lambda tie: run_text(tie, gather_text.result)]
        )
        clock.step([gather_hidden], [lambda tie: run_patch(tie, gather_patch.result)])
        clock.step([gather_hidden], [lambda tie: run_ffn(tie, gather_hidden.result)])

        out_group, in_group, mid_group, last_group = Group(), Group(), Group(), Group()

        def begin_out(tie):
            return out_group.sibling(tie, (v.active, v.df))

        def begin_in(tie):
            return in_group.sibling(tie, (v.h2, v.du))

        def begin_mid(tie):
            return mid_group.sibling(
                tie,
                (v.oc, v.dac),
                (v.h1, v.dqc),
                (v.attended, v.da),
                (v.pixels_all, v.dkv_all.reshape(2, -1, width)),
            )

        def begin_last(tie):
            return last_group.sibling(tie, (text, v.dqkv))

        def own_last(tie):
            return last_group.own(
                tie, (v.sums0, v.sums1, v.sums2, v.sums3, v.sums_kv, v.hidden_bias_grad)
            )

        clock.step([], [begin_out])
        clock.step([out_group.core_move()], [run_hidden_back, out_group.own], eager=True)
        move_out = out_group.move()
        clock.step([], [begin_in])
        clock.step(
            [move_out, in_group.core_move()],
            [run_cross_back, run_first_back, in_group.own, begin_mid],
            eager=True,
        )
        move_in = in_group.move()
        clock.step(
            [move_out, move_in, mid_group.core_move()],
            [run_self_back, run_patch_grad, mid_group.own, begin_last],
            eager=True,
        )
        move_mid, move_patch = mid_group.move(), Mover(patch_steps())
        clock.step(
            [move_out, move_in, move_mid, last_group.core_move(), move_patch],
            [own_last, run_text_grad],
            eager=True,
        )
        move_last = last_group.move()
        movers = [move_out, move_in, move_mid, move_last, move_patch]
        results = {}

        small_shapes = [
            shape((rows, part), F32)
            for rows in (biases.shape[0], norm_gains.shape[0], small_rows - wide_rows)
        ]

        def unpack(group, mover):
            def work(tie):
                results[mover] = group.unpack(
                    (tie(mover.result[0]), mover.result[1]),
                    small_shapes if group is last_group else (),
                )
                return results[mover]
            return work

        groups = [
            (out_group, move_out), (in_group, move_in), (mid_group, move_mid), (last_group, move_last)
        ]
        def ready():
            return [
                unpack(group, mover)
                for group, mover in groups
                if mover.done and mover not in results
            ]

        while not all(mover.done for mover in movers):
            clock.step(movers, ready, eager=True)
        for work in ready():
            work(clock.tie)
        (s_out,), (s_in,) = results[move_out], results[move_in]
        s_co, s_cq, s_so, s_kv = results[move_mid]
        s_qkv, s_biases, s_gains, s_hidden_bias = results[move_last]
    return (
        v.out_rows.reshape(text_input.shape),
        v.text_rows.reshape(text_input.shape),
        v.patch_rows,
        s_qkv,
        s_so,
        s_cq,
        s_kv,
        s_co,
        s_in,
        s_out,
        s_biases,
        s_gains,
        s_hidden_bias.reshape(-1),
    )


def solution(mesh):
    placed = (
        P(None, (DP, STREAM), None, None),
        P(None, (DP, STREAM), None, None),
        P(None, (DP, STREAM)),
        P(None, (DP, STREAM)),
        P(None, (DP, STREAM), None, None),
        P(None, DP, None),
        P(DP, None),
        P(DP, None),
        P(None, DP, None),
        P(DP, None),
        P(DP, None),
        P(DP, None),
        P(None, DP),
        P(None, DP),
        P(DP),
    )
    return jax.shard_map(
        on_device,
        mesh=mesh,
        in_specs=placed,
        out_specs=(
            P(None, (DP, STREAM), None, None),
            P(None, (DP, STREAM), None, None),
            P(None, (DP, STREAM), None, None),
            P(None, DP, None),
            P(DP, None),
            P(DP, None),
            P(None, DP, None),
            P(DP, None),
            P(DP, None),
            P(DP, None),
            P(None, DP),
            P(None, DP),
            P(DP),
        ),
        check_vma=False,
    )
```

```python
import functools
import types

import jax
import jax.numpy as jnp
from jax import lax
from jax.experimental import pallas as pl
from jax.experimental.pallas import tpu as pltpu
from jax.sharding import PartitionSpec as P

HEADS = 12
LANES = 384
PAD_ROWS = 16
MIB = 2**20
DP, STREAM = "dp", "stream"

EPSILON = 1e-06
ROOT_HALF = 0.7071067811865476
INV_ROOT_TAU = 0.3989422804014327

CORE = ((0, 1), (1, 0), (2, 3), (3, 2))
ACROSS = ((0, 2), (2, 0), (1, 3), (3, 1))
BESIDE = ((0, 1), (1, 0), (2, 3), (3, 2), (4, 5), (5, 4), (6, 7), (7, 6))
PAIR = ((0, 2), (2, 0), (1, 3), (3, 1), (4, 6), (6, 4), (5, 7), (7, 5))
HALFWAY = ((0, 4), (4, 0), (1, 5), (5, 1), (2, 6), (6, 2), (3, 7), (7, 3))
MIRROR = ((0, 6), (6, 0), (1, 7), (7, 1), (2, 4), (4, 2), (3, 5), (5, 3))

B_Q, B_V, B_SO, B_N1, B_CQ, B_CV, B_CO, B_N2, B_FO, B_N3, G_1, G_2, G_3 = range(13)


def low(value):
    return value.astype(jnp.bfloat16)


def wide(value):
    return value.astype(jnp.float32)


def dot(left, right):
    return jnp.dot(left, right, preferred_element_type=jnp.float32)


def dot_last(left, right):
    return lax.dot_general(
        left, right, (((1,), (1,)), ((), ())), preferred_element_type=jnp.float32
    )


def dot_first(left, right):
    return lax.dot_general(
        left, right, (((0,), (0,)), ((), ())), preferred_element_type=jnp.float32
    )


def pick(array, index, axis=0):
    return lax.dynamic_index_in_dim(array, index, axis, keepdims=False)


def place():
    dp_at, stream_at = lax.axis_index(DP), lax.axis_index(STREAM)
    return dp_at // 2, dp_at % 2, stream_at // 2, stream_at % 2


class Base:
    def __init__(self, array):
        self.array = array.reshape(-1, LANES)
        self.twin = None

    def exchange(self, tie):
        if self.twin is None:
            self.twin = lax.ppermute(tie(self.array), STREAM, CORE)
        return self.twin


class Piece:
    def __init__(self, base, row, dims):
        self.base, self.row, self.dims = base, row, dims

    def value(self):
        rows = 1
        for size in self.dims[:-1]:
            rows *= size
        return self.base.array[self.row : self.row + rows].reshape(self.dims)


class Clock:
    def __init__(self):
        self.before = []
        self.came = []

    def take(self, arrays):
        given = {}
        for array, (_, sends) in zip(arrays, self.came):
            row = 0
            base = Base(array) if sends[0][0].pieces else None
            for mover, at, sent in sends:
                part = array
                if base is not None:
                    part = Piece(base, row, sent.shape)
                    row += sent.size // LANES
                elif len(sends) > 1:
                    rows = sent.size // LANES
                    part = array[row : row + rows].reshape(sent.shape)
                    row += rows
                given.setdefault(mover, {})[at] = part
        self.came = []
        for mover, parts in given.items():
            mover.give([parts[at] for at in range(len(parts))])

    def step(self, moving=(), compute=(), eager=False):
        arrays = [array for array, _ in self.came]
        arrays, self.before = lax.optimization_barrier((arrays, self.before + arrays[:1]))
        self.take(arrays)
        ways = {}
        for mover in moving:
            if mover.done:
                continue
            for at, (array, axis, hops) in enumerate(mover.requests):
                alone = hops is CORE or array.shape[-1] != LANES
                key = (axis, hops, (mover, at) if alone else None)
                ways.setdefault(key, []).append((mover, at, array))
        joined = [
            sends[0][2]
            if len(sends) == 1
            else jnp.concatenate([array.reshape(-1, LANES) for _, _, array in sends])
            for sends in ways.values()
        ]
        joined, self.before = lax.optimization_barrier((joined, self.before))
        self.came = [
            (lax.ppermute(array, axis, hops), sends)
            for array, ((axis, hops, _), sends) in zip(joined, ways.items())
        ]
        after = []
        if eager:
            movers = [mover for sends in ways.values() for mover, _, _ in sends]
            self.take([array for array, _ in self.came])
            for mover in dict.fromkeys(movers):
                if mover.done:
                    after += jax.tree.leaves(mover.result)
                else:
                    after += [array for array, _, _ in mover.requests]
        for work in compute() if callable(compute) else compute:
            after += jax.tree.leaves(work(self.tie))
        if after:
            self.before = after

    def tie(self, array):
        return lax.optimization_barrier((array, self.before))[0]


class Mover:
    def __init__(self, steps, pieces=False):
        self.steps = steps
        self.pieces = pieces
        self.done = False
        self.result = None
        self.requests = next(steps)

    def give(self, came):
        try:
            self.requests = self.steps.send(came)
        except StopIteration as stop:
            self.done, self.result = True, stop.value


def special_mesh():
    return lax.axis_size(DP) == 8 and lax.axis_size(STREAM) == 4


VMEM = pl.BlockSpec(memory_space=pltpu.VMEM)
SMEM = pl.BlockSpec(memory_space=pltpu.SMEM)
ANY = pl.BlockSpec(memory_space=pl.ANY)


def call(kernel, out_shape, in_specs, scratch=(), mib=24, flops=0, out_specs=None, **more):
    return pl.pallas_call(
        kernel,
        out_shape=out_shape,
        in_specs=in_specs,
        out_specs=jax.tree.map(lambda _: VMEM, out_shape) if out_specs is None else out_specs,
        scratch_shapes=list(scratch),
        compiler_params=pltpu.CompilerParams(vmem_limit_bytes=mib * MIB),
        cost_estimate=pl.CostEstimate(flops=flops, bytes_accessed=4 * MIB, transcendentals=0),
        **more,
    )


def shape(dims, dtype=jnp.bfloat16):
    return jax.ShapeDtypeStruct(tuple(dims), dtype)


F32 = jnp.float32


def pack_shard(shard, units):
    if shard.ndim == 2:
        rows, _ = shard.shape
        split = shard.reshape(2, rows // 2, 2, units, LANES).transpose(2, 0, 3, 1, 4)
    else:
        _, rows, _ = shard.shape
        split = shard.reshape(units, 2, rows // 2, 2, LANES).transpose(3, 1, 0, 2, 4)
    return split.reshape(2, 2, units * rows // 2, LANES)


def pack_kernel(units, *refs):
    _, _, x_at, core_at = place()
    shards, (both, own, own_x) = refs[: len(units)], refs[len(units) :]
    row = 0
    for shard, (count, depth) in zip(shards, units):
        if len(shard.shape) == 4:
            both[:, :, row : row + depth] = shard[...]
            row += depth
            continue
        for unit in range(count):
            rows = slice(row, row + depth)
            for x in range(2):
                for c in range(2):
                    if len(shard.shape) == 3:
                        block = shard[unit, x * depth : (x + 1) * depth, c * LANES : (c + 1) * LANES]
                    else:
                        start = (c * count + unit) * LANES
                        block = shard[x * depth : (x + 1) * depth, start : start + LANES]
                    both[c, x, rows] = block
            row += depth
    own[...] = both[core_at]
    own_x[...] = both[core_at, x_at]


def pack_own_kernel(units, *refs):
    _, _, x_at, core_at = place()
    shards, out = refs[:-1], refs[-1]
    row = 0
    for shard, (count, depth) in zip(shards, units):
        for unit in range(count):
            start = (core_at * count + unit) * LANES
            out[row : row + depth] = shard[
                pl.ds(pl.multiple_of(x_at * depth, 16), depth),
                pl.ds(pl.multiple_of(start, 128), LANES),
            ]
            row += depth


def pack_group(shards, units):
    rows = sum(count * depth for count, depth in units)
    return call(
        functools.partial(pack_kernel, units),
        [shape((2, 2, rows, LANES)), shape((2, rows, LANES)), shape((rows, LANES))],
        [VMEM] * len(shards),
    )(*shards)


def pack_own(shards, units):
    rows = sum(count * depth for count, depth in units)
    return call(
        functools.partial(pack_own_kernel, units), shape((rows, LANES)), [VMEM] * len(shards)
    )(*shards)


def gather_steps(own_both, own, own_x):
    x_at = lax.axis_index(STREAM) // 2
    mate, half_z, mirror_z, beside = yield [
        (own, DP, PAIR),
        (own_x, DP, HALFWAY),
        (own_x, DP, MIRROR),
        (own, DP, BESIDE),
    ]
    mate_halves = mate.value()
    others = jnp.stack((pick(mate_halves, x_at), half_z.value(), mirror_z.value()))
    beside_others, half_x, mirror_x = yield [
        (others, DP, BESIDE),
        (half_z.value(), STREAM, ACROSS),
        (mirror_z.value(), STREAM, ACROSS),
    ]
    others_x, mate_x = yield [
        (beside_others.value()[1:], STREAM, ACROSS),
        (pick(mate_halves, 1 - x_at), DP, BESIDE),
    ]
    whole = Piece(Base(own_both), 0, own_both.shape)
    return (
        whole, mate, beside, half_z, mirror_z, half_x, mirror_x, beside_others, others_x, mate_x
    )


def piece_sources(pieces, tie):
    own, *received = pieces
    rows = own.dims[2]
    arrays, spec = [own.base.array], [(0, at * rows) for at in range(4)]
    known = {}

    def find(piece, theirs):
        key = (piece.base, theirs)
        if key not in known:
            known[key] = len(arrays)
            arrays.append(piece.base.exchange(tie) if theirs else piece.base.array)
        return known[key]

    for theirs in (False, True):
        mate, beside, half_z, mirror_z, half_x, mirror_x, others, others_x, mate_x = received
        blocks = [(mate, 0), (beside, 0), (mate, 1), (beside, 1)]
        blocks += [(half_z, 0), (mirror_z, 0), (half_x, 0), (mirror_x, 0)]
        blocks += [(others, 0), (others, 1), (others, 2), (mate_x, 0), (others_x, 0), (others_x, 1)]
        spec += [(find(piece, theirs), piece.row + block * rows) for piece, block in blocks]
    return arrays, tuple(spec)


def piece_places(spec, sources):
    z_at, y_at, x_at, core_at = place()
    _, z_mate, z_half, z_mirror = shard_slots(z_at)
    far_y, far_x = 1 - y_at, 1 - x_at
    places = [(z_at, y_at, x_from, core_from) for core_from in range(2) for x_from in range(2)]
    for core_from in (core_at, 1 - core_at):
        for x_from in range(2):
            places.append((z_mate, y_at, x_from, core_from))
            places.append((z_at, far_y, x_from, core_from))
        places += [
            (z_half, y_at, x_at, core_from),
            (z_mirror, y_at, x_at, core_from),
            (z_half, y_at, far_x, core_from),
            (z_mirror, y_at, far_x, core_from),
            (z_mate, far_y, x_at, core_from),
            (z_half, far_y, x_at, core_from),
            (z_mirror, far_y, x_at, core_from),
            (z_mate, far_y, far_x, core_from),
            (z_half, far_y, far_x, core_from),
            (z_mirror, far_y, far_x, core_from),
        ]
    return [(sources[at], row, *where) for (at, row), where in zip(spec, places)]


def piece_copies(units, spec, sources, wholes, sems):
    parts = piece_places(spec, sources)
    copies, row, sem = [], 0, 0
    for (count, depth), whole in zip(units, wholes):
        of_weight = []
        for source, first, z_from, y_from, x_from, core_from in parts:
            start = (z_from * 2 + y_from) * (2 * depth) + x_from * depth
            of_weight.append(
                pltpu.make_async_copy(
                    source.at[pl.ds(first + row, count * depth)].reshape(count, depth, LANES),
                    whole.at[core_from, :, pl.ds(pl.multiple_of(start, 16), depth)],
                    sems.at[sem],
                )
            )
            sem += 1
        copies.append(of_weight)
        row += count * depth
    return copies


def gather_plain(shards, units):
    packed = [
        shard if shard.ndim == 4 else pack_shard(shard, count)
        for shard, (count, _) in zip(shards, units)
    ]
    whole = lax.all_gather(jnp.concatenate(packed, axis=2), DP, axis=0, tiled=False)
    results = []
    row = 0
    for count, depth in units:
        part = whole[:, :, :, row : row + count * depth]
        part = part.reshape(-1, 2, 2, count, depth, LANES).transpose(1, 3, 0, 2, 4, 5)
        results.append(part.reshape(2, count, -1, LANES))
        row += count * depth
    return results


def shard_slots(z_at):
    return z_at, z_at + 1 - 2 * (z_at % 2), (z_at + 2) % 4, 3 - z_at


def grad_columns(right, core, units):
    blocks = []
    for lead in [None] if len(right.shape) == 2 else range(right.shape[0]):
        of_lead = right if lead is None else right.at[lead]
        start = pl.multiple_of(core * (units * LANES), 128)
        blocks.append(of_lead[:, pl.ds(start, units * LANES)])
    return blocks[0] if len(blocks) == 1 else jnp.concatenate(blocks, axis=1)


def sibling_grad_kernel(jobs, *refs):
    operands, out = refs[:-1], refs[-1]
    core_at = lax.axis_index(STREAM) % 2
    row = 0
    for at, (units, blocks, depth) in enumerate(jobs):
        left, right = operands[2 * at], operands[2 * at + 1]
        product = low(dot_first(left[...], grad_columns(right, 1 - core_at, units)))
        for block in range(blocks):
            columns = product[:, block * LANES : (block + 1) * LANES]
            out[:, :, row : row + depth] = columns.reshape(8, 2, depth, LANES)
            row += depth


TO_X = ((2, False, False), (3, False, False), (2, True, False), (3, True, False))
TO_Y_A = ((0, False, True), (1, False, True))
TO_Z_A = ((1, False, False), (1, True, False))
TO_Y_B = ((2, False, True), (3, False, True), (0, False, False))
TO_Z_B = ((1, True, True),)
TO_Z_C = ((2, True, True), (3, True, True))
OWN = ((0, True, True), (0, True, False))
PARTS = (TO_X, TO_Y_A, TO_Z_A, TO_Y_B, TO_Z_B, TO_Z_C, OWN)


def part_at(part):
    z_at, y_at, x_at, _ = place()
    slot, own_y, own_x = part
    return (
        shard_slots(z_at)[slot] * 2 + (y_at if own_y else 1 - y_at),
        x_at if own_x else 1 - x_at,
    )


def small_grad_rows(sums, hidden_bias, work):
    sums0, sums1, sums2, sums3, sums_kv = sums
    rows = (
        (sums0, 0), (sums0, 1), (sums1, 2), (sums1, 1), (sums1, 3), (sums_kv, 0), (sums2, 2),
        (sums2, 1), (sums3, 2), (sums3, 1), (sums1, 0), (sums2, 0), (sums3, 0),
    )
    part = sums0.shape[1] // 8
    work[...] = jnp.zeros_like(work)
    for dp_to in range(8):
        columns = slice(dp_to * part, (dp_to + 1) * part)
        for row, (array, at) in enumerate(rows):
            work[dp_to, row : row + 1, :part] = array[at : at + 1, columns]
        for j in range(hidden_bias.shape[1] // part):
            at = len(rows) + j
            work[dp_to, at : at + 1, :part] = hidden_bias[
                dp_to : dp_to + 1, j * part : (j + 1) * part
            ]


def own_grad_kernel(jobs, sent, small, *refs):
    inputs = 2 * len(jobs) + len(sent)
    operands, came = refs[: 2 * len(jobs)], refs[2 * len(jobs) : inputs]
    extra = refs[inputs : inputs + 6 * small]
    outs = refs[inputs + 6 * small : inputs + 6 * small + len(PARTS)]
    work, *small_work = refs[inputs + 6 * small + len(PARTS) :]
    core_at = lax.axis_index(STREAM) % 2
    row = 0
    for at, (units, blocks, depth) in enumerate(jobs):
        left, right = operands[2 * at], operands[2 * at + 1]
        product = dot_first(left[...], grad_columns(right, core_at, units))
        array, came_row = sent[at]
        for block in range(blocks):
            columns = product[:, block * LANES : (block + 1) * LANES]
            rows = slice(row, row + depth)
            work[:, :, :depth] = columns.reshape(8, 2, depth, LANES) + wide(
                came[array][:, :, came_row : came_row + depth]
            )
            for out, parts in zip(outs, PARTS):
                for j, part in enumerate(parts):
                    dp_from, x_from = part_at(part)
                    out[j, rows] = low(work[dp_from, x_from, :depth])
            row += depth
            came_row += depth
    if small:
        small_grad_rows(extra[:5], extra[5], small_work[0])
        for out, parts in zip(outs, PARTS):
            for j, part in enumerate(parts):
                dp_from, x_from = part_at(part)
                rows = pl.ds(pl.multiple_of(x_from * PAD_ROWS, PAD_ROWS), PAD_ROWS)
                out[j, row : row + PAD_ROWS] = low(small_work[0][dp_from, rows])


def reduce_steps(to_x, to_y_a, to_z_a, to_y_b, to_z_b, to_z_c, own):
    from_y_a, from_x, from_z_a = yield [
        (to_y_a, DP, BESIDE),
        (to_x, STREAM, ACROSS),
        (to_z_a, DP, PAIR),
    ]
    arrived = jnp.concatenate((from_x[:2], from_z_a[:1]))
    from_y_b, mate = yield [
        (low(wide(to_y_b) + wide(arrived)), DP, BESIDE),
        (low(wide(to_z_b) + wide(from_y_a[1:])), DP, PAIR),
    ]
    far = wide(to_z_c) + wide(from_x[2:]) + wide(from_y_b[:2])
    (by_mate,) = yield [(low(far[1]), DP, PAIR)]
    (half,) = yield [(low(far[0] + wide(by_mate)), DP, HALFWAY)]
    total = low(
        jnp.stack(
            (
                wide(own[0]) + wide(from_y_a[0]) + wide(mate[0]) + wide(half),
                wide(own[1]) + wide(from_y_b[2]) + wide(from_z_a[1]),
            )
        )
    )
    (from_x,) = yield [(total, STREAM, ACROSS)]
    total = low(wide(total) + wide(from_x[::-1]))
    return total, lax.ppermute(total, STREAM, CORE)


def unpack_kernel(jobs, small, mine, other, *outs):
    _, _, x_at, core_at = place()
    for source, core_from in ((mine, core_at), (other, 1 - core_at)):
        for j in range(2):
            x_from = x_at if j == 0 else 1 - x_at
            for out_at, lead, units, row, depth in jobs:
                out = outs[out_at] if lead is None else outs[out_at].at[lead]
                for unit in range(units):
                    at = row + unit * depth
                    start = core_from * (units * LANES) + unit * LANES
                    out[
                        pl.ds(pl.multiple_of(x_from * depth, 8), depth),
                        pl.ds(pl.multiple_of(start, 128), LANES),
                    ] = wide(source[j, at : at + depth])
    if small is not None:
        biases, gains, hidden_bias, work = outs[-4:]
        for j in range(2):
            x_from = x_at if j == 0 else 1 - x_at
            rows = slice(small, small + PAD_ROWS)
            work[pl.ds(pl.multiple_of(x_from * PAD_ROWS, 8), PAD_ROWS)] = wide(
                mine[j, rows]
            ) + wide(other[j, rows])
        part = biases.shape[1]
        biases[...] = work[:G_1, :part]
        gains[...] = work[G_1 : G_3 + 1, :part]
        hidden_bias[...] = work[G_3 + 1 : G_3 + 1 + hidden_bias.shape[0], :part]


def reduce_plain(parts):
    shards = []
    for left, right in parts:
        if right.ndim == 2:
            whole = low(dot_first(left, right))
            own = lax.psum_scatter(whole, DP, scatter_dimension=0, tiled=True)
        else:
            whole = low(jnp.stack([dot_first(left, r) for r in right]))
            own = lax.psum_scatter(whole, DP, scatter_dimension=1, tiled=True)
        shards.append(wide(lax.psum(own, STREAM)))
    return shards


class Group:
    def __init__(self):
        self.operands, self.jobs, self.out_jobs, self.out_shapes = [], [], [], []
        self.rows, self.flops, self.sent, self.came, self.from_sent = 0, 0, [], [], []

    def sibling(self, tie, *parts):
        jobs, operands, rows, flops = [], [], 0, 0
        for left, right in parts:
            operands += [left, right]
            depth = left.shape[1] // 16
            units = right.shape[-1] // (2 * LANES)
            leads = [None] if right.ndim == 2 else range(right.shape[0])
            jobs.append((units, units * len(leads), depth))
            self.from_sent.append((len(self.sent), rows))
            for lead in leads:
                self.out_jobs.append(
                    (len(self.out_shapes), lead, units, self.rows + rows, depth)
                )
                rows += units * depth
            self.out_shapes.append(
                shape((*right.shape[:-2], 2 * depth, right.shape[-1]), F32)
            )
            flops += left.shape[0] * left.shape[1] * right.size // right.shape[-2]
        self.sent.append(
            call(
                functools.partial(sibling_grad_kernel, jobs),
                shape((8, 2, rows, LANES)),
                [VMEM] * len(operands),
                flops=flops,
            )(tie(operands[0]), *operands[1:])
        )
        self.jobs += jobs
        self.operands += operands
        self.rows += rows
        self.flops += flops
        return self.sent[-1]

    def core_move(self):
        def steps(sent):
            (came,) = yield [(sent, STREAM, CORE)]
            self.came.append(came)

        return Mover(steps(self.sent[-1]))

    def own(self, tie, small=()):
        deepest = max(job[-1] for job in self.jobs)
        scratch = [pltpu.VMEM((8, 2, deepest, LANES), F32)]
        if small:
            scratch.append(pltpu.VMEM((8, 2 * PAD_ROWS, LANES), F32))
        rows = self.rows + PAD_ROWS * bool(small)
        came = [self.came[array] for array, _ in self.from_sent]
        self.parts = call(
            functools.partial(
                own_grad_kernel,
                self.jobs,
                [(at, row) for at, (_, row) in enumerate(self.from_sent)],
                bool(small),
            ),
            [shape((len(parts), rows, LANES)) for parts in PARTS],
            [VMEM] * (len(self.operands) + len(came) + len(small)),
            scratch,
            flops=self.flops,
        )(tie(self.operands[0]), *self.operands[1:], *came, *small)
        return self.parts

    def move(self):
        return Mover(reduce_steps(*self.parts))

    def unpack(self, moved, small=()):
        return call(
            functools.partial(unpack_kernel, self.out_jobs, self.rows if small else None),
            [*self.out_shapes, *small],
            [VMEM, VMEM],
            [pltpu.VMEM((2 * PAD_ROWS, LANES), F32)] * bool(small),
        )(*moved)


def norm_parts(summed):
    center = summed - jnp.mean(summed, axis=-1, keepdims=True)
    inverse = lax.rsqrt(jnp.mean(center * center, axis=-1, keepdims=True) + EPSILON)
    return center * inverse, inverse


def norm_back(upstream, normed, inverse, gain):
    scaled = upstream * gain
    return inverse * (
        scaled
        - jnp.mean(scaled, axis=-1, keepdims=True)
        - normed * jnp.mean(scaled * normed, axis=-1, keepdims=True)
    )


def heads_apart(four):
    head = lax.broadcasted_iota(jnp.int32, four.shape, 1) // 64
    return low(jnp.concatenate([jnp.where(head == j, four, 0.0) for j in range(4)], axis=0))


def heads_joined(stacked):
    rows = stacked.shape[0] // 4
    head = lax.broadcasted_iota(jnp.int32, (rows, stacked.shape[1]), 1) // 64
    made = stacked[:rows]
    for j in range(1, 4):
        made = jnp.where(head == j, stacked[j * rows : (j + 1) * rows], made)
    return made


def quads():
    return [slice(j * 256, (j + 1) * 256) for j in range(HEADS // 4)]


def softmax(scores):
    raised = jnp.exp(scores - jnp.max(scores, axis=-1, keepdims=True))
    return raised * (1.0 / jnp.sum(raised, axis=-1, keepdims=True))


def score_back(weight, back):
    return low(weight * (back - jnp.sum(back * weight, axis=-1, keepdims=True)))


def row_sum(value):
    return jnp.sum(value, axis=0, keepdims=True)


def self_kernel(seq, lengths, x_ref, w_ref, vec, qkv_ref, out_ref, q, k, v, o):
    tokens = x_ref.shape[0]
    for j, (scratch, bias) in enumerate(((q, B_Q), (k, None), (v, B_V))):
        for c in range(2):
            columns = slice(c * LANES, (c + 1) * LANES)
            made = dot(x_ref[...], w_ref[c, j])
            if bias is not None:
                made = made + vec[bias : bias + 1, columns]
            made = low(made)
            qkv_ref[j, :, columns] = made
            scratch[:, columns] = wide(made)

    def step(r, _):
        rows = pl.ds(pl.multiple_of(r * seq, 8), seq)
        valid = lax.broadcasted_iota(jnp.int32, (4 * seq, seq), 1) < lengths[r]
        asked = [heads_apart(q[rows, c] * 0.125) for c in quads()]
        scores = [dot_last(a, low(k[rows, c])) for a, c in zip(asked, quads())]
        weights = [softmax(jnp.where(valid, score, -jnp.inf)) for score in scores]
        made = [dot(low(w), low(v[rows, c])) for w, c in zip(weights, quads())]
        for part, c in zip(made, quads()):
            o[rows, c] = heads_joined(part)
        return 0

    lax.fori_loop(0, tokens // seq, step, 0, unroll=2)
    out_ref[...] = low(o[...])


def first_norm_kernel(seq, o_ref, x_ref, wso, wcq, vec, normed, inverse, h_low, qc, z):
    for c in range(2):
        columns = slice(c * LANES, (c + 1) * LANES)
        z[:, columns] = (
            dot(o_ref[...], wso[c, 0])
            + vec[B_SO : B_SO + 1, columns]
            + wide(x_ref[:, columns])
        )
    made, scale = norm_parts(z[...])
    normed[...] = made
    inverse[...] = scale
    h_low[...] = low(made * vec[G_1 : G_1 + 1] + vec[B_N1 : B_N1 + 1])
    for c in range(2):
        columns = slice(c * LANES, (c + 1) * LANES)
        qc[:, columns] = low(dot(h_low[...], wcq[c, 0]) + vec[B_CQ : B_CQ + 1, columns])


def pixel_kernel(patch_ref, out_ref):
    images, patches, _ = patch_ref.shape
    out_ref[:, :patches] = patch_ref[...]
    out_ref[:, patches:] = jnp.zeros_like(out_ref[:, patches:])


def image_kernel(pixels, w_ref, vec, kv_ref):
    slots, _, images, padded, _ = kv_ref.shape
    for slot in range(slots):
        for c in range(2):
            columns = slice(c * LANES, (c + 1) * LANES)
            for j in range(2):
                made = dot(pixels[slot].reshape(images * padded, -1), w_ref[c, j])
                if j == 1:
                    made = made + vec[B_CV : B_CV + 1, columns]
                kv_ref[slot, j, :, :, columns] = low(made).reshape(images, padded, LANES)


def cross_kernel(
    seq, patches, micro_rows, slots, qc, kv, n1, wco, vec, oc, n2, inverse, h_low, q, o
):
    q[...] = wide(qc[...]) * 0.125
    tokens = qc.shape[0]
    padded = kv.shape[3]
    there = lax.broadcasted_iota(jnp.int32, (4 * seq, padded), 1) < patches

    def step(r, _):
        rows = pl.ds(pl.multiple_of(r * seq, 8), seq)
        slot, m = slots[r], r // micro_rows
        asked = [heads_apart(q[rows, c]) for c in quads()]
        scores = [dot_last(a, kv[slot, 0, m, :, c]) for a, c in zip(asked, quads())]
        weights = [softmax(jnp.where(there, score, -jnp.inf)) for score in scores]
        made = [dot(low(w), kv[slot, 1, m, :, c]) for w, c in zip(weights, quads())]
        for part, c in zip(made, quads()):
            o[rows, c] = heads_joined(part)
        return 0

    lax.fori_loop(0, tokens // seq, step, 0, unroll=2)
    oc[...] = low(o[...])
    for c in range(2):
        columns = slice(c * LANES, (c + 1) * LANES)
        first = n1[:, columns] * vec[G_1 : G_1 + 1, columns] + vec[B_N1 : B_N1 + 1, columns]
        o[:, columns] = first + dot(oc[...], wco[c, 0]) + vec[B_CO : B_CO + 1, columns]
    made, scale = norm_parts(o[...])
    n2[...] = made
    inverse[...] = scale
    h_low[...] = low(made * vec[G_2 : G_2 + 1] + vec[B_N2 : B_N2 + 1])


def small_rows_kernel(shards, vec, hidden_bias, part):
    wide_rows = G_3 + 1
    vec[...] = jnp.zeros_like(vec)
    for dp_from in range(8):
        rows = wide(shards[dp_from * 2 * PAD_ROWS : (dp_from + 1) * 2 * PAD_ROWS])
        vec[:wide_rows, dp_from * part : (dp_from + 1) * part] = rows[:wide_rows, :part]
        for j in range(LANES // part):
            hidden_bias[dp_from : dp_from + 1, j * part : (j + 1) * part] = rows[
                wide_rows + j : wide_rows + j + 1, :part
            ]


def take_weights(units, spec, sources, wholes, outs, in_sems, out_sems, kept):
    if spec is None:
        copies = [
            [pltpu.make_async_copy(source, whole, in_sems.at[at])]
            for at, (source, whole) in enumerate(zip(sources, wholes))
        ]
    else:
        copies = piece_copies(units, spec, sources, wholes, in_sems)
    for of_weight in copies:
        for copy in of_weight:
            copy.start()

    def take(at):
        for copy in copies[at]:
            copy.wait()
        if outs[at] is not None:
            send(wholes[at], outs[at])

    def send(source, target):
        kept.append(pltpu.make_async_copy(source, target, out_sems.at[len(kept)]))
        kept[-1].start()

    return take, send


def text_kernel(units, gathered, spec, seq, lengths, text, *refs):
    sources, refs = refs[:gathered], refs[gathered:]
    if spec is None:
        small, refs = refs[:2], refs[2:]
    outs, refs = refs[:11], refs[11:]
    vec, hidden_bias, attended, n1, inverse1, h1, qc, qkv_out, *w_outs = outs
    wholes, (qkv, q, k, v, o, in_sems, out_sems) = refs[:4], refs[4:]
    w_small, w_qkv, w_so, w_cq = wholes
    kept = []
    take, send = take_weights(
        units, spec, sources, wholes, (None, *w_outs), in_sems, out_sems, kept
    )
    take(0)
    if spec is None:
        vec[...], hidden_bias[...] = small[0][...], small[1][...]
    else:
        small_rows_kernel(w_small.at[0, 0], vec, hidden_bias, text.shape[1] // 8)
    take(1)
    self_kernel(seq, lengths, text, w_qkv, vec, qkv, attended, q, k, v, o)
    send(qkv, qkv_out)
    take(2)
    take(3)
    first_norm_kernel(seq, attended, text, w_so, w_cq, vec, n1, inverse1, h1, qc, o)
    for copy in kept:
        copy.wait()


def patch_kernel(units, gathered, spec, seq, patches, micro_rows, slots, qc, n1, vec, *refs):
    sources, held, refs = refs[:gathered], refs[gathered : gathered + 4], refs[gathered + 4 :]
    (oc, n2, inverse2, h2, kv_out, pixels_out, *w_outs), refs = refs[:8], refs[8:]
    wholes, (kv, pixels, q, o, in_sems, pixel_sems, out_sems) = refs[:2], refs[2:]
    w_kv, w_co = wholes
    pixel_copies = [
        pltpu.make_async_copy(image, pixels.at[at], pixel_sems.at[at])
        for at, image in enumerate(held)
    ]
    for copy in pixel_copies:
        copy.start()
    kept = []
    take, send = take_weights(units, spec, sources, wholes, w_outs, in_sems, out_sems, kept)
    for copy in pixel_copies:
        copy.wait()
    send(pixels, pixels_out)
    take(0)
    image_kernel(pixels, w_kv, vec, kv)
    send(kv, kv_out)
    take(1)
    cross_kernel(
        seq, patches, micro_rows, slots, qc, kv, n1, w_co, vec, oc, n2, inverse2, h2, q, o
    )
    for copy in kept:
        copy.wait()


def hidden_weights(w, block, in_units):
    core, unit = divmod(block, in_units)
    depth = w.shape[3] // 2 // in_units
    return w[:, :, core, unit * depth : (unit + 1) * depth].reshape(-1, LANES)


def ffn_kernel(
    gathered, spec, in_units, seq, lengths, h2, bias, n2, cot, vec, *refs
):
    sources, refs = refs[:gathered], refs[gathered:]
    out, dz, df, rows_out, active, slope, w_out, w, total, in_sems, out_sem = refs
    if spec is None:
        copies = [pltpu.make_async_copy(sources[0], w, in_sems.at[0])]
    else:
        copies = [
            pltpu.make_async_copy(
                source.at[pl.ds(first, w.shape[3])],
                w.at[z_from * 2 + y_from, x_from, core_from],
                in_sems.at[at],
            )
            for at, (source, first, z_from, y_from, x_from, core_from) in enumerate(
                piece_places(spec, sources)
            )
        ]
    for copy in copies:
        copy.start()
    for copy in copies:
        copy.wait()
    keep = pltpu.make_async_copy(w, w_out, out_sem.at[0])
    keep.start()
    for block in range(2 * in_units):
        columns = slice(block * LANES, (block + 1) * LANES)
        pre = dot(h2[...], hidden_weights(w, block, in_units)) + bias[block : block + 1]
        cumulative = 0.5 * (1.0 + lax.erf(pre * ROOT_HALF))
        active[:, columns] = low(pre * cumulative)
        slope[:, columns] = low(cumulative + pre * INV_ROOT_TAU * jnp.exp(-0.5 * pre * pre))
    half_rows = w.shape[3] // 2
    for c in range(2):
        columns = slice(c * LANES, (c + 1) * LANES)
        made = None
        for part in range(4):
            weights = w[2 * part : 2 * part + 2, :, c, half_rows:].reshape(-1, LANES)
            depth = weights.shape[0]
            term = dot(active[:, part * depth : (part + 1) * depth], weights)
            made = term if made is None else made + term
        total[:, columns] = made

    def step(r, sums):
        rows = pl.ds(pl.multiple_of(r * seq, 8), seq)
        second = n2[rows, :] * vec[G_2 : G_2 + 1] + vec[B_N2 : B_N2 + 1]
        made, scale = norm_parts(second + total[rows, :] + vec[B_FO : B_FO + 1])
        out[r] = low(made * vec[G_3 : G_3 + 1] + vec[B_N3 : B_N3 + 1])
        valid = lax.broadcasted_iota(jnp.int32, made.shape, 0) < lengths[r]
        upstream = jnp.where(valid, wide(cot[r]), 0.0)
        back = norm_back(upstream, made, scale, vec[G_3 : G_3 + 1])
        dz[rows, :] = back
        gain, shift, lowered = sums
        return (
            gain + row_sum(upstream * made),
            shift + row_sum(upstream),
            lowered + row_sum(wide(low(back))),
        )

    zero = jnp.zeros((1, total.shape[1]), F32)
    sums = lax.fori_loop(0, out.shape[0], step, (zero, zero, zero), unroll=2)
    df[...] = low(dz[...])
    for j in range(3):
        rows_out[j : j + 1] = sums[j]
    rows_out[3:8] = jnp.zeros((5, total.shape[1]), F32)
    keep.wait()


def norm_back_rows(total, dz_ref, normed, inverse, gain, dz, low_ref, rows_out, step_rows):
    def step(r, sums):
        rows = pl.ds(pl.multiple_of(r * step_rows, 8), step_rows)
        upstream = total[rows, :] + dz_ref[rows, :]
        made = normed[rows, :]
        back = norm_back(upstream, made, inverse[rows, :], gain)
        dz[rows, :] = back
        return (
            sums[0] + row_sum(upstream * made),
            sums[1] + row_sum(upstream),
            sums[2] + row_sum(wide(low(back))),
        )

    zero = jnp.zeros((1, total.shape[1]), F32)
    sums = lax.fori_loop(0, total.shape[0] // step_rows, step, (zero, zero, zero))
    low_ref[...] = low(dz[...])
    for j in range(3):
        rows_out[j : j + 1] = sums[j]
    rows_out[3:8] = jnp.zeros((5, total.shape[1]), F32)


def hidden_back_kernel(
    seq, df, wout, win, slope, dz3, n2, inverse, vec, du, bias_out, dz2, dac, rows_out, total
):
    i = pl.program_id(0)

    @pl.when(i == 0)
    def _():
        total[...] = jnp.zeros_like(total)

    raw = dot_last(df[:, :LANES], wout[0, :, 0].reshape(-1, LANES))
    raw = raw + dot_last(df[:, LANES:], wout[0, :, 1].reshape(-1, LANES))
    made = low(raw * wide(slope[...]))
    du[...] = made
    bias_out[pl.ds(i, 1), :] = row_sum(wide(made))
    total[...] += dot_last(made, win[:, :, 0].reshape(-1, LANES))

    @pl.when(i == pl.num_programs(0) - 1)
    def _():
        norm_back_rows(
            total, dz3, n2, inverse, vec[G_2 : G_2 + 1], dz2, dac, rows_out, seq
        )


def cross_back_kernel(
    seq, patches, micro_rows, slots, dac, qc, kv, wco, dqc, dkv_out, dkv, q, do, dq
):
    q[...] = wide(qc[...]) * 0.125
    do[...] = wide(
        low(dot_last(dac[:, :LANES], wco[0, 0]) + dot_last(dac[:, LANES:], wco[1, 0]))
    )
    dkv[...] = jnp.zeros_like(dkv)
    tokens = qc.shape[0]
    padded = kv.shape[3]
    there = lax.broadcasted_iota(jnp.int32, (4 * seq, padded), 1) < patches

    def step(r, _):
        rows = pl.ds(pl.multiple_of(r * seq, 8), seq)
        slot, m = slots[r], r // micro_rows
        asked = [heads_apart(q[rows, c]) for c in quads()]
        came = [heads_apart(do[rows, c]) for c in quads()]
        keys = [kv[slot, 0, m, :, c] for c in quads()]
        values = [kv[slot, 1, m, :, c] for c in quads()]
        scores = [dot_last(a, key) for a, key in zip(asked, keys)]
        backs = [dot_last(d, value) for d, value in zip(came, values)]
        weights = [softmax(jnp.where(there, score, -jnp.inf)) for score in scores]
        backs = [score_back(w, b) for w, b in zip(weights, backs)]
        queries = [heads_joined(dot(b, key)) for b, key in zip(backs, keys)]
        key_parts = [dot_first(b, a) for b, a in zip(backs, asked)]
        value_parts = [dot_first(low(w), d) for w, d in zip(weights, came)]
        for j, c in enumerate(quads()):
            dq[rows, c] = queries[j] * 0.125
            dkv[0, slot, m, :, c] += key_parts[j]
            dkv[1, slot, m, :, c] += value_parts[j]
        return 0

    lax.fori_loop(0, tokens // seq, step, 0, unroll=2)
    dqc[...] = low(dq[...])
    dkv_out[...] = low(dkv[...])


def first_back_kernel(seq, dqc, wcq, dz2, n1, inverse, vec, dz1, da, rows_out, total):
    total[...] = dot_last(dqc[:, :LANES], wcq[0, 0]) + dot_last(dqc[:, LANES:], wcq[1, 0])
    norm_back_rows(total, dz2, n1, inverse, vec[G_1 : G_1 + 1], dz1, da, rows_out, seq)
    rows_out[3:4] = row_sum(wide(dqc[...]))


def self_back_kernel(seq, lengths, da, qkv, wso, dqkv, rows_out, q, k, v, do, dq, dk, dv):
    q[...] = wide(qkv[0]) * 0.125
    k[...] = wide(qkv[1])
    v[...] = wide(qkv[2])
    do[...] = wide(low(dot_last(da[:, :LANES], wso[0, 0]) + dot_last(da[:, LANES:], wso[1, 0])))
    tokens = da.shape[0]

    def step(r, _):
        rows = pl.ds(pl.multiple_of(r * seq, 8), seq)
        valid = lax.broadcasted_iota(jnp.int32, (4 * seq, seq), 1) < lengths[r]
        asked = [heads_apart(q[rows, c]) for c in quads()]
        came = [heads_apart(do[rows, c]) for c in quads()]
        keys = [low(k[rows, c]) for c in quads()]
        values = [low(v[rows, c]) for c in quads()]
        scores = [dot_last(a, key) for a, key in zip(asked, keys)]
        backs = [dot_last(d, value) for d, value in zip(came, values)]
        weights = [softmax(jnp.where(valid, score, -jnp.inf)) for score in scores]
        backs = [score_back(w, b) for w, b in zip(weights, backs)]
        queries = [heads_joined(dot(b, key)) for b, key in zip(backs, keys)]
        key_parts = [dot_first(b, a) for b, a in zip(backs, asked)]
        value_parts = [dot_first(low(w), d) for w, d in zip(weights, came)]
        for j, c in enumerate(quads()):
            dq[rows, c] = queries[j] * 0.125
            dk[rows, c] = key_parts[j]
            dv[rows, c] = value_parts[j]
        return 0

    lax.fori_loop(0, tokens // seq, step, 0, unroll=2)
    for j, made in enumerate((dq, dk, dv)):
        dqkv[j] = low(made[...])
    rows_out[0:1] = row_sum(wide(dqkv[0]))
    rows_out[1:2] = row_sum(wide(dqkv[2]))
    rows_out[2:8] = jnp.zeros((6, q.shape[1]), F32)


def text_grad_kernel(dz1, dqkv, w_ref, out, total):
    total[...] = dz1[...]
    for j in range(3):
        for c in range(2):
            total[...] += dot_last(dqkv[j, :, c * LANES : (c + 1) * LANES], w_ref[c, j])
    seq = out.shape[1]
    for r in range(out.shape[0]):
        out[r] = low(total[r * seq : (r + 1) * seq, :])


def patch_grad_kernel(dkv, w_ref, kept, sent, rows_out):
    _, slots, images, padded, width = dkv.shape
    rows = images * padded
    total = jnp.zeros((1, width), F32)
    for slot in range(slots):
        made = None
        for j in range(2):
            grad = dkv[j, slot].reshape(rows, width)
            for c in range(2):
                term = dot_last(grad[:, c * LANES : (c + 1) * LANES], w_ref[c, j])
                made = term if made is None else made + term
        out = sent if slot % 2 else kept
        out[slot // 2] = low(made).reshape(images, padded, w_ref.shape[2])
        total = total + row_sum(wide(grad))
    rows_out[0:1] = total
    rows_out[1:8] = jnp.zeros((7, width), F32)


def on_device(
    text_input,
    patch_input,
    text_lengths,
    image_of_row,
    cotangent,
    self_qkv,
    self_out,
    cross_q,
    cross_kv,
    cross_out,
    ffn_in,
    ffn_out,
    biases,
    norm_gains,
    ffn_bias,
):
    dp = lax.axis_size(DP)
    micros, row_count, seq, width = text_input.shape
    patches, patch_width = patch_input.shape[2:]
    rows_all = micros * row_count
    tokens = rows_all * seq
    hidden = ffn_in.shape[1]
    padded = -(-patches // 16) * 16
    images = micros * patch_input.shape[1]

    part = biases.shape[1]
    small = jnp.concatenate((biases, norm_gains, ffn_bias.reshape(-1, part)))
    small_rows = small.shape[0]
    wide_rows = biases.shape[0] + norm_gains.shape[0]
    small = jnp.pad(small, ((0, 2 * PAD_ROWS - small_rows), (0, LANES - part)))
    small = jnp.broadcast_to(small.reshape(2, PAD_ROWS, LANES), (2, 2, PAD_ROWS, LANES))

    half = width // dp // 2
    half_v = cross_kv.shape[1] // 2
    in_units = hidden // (2 * LANES)
    text_group = (
        (small, self_qkv, self_out, cross_q),
        ((1, PAD_ROWS), (3, half), (1, half), (1, half)),
    )
    patch_group = ((cross_kv, cross_out), ((2, half_v), (1, half)))
    hidden_group = ((ffn_in, ffn_out), ((in_units, half), (1, ffn_out.shape[0] // 2)))

    text = text_input.reshape(tokens, width)
    pixels = call(pixel_kernel, shape((images, padded, patch_width)), [VMEM])(
        patch_input.reshape(images, patches, patch_width)
    )
    lengths = text_lengths.reshape(-1)
    slots = image_of_row.reshape(-1) ^ lax.axis_index(STREAM)
    flat = (tokens, width)
    full = pltpu.VMEM(flat, F32)
    flops = 2 * tokens * width * width
    steps = hidden // LANES
    chunks = hidden // width
    kv_shape = (4, 2, images, padded, width)
    in_block = pl.BlockSpec(
        (8, 2, 1, width // 16, LANES), lambda i: (0, 0, i // in_units, i % in_units, 0)
    )
    v = types.SimpleNamespace()

    bf16 = jnp.bfloat16

    def pixel_steps():
        (v.across,) = yield [(pixels, STREAM, ACROSS)]
        v.beside, v.apart = yield [(pixels, STREAM, CORE), (v.across, STREAM, CORE)]

    def run_text(tie, sources, spec=None, small_inputs=()):
        units = text_group[1]
        wholes = [(2, 1, 16 * PAD_ROWS, LANES)]
        wholes += [(2, count, depth * 2 * dp, LANES) for count, depth in units[1:]]
        outs = [
            shape((16, width), F32), shape((steps, LANES), F32), shape(flat), shape(flat, F32),
            shape((tokens, 1), F32), shape(flat), shape(flat), shape((3, *flat)),
            *[shape(dims) for dims in wholes[1:]],
        ]
        (
            v.vec, v.hidden_bias, v.attended, v.n1, v.inverse1, v.h1, v.qc, v.qkv,
            v.w_qkv, v.w_so, v.w_cq,
        ) = call(
            functools.partial(text_kernel, units, len(sources), spec, seq),
            outs,
            [SMEM, VMEM] + [ANY] * len(sources) + [VMEM] * len(small_inputs),
            [
                *[pltpu.VMEM(dims, bf16) for dims in wholes],
                pltpu.VMEM((3, *flat), bf16), full, full, full, full,
                pltpu.SemaphoreType.DMA((32 * len(units),)), pltpu.SemaphoreType.DMA((4,)),
            ],
            out_specs=[VMEM] * 7 + [ANY] * 4,
            mib=60,
            flops=8 * flops,
        )(lengths, tie(text), *sources, *small_inputs)
        return v.qc

    def run_patch(tie, sources, spec=None):
        units = patch_group[1]
        wholes = [(2, count, depth * 2 * dp, LANES) for count, depth in units]
        pixels_shape = (4, images, padded, patch_width)
        outs = [
            shape(flat), shape(flat, F32), shape((tokens, 1), F32), shape(flat),
            shape(kv_shape), shape(pixels_shape), *[shape(dims) for dims in wholes],
        ]
        v.oc, v.n2, v.inverse2, v.h2, v.kv, pixels_all, v.w_kv, v.w_co = call(
            functools.partial(patch_kernel, units, len(sources), spec, seq, patches, row_count),
            outs,
            [SMEM, VMEM, VMEM, VMEM] + [ANY] * (len(sources) + 4),
            [
                *[pltpu.VMEM(dims, bf16) for dims in wholes],
                pltpu.VMEM(kv_shape, bf16), pltpu.VMEM(pixels_shape, bf16), full, full,
                pltpu.SemaphoreType.DMA((32 * len(units),)), pltpu.SemaphoreType.DMA((4,)),
                pltpu.SemaphoreType.DMA((4,)),
            ],
            out_specs=[VMEM] * 4 + [ANY] * 4,
            mib=60,
            flops=18 * flops,
        )(slots, tie(v.qc), v.n1, v.vec, *sources, pixels, v.beside, v.across, v.apart)
        v.pixels_all = pixels_all.reshape(-1, patch_width)
        return v.h2

    def run_ffn(tie, sources, spec=None):
        w_shape = (8, 2, 2, hidden // 8, LANES)
        v.out_rows, v.dz3, v.df, v.sums3, v.active, v.slope, v.w_hidden = call(
            functools.partial(ffn_kernel, len(sources), spec, in_units, seq),
            [
                shape((rows_all, seq, width)), shape(flat, F32), shape(flat),
                shape((8, width), F32), shape((tokens, hidden)), shape((tokens, hidden)),
                shape(w_shape),
            ],
            [SMEM] + [VMEM] * 5 + [ANY] * len(sources),
            [
                pltpu.VMEM(w_shape, bf16), full, pltpu.SemaphoreType.DMA((32,)),
                pltpu.SemaphoreType.DMA((1,)),
            ],
            out_specs=[VMEM] * 6 + [ANY],
            flops=8 * flops,
        )(
            lengths, tie(v.h2), v.hidden_bias, v.n2,
            cotangent.reshape(rows_all, seq, width), v.vec, *sources,
        )
        return v.df

    def run_hidden_back(tie):
        v.du, v.hidden_bias_grad, v.dz2, v.dac, v.sums2 = call(
            functools.partial(hidden_back_kernel, seq),
            [
                shape((tokens, hidden)),
                shape((steps, LANES), F32),
                shape(flat, F32),
                shape(flat),
                shape((8, width), F32),
            ],
            [
                VMEM,
                pl.BlockSpec((1, 2, 2, hidden // 16, LANES), lambda i: (i, 0, 0, 1, 0)),
                in_block,
                pl.BlockSpec((tokens, LANES), lambda i: (0, i)),
                VMEM,
                VMEM,
                VMEM,
                VMEM,
            ],
            [full],
            out_specs=[pl.BlockSpec((tokens, LANES), lambda i: (0, i)), VMEM, VMEM, VMEM, VMEM],
            grid=(steps,),
            flops=8 * flops,
        )(
            tie(v.df), v.w_hidden, v.w_hidden, v.slope, v.dz3, v.n2, v.inverse2,
            v.vec,
        )
        return v.dac

    def run_cross_back(tie):
        v.dqc, v.dkv_all = call(
            functools.partial(cross_back_kernel, seq, patches, row_count),
            [shape(flat), shape((2, 4, images, padded, width))],
            [SMEM, VMEM, VMEM, VMEM, VMEM],
            [pltpu.VMEM((2, 4, images, padded, width), F32), full, full, full],
            flops=4 * flops,
        )(slots, tie(v.dac), v.qc, v.kv, v.w_co)
        return v.dqc

    def patch_steps():
        (came,) = yield [(v.patch_sent, STREAM, CORE)]
        made = wide(v.patch_kept) + wide(came)
        (across,) = yield [(low(made[1]), STREAM, ACROSS)]
        v.patch_rows = low(made[0] + wide(across))[:, :patches].reshape(patch_input.shape)

    def run_first_back(tie):
        v.dz1, v.da, v.sums1 = call(
            functools.partial(first_back_kernel, seq),
            [shape(flat, F32), shape(flat), shape((8, width), F32)],
            [VMEM] * 6,
            [full],
            flops=flops,
        )(tie(v.dqc), v.w_cq, v.dz2, v.n1, v.inverse1, v.vec)
        return v.da

    def run_self_back(tie):
        v.dqkv, v.sums0 = call(
            functools.partial(self_back_kernel, seq),
            [shape((3, *flat)), shape((8, width), F32)],
            [SMEM, VMEM, VMEM, VMEM],
            [full] * 7,
            flops=4 * flops,
        )(lengths, tie(v.da), v.qkv, v.w_so)
        return v.dqkv

    def run_patch_grad(tie):
        v.patch_kept, v.patch_sent, v.sums_kv = call(
            patch_grad_kernel,
            [shape((2, images, padded, patch_width))] * 2 + [shape((8, width), F32)],
            [VMEM] * 2,
            flops=16 * flops,
        )(tie(v.dkv_all), v.w_kv)
        return v.patch_sent

    def run_text_grad(tie):
        v.text_rows = call(
            text_grad_kernel,
            shape((rows_all, seq, width)),
            [VMEM] * 3,
            [full],
            flops=3 * flops,
        )(tie(v.dz1), v.dqkv, v.w_qkv)
        return v.text_rows

    def small_grads():
        sums0, sums1, sums2, sums3, sums_kv = v.sums0, v.sums1, v.sums2, v.sums3, v.sums_kv
        grads = jnp.concatenate(
            (
                sums0[0:2], sums1[2:3], sums1[1:2], sums1[3:4], sums_kv[0:1], sums2[2:3],
                sums2[1:2], sums3[2:3], sums3[1:2], sums1[0:1], sums2[0:1], sums3[0:1],
            )
        )
        return jnp.concatenate(
            (
                grads.reshape(wide_rows, dp, part).transpose(1, 0, 2),
                v.hidden_bias_grad.reshape(dp, -1, part),
            ),
            axis=1,
        )

    def run_all(moves):
        mover = Mover(moves)
        while not mover.done:
            mover.give([lax.ppermute(array, axis, hops) for array, axis, hops in mover.requests])

    if not special_mesh():
        def free(array):
            return array

        w_small, *wholes = gather_plain(*text_group)
        patch_wholes = gather_plain(*patch_group)
        values = wide(w_small[0, 0].reshape(dp, 2 * PAD_ROWS, LANES)[:, :small_rows, :part])
        vec = values[:, :wide_rows].transpose(1, 0, 2).reshape(wide_rows, width)
        vec = jnp.pad(vec, ((0, 16 - wide_rows), (0, 0)))
        hidden_bias = values[:, wide_rows:].reshape(-1, LANES)
        w_small = w_small[:, :, : 16 * PAD_ROWS]
        w_in = lax.all_gather(ffn_in, DP, axis=0, tiled=True)
        w_out = lax.all_gather(ffn_out, DP, axis=0, tiled=True)
        w_in = w_in.reshape(8, 2, width // 16, 2, in_units, LANES).transpose(0, 1, 3, 4, 2, 5)
        w_in = w_in.reshape(8, 2, 2, -1, LANES)
        w_out = w_out.reshape(8, 2, hidden // 16, 2, LANES).transpose(0, 1, 3, 2, 4)
        w_hidden = jnp.concatenate((w_in, w_out), axis=3)
        run_all(pixel_steps())
        run_text(free, (w_small, *wholes), None, (vec, hidden_bias))
        run_patch(free, patch_wholes)
        run_ffn(free, (w_hidden,))
        for work in (run_hidden_back, run_cross_back, run_patch_grad):
            work(free)
        run_all(patch_steps())
        for work in (run_first_back, run_self_back, run_text_grad):
            work(free)
        s_out, s_in, s_co, s_cq, s_so, s_kv, s_qkv = reduce_plain(
            (
                (v.active, v.df), (v.h2, v.du), (v.oc, v.dac), (v.h1, v.dqc),
                (v.attended, v.da), (v.pixels_all, v.dkv_all.reshape(2, -1, width)), (text, v.dqkv),
            )
        )
        s_small = lax.psum_scatter(low(small_grads()), DP, scatter_dimension=0, tiled=True)
        s_small = wide(lax.psum(s_small, STREAM))[0]
        s_biases = s_small[: biases.shape[0]]
        s_gains = s_small[biases.shape[0] : wide_rows]
        s_hidden_bias = s_small[wide_rows:]
    else:
        clock = Clock()
        gather_text, gather_patch, gather_hidden = (
            Mover(gather_steps(*pack_group(*group)), pieces=True)
            for group in (text_group, patch_group, hidden_group)
        )
        move_pixels = Mover(pixel_steps())
        clock.step([gather_text, move_pixels])
        clock.step([gather_text, gather_patch])
        clock.step([gather_hidden, gather_text, gather_patch])
        clock.step(
            [gather_hidden, gather_patch, move_pixels], [lambda tie: run_text(tie, *piece_sources(gather_text.result, tie))]
        )
        clock.step([gather_hidden], [lambda tie: run_patch(tie, *piece_sources(gather_patch.result, tie))])
        clock.step([gather_hidden], [lambda tie: run_ffn(tie, *piece_sources(gather_hidden.result, tie))])

        out_group, in_group, mid_group, last_group = Group(), Group(), Group(), Group()

        def begin_out(tie):
            return out_group.sibling(tie, (v.active, v.df))

        def begin_in(tie):
            return in_group.sibling(tie, (v.h2, v.du))

        def begin_mid(tie):
            return mid_group.sibling(
                tie,
                (v.oc, v.dac),
                (v.h1, v.dqc),
                (v.attended, v.da),
                (v.pixels_all, v.dkv_all.reshape(2, -1, width)),
            )

        def begin_last(tie):
            return last_group.sibling(tie, (text, v.dqkv))

        def own_last(tie):
            return last_group.own(
                tie, (v.sums0, v.sums1, v.sums2, v.sums3, v.sums_kv, v.hidden_bias_grad)
            )

        clock.step([], [begin_out])
        clock.step([out_group.core_move()], [run_hidden_back, out_group.own], eager=True)
        move_out = out_group.move()
        clock.step([], [begin_in])
        clock.step(
            [move_out, in_group.core_move()],
            [run_cross_back, run_first_back, in_group.own, begin_mid],
            eager=True,
        )
        move_in = in_group.move()
        clock.step(
            [move_out, move_in, mid_group.core_move()],
            [run_self_back, run_patch_grad, mid_group.own, begin_last],
            eager=True,
        )
        move_mid, move_patch = mid_group.move(), Mover(patch_steps())
        clock.step(
            [move_out, move_in, move_mid, last_group.core_move(), move_patch],
            [own_last, run_text_grad],
            eager=True,
        )
        move_last = last_group.move()
        movers = [move_out, move_in, move_mid, move_last, move_patch]
        results = {}

        small_shapes = [
            shape((rows, part), F32)
            for rows in (biases.shape[0], norm_gains.shape[0], small_rows - wide_rows)
        ]

        def unpack(group, mover):
            def work(tie):
                results[mover] = group.unpack(
                    (tie(mover.result[0]), mover.result[1]),
                    small_shapes if group is last_group else (),
                )
                return results[mover]
            return work

        groups = [
            (out_group, move_out), (in_group, move_in), (mid_group, move_mid), (last_group, move_last)
        ]
        def ready():
            return [
                unpack(group, mover)
                for group, mover in groups
                if mover.done and mover not in results
            ]

        while not all(mover.done for mover in movers):
            clock.step(movers, ready, eager=True)
        for work in ready():
            work(clock.tie)
        (s_out,), (s_in,) = results[move_out], results[move_in]
        s_co, s_cq, s_so, s_kv = results[move_mid]
        s_qkv, s_biases, s_gains, s_hidden_bias = results[move_last]
    return (
        v.out_rows.reshape(text_input.shape),
        v.text_rows.reshape(text_input.shape),
        v.patch_rows,
        s_qkv,
        s_so,
        s_cq,
        s_kv,
        s_co,
        s_in,
        s_out,
        s_biases,
        s_gains,
        s_hidden_bias.reshape(-1),
    )


def solution(mesh):
    placed = (
        P(None, (DP, STREAM), None, None),
        P(None, (DP, STREAM), None, None),
        P(None, (DP, STREAM)),
        P(None, (DP, STREAM)),
        P(None, (DP, STREAM), None, None),
        P(None, DP, None),
        P(DP, None),
        P(DP, None),
        P(None, DP, None),
        P(DP, None),
        P(DP, None),
        P(DP, None),
        P(None, DP),
        P(None, DP),
        P(DP),
    )
    return jax.shard_map(
        on_device,
        mesh=mesh,
        in_specs=placed,
        out_specs=(
            P(None, (DP, STREAM), None, None),
            P(None, (DP, STREAM), None, None),
            P(None, (DP, STREAM), None, None),
            P(None, DP, None),
            P(DP, None),
            P(DP, None),
            P(None, DP, None),
            P(DP, None),
            P(DP, None),
            P(DP, None),
            P(None, DP),
            P(None, DP),
            P(DP),
        ),
        check_vma=False,
    )
```

```python
import functools
import types

import jax
import jax.numpy as jnp
from jax import lax
from jax.experimental import pallas as pl
from jax.experimental.pallas import tpu as pltpu
from jax.sharding import PartitionSpec as P

HEADS = 12
LANES = 384
PAD_ROWS = 16
MIB = 2**20
DP, STREAM = "dp", "stream"

EPSILON = 1e-06
ROOT_HALF = 0.7071067811865476
INV_ROOT_TAU = 0.3989422804014327

CORE = ((0, 1), (1, 0), (2, 3), (3, 2))
ACROSS = ((0, 2), (2, 0), (1, 3), (3, 1))
BESIDE = ((0, 1), (1, 0), (2, 3), (3, 2), (4, 5), (5, 4), (6, 7), (7, 6))
PAIR = ((0, 2), (2, 0), (1, 3), (3, 1), (4, 6), (6, 4), (5, 7), (7, 5))
HALFWAY = ((0, 4), (4, 0), (1, 5), (5, 1), (2, 6), (6, 2), (3, 7), (7, 3))
MIRROR = ((0, 6), (6, 0), (1, 7), (7, 1), (2, 4), (4, 2), (3, 5), (5, 3))

B_Q, B_V, B_SO, B_N1, B_CQ, B_CV, B_CO, B_N2, B_FO, B_N3, G_1, G_2, G_3 = range(13)


def low(value):
    return value.astype(jnp.bfloat16)


def wide(value):
    return value.astype(jnp.float32)


def dot(left, right):
    return jnp.dot(left, right, preferred_element_type=jnp.float32)


def dot_last(left, right):
    return lax.dot_general(
        left, right, (((1,), (1,)), ((), ())), preferred_element_type=jnp.float32
    )


def dot_first(left, right):
    return lax.dot_general(
        left, right, (((0,), (0,)), ((), ())), preferred_element_type=jnp.float32
    )


def pick(array, index, axis=0):
    return lax.dynamic_index_in_dim(array, index, axis, keepdims=False)


def place():
    dp_at, stream_at = lax.axis_index(DP), lax.axis_index(STREAM)
    return dp_at // 2, dp_at % 2, stream_at // 2, stream_at % 2


class Base:
    def __init__(self, array):
        self.array = array.reshape(-1, LANES)
        self.twin = None

    def exchange(self, tie):
        if self.twin is None:
            self.twin = lax.ppermute(tie(self.array), STREAM, CORE)
        return self.twin


class Piece:
    def __init__(self, base, row, dims):
        self.base, self.row, self.dims = base, row, dims

    def value(self):
        rows = 1
        for size in self.dims[:-1]:
            rows *= size
        return self.base.array[self.row : self.row + rows].reshape(self.dims)


class Clock:
    def __init__(self):
        self.before = []
        self.came = []
        self.bases = []

    def take(self, arrays):
        given = {}
        for array, (_, sends) in zip(arrays, self.came):
            row = 0
            base = Base(array) if sends[0][0].pieces else None
            for mover, at, sent in sends:
                part = array
                if base is not None:
                    part = Piece(base, row, sent.shape)
                    row += sent.size // LANES
                elif len(sends) > 1:
                    rows = sent.size // LANES
                    part = array[row : row + rows].reshape(sent.shape)
                    row += rows
                given.setdefault(mover, {})[at] = part
        self.came = []
        for mover, parts in given.items():
            mover.give([parts[at] for at in range(len(parts))])

    def step(self, moving=(), compute=(), eager=False):
        arrays = [array for array, _ in self.came]
        twins = [base.exchange(self.tie) for base in self.bases]
        arrays, twins, self.before = lax.optimization_barrier(
            (arrays, twins, self.before + arrays[:1])
        )
        for base, twin in zip(self.bases, twins):
            base.twin = twin
        self.bases = []
        self.take(arrays)
        ways = {}
        for mover in moving:
            if mover.done:
                continue
            for at, (array, axis, hops) in enumerate(mover.requests):
                alone = hops is CORE or array.shape[-1] != LANES
                key = (axis, hops, (mover, at) if alone else None)
                ways.setdefault(key, []).append((mover, at, array))
        joined = [
            sends[0][2]
            if len(sends) == 1
            else jnp.concatenate([array.reshape(-1, LANES) for _, _, array in sends])
            for sends in ways.values()
        ]
        joined, self.before = lax.optimization_barrier((joined, self.before))
        self.came = [
            (lax.ppermute(array, axis, hops), sends)
            for array, ((axis, hops, _), sends) in zip(joined, ways.items())
        ]
        after = []
        if eager:
            movers = [mover for sends in ways.values() for mover, _, _ in sends]
            self.take([array for array, _ in self.came])
            for mover in dict.fromkeys(movers):
                if mover.done:
                    after += jax.tree.leaves(mover.result)
                else:
                    after += [array for array, _, _ in mover.requests]
        for work in compute() if callable(compute) else compute:
            after += jax.tree.leaves(work(self.tie))
        if after:
            self.before = after

    def tie(self, array):
        return lax.optimization_barrier((array, self.before))[0]


class Mover:
    def __init__(self, steps, pieces=False):
        self.given = []
        self.steps = steps
        self.pieces = pieces
        self.done = False
        self.result = None
        self.requests = next(steps)

    def give(self, came):
        self.given = came
        try:
            self.requests = self.steps.send(came)
        except StopIteration as stop:
            self.done, self.result = True, stop.value


def special_mesh():
    return lax.axis_size(DP) == 8 and lax.axis_size(STREAM) == 4


VMEM = pl.BlockSpec(memory_space=pltpu.VMEM)
SMEM = pl.BlockSpec(memory_space=pltpu.SMEM)
ANY = pl.BlockSpec(memory_space=pl.ANY)


def call(kernel, out_shape, in_specs, scratch=(), mib=24, flops=0, out_specs=None, **more):
    return pl.pallas_call(
        kernel,
        out_shape=out_shape,
        in_specs=in_specs,
        out_specs=jax.tree.map(lambda _: VMEM, out_shape) if out_specs is None else out_specs,
        scratch_shapes=list(scratch),
        compiler_params=pltpu.CompilerParams(vmem_limit_bytes=mib * MIB),
        cost_estimate=pl.CostEstimate(flops=flops, bytes_accessed=4 * MIB, transcendentals=0),
        **more,
    )


def shape(dims, dtype=jnp.bfloat16):
    return jax.ShapeDtypeStruct(tuple(dims), dtype)


F32 = jnp.float32


def pack_shard(shard, units):
    if shard.ndim == 2:
        rows, _ = shard.shape
        split = shard.reshape(2, rows // 2, 2, units, LANES).transpose(2, 0, 3, 1, 4)
    else:
        _, rows, _ = shard.shape
        split = shard.reshape(units, 2, rows // 2, 2, LANES).transpose(3, 1, 0, 2, 4)
    return split.reshape(2, 2, units * rows // 2, LANES)


def pack_kernel(units, *refs):
    _, _, x_at, core_at = place()
    shards, (both, own, own_x) = refs[: len(units)], refs[len(units) :]
    row = 0
    for shard, (count, depth) in zip(shards, units):
        if len(shard.shape) == 4:
            both[:, :, row : row + depth] = shard[...]
            row += depth
            continue
        for unit in range(count):
            rows = slice(row, row + depth)
            for x in range(2):
                for c in range(2):
                    if len(shard.shape) == 3:
                        block = shard[unit, x * depth : (x + 1) * depth, c * LANES : (c + 1) * LANES]
                    else:
                        start = (c * count + unit) * LANES
                        block = shard[x * depth : (x + 1) * depth, start : start + LANES]
                    both[c, x, rows] = block
            row += depth
    own[...] = both[core_at]
    own_x[...] = both[core_at, x_at]


def pack_own_kernel(units, *refs):
    _, _, x_at, core_at = place()
    shards, out = refs[:-1], refs[-1]
    row = 0
    for shard, (count, depth) in zip(shards, units):
        for unit in range(count):
            start = (core_at * count + unit) * LANES
            out[row : row + depth] = shard[
                pl.ds(pl.multiple_of(x_at * depth, 16), depth),
                pl.ds(pl.multiple_of(start, 128), LANES),
            ]
            row += depth


def pack_group(shards, units):
    rows = sum(count * depth for count, depth in units)
    return call(
        functools.partial(pack_kernel, units),
        [shape((2, 2, rows, LANES)), shape((2, rows, LANES)), shape((rows, LANES))],
        [VMEM] * len(shards),
    )(*shards)


def pack_own(shards, units):
    rows = sum(count * depth for count, depth in units)
    return call(
        functools.partial(pack_own_kernel, units), shape((rows, LANES)), [VMEM] * len(shards)
    )(*shards)


def gather_steps(own_both, own, own_x):
    x_at = lax.axis_index(STREAM) // 2
    mate, half_z, mirror_z, beside = yield [
        (own, DP, PAIR),
        (own_x, DP, HALFWAY),
        (own_x, DP, MIRROR),
        (own, DP, BESIDE),
    ]
    mate_halves = mate.value()
    others = jnp.stack((pick(mate_halves, x_at), half_z.value(), mirror_z.value()))
    beside_others, half_x, mirror_x = yield [
        (others, DP, BESIDE),
        (half_z.value(), STREAM, ACROSS),
        (mirror_z.value(), STREAM, ACROSS),
    ]
    others_x, mate_x = yield [
        (beside_others.value()[1:], STREAM, ACROSS),
        (pick(mate_halves, 1 - x_at), DP, BESIDE),
    ]
    whole = Piece(Base(own_both), 0, own_both.shape)
    return (
        whole, mate, beside, half_z, mirror_z, half_x, mirror_x, beside_others, others_x, mate_x
    )


def piece_sources(pieces, tie):
    own, *received = pieces
    rows = own.dims[2]
    arrays, spec = [own.base.array], [(0, at * rows) for at in range(4)]
    known = {}

    def find(piece, theirs):
        key = (piece.base, theirs)
        if key not in known:
            known[key] = len(arrays)
            arrays.append(piece.base.exchange(tie) if theirs else piece.base.array)
        return known[key]

    for theirs in (False, True):
        mate, beside, half_z, mirror_z, half_x, mirror_x, others, others_x, mate_x = received
        blocks = [(mate, 0), (beside, 0), (mate, 1), (beside, 1)]
        blocks += [(half_z, 0), (mirror_z, 0), (half_x, 0), (mirror_x, 0)]
        blocks += [(others, 0), (others, 1), (others, 2), (mate_x, 0), (others_x, 0), (others_x, 1)]
        spec += [(find(piece, theirs), piece.row + block * rows) for piece, block in blocks]
    return arrays, tuple(spec)


def piece_places(spec, sources):
    z_at, y_at, x_at, core_at = place()
    _, z_mate, z_half, z_mirror = shard_slots(z_at)
    far_y, far_x = 1 - y_at, 1 - x_at
    places = [(z_at, y_at, x_from, core_from) for core_from in range(2) for x_from in range(2)]
    for core_from in (core_at, 1 - core_at):
        for x_from in range(2):
            places.append((z_mate, y_at, x_from, core_from))
            places.append((z_at, far_y, x_from, core_from))
        places += [
            (z_half, y_at, x_at, core_from),
            (z_mirror, y_at, x_at, core_from),
            (z_half, y_at, far_x, core_from),
            (z_mirror, y_at, far_x, core_from),
            (z_mate, far_y, x_at, core_from),
            (z_half, far_y, x_at, core_from),
            (z_mirror, far_y, x_at, core_from),
            (z_mate, far_y, far_x, core_from),
            (z_half, far_y, far_x, core_from),
            (z_mirror, far_y, far_x, core_from),
        ]
    return [(sources[at], row, *where) for (at, row), where in zip(spec, places)]


def piece_copies(units, spec, sources, wholes, sems):
    parts = piece_places(spec, sources)
    copies, row, sem = [], 0, 0
    for (count, depth), whole in zip(units, wholes):
        of_weight = []
        for source, first, z_from, y_from, x_from, core_from in parts:
            start = (z_from * 2 + y_from) * (2 * depth) + x_from * depth
            of_weight.append(
                pltpu.make_async_copy(
                    source.at[pl.ds(first + row, count * depth)].reshape(count, depth, LANES),
                    whole.at[core_from, :, pl.ds(pl.multiple_of(start, 16), depth)],
                    sems.at[sem],
                )
            )
            sem += 1
        copies.append(of_weight)
        row += count * depth
    return copies


def gather_plain(shards, units):
    packed = [
        shard if shard.ndim == 4 else pack_shard(shard, count)
        for shard, (count, _) in zip(shards, units)
    ]
    whole = lax.all_gather(jnp.concatenate(packed, axis=2), DP, axis=0, tiled=False)
    results = []
    row = 0
    for count, depth in units:
        part = whole[:, :, :, row : row + count * depth]
        part = part.reshape(-1, 2, 2, count, depth, LANES).transpose(1, 3, 0, 2, 4, 5)
        results.append(part.reshape(2, count, -1, LANES))
        row += count * depth
    return results


def shard_slots(z_at):
    return z_at, z_at + 1 - 2 * (z_at % 2), (z_at + 2) % 4, 3 - z_at


def grad_columns(right, core, units):
    blocks = []
    for lead in [None] if len(right.shape) == 2 else range(right.shape[0]):
        of_lead = right if lead is None else right.at[lead]
        start = pl.multiple_of(core * (units * LANES), 128)
        blocks.append(of_lead[:, pl.ds(start, units * LANES)])
    return blocks[0] if len(blocks) == 1 else jnp.concatenate(blocks, axis=1)


def sibling_grad_kernel(jobs, *refs):
    operands, out = refs[:-1], refs[-1]
    core_at = lax.axis_index(STREAM) % 2
    row = 0
    for at, (units, blocks, depth) in enumerate(jobs):
        left, right = operands[2 * at], operands[2 * at + 1]
        product = low(dot_first(left[...], grad_columns(right, 1 - core_at, units)))
        for block in range(blocks):
            columns = product[:, block * LANES : (block + 1) * LANES]
            out[:, :, row : row + depth] = columns.reshape(8, 2, depth, LANES)
            row += depth


TO_X = ((2, False, False), (3, False, False), (2, True, False), (3, True, False))
TO_Y_A = ((0, False, True), (1, False, True))
TO_Z_A = ((1, False, False), (1, True, False))
TO_Y_B = ((2, False, True), (3, False, True), (0, False, False))
TO_Z_B = ((1, True, True),)
TO_Z_C = ((2, True, True), (3, True, True))
OWN = ((0, True, True), (0, True, False))
PARTS = (TO_X, TO_Y_A, TO_Z_A, TO_Y_B, TO_Z_B, TO_Z_C, OWN)


def part_at(part):
    z_at, y_at, x_at, _ = place()
    slot, own_y, own_x = part
    return (
        shard_slots(z_at)[slot] * 2 + (y_at if own_y else 1 - y_at),
        x_at if own_x else 1 - x_at,
    )


def small_grad_rows(sums, hidden_bias, work):
    sums0, sums1, sums2, sums3, sums_kv = sums
    rows = (
        (sums0, 0), (sums0, 1), (sums1, 2), (sums1, 1), (sums1, 3), (sums_kv, 0), (sums2, 2),
        (sums2, 1), (sums3, 2), (sums3, 1), (sums1, 0), (sums2, 0), (sums3, 0),
    )
    part = sums0.shape[1] // 8
    work[...] = jnp.zeros_like(work)
    for dp_to in range(8):
        columns = slice(dp_to * part, (dp_to + 1) * part)
        for row, (array, at) in enumerate(rows):
            work[dp_to, row : row + 1, :part] = array[at : at + 1, columns]
        for j in range(hidden_bias.shape[1] // part):
            at = len(rows) + j
            work[dp_to, at : at + 1, :part] = hidden_bias[
                dp_to : dp_to + 1, j * part : (j + 1) * part
            ]


def own_grad_kernel(jobs, sent, small, *refs):
    inputs = 2 * len(jobs) + len(sent)
    operands, came = refs[: 2 * len(jobs)], refs[2 * len(jobs) : inputs]
    extra = refs[inputs : inputs + 6 * small]
    outs = refs[inputs + 6 * small : inputs + 6 * small + len(PARTS)]
    work, *small_work = refs[inputs + 6 * small + len(PARTS) :]
    core_at = lax.axis_index(STREAM) % 2
    row = 0
    for at, (units, blocks, depth) in enumerate(jobs):
        left, right = operands[2 * at], operands[2 * at + 1]
        product = dot_first(left[...], grad_columns(right, core_at, units))
        array, came_row = sent[at]
        for block in range(blocks):
            columns = product[:, block * LANES : (block + 1) * LANES]
            rows = slice(row, row + depth)
            work[:, :, :depth] = columns.reshape(8, 2, depth, LANES) + wide(
                came[array][:, :, came_row : came_row + depth]
            )
            for out, parts in zip(outs, PARTS):
                for j, part in enumerate(parts):
                    dp_from, x_from = part_at(part)
                    out[j, rows] = low(work[dp_from, x_from, :depth])
            row += depth
            came_row += depth
    if small:
        small_grad_rows(extra[:5], extra[5], small_work[0])
        for out, parts in zip(outs, PARTS):
            for j, part in enumerate(parts):
                dp_from, x_from = part_at(part)
                rows = pl.ds(pl.multiple_of(x_from * PAD_ROWS, PAD_ROWS), PAD_ROWS)
                out[j, row : row + PAD_ROWS] = low(small_work[0][dp_from, rows])


def reduce_steps(to_x, to_y_a, to_z_a, to_y_b, to_z_b, to_z_c, own):
    from_y_a, from_x, from_z_a = yield [
        (to_y_a, DP, BESIDE),
        (to_x, STREAM, ACROSS),
        (to_z_a, DP, PAIR),
    ]
    arrived = jnp.concatenate((from_x[:2], from_z_a[:1]))
    from_y_b, mate = yield [
        (low(wide(to_y_b) + wide(arrived)), DP, BESIDE),
        (low(wide(to_z_b) + wide(from_y_a[1:])), DP, PAIR),
    ]
    far = wide(to_z_c) + wide(from_x[2:]) + wide(from_y_b[:2])
    (by_mate,) = yield [(low(far[1]), DP, PAIR)]
    (half,) = yield [(low(far[0] + wide(by_mate)), DP, HALFWAY)]
    total = low(
        jnp.stack(
            (
                wide(own[0]) + wide(from_y_a[0]) + wide(mate[0]) + wide(half),
                wide(own[1]) + wide(from_y_b[2]) + wide(from_z_a[1]),
            )
        )
    )
    (from_x,) = yield [(total, STREAM, ACROSS)]
    total = low(wide(total) + wide(from_x[::-1]))
    return total, lax.ppermute(total, STREAM, CORE)


def unpack_kernel(jobs, small, mine, other, *outs):
    _, _, x_at, core_at = place()
    for source, core_from in ((mine, core_at), (other, 1 - core_at)):
        for j in range(2):
            x_from = x_at if j == 0 else 1 - x_at
            for out_at, lead, units, row, depth in jobs:
                out = outs[out_at] if lead is None else outs[out_at].at[lead]
                for unit in range(units):
                    at = row + unit * depth
                    start = core_from * (units * LANES) + unit * LANES
                    out[
                        pl.ds(pl.multiple_of(x_from * depth, 8), depth),
                        pl.ds(pl.multiple_of(start, 128), LANES),
                    ] = wide(source[j, at : at + depth])
    if small is not None:
        biases, gains, hidden_bias, work = outs[-4:]
        for j in range(2):
            x_from = x_at if j == 0 else 1 - x_at
            rows = slice(small, small + PAD_ROWS)
            work[pl.ds(pl.multiple_of(x_from * PAD_ROWS, 8), PAD_ROWS)] = wide(
                mine[j, rows]
            ) + wide(other[j, rows])
        part = biases.shape[1]
        biases[...] = work[:G_1, :part]
        gains[...] = work[G_1 : G_3 + 1, :part]
        hidden_bias[...] = work[G_3 + 1 : G_3 + 1 + hidden_bias.shape[0], :part]


def reduce_plain(parts):
    shards = []
    for left, right in parts:
        if right.ndim == 2:
            whole = low(dot_first(left, right))
            own = lax.psum_scatter(whole, DP, scatter_dimension=0, tiled=True)
        else:
            whole = low(jnp.stack([dot_first(left, r) for r in right]))
            own = lax.psum_scatter(whole, DP, scatter_dimension=1, tiled=True)
        shards.append(wide(lax.psum(own, STREAM)))
    return shards


class Group:
    def __init__(self):
        self.operands, self.jobs, self.out_jobs, self.out_shapes = [], [], [], []
        self.rows, self.flops, self.sent, self.came, self.from_sent = 0, 0, [], [], []

    def sibling(self, tie, *parts):
        jobs, operands, rows, flops = [], [], 0, 0
        for left, right in parts:
            operands += [left, right]
            depth = left.shape[1] // 16
            units = right.shape[-1] // (2 * LANES)
            leads = [None] if right.ndim == 2 else range(right.shape[0])
            jobs.append((units, units * len(leads), depth))
            self.from_sent.append((len(self.sent), rows))
            for lead in leads:
                self.out_jobs.append(
                    (len(self.out_shapes), lead, units, self.rows + rows, depth)
                )
                rows += units * depth
            self.out_shapes.append(
                shape((*right.shape[:-2], 2 * depth, right.shape[-1]), F32)
            )
            flops += left.shape[0] * left.shape[1] * right.size // right.shape[-2]
        self.sent.append(
            call(
                functools.partial(sibling_grad_kernel, jobs),
                shape((8, 2, rows, LANES)),
                [VMEM] * len(operands),
                flops=flops,
            )(tie(operands[0]), *operands[1:])
        )
        self.jobs += jobs
        self.operands += operands
        self.rows += rows
        self.flops += flops
        return self.sent[-1]

    def core_move(self):
        def steps(sent):
            (came,) = yield [(sent, STREAM, CORE)]
            self.came.append(came)

        return Mover(steps(self.sent[-1]))

    def own(self, tie, small=()):
        deepest = max(job[-1] for job in self.jobs)
        scratch = [pltpu.VMEM((8, 2, deepest, LANES), F32)]
        if small:
            scratch.append(pltpu.VMEM((8, 2 * PAD_ROWS, LANES), F32))
        rows = self.rows + PAD_ROWS * bool(small)
        came = [self.came[array] for array, _ in self.from_sent]
        self.parts = call(
            functools.partial(
                own_grad_kernel,
                self.jobs,
                [(at, row) for at, (_, row) in enumerate(self.from_sent)],
                bool(small),
            ),
            [shape((len(parts), rows, LANES)) for parts in PARTS],
            [VMEM] * (len(self.operands) + len(came) + len(small)),
            scratch,
            flops=self.flops,
        )(tie(self.operands[0]), *self.operands[1:], *came, *small)
        return self.parts

    def move(self):
        return Mover(reduce_steps(*self.parts))

    def unpack(self, moved, small=()):
        return call(
            functools.partial(unpack_kernel, self.out_jobs, self.rows if small else None),
            [*self.out_shapes, *small],
            [VMEM, VMEM],
            [pltpu.VMEM((2 * PAD_ROWS, LANES), F32)] * bool(small),
        )(*moved)


def norm_parts(summed):
    center = summed - jnp.mean(summed, axis=-1, keepdims=True)
    inverse = lax.rsqrt(jnp.mean(center * center, axis=-1, keepdims=True) + EPSILON)
    return center * inverse, inverse


def norm_back(upstream, normed, inverse, gain):
    scaled = upstream * gain
    return inverse * (
        scaled
        - jnp.mean(scaled, axis=-1, keepdims=True)
        - normed * jnp.mean(scaled * normed, axis=-1, keepdims=True)
    )


def heads_apart(four):
    head = lax.broadcasted_iota(jnp.int32, four.shape, 1) // 64
    return low(jnp.concatenate([jnp.where(head == j, four, 0.0) for j in range(4)], axis=0))


def heads_joined(stacked):
    rows = stacked.shape[0] // 4
    head = lax.broadcasted_iota(jnp.int32, (rows, stacked.shape[1]), 1) // 64
    made = stacked[:rows]
    for j in range(1, 4):
        made = jnp.where(head == j, stacked[j * rows : (j + 1) * rows], made)
    return made


def quads():
    return [slice(j * 256, (j + 1) * 256) for j in range(HEADS // 4)]


def softmax(scores):
    raised = jnp.exp(scores - jnp.max(scores, axis=-1, keepdims=True))
    return raised * (1.0 / jnp.sum(raised, axis=-1, keepdims=True))


def score_back(weight, back):
    return low(weight * (back - jnp.sum(back * weight, axis=-1, keepdims=True)))


def row_sum(value):
    return jnp.sum(value, axis=0, keepdims=True)


def self_kernel(seq, lengths, x_ref, w_ref, vec, qkv_ref, out_ref, q, k, v, o):
    tokens = x_ref.shape[0]
    for j, (scratch, bias) in enumerate(((q, B_Q), (k, None), (v, B_V))):
        for c in range(2):
            columns = slice(c * LANES, (c + 1) * LANES)
            made = dot(x_ref[...], w_ref[c, j])
            if bias is not None:
                made = made + vec[bias : bias + 1, columns]
            made = low(made)
            qkv_ref[j, :, columns] = made
            scratch[:, columns] = wide(made)

    def step(r, _):
        rows = pl.ds(pl.multiple_of(r * seq, 8), seq)
        valid = lax.broadcasted_iota(jnp.int32, (4 * seq, seq), 1) < lengths[r]
        asked = [heads_apart(q[rows, c] * 0.125) for c in quads()]
        scores = [dot_last(a, low(k[rows, c])) for a, c in zip(asked, quads())]
        weights = [softmax(jnp.where(valid, score, -jnp.inf)) for score in scores]
        made = [dot(low(w), low(v[rows, c])) for w, c in zip(weights, quads())]
        for part, c in zip(made, quads()):
            o[rows, c] = heads_joined(part)
        return 0

    lax.fori_loop(0, tokens // seq, step, 0, unroll=2)
    out_ref[...] = low(o[...])


def first_norm_kernel(seq, o_ref, x_ref, wso, wcq, vec, normed, inverse, h_low, qc, z):
    for c in range(2):
        columns = slice(c * LANES, (c + 1) * LANES)
        z[:, columns] = (
            dot(o_ref[...], wso[c, 0])
            + vec[B_SO : B_SO + 1, columns]
            + wide(x_ref[:, columns])
        )
    made, scale = norm_parts(z[...])
    normed[...] = made
    inverse[...] = scale
    h_low[...] = low(made * vec[G_1 : G_1 + 1] + vec[B_N1 : B_N1 + 1])
    for c in range(2):
        columns = slice(c * LANES, (c + 1) * LANES)
        qc[:, columns] = low(dot(h_low[...], wcq[c, 0]) + vec[B_CQ : B_CQ + 1, columns])


def pixel_kernel(patch_ref, out_ref):
    images, patches, _ = patch_ref.shape
    out_ref[:, :patches] = patch_ref[...]
    out_ref[:, patches:] = jnp.zeros_like(out_ref[:, patches:])


def image_kernel(pixels, w_ref, vec, kv_ref):
    slots, _, images, padded, width = kv_ref.shape
    rows = images * padded
    flat = pixels[...].reshape(slots * rows, -1)
    for j in range(2):
        made = dot(flat, jnp.concatenate((w_ref[0, j], w_ref[1, j]), axis=1))
        if j == 1:
            made = made + vec[B_CV : B_CV + 1]
        for slot in range(slots):
            part = made[slot * rows : (slot + 1) * rows]
            kv_ref[slot, j] = low(part).reshape(images, padded, width)


def cross_kernel(
    seq, patches, micro_rows, slots, qc, kv, n1, wco, vec, oc, n2, inverse, h_low, q, o
):
    q[...] = wide(qc[...]) * 0.125
    tokens = qc.shape[0]
    padded = kv.shape[3]
    there = lax.broadcasted_iota(jnp.int32, (4 * seq, padded), 1) < patches

    def step(r, _):
        rows = pl.ds(pl.multiple_of(r * seq, 8), seq)
        slot, m = slots[r], r // micro_rows
        asked = [heads_apart(q[rows, c]) for c in quads()]
        scores = [dot_last(a, kv[slot, 0, m, :, c]) for a, c in zip(asked, quads())]
        weights = [softmax(jnp.where(there, score, -jnp.inf)) for score in scores]
        made = [dot(low(w), kv[slot, 1, m, :, c]) for w, c in zip(weights, quads())]
        for part, c in zip(made, quads()):
            o[rows, c] = heads_joined(part)
        return 0

    lax.fori_loop(0, tokens // seq, step, 0, unroll=2)
    oc[...] = low(o[...])
    for c in range(2):
        columns = slice(c * LANES, (c + 1) * LANES)
        first = n1[:, columns] * vec[G_1 : G_1 + 1, columns] + vec[B_N1 : B_N1 + 1, columns]
        o[:, columns] = first + dot(oc[...], wco[c, 0]) + vec[B_CO : B_CO + 1, columns]
    made, scale = norm_parts(o[...])
    n2[...] = made
    inverse[...] = scale
    h_low[...] = low(made * vec[G_2 : G_2 + 1] + vec[B_N2 : B_N2 + 1])


def small_rows_kernel(shards, vec, hidden_bias, part):
    wide_rows = G_3 + 1
    vec[...] = jnp.zeros_like(vec)
    for dp_from in range(8):
        rows = wide(shards[dp_from * 2 * PAD_ROWS : (dp_from + 1) * 2 * PAD_ROWS])
        vec[:wide_rows, dp_from * part : (dp_from + 1) * part] = rows[:wide_rows, :part]
        for j in range(LANES // part):
            hidden_bias[dp_from : dp_from + 1, j * part : (j + 1) * part] = rows[
                wide_rows + j : wide_rows + j + 1, :part
            ]


def take_weights(units, spec, sources, wholes, outs, in_sems, out_sems, kept):
    if spec is None:
        copies = [
            [pltpu.make_async_copy(source, whole, in_sems.at[at])]
            for at, (source, whole) in enumerate(zip(sources, wholes))
        ]
    else:
        copies = piece_copies(units, spec, sources, wholes, in_sems)
    for of_weight in copies:
        for copy in of_weight:
            copy.start()

    def take(at):
        for copy in copies[at]:
            copy.wait()
        if outs[at] is not None:
            send(wholes[at], outs[at])

    def send(source, target):
        kept.append(pltpu.make_async_copy(source, target, out_sems.at[len(kept)]))
        kept[-1].start()

    return take, send


def text_kernel(units, gathered, spec, seq, lengths, text, *refs):
    sources, refs = refs[:gathered], refs[gathered:]
    if spec is None:
        small, refs = refs[:2], refs[2:]
    outs, refs = refs[:11], refs[11:]
    vec, hidden_bias, attended, n1, inverse1, h1, qc, qkv_out, *w_outs = outs
    wholes, (qkv, q, k, v, o, in_sems, out_sems) = refs[:4], refs[4:]
    w_small, w_qkv, w_so, w_cq = wholes
    kept = []
    take, send = take_weights(
        units, spec, sources, wholes, (None, *w_outs), in_sems, out_sems, kept
    )
    take(0)
    if spec is None:
        vec[...], hidden_bias[...] = small[0][...], small[1][...]
    else:
        small_rows_kernel(w_small.at[0, 0], vec, hidden_bias, text.shape[1] // 8)
    take(1)
    self_kernel(seq, lengths, text, w_qkv, vec, qkv, attended, q, k, v, o)
    send(qkv, qkv_out)
    take(2)
    take(3)
    first_norm_kernel(seq, attended, text, w_so, w_cq, vec, n1, inverse1, h1, qc, o)
    for copy in kept:
        copy.wait()


def patch_kernel(units, gathered, spec, seq, patches, micro_rows, slots, qc, n1, vec, *refs):
    sources, held, refs = refs[:gathered], refs[gathered : gathered + 4], refs[gathered + 4 :]
    (oc, n2, inverse2, h2, kv_out, pixels_out, *w_outs), refs = refs[:8], refs[8:]
    wholes, (kv, pixels, q, o, in_sems, pixel_sems, out_sems) = refs[:2], refs[2:]
    w_kv, w_co = wholes
    pixel_copies = [
        pltpu.make_async_copy(image, pixels.at[at], pixel_sems.at[at])
        for at, image in enumerate(held)
    ]
    for copy in pixel_copies:
        copy.start()
    kept = []
    take, send = take_weights(units, spec, sources, wholes, w_outs, in_sems, out_sems, kept)
    for copy in pixel_copies:
        copy.wait()
    send(pixels, pixels_out)
    take(0)
    image_kernel(pixels, w_kv, vec, kv)
    send(kv, kv_out)
    take(1)
    cross_kernel(
        seq, patches, micro_rows, slots, qc, kv, n1, w_co, vec, oc, n2, inverse2, h2, q, o
    )
    for copy in kept:
        copy.wait()


def hidden_weights(w, block, in_units):
    core, unit = divmod(block, in_units)
    depth = w.shape[3] // 2 // in_units
    return w[:, :, core, unit * depth : (unit + 1) * depth].reshape(-1, LANES)


def ffn_kernel(
    gathered, spec, in_units, seq, lengths, h2, bias, n2, cot, vec, *refs
):
    sources, refs = refs[:gathered], refs[gathered:]
    out, dz, df, rows_out, active, slope, w_out, w, total, in_sems, out_sem = refs
    if spec is None:
        copies = [pltpu.make_async_copy(sources[0], w, in_sems.at[0])]
    else:
        copies = [
            pltpu.make_async_copy(
                source.at[pl.ds(first, w.shape[3])],
                w.at[z_from * 2 + y_from, x_from, core_from],
                in_sems.at[at],
            )
            for at, (source, first, z_from, y_from, x_from, core_from) in enumerate(
                piece_places(spec, sources)
            )
        ]
    for copy in copies:
        copy.start()
    for copy in copies:
        copy.wait()
    keep = pltpu.make_async_copy(w, w_out, out_sem.at[0])
    keep.start()
    for block in range(2 * in_units):
        columns = slice(block * LANES, (block + 1) * LANES)
        pre = dot(h2[...], hidden_weights(w, block, in_units)) + bias[block : block + 1]
        cumulative = 0.5 * (1.0 + lax.erf(pre * ROOT_HALF))
        active[:, columns] = low(pre * cumulative)
        slope[:, columns] = low(cumulative + pre * INV_ROOT_TAU * jnp.exp(-0.5 * pre * pre))
    half_rows = w.shape[3] // 2
    for c in range(2):
        columns = slice(c * LANES, (c + 1) * LANES)
        made = None
        for part in range(4):
            weights = w[2 * part : 2 * part + 2, :, c, half_rows:].reshape(-1, LANES)
            depth = weights.shape[0]
            term = dot(active[:, part * depth : (part + 1) * depth], weights)
            made = term if made is None else made + term
        total[:, columns] = made

    def step(r, sums):
        rows = pl.ds(pl.multiple_of(r * seq, 8), seq)
        second = n2[rows, :] * vec[G_2 : G_2 + 1] + vec[B_N2 : B_N2 + 1]
        made, scale = norm_parts(second + total[rows, :] + vec[B_FO : B_FO + 1])
        out[r] = low(made * vec[G_3 : G_3 + 1] + vec[B_N3 : B_N3 + 1])
        valid = lax.broadcasted_iota(jnp.int32, made.shape, 0) < lengths[r]
        upstream = jnp.where(valid, wide(cot[r]), 0.0)
        back = norm_back(upstream, made, scale, vec[G_3 : G_3 + 1])
        dz[rows, :] = back
        gain, shift, lowered = sums
        return (
            gain + row_sum(upstream * made),
            shift + row_sum(upstream),
            lowered + row_sum(wide(low(back))),
        )

    zero = jnp.zeros((1, total.shape[1]), F32)
    sums = lax.fori_loop(0, out.shape[0], step, (zero, zero, zero), unroll=2)
    df[...] = low(dz[...])
    for j in range(3):
        rows_out[j : j + 1] = sums[j]
    rows_out[3:8] = jnp.zeros((5, total.shape[1]), F32)
    keep.wait()


def norm_back_rows(total, dz_ref, normed, inverse, gain, dz, low_ref, rows_out, step_rows):
    def step(r, sums):
        rows = pl.ds(pl.multiple_of(r * step_rows, 8), step_rows)
        upstream = total[rows, :] + dz_ref[rows, :]
        made = normed[rows, :]
        back = norm_back(upstream, made, inverse[rows, :], gain)
        dz[rows, :] = back
        return (
            sums[0] + row_sum(upstream * made),
            sums[1] + row_sum(upstream),
            sums[2] + row_sum(wide(low(back))),
        )

    zero = jnp.zeros((1, total.shape[1]), F32)
    sums = lax.fori_loop(0, total.shape[0] // step_rows, step, (zero, zero, zero))
    low_ref[...] = low(dz[...])
    for j in range(3):
        rows_out[j : j + 1] = sums[j]
    rows_out[3:8] = jnp.zeros((5, total.shape[1]), F32)


def hidden_back_kernel(
    seq, df, wout, win, slope, dz3, n2, inverse, vec, du, bias_out, dz2, dac, rows_out, total
):
    i = pl.program_id(0)

    @pl.when(i == 0)
    def _():
        total[...] = jnp.zeros_like(total)

    raw = dot_last(df[:, :LANES], wout[0, :, 0].reshape(-1, LANES))
    raw = raw + dot_last(df[:, LANES:], wout[0, :, 1].reshape(-1, LANES))
    made = low(raw * wide(slope[...]))
    du[...] = made
    bias_out[pl.ds(i, 1), :] = row_sum(wide(made))
    total[...] += dot_last(made, win[:, :, 0].reshape(-1, LANES))

    @pl.when(i == pl.num_programs(0) - 1)
    def _():
        norm_back_rows(
            total, dz3, n2, inverse, vec[G_2 : G_2 + 1], dz2, dac, rows_out, seq
        )


def cross_back_kernel(
    seq, patches, micro_rows, slots, dac, qc, kv, wco, dqc, dkv_out, dkv, q, do, dq
):
    q[...] = wide(qc[...]) * 0.125
    do[...] = wide(
        low(dot_last(dac[:, :LANES], wco[0, 0]) + dot_last(dac[:, LANES:], wco[1, 0]))
    )
    dkv[...] = jnp.zeros_like(dkv)
    tokens = qc.shape[0]
    padded = kv.shape[3]
    there = lax.broadcasted_iota(jnp.int32, (4 * seq, padded), 1) < patches

    def step(r, _):
        rows = pl.ds(pl.multiple_of(r * seq, 8), seq)
        slot, m = slots[r], r // micro_rows
        asked = [heads_apart(q[rows, c]) for c in quads()]
        came = [heads_apart(do[rows, c]) for c in quads()]
        keys = [kv[slot, 0, m, :, c] for c in quads()]
        values = [kv[slot, 1, m, :, c] for c in quads()]
        scores = [dot_last(a, key) for a, key in zip(asked, keys)]
        backs = [dot_last(d, value) for d, value in zip(came, values)]
        weights = [softmax(jnp.where(there, score, -jnp.inf)) for score in scores]
        backs = [score_back(w, b) for w, b in zip(weights, backs)]
        queries = [heads_joined(dot(b, key)) for b, key in zip(backs, keys)]
        key_parts = [dot_first(b, a) for b, a in zip(backs, asked)]
        value_parts = [dot_first(low(w), d) for w, d in zip(weights, came)]
        for j, c in enumerate(quads()):
            dq[rows, c] = queries[j] * 0.125
            dkv[0, slot, m, :, c] += key_parts[j]
            dkv[1, slot, m, :, c] += value_parts[j]
        return 0

    lax.fori_loop(0, tokens // seq, step, 0, unroll=2)
    dqc[...] = low(dq[...])
    dkv_out[...] = low(dkv[...])


def first_back_kernel(seq, dqc, wcq, dz2, n1, inverse, vec, dz1, da, rows_out, total):
    total[...] = dot_last(dqc[:, :LANES], wcq[0, 0]) + dot_last(dqc[:, LANES:], wcq[1, 0])
    norm_back_rows(total, dz2, n1, inverse, vec[G_1 : G_1 + 1], dz1, da, rows_out, seq)
    rows_out[3:4] = row_sum(wide(dqc[...]))


def self_back_kernel(seq, lengths, da, qkv, wso, dqkv, rows_out, q, k, v, do, dq, dk, dv):
    q[...] = wide(qkv[0]) * 0.125
    k[...] = wide(qkv[1])
    v[...] = wide(qkv[2])
    do[...] = wide(low(dot_last(da[:, :LANES], wso[0, 0]) + dot_last(da[:, LANES:], wso[1, 0])))
    tokens = da.shape[0]

    def step(r, _):
        rows = pl.ds(pl.multiple_of(r * seq, 8), seq)
        valid = lax.broadcasted_iota(jnp.int32, (4 * seq, seq), 1) < lengths[r]
        asked = [heads_apart(q[rows, c]) for c in quads()]
        came = [heads_apart(do[rows, c]) for c in quads()]
        keys = [low(k[rows, c]) for c in quads()]
        values = [low(v[rows, c]) for c in quads()]
        scores = [dot_last(a, key) for a, key in zip(asked, keys)]
        backs = [dot_last(d, value) for d, value in zip(came, values)]
        weights = [softmax(jnp.where(valid, score, -jnp.inf)) for score in scores]
        backs = [score_back(w, b) for w, b in zip(weights, backs)]
        queries = [heads_joined(dot(b, key)) for b, key in zip(backs, keys)]
        key_parts = [dot_first(b, a) for b, a in zip(backs, asked)]
        value_parts = [dot_first(low(w), d) for w, d in zip(weights, came)]
        for j, c in enumerate(quads()):
            dq[rows, c] = queries[j] * 0.125
            dk[rows, c] = key_parts[j]
            dv[rows, c] = value_parts[j]
        return 0

    lax.fori_loop(0, tokens // seq, step, 0, unroll=2)
    for j, made in enumerate((dq, dk, dv)):
        dqkv[j] = low(made[...])
    rows_out[0:1] = row_sum(wide(dqkv[0]))
    rows_out[1:2] = row_sum(wide(dqkv[2]))
    rows_out[2:8] = jnp.zeros((6, q.shape[1]), F32)


def text_grad_kernel(dz1, dqkv, w_ref, out, total):
    total[...] = dz1[...]
    for j in range(3):
        for c in range(2):
            total[...] += dot_last(dqkv[j, :, c * LANES : (c + 1) * LANES], w_ref[c, j])
    seq = out.shape[1]
    for r in range(out.shape[0]):
        out[r] = low(total[r * seq : (r + 1) * seq, :])


def patch_grad_kernel(dkv, w_ref, kept, sent, rows_out):
    _, slots, images, padded, width = dkv.shape
    rows = images * padded
    total = jnp.zeros((1, width), F32)
    for slot in range(slots):
        made = None
        for j in range(2):
            grad = dkv[j, slot].reshape(rows, width)
            for c in range(2):
                term = dot_last(grad[:, c * LANES : (c + 1) * LANES], w_ref[c, j])
                made = term if made is None else made + term
        out = sent if slot % 2 else kept
        out[slot // 2] = low(made).reshape(images, padded, w_ref.shape[2])
        total = total + row_sum(wide(grad))
    rows_out[0:1] = total
    rows_out[1:8] = jnp.zeros((7, width), F32)


def on_device(
    text_input,
    patch_input,
    text_lengths,
    image_of_row,
    cotangent,
    self_qkv,
    self_out,
    cross_q,
    cross_kv,
    cross_out,
    ffn_in,
    ffn_out,
    biases,
    norm_gains,
    ffn_bias,
):
    dp = lax.axis_size(DP)
    micros, row_count, seq, width = text_input.shape
    patches, patch_width = patch_input.shape[2:]
    rows_all = micros * row_count
    tokens = rows_all * seq
    hidden = ffn_in.shape[1]
    padded = -(-patches // 16) * 16
    images = micros * patch_input.shape[1]

    part = biases.shape[1]
    small = jnp.concatenate((biases, norm_gains, ffn_bias.reshape(-1, part)))
    small_rows = small.shape[0]
    wide_rows = biases.shape[0] + norm_gains.shape[0]
    small = jnp.pad(small, ((0, 2 * PAD_ROWS - small_rows), (0, LANES - part)))
    small = jnp.broadcast_to(small.reshape(2, PAD_ROWS, LANES), (2, 2, PAD_ROWS, LANES))

    half = width // dp // 2
    half_v = cross_kv.shape[1] // 2
    in_units = hidden // (2 * LANES)
    text_group = (
        (small, self_qkv, self_out, cross_q),
        ((1, PAD_ROWS), (3, half), (1, half), (1, half)),
    )
    patch_group = ((cross_kv, cross_out), ((2, half_v), (1, half)))
    hidden_group = ((ffn_in, ffn_out), ((in_units, half), (1, ffn_out.shape[0] // 2)))

    text = text_input.reshape(tokens, width)
    pixels = call(pixel_kernel, shape((images, padded, patch_width)), [VMEM])(
        patch_input.reshape(images, patches, patch_width)
    )
    lengths = text_lengths.reshape(-1)
    slots = image_of_row.reshape(-1) ^ lax.axis_index(STREAM)
    flat = (tokens, width)
    full = pltpu.VMEM(flat, F32)
    flops = 2 * tokens * width * width
    steps = hidden // LANES
    chunks = hidden // width
    kv_shape = (4, 2, images, padded, width)
    in_block = pl.BlockSpec(
        (8, 2, 1, width // 16, LANES), lambda i: (0, 0, i // in_units, i % in_units, 0)
    )
    v = types.SimpleNamespace()

    bf16 = jnp.bfloat16

    def pixel_steps():
        (v.across,) = yield [(pixels, STREAM, ACROSS)]
        v.beside, v.apart = yield [(pixels, STREAM, CORE), (v.across, STREAM, CORE)]

    def run_text(tie, sources, spec=None, small_inputs=()):
        units = text_group[1]
        wholes = [(2, 1, 16 * PAD_ROWS, LANES)]
        wholes += [(2, count, depth * 2 * dp, LANES) for count, depth in units[1:]]
        outs = [
            shape((16, width), F32), shape((steps, LANES), F32), shape(flat), shape(flat, F32),
            shape((tokens, 1), F32), shape(flat), shape(flat), shape((3, *flat)),
            *[shape(dims) for dims in wholes[1:]],
        ]
        (
            v.vec, v.hidden_bias, v.attended, v.n1, v.inverse1, v.h1, v.qc, v.qkv,
            v.w_qkv, v.w_so, v.w_cq,
        ) = call(
            functools.partial(text_kernel, units, len(sources), spec, seq),
            outs,
            [SMEM, VMEM] + [ANY] * len(sources) + [VMEM] * len(small_inputs),
            [
                *[pltpu.VMEM(dims, bf16) for dims in wholes],
                pltpu.VMEM((3, *flat), bf16), full, full, full, full,
                pltpu.SemaphoreType.DMA((32 * len(units),)), pltpu.SemaphoreType.DMA((4,)),
            ],
            out_specs=[VMEM] * 7 + [ANY] * 4,
            mib=60,
            flops=8 * flops,
        )(lengths, tie(text), *sources, *small_inputs)
        return v.qc

    def run_patch(tie, sources, spec=None):
        units = patch_group[1]
        wholes = [(2, count, depth * 2 * dp, LANES) for count, depth in units]
        pixels_shape = (4, images, padded, patch_width)
        outs = [
            shape(flat), shape(flat, F32), shape((tokens, 1), F32), shape(flat),
            shape(kv_shape), shape(pixels_shape), *[shape(dims) for dims in wholes],
        ]
        v.oc, v.n2, v.inverse2, v.h2, v.kv, pixels_all, v.w_kv, v.w_co = call(
            functools.partial(patch_kernel, units, len(sources), spec, seq, patches, row_count),
            outs,
            [SMEM, VMEM, VMEM, VMEM] + [ANY] * (len(sources) + 4),
            [
                *[pltpu.VMEM(dims, bf16) for dims in wholes],
                pltpu.VMEM(kv_shape, bf16), pltpu.VMEM(pixels_shape, bf16), full, full,
                pltpu.SemaphoreType.DMA((32 * len(units),)), pltpu.SemaphoreType.DMA((4,)),
                pltpu.SemaphoreType.DMA((4,)),
            ],
            out_specs=[VMEM] * 4 + [ANY] * 4,
            mib=60,
            flops=18 * flops,
        )(slots, tie(v.qc), v.n1, v.vec, *sources, pixels, v.beside, v.across, v.apart)
        v.pixels_all = pixels_all.reshape(-1, patch_width)
        return v.h2

    def run_ffn(tie, sources, spec=None):
        w_shape = (8, 2, 2, hidden // 8, LANES)
        v.out_rows, v.dz3, v.df, v.sums3, v.active, v.slope, v.w_hidden = call(
            functools.partial(ffn_kernel, len(sources), spec, in_units, seq),
            [
                shape((rows_all, seq, width)), shape(flat, F32), shape(flat),
                shape((8, width), F32), shape((tokens, hidden)), shape((tokens, hidden)),
                shape(w_shape),
            ],
            [SMEM] + [VMEM] * 5 + [ANY] * len(sources),
            [
                pltpu.VMEM(w_shape, bf16), full, pltpu.SemaphoreType.DMA((32,)),
                pltpu.SemaphoreType.DMA((1,)),
            ],
            out_specs=[VMEM] * 6 + [ANY],
            flops=8 * flops,
        )(
            lengths, tie(v.h2), v.hidden_bias, v.n2,
            cotangent.reshape(rows_all, seq, width), v.vec, *sources,
        )
        return v.df

    def run_hidden_back(tie):
        v.du, v.hidden_bias_grad, v.dz2, v.dac, v.sums2 = call(
            functools.partial(hidden_back_kernel, seq),
            [
                shape((tokens, hidden)),
                shape((steps, LANES), F32),
                shape(flat, F32),
                shape(flat),
                shape((8, width), F32),
            ],
            [
                VMEM,
                pl.BlockSpec((1, 2, 2, hidden // 16, LANES), lambda i: (i, 0, 0, 1, 0)),
                in_block,
                pl.BlockSpec((tokens, LANES), lambda i: (0, i)),
                VMEM,
                VMEM,
                VMEM,
                VMEM,
            ],
            [full],
            out_specs=[pl.BlockSpec((tokens, LANES), lambda i: (0, i)), VMEM, VMEM, VMEM, VMEM],
            grid=(steps,),
            flops=8 * flops,
        )(
            tie(v.df), v.w_hidden, v.w_hidden, v.slope, v.dz3, v.n2, v.inverse2,
            v.vec,
        )
        return v.dac

    def run_cross_back(tie):
        v.dqc, v.dkv_all = call(
            functools.partial(cross_back_kernel, seq, patches, row_count),
            [shape(flat), shape((2, 4, images, padded, width))],
            [SMEM, VMEM, VMEM, VMEM, VMEM],
            [pltpu.VMEM((2, 4, images, padded, width), F32), full, full, full],
            flops=4 * flops,
        )(slots, tie(v.dac), v.qc, v.kv, v.w_co)
        return v.dqc

    def patch_steps():
        (came,) = yield [(v.patch_sent, STREAM, CORE)]
        made = wide(v.patch_kept) + wide(came)
        (across,) = yield [(low(made[1]), STREAM, ACROSS)]
        v.patch_rows = low(made[0] + wide(across))[:, :patches].reshape(patch_input.shape)

    def run_first_back(tie):
        v.dz1, v.da, v.sums1 = call(
            functools.partial(first_back_kernel, seq),
            [shape(flat, F32), shape(flat), shape((8, width), F32)],
            [VMEM] * 6,
            [full],
            flops=flops,
        )(tie(v.dqc), v.w_cq, v.dz2, v.n1, v.inverse1, v.vec)
        return v.da

    def run_self_back(tie):
        v.dqkv, v.sums0 = call(
            functools.partial(self_back_kernel, seq),
            [shape((3, *flat)), shape((8, width), F32)],
            [SMEM, VMEM, VMEM, VMEM],
            [full] * 7,
            flops=4 * flops,
        )(lengths, tie(v.da), v.qkv, v.w_so)
        return v.dqkv

    def run_patch_grad(tie):
        v.patch_kept, v.patch_sent, v.sums_kv = call(
            patch_grad_kernel,
            [shape((2, images, padded, patch_width))] * 2 + [shape((8, width), F32)],
            [VMEM] * 2,
            flops=16 * flops,
        )(tie(v.dkv_all), v.w_kv)
        return v.patch_sent

    def run_text_grad(tie):
        v.text_rows = call(
            text_grad_kernel,
            shape((rows_all, seq, width)),
            [VMEM] * 3,
            [full],
            flops=3 * flops,
        )(tie(v.dz1), v.dqkv, v.w_qkv)
        return v.text_rows

    def small_grads():
        sums0, sums1, sums2, sums3, sums_kv = v.sums0, v.sums1, v.sums2, v.sums3, v.sums_kv
        grads = jnp.concatenate(
            (
                sums0[0:2], sums1[2:3], sums1[1:2], sums1[3:4], sums_kv[0:1], sums2[2:3],
                sums2[1:2], sums3[2:3], sums3[1:2], sums1[0:1], sums2[0:1], sums3[0:1],
            )
        )
        return jnp.concatenate(
            (
                grads.reshape(wide_rows, dp, part).transpose(1, 0, 2),
                v.hidden_bias_grad.reshape(dp, -1, part),
            ),
            axis=1,
        )

    def run_all(moves):
        finish(Mover(moves))

    def finish(mover):
        while not mover.done:
            mover.give([lax.ppermute(array, axis, hops) for array, axis, hops in mover.requests])

    if not special_mesh():
        def free(array):
            return array

        w_small, *wholes = gather_plain(*text_group)
        patch_wholes = gather_plain(*patch_group)
        values = wide(w_small[0, 0].reshape(dp, 2 * PAD_ROWS, LANES)[:, :small_rows, :part])
        vec = values[:, :wide_rows].transpose(1, 0, 2).reshape(wide_rows, width)
        vec = jnp.pad(vec, ((0, 16 - wide_rows), (0, 0)))
        hidden_bias = values[:, wide_rows:].reshape(-1, LANES)
        w_small = w_small[:, :, : 16 * PAD_ROWS]
        w_in = lax.all_gather(ffn_in, DP, axis=0, tiled=True)
        w_out = lax.all_gather(ffn_out, DP, axis=0, tiled=True)
        w_in = w_in.reshape(8, 2, width // 16, 2, in_units, LANES).transpose(0, 1, 3, 4, 2, 5)
        w_in = w_in.reshape(8, 2, 2, -1, LANES)
        w_out = w_out.reshape(8, 2, hidden // 16, 2, LANES).transpose(0, 1, 3, 2, 4)
        w_hidden = jnp.concatenate((w_in, w_out), axis=3)
        run_all(pixel_steps())
        run_text(free, (w_small, *wholes), None, (vec, hidden_bias))
        run_patch(free, patch_wholes)
        run_ffn(free, (w_hidden,))
        for work in (run_hidden_back, run_cross_back, run_patch_grad):
            work(free)
        run_all(patch_steps())
        for work in (run_first_back, run_self_back, run_text_grad):
            work(free)
        s_out, s_in, s_co, s_cq, s_so, s_kv, s_qkv = reduce_plain(
            (
                (v.active, v.df), (v.h2, v.du), (v.oc, v.dac), (v.h1, v.dqc),
                (v.attended, v.da), (v.pixels_all, v.dkv_all.reshape(2, -1, width)), (text, v.dqkv),
            )
        )
        s_small = lax.psum_scatter(low(small_grads()), DP, scatter_dimension=0, tiled=True)
        s_small = wide(lax.psum(s_small, STREAM))[0]
        s_biases = s_small[: biases.shape[0]]
        s_gains = s_small[biases.shape[0] : wide_rows]
        s_hidden_bias = s_small[wide_rows:]
    else:
        clock = Clock()
        gather_text, gather_patch, gather_hidden = (
            Mover(gather_steps(*pack_group(*group)), pieces=True)
            for group in (text_group, patch_group, hidden_group)
        )
        move_pixels = Mover(pixel_steps())
        clock.step([gather_text, move_pixels])
        clock.step([gather_text, gather_patch])
        clock.step([gather_hidden, gather_text, gather_patch])
        first_hidden = gather_hidden.given
        clock.step(
            [gather_hidden, gather_patch, move_pixels], [lambda tie: run_text(tie, *piece_sources(gather_text.result, tie))]
        )
        hidden_bases = [piece.base for piece in (*first_hidden, *gather_hidden.given)]

        def early(tie):
            for base in dict.fromkeys(hidden_bases):
                base.exchange(tie)
                clock.bases.append(base)
            return ()

        clock.step([gather_hidden], [early, lambda tie: run_patch(tie, *piece_sources(gather_patch.result, tie))])
        clock.step([gather_hidden], [lambda tie: run_ffn(tie, *piece_sources(gather_hidden.result, tie))])

        out_group, in_group, mid_group, last_group = Group(), Group(), Group(), Group()

        def begin_out(tie):
            return out_group.sibling(tie, (v.active, v.df))

        def begin_in(tie):
            return in_group.sibling(tie, (v.h2, v.du))

        def begin_mid(tie):
            return mid_group.sibling(
                tie,
                (v.oc, v.dac),
                (v.h1, v.dqc),
                (v.attended, v.da),
                (v.pixels_all, v.dkv_all.reshape(2, -1, width)),
            )

        def begin_last(tie):
            return last_group.sibling(tie, (text, v.dqkv))

        def own_last(tie):
            return last_group.own(
                tie, (v.sums0, v.sums1, v.sums2, v.sums3, v.sums_kv, v.hidden_bias_grad)
            )

        clock.step([], [begin_out])
        clock.step([out_group.core_move()], [run_hidden_back, out_group.own], eager=True)
        move_out = out_group.move()
        clock.step([], [begin_in])
        clock.step(
            [move_out, in_group.core_move()],
            [run_cross_back, run_first_back, in_group.own, begin_mid],
            eager=True,
        )
        move_in = in_group.move()
        clock.step(
            [move_out, move_in, mid_group.core_move()],
            [run_self_back, run_patch_grad, mid_group.own, begin_last],
            eager=True,
        )
        move_mid, move_patch = mid_group.move(), Mover(patch_steps())
        clock.step(
            [move_out, move_in, move_mid, last_group.core_move(), move_patch],
            [own_last, run_text_grad],
            eager=True,
        )
        move_last = last_group.move()
        movers = [move_out, move_in, move_mid, move_last, move_patch]
        results = {}

        small_shapes = [
            shape((rows, part), F32)
            for rows in (biases.shape[0], norm_gains.shape[0], small_rows - wide_rows)
        ]

        def unpack(group, mover):
            def work(tie):
                results[mover] = group.unpack(
                    (tie(mover.result[0]), mover.result[1]),
                    small_shapes if group is last_group else (),
                )
                return results[mover]
            return work

        groups = [
            (out_group, move_out), (in_group, move_in), (mid_group, move_mid), (last_group, move_last)
        ]
        def ready():
            return [
                unpack(group, mover)
                for group, mover in groups
                if mover.done and mover not in results
            ]

        for _ in range(3):
            clock.step(movers, ready, eager=True)
        for mover in movers:
            if not mover.done:
                finish(mover)
        for work in ready():
            work(clock.tie)
        (s_out,), (s_in,) = results[move_out], results[move_in]
        s_co, s_cq, s_so, s_kv = results[move_mid]
        s_qkv, s_biases, s_gains, s_hidden_bias = results[move_last]
    return (
        v.out_rows.reshape(text_input.shape),
        v.text_rows.reshape(text_input.shape),
        v.patch_rows,
        s_qkv,
        s_so,
        s_cq,
        s_kv,
        s_co,
        s_in,
        s_out,
        s_biases,
        s_gains,
        s_hidden_bias.reshape(-1),
    )


def solution(mesh):
    placed = (
        P(None, (DP, STREAM), None, None),
        P(None, (DP, STREAM), None, None),
        P(None, (DP, STREAM)),
        P(None, (DP, STREAM)),
        P(None, (DP, STREAM), None, None),
        P(None, DP, None),
        P(DP, None),
        P(DP, None),
        P(None, DP, None),
        P(DP, None),
        P(DP, None),
        P(DP, None),
        P(None, DP),
        P(None, DP),
        P(DP),
    )
    return jax.shard_map(
        on_device,
        mesh=mesh,
        in_specs=placed,
        out_specs=(
            P(None, (DP, STREAM), None, None),
            P(None, (DP, STREAM), None, None),
            P(None, (DP, STREAM), None, None),
            P(None, DP, None),
            P(DP, None),
            P(DP, None),
            P(None, DP, None),
            P(DP, None),
            P(DP, None),
            P(DP, None),
            P(None, DP),
            P(None, DP),
            P(DP),
        ),
        check_vma=False,
    )
```

```python
import functools
import types

import jax
import jax.numpy as jnp
from jax import lax
from jax.experimental import pallas as pl
from jax.experimental.pallas import tpu as pltpu
from jax.sharding import PartitionSpec as P

HEADS = 12
LANES = 384
PAD_ROWS = 16
MIB = 2**20
DP, STREAM = "dp", "stream"

EPSILON = 1e-06
ROOT_HALF = 0.7071067811865476
INV_ROOT_TAU = 0.3989422804014327

CORE = ((0, 1), (1, 0), (2, 3), (3, 2))
ACROSS = ((0, 2), (2, 0), (1, 3), (3, 1))
BESIDE = ((0, 1), (1, 0), (2, 3), (3, 2), (4, 5), (5, 4), (6, 7), (7, 6))
PAIR = ((0, 2), (2, 0), (1, 3), (3, 1), (4, 6), (6, 4), (5, 7), (7, 5))
HALFWAY = ((0, 4), (4, 0), (1, 5), (5, 1), (2, 6), (6, 2), (3, 7), (7, 3))
MIRROR = ((0, 6), (6, 0), (1, 7), (7, 1), (2, 4), (4, 2), (3, 5), (5, 3))

B_Q, B_V, B_SO, B_N1, B_CQ, B_CV, B_CO, B_N2, B_FO, B_N3, G_1, G_2, G_3 = range(13)


def low(value):
    return value.astype(jnp.bfloat16)


def wide(value):
    return value.astype(jnp.float32)


def dot(left, right):
    return jnp.dot(left, right, preferred_element_type=jnp.float32)


def dot_last(left, right):
    return lax.dot_general(
        left, right, (((1,), (1,)), ((), ())), preferred_element_type=jnp.float32
    )


def dot_first(left, right):
    return lax.dot_general(
        left, right, (((0,), (0,)), ((), ())), preferred_element_type=jnp.float32
    )


def pick(array, index, axis=0):
    return lax.dynamic_index_in_dim(array, index, axis, keepdims=False)


def place():
    dp_at, stream_at = lax.axis_index(DP), lax.axis_index(STREAM)
    return dp_at // 2, dp_at % 2, stream_at // 2, stream_at % 2


class Base:
    def __init__(self, array):
        self.array = array.reshape(-1, LANES)
        self.twin = None

    def exchange(self, tie):
        if self.twin is None:
            self.twin = lax.ppermute(tie(self.array), STREAM, CORE)
        return self.twin


class Piece:
    def __init__(self, base, row, dims):
        self.base, self.row, self.dims = base, row, dims

    def value(self):
        rows = 1
        for size in self.dims[:-1]:
            rows *= size
        return self.base.array[self.row : self.row + rows].reshape(self.dims)


class Clock:
    def __init__(self):
        self.before = []
        self.came = []
        self.bases = []

    def take(self, arrays):
        given = {}
        for array, (_, sends) in zip(arrays, self.came):
            row = 0
            base = Base(array) if sends[0][0].pieces else None
            for mover, at, sent in sends:
                part = array
                if base is not None:
                    part = Piece(base, row, sent.shape)
                    row += sent.size // LANES
                elif len(sends) > 1:
                    rows = sent.size // LANES
                    part = array[row : row + rows].reshape(sent.shape)
                    row += rows
                given.setdefault(mover, {})[at] = part
        self.came = []
        for mover, parts in given.items():
            mover.give([parts[at] for at in range(len(parts))])

    def step(self, moving=(), compute=(), eager=False, last=False):
        arrays = [array for array, _ in self.came]
        twins = [base.exchange(self.tie) for base in self.bases]
        arrays, twins, self.before = lax.optimization_barrier(
            (arrays, twins, self.before + arrays[:1])
        )
        for base, twin in zip(self.bases, twins):
            base.twin = twin
        self.bases = []
        self.take(arrays)
        ways = {}
        for mover in moving:
            if mover.done:
                continue
            for at, (array, axis, hops) in enumerate(mover.requests):
                alone = hops is CORE or array.shape[-1] != LANES
                key = (axis, hops, (mover, at) if alone else None)
                ways.setdefault(key, []).append((mover, at, array))
        joined = [
            sends[0][2]
            if len(sends) == 1
            else jnp.concatenate([array.reshape(-1, LANES) for _, _, array in sends])
            for sends in ways.values()
        ]
        joined, self.before = lax.optimization_barrier((joined, self.before))
        self.came = [
            (lax.ppermute(array, axis, hops), sends)
            for array, ((axis, hops, _), sends) in zip(joined, ways.items())
        ]
        early = []
        if last:
            early = [item for item in self.came if item[1][0][0].early]
            self.came = [item for item in self.came if not item[1][0][0].early]
            for array, sends in early:
                sends[0][0].give([array])
        after = []

        def compute_all():
            for work in compute() if callable(compute) else compute:
                after.extend(jax.tree.leaves(work(self.tie)))

        if last:
            compute_all()
        if eager:
            movers = [mover for _, sends in self.came for mover, _, _ in sends]
            arrays = [array for array, _ in self.came]
            if last:
                arrays, after = lax.optimization_barrier((arrays, after))
            self.take(arrays)
            for mover in dict.fromkeys(movers):
                if mover.done:
                    after += jax.tree.leaves(mover.result)
                else:
                    after += [array for array, _, _ in mover.requests]
        if not last:
            compute_all()
        if after:
            self.before = after

    def tie(self, array):
        return lax.optimization_barrier((array, self.before))[0]


class Mover:
    def __init__(self, steps, pieces=False, early=False):
        self.given = []
        self.steps = steps
        self.pieces = pieces
        self.early = early
        self.done = False
        self.result = None
        self.requests = next(steps)

    def give(self, came):
        self.given = came
        try:
            self.requests = self.steps.send(came)
        except StopIteration as stop:
            self.done, self.result = True, stop.value


def special_mesh():
    return lax.axis_size(DP) == 8 and lax.axis_size(STREAM) == 4


VMEM = pl.BlockSpec(memory_space=pltpu.VMEM)
SMEM = pl.BlockSpec(memory_space=pltpu.SMEM)
ANY = pl.BlockSpec(memory_space=pl.ANY)


def call(kernel, out_shape, in_specs, scratch=(), mib=20, flops=0, out_specs=None, **more):
    return pl.pallas_call(
        kernel,
        out_shape=out_shape,
        in_specs=in_specs,
        out_specs=jax.tree.map(lambda _: VMEM, out_shape) if out_specs is None else out_specs,
        scratch_shapes=list(scratch),
        compiler_params=pltpu.CompilerParams(vmem_limit_bytes=mib * MIB),
        cost_estimate=pl.CostEstimate(flops=flops, bytes_accessed=4 * MIB, transcendentals=0),
        **more,
    )


def shape(dims, dtype=jnp.bfloat16):
    return jax.ShapeDtypeStruct(tuple(dims), dtype)


F32 = jnp.float32


def pack_shard(shard, units):
    if shard.ndim == 2:
        rows, _ = shard.shape
        split = shard.reshape(2, rows // 2, 2, units, LANES).transpose(2, 0, 3, 1, 4)
    else:
        _, rows, _ = shard.shape
        split = shard.reshape(units, 2, rows // 2, 2, LANES).transpose(3, 1, 0, 2, 4)
    return split.reshape(2, 2, units * rows // 2, LANES)


def pack_kernel(units, *refs):
    _, _, x_at, core_at = place()
    shards, (both, own, own_x) = refs[: len(units)], refs[len(units) :]
    row = 0
    for shard, (count, depth) in zip(shards, units):
        if len(shard.shape) == 4:
            both[:, :, row : row + depth] = shard[...]
            row += depth
            continue
        for unit in range(count):
            rows = slice(row, row + depth)
            for x in range(2):
                for c in range(2):
                    if len(shard.shape) == 3:
                        block = shard[unit, x * depth : (x + 1) * depth, c * LANES : (c + 1) * LANES]
                    else:
                        start = (c * count + unit) * LANES
                        block = shard[x * depth : (x + 1) * depth, start : start + LANES]
                    both[c, x, rows] = block
            row += depth
    own[...] = both[core_at]
    own_x[...] = both[core_at, x_at]


def pack_own_kernel(units, *refs):
    _, _, x_at, core_at = place()
    shards, out = refs[:-1], refs[-1]
    row = 0
    for shard, (count, depth) in zip(shards, units):
        for unit in range(count):
            start = (core_at * count + unit) * LANES
            out[row : row + depth] = shard[
                pl.ds(pl.multiple_of(x_at * depth, 16), depth),
                pl.ds(pl.multiple_of(start, 128), LANES),
            ]
            row += depth


def pack_group(shards, units):
    rows = sum(count * depth for count, depth in units)
    return call(
        functools.partial(pack_kernel, units),
        [shape((2, 2, rows, LANES)), shape((2, rows, LANES)), shape((rows, LANES))],
        [VMEM] * len(shards),
    )(*shards)


def pack_own(shards, units):
    rows = sum(count * depth for count, depth in units)
    return call(
        functools.partial(pack_own_kernel, units), shape((rows, LANES)), [VMEM] * len(shards)
    )(*shards)


def gather_steps(own_both, own, own_x):
    x_at = lax.axis_index(STREAM) // 2
    mate, half_z, mirror_z, beside = yield [
        (own, DP, PAIR),
        (own_x, DP, HALFWAY),
        (own_x, DP, MIRROR),
        (own, DP, BESIDE),
    ]
    mate_halves = mate.value()
    others = jnp.stack((pick(mate_halves, x_at), half_z.value(), mirror_z.value()))
    beside_others, half_x, mirror_x = yield [
        (others, DP, BESIDE),
        (half_z.value(), STREAM, ACROSS),
        (mirror_z.value(), STREAM, ACROSS),
    ]
    others_x, mate_x = yield [
        (beside_others.value()[1:], STREAM, ACROSS),
        (pick(mate_halves, 1 - x_at), DP, BESIDE),
    ]
    whole = Piece(Base(own_both), 0, own_both.shape)
    return (
        whole, mate, beside, half_z, mirror_z, half_x, mirror_x, beside_others, others_x, mate_x
    )


def piece_sources(pieces, tie):
    own, *received = pieces
    rows = own.dims[2]
    arrays, spec = [own.base.array], [(0, at * rows) for at in range(4)]
    known = {}

    def find(piece, theirs):
        key = (piece.base, theirs)
        if key not in known:
            known[key] = len(arrays)
            arrays.append(piece.base.exchange(tie) if theirs else piece.base.array)
        return known[key]

    for theirs in (False, True):
        mate, beside, half_z, mirror_z, half_x, mirror_x, others, others_x, mate_x = received
        blocks = [(mate, 0), (beside, 0), (mate, 1), (beside, 1)]
        blocks += [(half_z, 0), (mirror_z, 0), (half_x, 0), (mirror_x, 0)]
        blocks += [(others, 0), (others, 1), (others, 2), (mate_x, 0), (others_x, 0), (others_x, 1)]
        spec += [(find(piece, theirs), piece.row + block * rows) for piece, block in blocks]
    return arrays, tuple(spec)


def piece_places(spec, sources):
    z_at, y_at, x_at, core_at = place()
    _, z_mate, z_half, z_mirror = shard_slots(z_at)
    far_y, far_x = 1 - y_at, 1 - x_at
    places = [(z_at, y_at, x_from, core_from) for core_from in range(2) for x_from in range(2)]
    for core_from in (core_at, 1 - core_at):
        for x_from in range(2):
            places.append((z_mate, y_at, x_from, core_from))
            places.append((z_at, far_y, x_from, core_from))
        places += [
            (z_half, y_at, x_at, core_from),
            (z_mirror, y_at, x_at, core_from),
            (z_half, y_at, far_x, core_from),
            (z_mirror, y_at, far_x, core_from),
            (z_mate, far_y, x_at, core_from),
            (z_half, far_y, x_at, core_from),
            (z_mirror, far_y, x_at, core_from),
            (z_mate, far_y, far_x, core_from),
            (z_half, far_y, far_x, core_from),
            (z_mirror, far_y, far_x, core_from),
        ]
    return [(sources[at], row, *where) for (at, row), where in zip(spec, places)]


def piece_copies(units, spec, sources, wholes, sems):
    parts = piece_places(spec, sources)
    copies, row, sem = [], 0, 0
    for (count, depth), whole in zip(units, wholes):
        of_weight = []
        for source, first, z_from, y_from, x_from, core_from in parts:
            start = (z_from * 2 + y_from) * (2 * depth) + x_from * depth
            of_weight.append(
                pltpu.make_async_copy(
                    source.at[pl.ds(first + row, count * depth)].reshape(count, depth, LANES),
                    whole.at[core_from, :, pl.ds(pl.multiple_of(start, 16), depth)],
                    sems.at[sem],
                )
            )
            sem += 1
        copies.append(of_weight)
        row += count * depth
    return copies


def gather_plain(shards, units):
    packed = [
        shard if shard.ndim == 4 else pack_shard(shard, count)
        for shard, (count, _) in zip(shards, units)
    ]
    whole = lax.all_gather(jnp.concatenate(packed, axis=2), DP, axis=0, tiled=False)
    results = []
    row = 0
    for count, depth in units:
        part = whole[:, :, :, row : row + count * depth]
        part = part.reshape(-1, 2, 2, count, depth, LANES).transpose(1, 3, 0, 2, 4, 5)
        results.append(part.reshape(2, count, -1, LANES))
        row += count * depth
    return results


def shard_slots(z_at):
    return z_at, z_at + 1 - 2 * (z_at % 2), (z_at + 2) % 4, 3 - z_at


def grad_columns(right, core, units):
    blocks = []
    for lead in [None] if len(right.shape) == 2 else range(right.shape[0]):
        of_lead = right if lead is None else right.at[lead]
        start = pl.multiple_of(core * (units * LANES), 128)
        blocks.append(of_lead[:, pl.ds(start, units * LANES)])
    return blocks[0] if len(blocks) == 1 else jnp.concatenate(blocks, axis=1)


def sibling_grad_kernel(jobs, *refs):
    operands, out = refs[:-1], refs[-1]
    core_at = lax.axis_index(STREAM) % 2
    row = 0
    for at, (units, blocks, depth) in enumerate(jobs):
        left, right = operands[2 * at], operands[2 * at + 1]
        product = low(dot_first(left[...], grad_columns(right, 1 - core_at, units)))
        for block in range(blocks):
            columns = product[:, block * LANES : (block + 1) * LANES]
            out[:, :, row : row + depth] = columns.reshape(8, 2, depth, LANES)
            row += depth


TO_X = ((2, False, False), (3, False, False), (2, True, False), (3, True, False))
TO_Y_A = ((0, False, True), (1, False, True))
TO_Z_A = ((1, False, False), (1, True, False))
TO_Y_B = ((2, False, True), (3, False, True), (0, False, False))
TO_Z_B = ((1, True, True),)
TO_Z_C = ((2, True, True), (3, True, True))
OWN = ((0, True, True), (0, True, False))
PARTS = (TO_X, TO_Y_A, TO_Z_A, TO_Y_B, TO_Z_B, TO_Z_C, OWN)


def part_at(part):
    z_at, y_at, x_at, _ = place()
    slot, own_y, own_x = part
    return (
        shard_slots(z_at)[slot] * 2 + (y_at if own_y else 1 - y_at),
        x_at if own_x else 1 - x_at,
    )


def small_grad_rows(sums, hidden_bias, work):
    sums0, sums1, sums2, sums3, sums_kv = sums
    rows = (
        (sums0, 0), (sums0, 1), (sums1, 2), (sums1, 1), (sums1, 3), (sums_kv, 0), (sums2, 2),
        (sums2, 1), (sums3, 2), (sums3, 1), (sums1, 0), (sums2, 0), (sums3, 0),
    )
    part = sums0.shape[1] // 8
    work[...] = jnp.zeros_like(work)
    for dp_to in range(8):
        columns = slice(dp_to * part, (dp_to + 1) * part)
        for row, (array, at) in enumerate(rows):
            work[dp_to, row : row + 1, :part] = array[at : at + 1, columns]
        for j in range(hidden_bias.shape[1] // part):
            at = len(rows) + j
            work[dp_to, at : at + 1, :part] = hidden_bias[
                dp_to : dp_to + 1, j * part : (j + 1) * part
            ]


def own_grad_kernel(jobs, sent, small, *refs):
    inputs = 2 * len(jobs) + len(sent)
    operands, came = refs[: 2 * len(jobs)], refs[2 * len(jobs) : inputs]
    extra = refs[inputs : inputs + 6 * small]
    outs = refs[inputs + 6 * small : inputs + 6 * small + len(PARTS)]
    work, *small_work = refs[inputs + 6 * small + len(PARTS) :]
    core_at = lax.axis_index(STREAM) % 2
    row = 0
    for at, (units, blocks, depth) in enumerate(jobs):
        left, right = operands[2 * at], operands[2 * at + 1]
        product = dot_first(left[...], grad_columns(right, core_at, units))
        array, came_row = sent[at]
        for block in range(blocks):
            columns = product[:, block * LANES : (block + 1) * LANES]
            rows = slice(row, row + depth)
            work[:, :, :depth] = columns.reshape(8, 2, depth, LANES) + wide(
                came[array][:, :, came_row : came_row + depth]
            )
            for out, parts in zip(outs, PARTS):
                for j, part in enumerate(parts):
                    dp_from, x_from = part_at(part)
                    out[j, rows] = low(work[dp_from, x_from, :depth])
            row += depth
            came_row += depth
    if small:
        small_grad_rows(extra[:5], extra[5], small_work[0])
        for out, parts in zip(outs, PARTS):
            for j, part in enumerate(parts):
                dp_from, x_from = part_at(part)
                rows = pl.ds(pl.multiple_of(x_from * PAD_ROWS, PAD_ROWS), PAD_ROWS)
                out[j, row : row + PAD_ROWS] = low(small_work[0][dp_from, rows])


def reduce_steps(to_x, to_y_a, to_z_a, to_y_b, to_z_b, to_z_c, own):
    from_y_a, from_x, from_z_a = yield [
        (to_y_a, DP, BESIDE),
        (to_x, STREAM, ACROSS),
        (to_z_a, DP, PAIR),
    ]
    arrived = jnp.concatenate((from_x[:2], from_z_a[:1]))
    from_y_b, mate = yield [
        (low(wide(to_y_b) + wide(arrived)), DP, BESIDE),
        (low(wide(to_z_b) + wide(from_y_a[1:])), DP, PAIR),
    ]
    far = wide(to_z_c) + wide(from_x[2:]) + wide(from_y_b[:2])
    (by_mate,) = yield [(low(far[1]), DP, PAIR)]
    (half,) = yield [(low(far[0] + wide(by_mate)), DP, HALFWAY)]
    total = low(
        jnp.stack(
            (
                wide(own[0]) + wide(from_y_a[0]) + wide(mate[0]) + wide(half),
                wide(own[1]) + wide(from_y_b[2]) + wide(from_z_a[1]),
            )
        )
    )
    (from_x,) = yield [(total, STREAM, ACROSS)]
    total = low(wide(total) + wide(from_x[::-1]))
    return total, lax.ppermute(total, STREAM, CORE)


def unpack_kernel(jobs, small, mine, other, *outs):
    _, _, x_at, core_at = place()
    for source, core_from in ((mine, core_at), (other, 1 - core_at)):
        for j in range(2):
            x_from = x_at if j == 0 else 1 - x_at
            for out_at, lead, units, row, depth in jobs:
                out = outs[out_at] if lead is None else outs[out_at].at[lead]
                for unit in range(units):
                    at = row + unit * depth
                    start = core_from * (units * LANES) + unit * LANES
                    out[
                        pl.ds(pl.multiple_of(x_from * depth, 8), depth),
                        pl.ds(pl.multiple_of(start, 128), LANES),
                    ] = wide(source[j, at : at + depth])
    if small is not None:
        biases, gains, hidden_bias, work = outs[-4:]
        for j in range(2):
            x_from = x_at if j == 0 else 1 - x_at
            rows = slice(small, small + PAD_ROWS)
            work[pl.ds(pl.multiple_of(x_from * PAD_ROWS, 8), PAD_ROWS)] = wide(
                mine[j, rows]
            ) + wide(other[j, rows])
        part = biases.shape[1]
        biases[...] = work[:G_1, :part]
        gains[...] = work[G_1 : G_3 + 1, :part]
        hidden_bias[...] = work[G_3 + 1 : G_3 + 1 + hidden_bias.shape[0], :part]


def reduce_plain(parts):
    shards = []
    for left, right in parts:
        if right.ndim == 2:
            whole = low(dot_first(left, right))
            own = lax.psum_scatter(whole, DP, scatter_dimension=0, tiled=True)
        else:
            whole = low(jnp.stack([dot_first(left, r) for r in right]))
            own = lax.psum_scatter(whole, DP, scatter_dimension=1, tiled=True)
        shards.append(wide(lax.psum(own, STREAM)))
    return shards


class Group:
    def __init__(self):
        self.operands, self.jobs, self.out_jobs, self.out_shapes = [], [], [], []
        self.rows, self.flops, self.sent, self.came, self.from_sent = 0, 0, [], [], []

    def sibling(self, tie, *parts):
        jobs, operands, rows, flops = [], [], 0, 0
        for left, right in parts:
            operands += [left, right]
            depth = left.shape[1] // 16
            units = right.shape[-1] // (2 * LANES)
            leads = [None] if right.ndim == 2 else range(right.shape[0])
            jobs.append((units, units * len(leads), depth))
            self.from_sent.append((len(self.sent), rows))
            for lead in leads:
                self.out_jobs.append(
                    (len(self.out_shapes), lead, units, self.rows + rows, depth)
                )
                rows += units * depth
            self.out_shapes.append(
                shape((*right.shape[:-2], 2 * depth, right.shape[-1]), F32)
            )
            flops += left.shape[0] * left.shape[1] * right.size // right.shape[-2]
        self.sent.append(
            call(
                functools.partial(sibling_grad_kernel, jobs),
                shape((8, 2, rows, LANES)),
                [VMEM] * len(operands),
                flops=flops,
            )(tie(operands[0]), *operands[1:])
        )
        self.jobs += jobs
        self.operands += operands
        self.rows += rows
        self.flops += flops
        return self.sent[-1]

    def core_move(self):
        def steps(sent):
            (came,) = yield [(sent, STREAM, CORE)]
            self.came.append(came)

        return Mover(steps(self.sent[-1]), early=True)

    def own(self, tie, small=()):
        deepest = max(job[-1] for job in self.jobs)
        scratch = [pltpu.VMEM((8, 2, deepest, LANES), F32)]
        if small:
            scratch.append(pltpu.VMEM((8, 2 * PAD_ROWS, LANES), F32))
        rows = self.rows + PAD_ROWS * bool(small)
        came = [self.came[array] for array, _ in self.from_sent]
        self.parts = call(
            functools.partial(
                own_grad_kernel,
                self.jobs,
                [(at, row) for at, (_, row) in enumerate(self.from_sent)],
                bool(small),
            ),
            [shape((len(parts), rows, LANES)) for parts in PARTS],
            [VMEM] * (len(self.operands) + len(came) + len(small)),
            scratch,
            flops=self.flops,
        )(tie(self.operands[0]), *self.operands[1:], *came, *small)
        return self.parts

    def move(self):
        return Mover(reduce_steps(*self.parts))

    def unpack(self, moved, small=()):
        return call(
            functools.partial(unpack_kernel, self.out_jobs, self.rows if small else None),
            [*self.out_shapes, *small],
            [VMEM, VMEM],
            [pltpu.VMEM((2 * PAD_ROWS, LANES), F32)] * bool(small),
        )(*moved)


def norm_parts(summed):
    center = summed - jnp.mean(summed, axis=-1, keepdims=True)
    inverse = lax.rsqrt(jnp.mean(center * center, axis=-1, keepdims=True) + EPSILON)
    return center * inverse, inverse


def norm_back(upstream, normed, inverse, gain):
    scaled = upstream * gain
    return inverse * (
        scaled
        - jnp.mean(scaled, axis=-1, keepdims=True)
        - normed * jnp.mean(scaled * normed, axis=-1, keepdims=True)
    )


def heads_apart(four):
    head = lax.broadcasted_iota(jnp.int32, four.shape, 1) // 64
    return low(jnp.concatenate([jnp.where(head == j, four, 0.0) for j in range(4)], axis=0))


def heads_joined(stacked):
    rows = stacked.shape[0] // 4
    head = lax.broadcasted_iota(jnp.int32, (rows, stacked.shape[1]), 1) // 64
    made = stacked[:rows]
    for j in range(1, 4):
        made = jnp.where(head == j, stacked[j * rows : (j + 1) * rows], made)
    return made


def quads():
    return [slice(j * 256, (j + 1) * 256) for j in range(HEADS // 4)]


def softmax(scores):
    raised = jnp.exp(scores - jnp.max(scores, axis=-1, keepdims=True))
    return raised * (1.0 / jnp.sum(raised, axis=-1, keepdims=True))


def score_back(weight, back):
    return low(weight * (back - jnp.sum(back * weight, axis=-1, keepdims=True)))


def row_sum(value):
    return jnp.sum(value, axis=0, keepdims=True)


def self_kernel(seq, lengths, x_ref, w_ref, vec, qkv_ref, out_ref, q, k, v, o):
    tokens = x_ref.shape[0]
    for j, (scratch, bias) in enumerate(((q, B_Q), (k, None), (v, B_V))):
        for c in range(2):
            columns = slice(c * LANES, (c + 1) * LANES)
            made = dot(x_ref[...], w_ref[c, j])
            if bias is not None:
                made = made + vec[bias : bias + 1, columns]
            made = low(made)
            qkv_ref[j, :, columns] = made
            scratch[:, columns] = wide(made)

    def step(r, _):
        rows = pl.ds(pl.multiple_of(r * seq, 8), seq)
        valid = lax.broadcasted_iota(jnp.int32, (4 * seq, seq), 1) < lengths[r]
        asked = [heads_apart(q[rows, c] * 0.125) for c in quads()]
        scores = [dot_last(a, low(k[rows, c])) for a, c in zip(asked, quads())]
        weights = [softmax(jnp.where(valid, score, -jnp.inf)) for score in scores]
        made = [dot(low(w), low(v[rows, c])) for w, c in zip(weights, quads())]
        for part, c in zip(made, quads()):
            o[rows, c] = heads_joined(part)
        return 0

    lax.fori_loop(0, tokens // seq, step, 0, unroll=2)
    out_ref[...] = low(o[...])


def first_norm_kernel(seq, o_ref, x_ref, wso, wcq, vec, normed, inverse, h_low, qc, z):
    for c in range(2):
        columns = slice(c * LANES, (c + 1) * LANES)
        z[:, columns] = (
            dot(o_ref[...], wso[c, 0])
            + vec[B_SO : B_SO + 1, columns]
            + wide(x_ref[:, columns])
        )
    made, scale = norm_parts(z[...])
    normed[...] = made
    inverse[...] = scale
    h_low[...] = low(made * vec[G_1 : G_1 + 1] + vec[B_N1 : B_N1 + 1])
    for c in range(2):
        columns = slice(c * LANES, (c + 1) * LANES)
        qc[:, columns] = low(dot(h_low[...], wcq[c, 0]) + vec[B_CQ : B_CQ + 1, columns])


def pixel_kernel(patch_ref, out_ref):
    images, patches, _ = patch_ref.shape
    out_ref[:, :patches] = patch_ref[...]
    out_ref[:, patches:] = jnp.zeros_like(out_ref[:, patches:])


def image_kernel(pixels, w_ref, vec, kv_ref):
    slots, _, images, padded, width = kv_ref.shape
    rows = images * padded
    flat = pixels[...].reshape(slots * rows, -1)
    for j in range(2):
        made = dot(flat, jnp.concatenate((w_ref[0, j], w_ref[1, j]), axis=1))
        if j == 1:
            made = made + vec[B_CV : B_CV + 1]
        for slot in range(slots):
            part = made[slot * rows : (slot + 1) * rows]
            kv_ref[slot, j] = low(part).reshape(images, padded, width)


def cross_kernel(
    seq, patches, micro_rows, slots, qc, kv, n1, wco, vec, oc, n2, inverse, h_low, q, o
):
    q[...] = wide(qc[...]) * 0.125
    tokens = qc.shape[0]
    padded = kv.shape[3]
    there = lax.broadcasted_iota(jnp.int32, (4 * seq, padded), 1) < patches

    def step(r, _):
        rows = pl.ds(pl.multiple_of(r * seq, 8), seq)
        slot, m = slots[r], r // micro_rows
        asked = [heads_apart(q[rows, c]) for c in quads()]
        scores = [dot_last(a, kv[slot, 0, m, :, c]) for a, c in zip(asked, quads())]
        weights = [softmax(jnp.where(there, score, -jnp.inf)) for score in scores]
        made = [dot(low(w), kv[slot, 1, m, :, c]) for w, c in zip(weights, quads())]
        for part, c in zip(made, quads()):
            o[rows, c] = heads_joined(part)
        return 0

    lax.fori_loop(0, tokens // seq, step, 0, unroll=2)
    oc[...] = low(o[...])
    for c in range(2):
        columns = slice(c * LANES, (c + 1) * LANES)
        first = n1[:, columns] * vec[G_1 : G_1 + 1, columns] + vec[B_N1 : B_N1 + 1, columns]
        o[:, columns] = first + dot(oc[...], wco[c, 0]) + vec[B_CO : B_CO + 1, columns]
    made, scale = norm_parts(o[...])
    n2[...] = made
    inverse[...] = scale
    h_low[...] = low(made * vec[G_2 : G_2 + 1] + vec[B_N2 : B_N2 + 1])


def small_rows_kernel(shards, vec, hidden_bias, part):
    wide_rows = G_3 + 1
    vec[...] = jnp.zeros_like(vec)
    for dp_from in range(8):
        rows = wide(shards[dp_from * 2 * PAD_ROWS : (dp_from + 1) * 2 * PAD_ROWS])
        vec[:wide_rows, dp_from * part : (dp_from + 1) * part] = rows[:wide_rows, :part]
        for j in range(LANES // part):
            hidden_bias[dp_from : dp_from + 1, j * part : (j + 1) * part] = rows[
                wide_rows + j : wide_rows + j + 1, :part
            ]


def take_weights(units, spec, sources, wholes, outs, in_sems, out_sems, kept):
    if spec is None:
        copies = [
            [pltpu.make_async_copy(source, whole, in_sems.at[at])]
            for at, (source, whole) in enumerate(zip(sources, wholes))
        ]
    else:
        copies = piece_copies(units, spec, sources, wholes, in_sems)
    for of_weight in copies:
        for copy in of_weight:
            copy.start()

    def take(at):
        for copy in copies[at]:
            copy.wait()
        if outs[at] is not None:
            send(wholes[at], outs[at])

    def send(source, target):
        kept.append(pltpu.make_async_copy(source, target, out_sems.at[len(kept)]))
        kept[-1].start()

    return take, send


def text_kernel(units, gathered, spec, seq, lengths, text, *refs):
    sources, refs = refs[:gathered], refs[gathered:]
    if spec is None:
        small, refs = refs[:2], refs[2:]
    outs, refs = refs[:11], refs[11:]
    vec, hidden_bias, attended, n1, inverse1, h1, qc, qkv_out, *w_outs = outs
    wholes, (qkv, q, k, v, o, in_sems, out_sems) = refs[:4], refs[4:]
    w_small, w_qkv, w_so, w_cq = wholes
    kept = []
    take, send = take_weights(
        units, spec, sources, wholes, (None, *w_outs), in_sems, out_sems, kept
    )
    take(0)
    if spec is None:
        vec[...], hidden_bias[...] = small[0][...], small[1][...]
    else:
        small_rows_kernel(w_small.at[0, 0], vec, hidden_bias, text.shape[1] // 8)
    take(1)
    self_kernel(seq, lengths, text, w_qkv, vec, qkv, attended, q, k, v, o)
    send(qkv, qkv_out)
    take(2)
    take(3)
    first_norm_kernel(seq, attended, text, w_so, w_cq, vec, n1, inverse1, h1, qc, o)
    for copy in kept:
        copy.wait()


def patch_kernel(units, gathered, spec, seq, patches, micro_rows, slots, qc, n1, vec, *refs):
    sources, held, refs = refs[:gathered], refs[gathered : gathered + 4], refs[gathered + 4 :]
    (oc, n2, inverse2, h2, kv_out, pixels_out, *w_outs), refs = refs[:8], refs[8:]
    wholes, (kv, pixels, q, o, in_sems, pixel_sems, out_sems) = refs[:2], refs[2:]
    w_kv, w_co = wholes
    pixel_copies = [
        pltpu.make_async_copy(image, pixels.at[at], pixel_sems.at[at])
        for at, image in enumerate(held)
    ]
    for copy in pixel_copies:
        copy.start()
    kept = []
    take, send = take_weights(units, spec, sources, wholes, w_outs, in_sems, out_sems, kept)
    for copy in pixel_copies:
        copy.wait()
    send(pixels, pixels_out)
    take(0)
    image_kernel(pixels, w_kv, vec, kv)
    send(kv, kv_out)
    take(1)
    cross_kernel(
        seq, patches, micro_rows, slots, qc, kv, n1, w_co, vec, oc, n2, inverse2, h2, q, o
    )
    for copy in kept:
        copy.wait()


def hidden_weights(w, block, in_units):
    core, unit = divmod(block, in_units)
    depth = w.shape[3] // 2 // in_units
    return w[:, :, core, unit * depth : (unit + 1) * depth].reshape(-1, LANES)


def ffn_kernel(
    gathered, spec, in_units, seq, lengths, h2, bias, n2, cot, vec, *refs
):
    sources, refs = refs[:gathered], refs[gathered:]
    out, dz, df, rows_out, active, slope, w_out, w, total, in_sems, out_sem = refs
    if spec is None:
        copies = [pltpu.make_async_copy(sources[0], w, in_sems.at[0])]
    else:
        copies = [
            pltpu.make_async_copy(
                source.at[pl.ds(first, w.shape[3])],
                w.at[z_from * 2 + y_from, x_from, core_from],
                in_sems.at[at],
            )
            for at, (source, first, z_from, y_from, x_from, core_from) in enumerate(
                piece_places(spec, sources)
            )
        ]
    for copy in copies:
        copy.start()
    for copy in copies:
        copy.wait()
    keep = pltpu.make_async_copy(w, w_out, out_sem.at[0])
    keep.start()
    for block in range(0, 2 * in_units, 2):
        columns = slice(block * LANES, (block + 2) * LANES)
        two = (block, block + 1)
        weights = jnp.concatenate([hidden_weights(w, b, in_units) for b in two], axis=1)
        shift = jnp.concatenate([bias[b : b + 1] for b in two], axis=1)
        pre = dot(h2[...], weights) + shift
        cumulative = 0.5 * (1.0 + lax.erf(pre * ROOT_HALF))
        active[:, columns] = low(pre * cumulative)
        slope[:, columns] = low(cumulative + pre * INV_ROOT_TAU * jnp.exp(-0.5 * pre * pre))
    half_rows = w.shape[3] // 2
    made = None
    for part in range(4):
        weights = jnp.concatenate(
            [w[2 * part : 2 * part + 2, :, c, half_rows:].reshape(-1, LANES) for c in range(2)],
            axis=1,
        )
        depth = weights.shape[0]
        term = dot(active[:, part * depth : (part + 1) * depth], weights)
        made = term if made is None else made + term
    total[...] = made

    def step(r, sums):
        rows = pl.ds(pl.multiple_of(r * seq, 8), seq)
        second = n2[rows, :] * vec[G_2 : G_2 + 1] + vec[B_N2 : B_N2 + 1]
        made, scale = norm_parts(second + total[rows, :] + vec[B_FO : B_FO + 1])
        out[r] = low(made * vec[G_3 : G_3 + 1] + vec[B_N3 : B_N3 + 1])
        valid = lax.broadcasted_iota(jnp.int32, made.shape, 0) < lengths[r]
        upstream = jnp.where(valid, wide(cot[r]), 0.0)
        back = norm_back(upstream, made, scale, vec[G_3 : G_3 + 1])
        dz[rows, :] = back
        gain, shift, lowered = sums
        return (
            gain + row_sum(upstream * made),
            shift + row_sum(upstream),
            lowered + row_sum(wide(low(back))),
        )

    zero = jnp.zeros((1, total.shape[1]), F32)
    sums = lax.fori_loop(0, out.shape[0], step, (zero, zero, zero), unroll=2)
    df[...] = low(dz[...])
    for j in range(3):
        rows_out[j : j + 1] = sums[j]
    rows_out[3:8] = jnp.zeros((5, total.shape[1]), F32)
    keep.wait()


def norm_back_rows(total, dz_ref, normed, inverse, gain, dz, low_ref, rows_out, step_rows):
    def step(r, sums):
        rows = pl.ds(pl.multiple_of(r * step_rows, 8), step_rows)
        upstream = total[rows, :] + dz_ref[rows, :]
        made = normed[rows, :]
        back = norm_back(upstream, made, inverse[rows, :], gain)
        dz[rows, :] = back
        return (
            sums[0] + row_sum(upstream * made),
            sums[1] + row_sum(upstream),
            sums[2] + row_sum(wide(low(back))),
        )

    zero = jnp.zeros((1, total.shape[1]), F32)
    sums = lax.fori_loop(0, total.shape[0] // step_rows, step, (zero, zero, zero))
    low_ref[...] = low(dz[...])
    for j in range(3):
        rows_out[j : j + 1] = sums[j]
    rows_out[3:8] = jnp.zeros((5, total.shape[1]), F32)


def hidden_back_kernel(
    seq, df, wout, win, slope, dz3, n2, inverse, vec, du, bias_out, dz2, dac, rows_out, total
):
    i = pl.program_id(0)

    @pl.when(i == 0)
    def _():
        total[...] = jnp.zeros_like(total)

    raw = dot_last(df[:, :LANES], wout[0, :, 0].reshape(-1, LANES))
    raw = raw + dot_last(df[:, LANES:], wout[0, :, 1].reshape(-1, LANES))
    made = low(raw * wide(slope[...]))
    du[...] = made
    bias_out[pl.ds(i, 1), :] = row_sum(wide(made))
    total[...] += dot_last(made, win[:, :, 0].reshape(-1, LANES))

    @pl.when(i == pl.num_programs(0) - 1)
    def _():
        norm_back_rows(
            total, dz3, n2, inverse, vec[G_2 : G_2 + 1], dz2, dac, rows_out, seq
        )


def cross_back_kernel(
    seq, patches, micro_rows, slots, dac, qc, kv, wco, dqc, dkv_out, dkv, q, do, dq
):
    q[...] = wide(qc[...]) * 0.125
    do[...] = wide(
        low(dot_last(dac[:, :LANES], wco[0, 0]) + dot_last(dac[:, LANES:], wco[1, 0]))
    )
    dkv[...] = jnp.zeros_like(dkv)
    tokens = qc.shape[0]
    padded = kv.shape[3]
    there = lax.broadcasted_iota(jnp.int32, (4 * seq, padded), 1) < patches

    def step(r, _):
        rows = pl.ds(pl.multiple_of(r * seq, 8), seq)
        slot, m = slots[r], r // micro_rows
        asked = [heads_apart(q[rows, c]) for c in quads()]
        came = [heads_apart(do[rows, c]) for c in quads()]
        keys = [kv[slot, 0, m, :, c] for c in quads()]
        values = [kv[slot, 1, m, :, c] for c in quads()]
        scores = [dot_last(a, key) for a, key in zip(asked, keys)]
        backs = [dot_last(d, value) for d, value in zip(came, values)]
        weights = [softmax(jnp.where(there, score, -jnp.inf)) for score in scores]
        backs = [score_back(w, b) for w, b in zip(weights, backs)]
        queries = [heads_joined(dot(b, key)) for b, key in zip(backs, keys)]
        key_parts = [dot_first(b, a) for b, a in zip(backs, asked)]
        value_parts = [dot_first(low(w), d) for w, d in zip(weights, came)]
        for j, c in enumerate(quads()):
            dq[rows, c] = queries[j] * 0.125
            dkv[0, slot, m, :, c] += key_parts[j]
            dkv[1, slot, m, :, c] += value_parts[j]
        return 0

    lax.fori_loop(0, tokens // seq, step, 0, unroll=2)
    dqc[...] = low(dq[...])
    dkv_out[...] = low(dkv[...])


def first_back_kernel(seq, dqc, wcq, dz2, n1, inverse, vec, dz1, da, rows_out, total):
    total[...] = dot_last(dqc[:, :LANES], wcq[0, 0]) + dot_last(dqc[:, LANES:], wcq[1, 0])
    norm_back_rows(total, dz2, n1, inverse, vec[G_1 : G_1 + 1], dz1, da, rows_out, seq)
    rows_out[3:4] = row_sum(wide(dqc[...]))


def self_back_kernel(seq, lengths, da, qkv, wso, dqkv, rows_out, q, k, v, do, dq, dk, dv):
    q[...] = wide(qkv[0]) * 0.125
    k[...] = wide(qkv[1])
    v[...] = wide(qkv[2])
    do[...] = wide(low(dot_last(da[:, :LANES], wso[0, 0]) + dot_last(da[:, LANES:], wso[1, 0])))
    tokens = da.shape[0]

    def step(r, _):
        rows = pl.ds(pl.multiple_of(r * seq, 8), seq)
        valid = lax.broadcasted_iota(jnp.int32, (4 * seq, seq), 1) < lengths[r]
        asked = [heads_apart(q[rows, c]) for c in quads()]
        came = [heads_apart(do[rows, c]) for c in quads()]
        keys = [low(k[rows, c]) for c in quads()]
        values = [low(v[rows, c]) for c in quads()]
        scores = [dot_last(a, key) for a, key in zip(asked, keys)]
        backs = [dot_last(d, value) for d, value in zip(came, values)]
        weights = [softmax(jnp.where(valid, score, -jnp.inf)) for score in scores]
        backs = [score_back(w, b) for w, b in zip(weights, backs)]
        queries = [heads_joined(dot(b, key)) for b, key in zip(backs, keys)]
        key_parts = [dot_first(b, a) for b, a in zip(backs, asked)]
        value_parts = [dot_first(low(w), d) for w, d in zip(weights, came)]
        for j, c in enumerate(quads()):
            dq[rows, c] = queries[j] * 0.125
            dk[rows, c] = key_parts[j]
            dv[rows, c] = value_parts[j]
        return 0

    lax.fori_loop(0, tokens // seq, step, 0, unroll=2)
    for j, made in enumerate((dq, dk, dv)):
        dqkv[j] = low(made[...])
    rows_out[0:1] = row_sum(wide(dqkv[0]))
    rows_out[1:2] = row_sum(wide(dqkv[2]))
    rows_out[2:8] = jnp.zeros((6, q.shape[1]), F32)


def text_grad_kernel(dz1, dqkv, w_ref, out, total):
    total[...] = dz1[...]
    for j in range(3):
        for c in range(2):
            total[...] += dot_last(dqkv[j, :, c * LANES : (c + 1) * LANES], w_ref[c, j])
    seq = out.shape[1]
    for r in range(out.shape[0]):
        out[r] = low(total[r * seq : (r + 1) * seq, :])


def patch_grad_kernel(dkv, w_ref, kept, sent, rows_out):
    _, slots, images, padded, width = dkv.shape
    rows = images * padded
    total = jnp.zeros((1, width), F32)
    for slot in range(slots):
        made = None
        for j in range(2):
            grad = dkv[j, slot].reshape(rows, width)
            for c in range(2):
                term = dot_last(grad[:, c * LANES : (c + 1) * LANES], w_ref[c, j])
                made = term if made is None else made + term
        out = sent if slot % 2 else kept
        out[slot // 2] = low(made).reshape(images, padded, w_ref.shape[2])
        total = total + row_sum(wide(grad))
    rows_out[0:1] = total
    rows_out[1:8] = jnp.zeros((7, width), F32)


def on_device(
    text_input,
    patch_input,
    text_lengths,
    image_of_row,
    cotangent,
    self_qkv,
    self_out,
    cross_q,
    cross_kv,
    cross_out,
    ffn_in,
    ffn_out,
    biases,
    norm_gains,
    ffn_bias,
):
    dp = lax.axis_size(DP)
    micros, row_count, seq, width = text_input.shape
    patches, patch_width = patch_input.shape[2:]
    rows_all = micros * row_count
    tokens = rows_all * seq
    hidden = ffn_in.shape[1]
    padded = -(-patches // 16) * 16
    images = micros * patch_input.shape[1]

    part = biases.shape[1]
    small = jnp.concatenate((biases, norm_gains, ffn_bias.reshape(-1, part)))
    small_rows = small.shape[0]
    wide_rows = biases.shape[0] + norm_gains.shape[0]
    small = jnp.pad(small, ((0, 2 * PAD_ROWS - small_rows), (0, LANES - part)))
    small = jnp.broadcast_to(small.reshape(2, PAD_ROWS, LANES), (2, 2, PAD_ROWS, LANES))

    half = width // dp // 2
    half_v = cross_kv.shape[1] // 2
    in_units = hidden // (2 * LANES)
    text_group = (
        (small, self_qkv, self_out, cross_q),
        ((1, PAD_ROWS), (3, half), (1, half), (1, half)),
    )
    patch_group = ((cross_kv, cross_out), ((2, half_v), (1, half)))
    hidden_group = ((ffn_in, ffn_out), ((in_units, half), (1, ffn_out.shape[0] // 2)))

    text = text_input.reshape(tokens, width)
    pixels = call(pixel_kernel, shape((images, padded, patch_width)), [VMEM])(
        patch_input.reshape(images, patches, patch_width)
    )
    lengths = text_lengths.reshape(-1)
    slots = image_of_row.reshape(-1) ^ lax.axis_index(STREAM)
    flat = (tokens, width)
    full = pltpu.VMEM(flat, F32)
    flops = 2 * tokens * width * width
    steps = hidden // LANES
    chunks = hidden // width
    kv_shape = (4, 2, images, padded, width)
    in_block = pl.BlockSpec(
        (8, 2, 1, width // 16, LANES), lambda i: (0, 0, i // in_units, i % in_units, 0)
    )
    v = types.SimpleNamespace()

    bf16 = jnp.bfloat16

    def pixel_steps():
        (v.across,) = yield [(pixels, STREAM, ACROSS)]
        v.beside, v.apart = yield [(pixels, STREAM, CORE), (v.across, STREAM, CORE)]

    def run_text(tie, sources, spec=None, small_inputs=()):
        units = text_group[1]
        wholes = [(2, 1, 16 * PAD_ROWS, LANES)]
        wholes += [(2, count, depth * 2 * dp, LANES) for count, depth in units[1:]]
        outs = [
            shape((16, width), F32), shape((steps, LANES), F32), shape(flat), shape(flat, F32),
            shape((tokens, 1), F32), shape(flat), shape(flat), shape((3, *flat)),
            *[shape(dims) for dims in wholes[1:]],
        ]
        (
            v.vec, v.hidden_bias, v.attended, v.n1, v.inverse1, v.h1, v.qc, v.qkv,
            v.w_qkv, v.w_so, v.w_cq,
        ) = call(
            functools.partial(text_kernel, units, len(sources), spec, seq),
            outs,
            [SMEM, VMEM] + [ANY] * len(sources) + [VMEM] * len(small_inputs),
            [
                *[pltpu.VMEM(dims, bf16) for dims in wholes],
                pltpu.VMEM((3, *flat), bf16), full, full, full, full,
                pltpu.SemaphoreType.DMA((32 * len(units),)), pltpu.SemaphoreType.DMA((4,)),
            ],
            out_specs=[VMEM] * 7 + [ANY] * 4,
            mib=60,
            flops=8 * flops,
        )(lengths, tie(text), *sources, *small_inputs)
        return v.qc

    def run_patch(tie, sources, spec=None):
        units = patch_group[1]
        wholes = [(2, count, depth * 2 * dp, LANES) for count, depth in units]
        pixels_shape = (4, images, padded, patch_width)
        outs = [
            shape(flat), shape(flat, F32), shape((tokens, 1), F32), shape(flat),
            shape(kv_shape), shape(pixels_shape), *[shape(dims) for dims in wholes],
        ]
        v.oc, v.n2, v.inverse2, v.h2, v.kv, pixels_all, v.w_kv, v.w_co = call(
            functools.partial(patch_kernel, units, len(sources), spec, seq, patches, row_count),
            outs,
            [SMEM, VMEM, VMEM, VMEM] + [ANY] * (len(sources) + 4),
            [
                *[pltpu.VMEM(dims, bf16) for dims in wholes],
                pltpu.VMEM(kv_shape, bf16), pltpu.VMEM(pixels_shape, bf16), full, full,
                pltpu.SemaphoreType.DMA((32 * len(units),)), pltpu.SemaphoreType.DMA((4,)),
                pltpu.SemaphoreType.DMA((4,)),
            ],
            out_specs=[VMEM] * 4 + [ANY] * 4,
            mib=60,
            flops=18 * flops,
        )(slots, tie(v.qc), v.n1, v.vec, *sources, pixels, v.beside, v.across, v.apart)
        v.pixels_all = pixels_all.reshape(-1, patch_width)
        return v.h2

    def run_ffn(tie, sources, spec=None):
        w_shape = (8, 2, 2, hidden // 8, LANES)
        v.out_rows, v.dz3, v.df, v.sums3, v.active, v.slope, v.w_hidden = call(
            functools.partial(ffn_kernel, len(sources), spec, in_units, seq),
            [
                shape((rows_all, seq, width)), shape(flat, F32), shape(flat),
                shape((8, width), F32), shape((tokens, hidden)), shape((tokens, hidden)),
                shape(w_shape),
            ],
            [SMEM] + [VMEM] * 5 + [ANY] * len(sources),
            [
                pltpu.VMEM(w_shape, bf16), full, pltpu.SemaphoreType.DMA((32,)),
                pltpu.SemaphoreType.DMA((1,)),
            ],
            out_specs=[VMEM] * 6 + [ANY],
            flops=8 * flops,
        )(
            lengths, tie(v.h2), v.hidden_bias, v.n2,
            cotangent.reshape(rows_all, seq, width), v.vec, *sources,
        )
        return v.df

    def run_hidden_back(tie):
        v.du, v.hidden_bias_grad, v.dz2, v.dac, v.sums2 = call(
            functools.partial(hidden_back_kernel, seq),
            [
                shape((tokens, hidden)),
                shape((steps, LANES), F32),
                shape(flat, F32),
                shape(flat),
                shape((8, width), F32),
            ],
            [
                VMEM,
                pl.BlockSpec((1, 2, 2, hidden // 16, LANES), lambda i: (i, 0, 0, 1, 0)),
                in_block,
                pl.BlockSpec((tokens, LANES), lambda i: (0, i)),
                VMEM,
                VMEM,
                VMEM,
                VMEM,
            ],
            [full],
            out_specs=[pl.BlockSpec((tokens, LANES), lambda i: (0, i)), VMEM, VMEM, VMEM, VMEM],
            grid=(steps,),
            flops=8 * flops,
        )(
            tie(v.df), v.w_hidden, v.w_hidden, v.slope, v.dz3, v.n2, v.inverse2,
            v.vec,
        )
        return v.dac

    def run_cross_back(tie):
        v.dqc, v.dkv_all = call(
            functools.partial(cross_back_kernel, seq, patches, row_count),
            [shape(flat), shape((2, 4, images, padded, width))],
            [SMEM, VMEM, VMEM, VMEM, VMEM],
            [pltpu.VMEM((2, 4, images, padded, width), F32), full, full, full],
            flops=4 * flops,
        )(slots, tie(v.dac), v.qc, v.kv, v.w_co)
        return v.dqc

    def patch_steps():
        (came,) = yield [(v.patch_sent, STREAM, CORE)]
        made = wide(v.patch_kept) + wide(came)
        (across,) = yield [(low(made[1]), STREAM, ACROSS)]
        v.patch_rows = low(made[0] + wide(across))[:, :patches].reshape(patch_input.shape)

    def run_first_back(tie):
        v.dz1, v.da, v.sums1 = call(
            functools.partial(first_back_kernel, seq),
            [shape(flat, F32), shape(flat), shape((8, width), F32)],
            [VMEM] * 6,
            [full],
            flops=flops,
        )(tie(v.dqc), v.w_cq, v.dz2, v.n1, v.inverse1, v.vec)
        return v.da

    def run_self_back(tie):
        v.dqkv, v.sums0 = call(
            functools.partial(self_back_kernel, seq),
            [shape((3, *flat)), shape((8, width), F32)],
            [SMEM, VMEM, VMEM, VMEM],
            [full] * 7,
            flops=4 * flops,
        )(lengths, tie(v.da), v.qkv, v.w_so)
        return v.dqkv

    def run_patch_grad(tie):
        v.patch_kept, v.patch_sent, v.sums_kv = call(
            patch_grad_kernel,
            [shape((2, images, padded, patch_width))] * 2 + [shape((8, width), F32)],
            [VMEM] * 2,
            flops=16 * flops,
        )(tie(v.dkv_all), v.w_kv)
        return v.patch_sent

    def run_text_grad(tie):
        v.text_rows = call(
            text_grad_kernel,
            shape((rows_all, seq, width)),
            [VMEM] * 3,
            [full],
            flops=3 * flops,
        )(tie(v.dz1), v.dqkv, v.w_qkv)
        return v.text_rows

    def small_grads():
        sums0, sums1, sums2, sums3, sums_kv = v.sums0, v.sums1, v.sums2, v.sums3, v.sums_kv
        grads = jnp.concatenate(
            (
                sums0[0:2], sums1[2:3], sums1[1:2], sums1[3:4], sums_kv[0:1], sums2[2:3],
                sums2[1:2], sums3[2:3], sums3[1:2], sums1[0:1], sums2[0:1], sums3[0:1],
            )
        )
        return jnp.concatenate(
            (
                grads.reshape(wide_rows, dp, part).transpose(1, 0, 2),
                v.hidden_bias_grad.reshape(dp, -1, part),
            ),
            axis=1,
        )

    def run_all(moves):
        finish(Mover(moves))

    def finish(mover):
        while not mover.done:
            mover.give([lax.ppermute(array, axis, hops) for array, axis, hops in mover.requests])

    if not special_mesh():
        def free(array):
            return array

        w_small, *wholes = gather_plain(*text_group)
        patch_wholes = gather_plain(*patch_group)
        values = wide(w_small[0, 0].reshape(dp, 2 * PAD_ROWS, LANES)[:, :small_rows, :part])
        vec = values[:, :wide_rows].transpose(1, 0, 2).reshape(wide_rows, width)
        vec = jnp.pad(vec, ((0, 16 - wide_rows), (0, 0)))
        hidden_bias = values[:, wide_rows:].reshape(-1, LANES)
        w_small = w_small[:, :, : 16 * PAD_ROWS]
        w_in = lax.all_gather(ffn_in, DP, axis=0, tiled=True)
        w_out = lax.all_gather(ffn_out, DP, axis=0, tiled=True)
        w_in = w_in.reshape(8, 2, width // 16, 2, in_units, LANES).transpose(0, 1, 3, 4, 2, 5)
        w_in = w_in.reshape(8, 2, 2, -1, LANES)
        w_out = w_out.reshape(8, 2, hidden // 16, 2, LANES).transpose(0, 1, 3, 2, 4)
        w_hidden = jnp.concatenate((w_in, w_out), axis=3)
        run_all(pixel_steps())
        run_text(free, (w_small, *wholes), None, (vec, hidden_bias))
        run_patch(free, patch_wholes)
        run_ffn(free, (w_hidden,))
        for work in (run_hidden_back, run_cross_back, run_patch_grad):
            work(free)
        run_all(patch_steps())
        for work in (run_first_back, run_self_back, run_text_grad):
            work(free)
        s_out, s_in, s_co, s_cq, s_so, s_kv, s_qkv = reduce_plain(
            (
                (v.active, v.df), (v.h2, v.du), (v.oc, v.dac), (v.h1, v.dqc),
                (v.attended, v.da), (v.pixels_all, v.dkv_all.reshape(2, -1, width)), (text, v.dqkv),
            )
        )
        s_small = lax.psum_scatter(low(small_grads()), DP, scatter_dimension=0, tiled=True)
        s_small = wide(lax.psum(s_small, STREAM))[0]
        s_biases = s_small[: biases.shape[0]]
        s_gains = s_small[biases.shape[0] : wide_rows]
        s_hidden_bias = s_small[wide_rows:]
    else:
        clock = Clock()
        gather_text, gather_patch, gather_hidden = (
            Mover(gather_steps(*pack_group(*group)), pieces=True)
            for group in (text_group, patch_group, hidden_group)
        )
        move_pixels = Mover(pixel_steps())
        clock.step([gather_text, move_pixels])
        clock.step([gather_text, gather_patch])
        clock.step([gather_hidden, gather_text, gather_patch])
        first_hidden = gather_hidden.given
        clock.step(
            [gather_hidden, gather_patch, move_pixels], [lambda tie: run_text(tie, *piece_sources(gather_text.result, tie))]
        )
        hidden_bases = [piece.base for piece in (*first_hidden, *gather_hidden.given)]

        def early(tie):
            for base in dict.fromkeys(hidden_bases):
                base.exchange(tie)
                clock.bases.append(base)
            return ()

        clock.step([gather_hidden], [early, lambda tie: run_patch(tie, *piece_sources(gather_patch.result, tie))])
        clock.step([gather_hidden], [lambda tie: run_ffn(tie, *piece_sources(gather_hidden.result, tie))])

        out_group, in_group, mid_group, last_group = Group(), Group(), Group(), Group()

        def begin_out(tie):
            return out_group.sibling(tie, (v.active, v.df))

        def begin_in(tie):
            return in_group.sibling(tie, (v.h2, v.du))

        def begin_mid(tie):
            return mid_group.sibling(
                tie,
                (v.oc, v.dac),
                (v.h1, v.dqc),
                (v.attended, v.da),
                (v.pixels_all, v.dkv_all.reshape(2, -1, width)),
            )

        def begin_last(tie):
            return last_group.sibling(tie, (text, v.dqkv))

        def own_last(tie):
            return last_group.own(
                tie, (v.sums0, v.sums1, v.sums2, v.sums3, v.sums_kv, v.hidden_bias_grad)
            )

        clock.step([], [begin_out])
        clock.step([out_group.core_move()], [run_hidden_back, out_group.own], eager=True)
        move_out = out_group.move()
        clock.step([], [begin_in])
        clock.step(
            [move_out, in_group.core_move()],
            [run_cross_back, run_first_back, in_group.own, begin_mid],
            eager=True,
        )
        move_in = in_group.move()
        clock.step(
            [move_out, move_in, mid_group.core_move()],
            [run_self_back, run_patch_grad, mid_group.own, begin_last],
            eager=True,
            last=True,
        )
        move_mid, move_patch = mid_group.move(), Mover(patch_steps())
        clock.step(
            [move_out, move_in, move_mid, last_group.core_move(), move_patch],
            [own_last, run_text_grad],
            eager=True,
        )
        move_last = last_group.move()
        movers = [move_out, move_in, move_mid, move_last, move_patch]
        results = {}

        small_shapes = [
            shape((rows, part), F32)
            for rows in (biases.shape[0], norm_gains.shape[0], small_rows - wide_rows)
        ]

        def unpack(group, mover):
            def work(tie):
                results[mover] = group.unpack(
                    (tie(mover.result[0]), mover.result[1]),
                    small_shapes if group is last_group else (),
                )
                return results[mover]
            return work

        groups = [
            (out_group, move_out), (in_group, move_in), (mid_group, move_mid), (last_group, move_last)
        ]
        def ready():
            return [
                unpack(group, mover)
                for group, mover in groups
                if mover.done and mover not in results
            ]

        for _ in range(3):
            clock.step(movers, ready, eager=True)
        for mover in movers:
            if not mover.done:
                finish(mover)
        for work in ready():
            work(clock.tie)
        (s_out,), (s_in,) = results[move_out], results[move_in]
        s_co, s_cq, s_so, s_kv = results[move_mid]
        s_qkv, s_biases, s_gains, s_hidden_bias = results[move_last]
    return (
        v.out_rows.reshape(text_input.shape),
        v.text_rows.reshape(text_input.shape),
        v.patch_rows,
        s_qkv,
        s_so,
        s_cq,
        s_kv,
        s_co,
        s_in,
        s_out,
        s_biases,
        s_gains,
        s_hidden_bias.reshape(-1),
    )


def solution(mesh):
    placed = (
        P(None, (DP, STREAM), None, None),
        P(None, (DP, STREAM), None, None),
        P(None, (DP, STREAM)),
        P(None, (DP, STREAM)),
        P(None, (DP, STREAM), None, None),
        P(None, DP, None),
        P(DP, None),
        P(DP, None),
        P(None, DP, None),
        P(DP, None),
        P(DP, None),
        P(DP, None),
        P(None, DP),
        P(None, DP),
        P(DP),
    )
    return jax.shard_map(
        on_device,
        mesh=mesh,
        in_specs=placed,
        out_specs=(
            P(None, (DP, STREAM), None, None),
            P(None, (DP, STREAM), None, None),
            P(None, (DP, STREAM), None, None),
            P(None, DP, None),
            P(DP, None),
            P(DP, None),
            P(None, DP, None),
            P(DP, None),
            P(DP, None),
            P(DP, None),
            P(None, DP),
            P(None, DP),
            P(DP),
        ),
        check_vma=False,
    )
```

```python
import functools
import types

import jax
import jax.numpy as jnp
from jax import lax
from jax.experimental import pallas as pl
from jax.experimental.pallas import tpu as pltpu
from jax.sharding import PartitionSpec as P

HEADS = 12
LANES = 384
PAD_ROWS = 16
MIB = 2**20
DP, STREAM = "dp", "stream"

EPSILON = 1e-06
ROOT_HALF = 0.7071067811865476
INV_ROOT_TAU = 0.3989422804014327

CORE = ((0, 1), (1, 0), (2, 3), (3, 2))
ACROSS = ((0, 2), (2, 0), (1, 3), (3, 1))
BESIDE = ((0, 1), (1, 0), (2, 3), (3, 2), (4, 5), (5, 4), (6, 7), (7, 6))
PAIR = ((0, 2), (2, 0), (1, 3), (3, 1), (4, 6), (6, 4), (5, 7), (7, 5))
HALFWAY = ((0, 4), (4, 0), (1, 5), (5, 1), (2, 6), (6, 2), (3, 7), (7, 3))
MIRROR = ((0, 6), (6, 0), (1, 7), (7, 1), (2, 4), (4, 2), (3, 5), (5, 3))

B_Q, B_V, B_SO, B_N1, B_CQ, B_CV, B_CO, B_N2, B_FO, B_N3, G_1, G_2, G_3 = range(13)


def low(value):
    return value.astype(jnp.bfloat16)


def wide(value):
    return value.astype(jnp.float32)


def dot(left, right):
    return jnp.dot(left, right, preferred_element_type=jnp.float32)


def dot_last(left, right):
    return lax.dot_general(
        left, right, (((1,), (1,)), ((), ())), preferred_element_type=jnp.float32
    )


def dot_first(left, right):
    return lax.dot_general(
        left, right, (((0,), (0,)), ((), ())), preferred_element_type=jnp.float32
    )


def pick(array, index, axis=0):
    return lax.dynamic_index_in_dim(array, index, axis, keepdims=False)


def place():
    dp_at, stream_at = lax.axis_index(DP), lax.axis_index(STREAM)
    return dp_at // 2, dp_at % 2, stream_at // 2, stream_at % 2


class Base:
    def __init__(self, array):
        self.array = array.reshape(-1, LANES)
        self.twin = None

    def exchange(self, tie):
        if self.twin is None:
            self.twin = lax.ppermute(tie(self.array), STREAM, CORE)
        return self.twin


class Piece:
    def __init__(self, base, row, dims):
        self.base, self.row, self.dims = base, row, dims

    def value(self):
        rows = 1
        for size in self.dims[:-1]:
            rows *= size
        return self.base.array[self.row : self.row + rows].reshape(self.dims)


class Clock:
    def __init__(self):
        self.before = []
        self.came = []
        self.bases = []

    def take(self, arrays):
        given = {}
        for array, (_, sends) in zip(arrays, self.came):
            row = 0
            base = Base(array) if sends[0][0].pieces else None
            for mover, at, sent in sends:
                part = array
                if base is not None:
                    part = Piece(base, row, sent.shape)
                    row += sent.size // LANES
                elif len(sends) > 1:
                    rows = sent.size // LANES
                    part = array[row : row + rows].reshape(sent.shape)
                    row += rows
                given.setdefault(mover, {})[at] = part
        self.came = []
        for mover, parts in given.items():
            mover.give([parts[at] for at in range(len(parts))])

    def step(self, moving=(), compute=(), eager=False, last=False):
        arrays = [array for array, _ in self.came]
        twins = [base.exchange(self.tie) for base in self.bases]
        arrays, twins, self.before = lax.optimization_barrier(
            (arrays, twins, self.before + arrays[:1])
        )
        for base, twin in zip(self.bases, twins):
            base.twin = twin
        self.bases = []
        self.take(arrays)
        ways = {}
        for mover in moving:
            if mover.done:
                continue
            for at, (array, axis, hops) in enumerate(mover.requests):
                alone = hops is CORE or array.shape[-1] != LANES
                key = (axis, hops, (mover, at) if alone else None)
                ways.setdefault(key, []).append((mover, at, array))
        joined = [
            sends[0][2]
            if len(sends) == 1
            else jnp.concatenate([array.reshape(-1, LANES) for _, _, array in sends])
            for sends in ways.values()
        ]
        joined, self.before = lax.optimization_barrier((joined, self.before))
        self.came = [
            (lax.ppermute(array, axis, hops), sends)
            for array, ((axis, hops, _), sends) in zip(joined, ways.items())
        ]
        early = []
        if last:
            early = [item for item in self.came if item[1][0][0].early]
            self.came = [item for item in self.came if not item[1][0][0].early]
            for array, sends in early:
                sends[0][0].give([array])
        after = []

        def compute_all():
            for work in compute() if callable(compute) else compute:
                after.extend(jax.tree.leaves(work(self.tie)))

        if last:
            compute_all()
        if eager:
            movers = [mover for _, sends in self.came for mover, _, _ in sends]
            arrays = [array for array, _ in self.came]
            if last:
                arrays, after = lax.optimization_barrier((arrays, after))
            self.take(arrays)
            for mover in dict.fromkeys(movers):
                if mover.done:
                    after += jax.tree.leaves(mover.result)
                else:
                    after += [array for array, _, _ in mover.requests]
        if not last:
            compute_all()
        if after:
            self.before = after

    def tie(self, array):
        return lax.optimization_barrier((array, self.before))[0]


class Mover:
    def __init__(self, steps, pieces=False, early=False):
        self.given = []
        self.steps = steps
        self.pieces = pieces
        self.early = early
        self.done = False
        self.result = None
        self.requests = next(steps)

    def give(self, came):
        self.given = came
        try:
            self.requests = self.steps.send(came)
        except StopIteration as stop:
            self.done, self.result = True, stop.value


def special_mesh():
    return lax.axis_size(DP) == 8 and lax.axis_size(STREAM) == 4


VMEM = pl.BlockSpec(memory_space=pltpu.VMEM)
SMEM = pl.BlockSpec(memory_space=pltpu.SMEM)
ANY = pl.BlockSpec(memory_space=pl.ANY)


def call(kernel, out_shape, in_specs, scratch=(), mib=18, flops=0, out_specs=None, **more):
    return pl.pallas_call(
        kernel,
        out_shape=out_shape,
        in_specs=in_specs,
        out_specs=jax.tree.map(lambda _: VMEM, out_shape) if out_specs is None else out_specs,
        scratch_shapes=list(scratch),
        compiler_params=pltpu.CompilerParams(vmem_limit_bytes=mib * MIB),
        cost_estimate=pl.CostEstimate(flops=flops, bytes_accessed=4 * MIB, transcendentals=0),
        **more,
    )


def shape(dims, dtype=jnp.bfloat16):
    return jax.ShapeDtypeStruct(tuple(dims), dtype)


F32 = jnp.float32


def pack_shard(shard, units):
    if shard.ndim == 2:
        rows, _ = shard.shape
        split = shard.reshape(2, rows // 2, 2, units, LANES).transpose(2, 0, 3, 1, 4)
    else:
        _, rows, _ = shard.shape
        split = shard.reshape(units, 2, rows // 2, 2, LANES).transpose(3, 1, 0, 2, 4)
    return split.reshape(2, 2, units * rows // 2, LANES)


def pack_kernel(units, *refs):
    _, _, x_at, core_at = place()
    shards, (both, own, own_x) = refs[: len(units)], refs[len(units) :]
    row = 0
    for shard, (count, depth) in zip(shards, units):
        if len(shard.shape) == 4:
            both[:, :, row : row + depth] = shard[...]
            row += depth
            continue
        for unit in range(count):
            rows = slice(row, row + depth)
            for x in range(2):
                for c in range(2):
                    if len(shard.shape) == 3:
                        block = shard[unit, x * depth : (x + 1) * depth, c * LANES : (c + 1) * LANES]
                    else:
                        start = (c * count + unit) * LANES
                        block = shard[x * depth : (x + 1) * depth, start : start + LANES]
                    both[c, x, rows] = block
            row += depth
    own[...] = both[core_at]
    own_x[...] = both[core_at, x_at]


def pack_own_kernel(units, *refs):
    _, _, x_at, core_at = place()
    shards, out = refs[:-1], refs[-1]
    row = 0
    for shard, (count, depth) in zip(shards, units):
        for unit in range(count):
            start = (core_at * count + unit) * LANES
            out[row : row + depth] = shard[
                pl.ds(pl.multiple_of(x_at * depth, 16), depth),
                pl.ds(pl.multiple_of(start, 128), LANES),
            ]
            row += depth


def pack_group(shards, units):
    rows = sum(count * depth for count, depth in units)
    return call(
        functools.partial(pack_kernel, units),
        [shape((2, 2, rows, LANES)), shape((2, rows, LANES)), shape((rows, LANES))],
        [VMEM] * len(shards),
    )(*shards)


def pack_own(shards, units):
    rows = sum(count * depth for count, depth in units)
    return call(
        functools.partial(pack_own_kernel, units), shape((rows, LANES)), [VMEM] * len(shards)
    )(*shards)


def gather_steps(own_both, own, own_x):
    x_at = lax.axis_index(STREAM) // 2
    mate, half_z, mirror_z, beside = yield [
        (own, DP, PAIR),
        (own_x, DP, HALFWAY),
        (own_x, DP, MIRROR),
        (own, DP, BESIDE),
    ]
    mate_halves = mate.value()
    others = jnp.stack((pick(mate_halves, x_at), half_z.value(), mirror_z.value()))
    beside_others, half_x, mirror_x = yield [
        (others, DP, BESIDE),
        (half_z.value(), STREAM, ACROSS),
        (mirror_z.value(), STREAM, ACROSS),
    ]
    others_x, mate_x = yield [
        (beside_others.value()[1:], STREAM, ACROSS),
        (pick(mate_halves, 1 - x_at), DP, BESIDE),
    ]
    whole = Piece(Base(own_both), 0, own_both.shape)
    return (
        whole, mate, beside, half_z, mirror_z, half_x, mirror_x, beside_others, others_x, mate_x
    )


def piece_sources(pieces, tie):
    own, *received = pieces
    rows = own.dims[2]
    arrays, spec = [own.base.array], [(0, at * rows) for at in range(4)]
    known = {}

    def find(piece, theirs):
        key = (piece.base, theirs)
        if key not in known:
            known[key] = len(arrays)
            arrays.append(piece.base.exchange(tie) if theirs else piece.base.array)
        return known[key]

    for theirs in (False, True):
        mate, beside, half_z, mirror_z, half_x, mirror_x, others, others_x, mate_x = received
        blocks = [(mate, 0), (beside, 0), (mate, 1), (beside, 1)]
        blocks += [(half_z, 0), (mirror_z, 0), (half_x, 0), (mirror_x, 0)]
        blocks += [(others, 0), (others, 1), (others, 2), (mate_x, 0), (others_x, 0), (others_x, 1)]
        spec += [(find(piece, theirs), piece.row + block * rows) for piece, block in blocks]
    return arrays, tuple(spec)


def piece_places(spec, sources):
    z_at, y_at, x_at, core_at = place()
    _, z_mate, z_half, z_mirror = shard_slots(z_at)
    far_y, far_x = 1 - y_at, 1 - x_at
    places = [(z_at, y_at, x_from, core_from) for core_from in range(2) for x_from in range(2)]
    for core_from in (core_at, 1 - core_at):
        for x_from in range(2):
            places.append((z_mate, y_at, x_from, core_from))
            places.append((z_at, far_y, x_from, core_from))
        places += [
            (z_half, y_at, x_at, core_from),
            (z_mirror, y_at, x_at, core_from),
            (z_half, y_at, far_x, core_from),
            (z_mirror, y_at, far_x, core_from),
            (z_mate, far_y, x_at, core_from),
            (z_half, far_y, x_at, core_from),
            (z_mirror, far_y, x_at, core_from),
            (z_mate, far_y, far_x, core_from),
            (z_half, far_y, far_x, core_from),
            (z_mirror, far_y, far_x, core_from),
        ]
    return [(sources[at], row, *where) for (at, row), where in zip(spec, places)]


def piece_copies(units, spec, sources, wholes, sems):
    parts = piece_places(spec, sources)
    copies, row, sem = [], 0, 0
    for (count, depth), whole in zip(units, wholes):
        of_weight = []
        for source, first, z_from, y_from, x_from, core_from in parts:
            start = (z_from * 2 + y_from) * (2 * depth) + x_from * depth
            of_weight.append(
                pltpu.make_async_copy(
                    source.at[pl.ds(first + row, count * depth)].reshape(count, depth, LANES),
                    whole.at[core_from, :, pl.ds(pl.multiple_of(start, 16), depth)],
                    sems.at[sem],
                )
            )
            sem += 1
        copies.append(of_weight)
        row += count * depth
    return copies


def gather_plain(shards, units):
    packed = [
        shard if shard.ndim == 4 else pack_shard(shard, count)
        for shard, (count, _) in zip(shards, units)
    ]
    whole = lax.all_gather(jnp.concatenate(packed, axis=2), DP, axis=0, tiled=False)
    results = []
    row = 0
    for count, depth in units:
        part = whole[:, :, :, row : row + count * depth]
        part = part.reshape(-1, 2, 2, count, depth, LANES).transpose(1, 3, 0, 2, 4, 5)
        results.append(part.reshape(2, count, -1, LANES))
        row += count * depth
    return results


def shard_slots(z_at):
    return z_at, z_at + 1 - 2 * (z_at % 2), (z_at + 2) % 4, 3 - z_at


def grad_columns(right, core, units):
    blocks = []
    for lead in [None] if len(right.shape) == 2 else range(right.shape[0]):
        of_lead = right if lead is None else right.at[lead]
        start = pl.multiple_of(core * (units * LANES), 128)
        blocks.append(of_lead[:, pl.ds(start, units * LANES)])
    return blocks[0] if len(blocks) == 1 else jnp.concatenate(blocks, axis=1)


def sibling_grad_kernel(jobs, *refs):
    operands, out = refs[:-1], refs[-1]
    core_at = lax.axis_index(STREAM) % 2
    row = 0
    for at, (units, blocks, depth) in enumerate(jobs):
        left, right = operands[2 * at], operands[2 * at + 1]
        product = low(dot_first(left[...], grad_columns(right, 1 - core_at, units)))
        for block in range(blocks):
            columns = product[:, block * LANES : (block + 1) * LANES]
            out[:, :, row : row + depth] = columns.reshape(8, 2, depth, LANES)
            row += depth


TO_X = ((2, False, False), (3, False, False), (2, True, False), (3, True, False))
TO_Y_A = ((0, False, True), (1, False, True))
TO_Z_A = ((1, False, False), (1, True, False))
TO_Y_B = ((2, False, True), (3, False, True), (0, False, False))
TO_Z_B = ((1, True, True),)
TO_Z_C = ((2, True, True), (3, True, True))
OWN = ((0, True, True), (0, True, False))
PARTS = (TO_X, TO_Y_A, TO_Z_A, TO_Y_B, TO_Z_B, TO_Z_C, OWN)


def part_at(part):
    z_at, y_at, x_at, _ = place()
    slot, own_y, own_x = part
    return (
        shard_slots(z_at)[slot] * 2 + (y_at if own_y else 1 - y_at),
        x_at if own_x else 1 - x_at,
    )


def small_grad_rows(sums, hidden_bias, work):
    sums0, sums1, sums2, sums3, sums_kv = sums
    rows = (
        (sums0, 0), (sums0, 1), (sums1, 2), (sums1, 1), (sums1, 3), (sums_kv, 0), (sums2, 2),
        (sums2, 1), (sums3, 2), (sums3, 1), (sums1, 0), (sums2, 0), (sums3, 0),
    )
    part = sums0.shape[1] // 8
    work[...] = jnp.zeros_like(work)
    for dp_to in range(8):
        columns = slice(dp_to * part, (dp_to + 1) * part)
        for row, (array, at) in enumerate(rows):
            work[dp_to, row : row + 1, :part] = array[at : at + 1, columns]
        for j in range(hidden_bias.shape[1] // part):
            at = len(rows) + j
            work[dp_to, at : at + 1, :part] = hidden_bias[
                dp_to : dp_to + 1, j * part : (j + 1) * part
            ]


def own_grad_kernel(jobs, sent, small, *refs):
    inputs = 2 * len(jobs) + len(sent)
    operands, came = refs[: 2 * len(jobs)], refs[2 * len(jobs) : inputs]
    extra = refs[inputs : inputs + 6 * small]
    outs = refs[inputs + 6 * small : inputs + 6 * small + len(PARTS)]
    work, *small_work = refs[inputs + 6 * small + len(PARTS) :]
    core_at = lax.axis_index(STREAM) % 2
    row = 0
    for at, (units, blocks, depth) in enumerate(jobs):
        left, right = operands[2 * at], operands[2 * at + 1]
        product = dot_first(left[...], grad_columns(right, core_at, units))
        array, came_row = sent[at]
        for block in range(blocks):
            columns = product[:, block * LANES : (block + 1) * LANES]
            rows = slice(row, row + depth)
            work[:, :, :depth] = columns.reshape(8, 2, depth, LANES) + wide(
                came[array][:, :, came_row : came_row + depth]
            )
            for out, parts in zip(outs, PARTS):
                for j, part in enumerate(parts):
                    dp_from, x_from = part_at(part)
                    out[j, rows] = low(work[dp_from, x_from, :depth])
            row += depth
            came_row += depth
    if small:
        small_grad_rows(extra[:5], extra[5], small_work[0])
        for out, parts in zip(outs, PARTS):
            for j, part in enumerate(parts):
                dp_from, x_from = part_at(part)
                rows = pl.ds(pl.multiple_of(x_from * PAD_ROWS, PAD_ROWS), PAD_ROWS)
                out[j, row : row + PAD_ROWS] = low(small_work[0][dp_from, rows])


def reduce_steps(to_x, to_y_a, to_z_a, to_y_b, to_z_b, to_z_c, own):
    from_y_a, from_x, from_z_a = yield [
        (to_y_a, DP, BESIDE),
        (to_x, STREAM, ACROSS),
        (to_z_a, DP, PAIR),
    ]
    arrived = jnp.concatenate((from_x[:2], from_z_a[:1]))
    from_y_b, mate = yield [
        (low(wide(to_y_b) + wide(arrived)), DP, BESIDE),
        (low(wide(to_z_b) + wide(from_y_a[1:])), DP, PAIR),
    ]
    far = wide(to_z_c) + wide(from_x[2:]) + wide(from_y_b[:2])
    (by_mate,) = yield [(low(far[1]), DP, PAIR)]
    (half,) = yield [(low(far[0] + wide(by_mate)), DP, HALFWAY)]
    total = low(
        jnp.stack(
            (
                wide(own[0]) + wide(from_y_a[0]) + wide(mate[0]) + wide(half),
                wide(own[1]) + wide(from_y_b[2]) + wide(from_z_a[1]),
            )
        )
    )
    (from_x,) = yield [(total, STREAM, ACROSS)]
    total = low(wide(total) + wide(from_x[::-1]))
    return total, lax.ppermute(total, STREAM, CORE)


def unpack_kernel(jobs, small, mine, other, *outs):
    _, _, x_at, core_at = place()
    for source, core_from in ((mine, core_at), (other, 1 - core_at)):
        for j in range(2):
            x_from = x_at if j == 0 else 1 - x_at
            for out_at, lead, units, row, depth in jobs:
                out = outs[out_at] if lead is None else outs[out_at].at[lead]
                for unit in range(units):
                    at = row + unit * depth
                    start = core_from * (units * LANES) + unit * LANES
                    out[
                        pl.ds(pl.multiple_of(x_from * depth, 8), depth),
                        pl.ds(pl.multiple_of(start, 128), LANES),
                    ] = wide(source[j, at : at + depth])
    if small is not None:
        biases, gains, hidden_bias, work = outs[-4:]
        for j in range(2):
            x_from = x_at if j == 0 else 1 - x_at
            rows = slice(small, small + PAD_ROWS)
            work[pl.ds(pl.multiple_of(x_from * PAD_ROWS, 8), PAD_ROWS)] = wide(
                mine[j, rows]
            ) + wide(other[j, rows])
        part = biases.shape[1]
        biases[...] = work[:G_1, :part]
        gains[...] = work[G_1 : G_3 + 1, :part]
        hidden_bias[...] = work[G_3 + 1 : G_3 + 1 + hidden_bias.shape[0], :part]


def reduce_plain(parts):
    shards = []
    for left, right in parts:
        if right.ndim == 2:
            whole = low(dot_first(left, right))
            own = lax.psum_scatter(whole, DP, scatter_dimension=0, tiled=True)
        else:
            whole = low(jnp.stack([dot_first(left, r) for r in right]))
            own = lax.psum_scatter(whole, DP, scatter_dimension=1, tiled=True)
        shards.append(wide(lax.psum(own, STREAM)))
    return shards


class Group:
    def __init__(self):
        self.operands, self.jobs, self.out_jobs, self.out_shapes = [], [], [], []
        self.rows, self.flops, self.sent, self.came, self.from_sent = 0, 0, [], [], []

    def sibling(self, tie, *parts):
        jobs, operands, rows, flops = [], [], 0, 0
        for left, right in parts:
            operands += [left, right]
            depth = left.shape[1] // 16
            units = right.shape[-1] // (2 * LANES)
            leads = [None] if right.ndim == 2 else range(right.shape[0])
            jobs.append((units, units * len(leads), depth))
            self.from_sent.append((len(self.sent), rows))
            for lead in leads:
                self.out_jobs.append(
                    (len(self.out_shapes), lead, units, self.rows + rows, depth)
                )
                rows += units * depth
            self.out_shapes.append(
                shape((*right.shape[:-2], 2 * depth, right.shape[-1]), F32)
            )
            flops += left.shape[0] * left.shape[1] * right.size // right.shape[-2]
        self.sent.append(
            call(
                functools.partial(sibling_grad_kernel, jobs),
                shape((8, 2, rows, LANES)),
                [VMEM] * len(operands),
                flops=flops,
            )(tie(operands[0]), *operands[1:])
        )
        self.jobs += jobs
        self.operands += operands
        self.rows += rows
        self.flops += flops
        return self.sent[-1]

    def core_move(self):
        def steps(sent):
            (came,) = yield [(sent, STREAM, CORE)]
            self.came.append(came)

        return Mover(steps(self.sent[-1]), early=True)

    def own(self, tie, small=()):
        deepest = max(job[-1] for job in self.jobs)
        scratch = [pltpu.VMEM((8, 2, deepest, LANES), F32)]
        if small:
            scratch.append(pltpu.VMEM((8, 2 * PAD_ROWS, LANES), F32))
        rows = self.rows + PAD_ROWS * bool(small)
        came = [self.came[array] for array, _ in self.from_sent]
        self.parts = call(
            functools.partial(
                own_grad_kernel,
                self.jobs,
                [(at, row) for at, (_, row) in enumerate(self.from_sent)],
                bool(small),
            ),
            [shape((len(parts), rows, LANES)) for parts in PARTS],
            [VMEM] * (len(self.operands) + len(came) + len(small)),
            scratch,
            flops=self.flops,
        )(tie(self.operands[0]), *self.operands[1:], *came, *small)
        return self.parts

    def move(self):
        return Mover(reduce_steps(*self.parts))

    def unpack(self, moved, small=()):
        return call(
            functools.partial(unpack_kernel, self.out_jobs, self.rows if small else None),
            [*self.out_shapes, *small],
            [VMEM, VMEM],
            [pltpu.VMEM((2 * PAD_ROWS, LANES), F32)] * bool(small),
        )(*moved)


def norm_parts(summed):
    center = summed - jnp.mean(summed, axis=-1, keepdims=True)
    inverse = lax.rsqrt(jnp.mean(center * center, axis=-1, keepdims=True) + EPSILON)
    return center * inverse, inverse


def norm_back(upstream, normed, inverse, gain):
    scaled = upstream * gain
    return inverse * (
        scaled
        - jnp.mean(scaled, axis=-1, keepdims=True)
        - normed * jnp.mean(scaled * normed, axis=-1, keepdims=True)
    )


def heads_apart(four):
    head = lax.broadcasted_iota(jnp.int32, four.shape, 1) // 64
    return low(jnp.concatenate([jnp.where(head == j, four, 0.0) for j in range(4)], axis=0))


def heads_joined(stacked):
    rows = stacked.shape[0] // 4
    head = lax.broadcasted_iota(jnp.int32, (rows, stacked.shape[1]), 1) // 64
    made = stacked[:rows]
    for j in range(1, 4):
        made = jnp.where(head == j, stacked[j * rows : (j + 1) * rows], made)
    return made


def quads():
    return [slice(j * 256, (j + 1) * 256) for j in range(HEADS // 4)]


def softmax(scores):
    raised = jnp.exp(scores - jnp.max(scores, axis=-1, keepdims=True))
    return raised * (1.0 / jnp.sum(raised, axis=-1, keepdims=True))


def score_back(weight, back):
    return low(weight * (back - jnp.sum(back * weight, axis=-1, keepdims=True)))


def row_sum(value):
    return jnp.sum(value, axis=0, keepdims=True)


def self_kernel(seq, lengths, x_ref, w_ref, vec, qkv_ref, out_ref, q, k, v, o):
    tokens = x_ref.shape[0]
    for j, (scratch, bias) in enumerate(((q, B_Q), (k, None), (v, B_V))):
        for c in range(2):
            columns = slice(c * LANES, (c + 1) * LANES)
            made = dot(x_ref[...], w_ref[c, j])
            if bias is not None:
                made = made + vec[bias : bias + 1, columns]
            made = low(made)
            qkv_ref[j, :, columns] = made
            scratch[:, columns] = wide(made)

    def step(r, _):
        rows = pl.ds(pl.multiple_of(r * seq, 8), seq)
        valid = lax.broadcasted_iota(jnp.int32, (4 * seq, seq), 1) < lengths[r]
        asked = [heads_apart(q[rows, c] * 0.125) for c in quads()]
        scores = [dot_last(a, low(k[rows, c])) for a, c in zip(asked, quads())]
        weights = [softmax(jnp.where(valid, score, -jnp.inf)) for score in scores]
        made = [dot(low(w), low(v[rows, c])) for w, c in zip(weights, quads())]
        for part, c in zip(made, quads()):
            o[rows, c] = heads_joined(part)
        return 0

    lax.fori_loop(0, tokens // seq, step, 0, unroll=2)
    out_ref[...] = low(o[...])


def first_norm_kernel(seq, o_ref, x_ref, wso, wcq, vec, normed, inverse, h_low, qc, z):
    for c in range(2):
        columns = slice(c * LANES, (c + 1) * LANES)
        z[:, columns] = (
            dot(o_ref[...], wso[c, 0])
            + vec[B_SO : B_SO + 1, columns]
            + wide(x_ref[:, columns])
        )
    made, scale = norm_parts(z[...])
    normed[...] = made
    inverse[...] = scale
    h_low[...] = low(made * vec[G_1 : G_1 + 1] + vec[B_N1 : B_N1 + 1])
    for c in range(2):
        columns = slice(c * LANES, (c + 1) * LANES)
        qc[:, columns] = low(dot(h_low[...], wcq[c, 0]) + vec[B_CQ : B_CQ + 1, columns])


def pixel_kernel(patch_ref, out_ref):
    images, patches, _ = patch_ref.shape
    out_ref[:, :patches] = patch_ref[...]
    out_ref[:, patches:] = jnp.zeros_like(out_ref[:, patches:])


def image_kernel(pixels, w_ref, vec, kv_ref):
    slots, _, images, padded, width = kv_ref.shape
    rows = images * padded
    flat = pixels[...].reshape(slots * rows, -1)
    for j in range(2):
        made = dot(flat, jnp.concatenate((w_ref[0, j], w_ref[1, j]), axis=1))
        if j == 1:
            made = made + vec[B_CV : B_CV + 1]
        for slot in range(slots):
            part = made[slot * rows : (slot + 1) * rows]
            kv_ref[slot, j] = low(part).reshape(images, padded, width)


def cross_kernel(
    seq, patches, micro_rows, slots, qc, kv, n1, wco, vec, oc, n2, inverse, h_low, q, o
):
    q[...] = wide(qc[...]) * 0.125
    tokens = qc.shape[0]
    padded = kv.shape[3]
    there = lax.broadcasted_iota(jnp.int32, (4 * seq, padded), 1) < patches

    def step(r, _):
        rows = pl.ds(pl.multiple_of(r * seq, 8), seq)
        slot, m = slots[r], r // micro_rows
        asked = [heads_apart(q[rows, c]) for c in quads()]
        scores = [dot_last(a, kv[slot, 0, m, :, c]) for a, c in zip(asked, quads())]
        weights = [softmax(jnp.where(there, score, -jnp.inf)) for score in scores]
        made = [dot(low(w), kv[slot, 1, m, :, c]) for w, c in zip(weights, quads())]
        for part, c in zip(made, quads()):
            o[rows, c] = heads_joined(part)
        return 0

    lax.fori_loop(0, tokens // seq, step, 0, unroll=2)
    oc[...] = low(o[...])
    for c in range(2):
        columns = slice(c * LANES, (c + 1) * LANES)
        first = n1[:, columns] * vec[G_1 : G_1 + 1, columns] + vec[B_N1 : B_N1 + 1, columns]
        o[:, columns] = first + dot(oc[...], wco[c, 0]) + vec[B_CO : B_CO + 1, columns]
    made, scale = norm_parts(o[...])
    n2[...] = made
    inverse[...] = scale
    h_low[...] = low(made * vec[G_2 : G_2 + 1] + vec[B_N2 : B_N2 + 1])


def small_rows_kernel(shards, vec, hidden_bias, part):
    wide_rows = G_3 + 1
    vec[...] = jnp.zeros_like(vec)
    for dp_from in range(8):
        rows = wide(shards[dp_from * 2 * PAD_ROWS : (dp_from + 1) * 2 * PAD_ROWS])
        vec[:wide_rows, dp_from * part : (dp_from + 1) * part] = rows[:wide_rows, :part]
        for j in range(LANES // part):
            hidden_bias[dp_from : dp_from + 1, j * part : (j + 1) * part] = rows[
                wide_rows + j : wide_rows + j + 1, :part
            ]


def take_weights(units, spec, sources, wholes, outs, in_sems, out_sems, kept):
    if spec is None:
        copies = [
            [pltpu.make_async_copy(source, whole, in_sems.at[at])]
            for at, (source, whole) in enumerate(zip(sources, wholes))
        ]
    else:
        copies = piece_copies(units, spec, sources, wholes, in_sems)
    for of_weight in copies:
        for copy in of_weight:
            copy.start()

    def take(at):
        for copy in copies[at]:
            copy.wait()
        if outs[at] is not None:
            send(wholes[at], outs[at])

    def send(source, target):
        kept.append(pltpu.make_async_copy(source, target, out_sems.at[len(kept)]))
        kept[-1].start()

    return take, send


def text_kernel(units, gathered, spec, seq, lengths, text, *refs):
    sources, refs = refs[:gathered], refs[gathered:]
    if spec is None:
        small, refs = refs[:2], refs[2:]
    outs, refs = refs[:11], refs[11:]
    vec, hidden_bias, attended, n1, inverse1, h1, qc, qkv_out, *w_outs = outs
    wholes, (qkv, q, k, v, o, in_sems, out_sems) = refs[:4], refs[4:]
    w_small, w_qkv, w_so, w_cq = wholes
    kept = []
    take, send = take_weights(
        units, spec, sources, wholes, (None, *w_outs), in_sems, out_sems, kept
    )
    take(0)
    if spec is None:
        vec[...], hidden_bias[...] = small[0][...], small[1][...]
    else:
        small_rows_kernel(w_small.at[0, 0], vec, hidden_bias, text.shape[1] // 8)
    take(1)
    self_kernel(seq, lengths, text, w_qkv, vec, qkv, attended, q, k, v, o)
    send(qkv, qkv_out)
    take(2)
    take(3)
    first_norm_kernel(seq, attended, text, w_so, w_cq, vec, n1, inverse1, h1, qc, o)
    for copy in kept:
        copy.wait()


def patch_kernel(units, gathered, spec, seq, patches, micro_rows, slots, qc, n1, vec, *refs):
    sources, held, refs = refs[:gathered], refs[gathered : gathered + 4], refs[gathered + 4 :]
    (oc, n2, inverse2, h2, kv_out, pixels_out, *w_outs), refs = refs[:8], refs[8:]
    wholes, (kv, pixels, q, o, in_sems, pixel_sems, out_sems) = refs[:2], refs[2:]
    w_kv, w_co = wholes
    pixel_copies = [
        pltpu.make_async_copy(image, pixels.at[at], pixel_sems.at[at])
        for at, image in enumerate(held)
    ]
    for copy in pixel_copies:
        copy.start()
    kept = []
    take, send = take_weights(units, spec, sources, wholes, w_outs, in_sems, out_sems, kept)
    for copy in pixel_copies:
        copy.wait()
    send(pixels, pixels_out)
    take(0)
    image_kernel(pixels, w_kv, vec, kv)
    send(kv, kv_out)
    take(1)
    cross_kernel(
        seq, patches, micro_rows, slots, qc, kv, n1, w_co, vec, oc, n2, inverse2, h2, q, o
    )
    for copy in kept:
        copy.wait()


def hidden_weights(w, block, in_units):
    core, unit = divmod(block, in_units)
    depth = w.shape[3] // 2 // in_units
    return w[:, :, core, unit * depth : (unit + 1) * depth].reshape(-1, LANES)


def ffn_kernel(
    gathered, spec, in_units, seq, lengths, h2, bias, n2, cot, vec, *refs
):
    sources, refs = refs[:gathered], refs[gathered:]
    out, dz, df, rows_out, active, slope, w_out, w, total, in_sems, out_sem = refs
    if spec is None:
        copies = [pltpu.make_async_copy(sources[0], w, in_sems.at[0])]
    else:
        copies = [
            pltpu.make_async_copy(
                source.at[pl.ds(first, w.shape[3])],
                w.at[z_from * 2 + y_from, x_from, core_from],
                in_sems.at[at],
            )
            for at, (source, first, z_from, y_from, x_from, core_from) in enumerate(
                piece_places(spec, sources)
            )
        ]
    for copy in copies:
        copy.start()
    for copy in copies:
        copy.wait()
    keep = pltpu.make_async_copy(w, w_out, out_sem.at[0])
    keep.start()
    for block in range(0, 2 * in_units, 2):
        columns = slice(block * LANES, (block + 2) * LANES)
        two = (block, block + 1)
        weights = jnp.concatenate([hidden_weights(w, b, in_units) for b in two], axis=1)
        shift = jnp.concatenate([bias[b : b + 1] for b in two], axis=1)
        pre = dot(h2[...], weights) + shift
        cumulative = 0.5 * (1.0 + lax.erf(pre * ROOT_HALF))
        active[:, columns] = low(pre * cumulative)
        slope[:, columns] = low(cumulative + pre * INV_ROOT_TAU * jnp.exp(-0.5 * pre * pre))
    half_rows = w.shape[3] // 2
    made = None
    for part in range(4):
        weights = jnp.concatenate(
            [w[2 * part : 2 * part + 2, :, c, half_rows:].reshape(-1, LANES) for c in range(2)],
            axis=1,
        )
        depth = weights.shape[0]
        term = dot(active[:, part * depth : (part + 1) * depth], weights)
        made = term if made is None else made + term
    total[...] = made

    def step(r, sums):
        rows = pl.ds(pl.multiple_of(r * seq, 8), seq)
        second = n2[rows, :] * vec[G_2 : G_2 + 1] + vec[B_N2 : B_N2 + 1]
        made, scale = norm_parts(second + total[rows, :] + vec[B_FO : B_FO + 1])
        out[r] = low(made * vec[G_3 : G_3 + 1] + vec[B_N3 : B_N3 + 1])
        valid = lax.broadcasted_iota(jnp.int32, made.shape, 0) < lengths[r]
        upstream = jnp.where(valid, wide(cot[r]), 0.0)
        back = norm_back(upstream, made, scale, vec[G_3 : G_3 + 1])
        dz[rows, :] = back
        gain, shift, lowered = sums
        return (
            gain + row_sum(upstream * made),
            shift + row_sum(upstream),
            lowered + row_sum(wide(low(back))),
        )

    zero = jnp.zeros((1, total.shape[1]), F32)
    sums = lax.fori_loop(0, out.shape[0], step, (zero, zero, zero), unroll=2)
    df[...] = low(dz[...])
    for j in range(3):
        rows_out[j : j + 1] = sums[j]
    rows_out[3:8] = jnp.zeros((5, total.shape[1]), F32)
    keep.wait()


def norm_back_rows(total, dz_ref, normed, inverse, gain, dz, low_ref, rows_out, step_rows):
    def step(r, sums):
        rows = pl.ds(pl.multiple_of(r * step_rows, 8), step_rows)
        upstream = total[rows, :] + dz_ref[rows, :]
        made = normed[rows, :]
        back = norm_back(upstream, made, inverse[rows, :], gain)
        dz[rows, :] = back
        return (
            sums[0] + row_sum(upstream * made),
            sums[1] + row_sum(upstream),
            sums[2] + row_sum(wide(low(back))),
        )

    zero = jnp.zeros((1, total.shape[1]), F32)
    sums = lax.fori_loop(0, total.shape[0] // step_rows, step, (zero, zero, zero))
    low_ref[...] = low(dz[...])
    for j in range(3):
        rows_out[j : j + 1] = sums[j]
    rows_out[3:8] = jnp.zeros((5, total.shape[1]), F32)


def hidden_back_kernel(
    seq, df, wout, win, slope, dz3, n2, inverse, vec, du, bias_out, dz2, dac, rows_out, total
):
    i = pl.program_id(0)

    @pl.when(i == 0)
    def _():
        total[...] = jnp.zeros_like(total)

    raw = dot_last(df[:, :LANES], wout[0, :, 0].reshape(-1, LANES))
    raw = raw + dot_last(df[:, LANES:], wout[0, :, 1].reshape(-1, LANES))
    made = low(raw * wide(slope[...]))
    du[...] = made
    bias_out[pl.ds(i, 1), :] = row_sum(wide(made))
    total[...] += dot_last(made, win[:, :, 0].reshape(-1, LANES))

    @pl.when(i == pl.num_programs(0) - 1)
    def _():
        norm_back_rows(
            total, dz3, n2, inverse, vec[G_2 : G_2 + 1], dz2, dac, rows_out, seq
        )


def cross_back_kernel(
    seq, patches, micro_rows, slots, dac, qc, kv, wco, dqc, dkv_out, dkv, q, do, dq
):
    q[...] = wide(qc[...]) * 0.125
    do[...] = wide(
        low(dot_last(dac[:, :LANES], wco[0, 0]) + dot_last(dac[:, LANES:], wco[1, 0]))
    )
    dkv[...] = jnp.zeros_like(dkv)
    tokens = qc.shape[0]
    padded = kv.shape[3]
    there = lax.broadcasted_iota(jnp.int32, (4 * seq, padded), 1) < patches

    def step(r, _):
        rows = pl.ds(pl.multiple_of(r * seq, 8), seq)
        slot, m = slots[r], r // micro_rows
        asked = [heads_apart(q[rows, c]) for c in quads()]
        came = [heads_apart(do[rows, c]) for c in quads()]
        keys = [kv[slot, 0, m, :, c] for c in quads()]
        values = [kv[slot, 1, m, :, c] for c in quads()]
        scores = [dot_last(a, key) for a, key in zip(asked, keys)]
        backs = [dot_last(d, value) for d, value in zip(came, values)]
        weights = [softmax(jnp.where(there, score, -jnp.inf)) for score in scores]
        backs = [score_back(w, b) for w, b in zip(weights, backs)]
        queries = [heads_joined(dot(b, key)) for b, key in zip(backs, keys)]
        key_parts = [dot_first(b, a) for b, a in zip(backs, asked)]
        value_parts = [dot_first(low(w), d) for w, d in zip(weights, came)]
        for j, c in enumerate(quads()):
            dq[rows, c] = queries[j] * 0.125
            dkv[0, slot, m, :, c] += key_parts[j]
            dkv[1, slot, m, :, c] += value_parts[j]
        return 0

    lax.fori_loop(0, tokens // seq, step, 0, unroll=2)
    dqc[...] = low(dq[...])
    dkv_out[...] = low(dkv[...])


def first_back_kernel(seq, dqc, wcq, dz2, n1, inverse, vec, dz1, da, rows_out, total):
    total[...] = dot_last(dqc[:, :LANES], wcq[0, 0]) + dot_last(dqc[:, LANES:], wcq[1, 0])
    norm_back_rows(total, dz2, n1, inverse, vec[G_1 : G_1 + 1], dz1, da, rows_out, seq)
    rows_out[3:4] = row_sum(wide(dqc[...]))


def self_back_kernel(seq, lengths, da, qkv, wso, dqkv, rows_out, q, k, v, do, dq, dk, dv):
    q[...] = wide(qkv[0]) * 0.125
    k[...] = wide(qkv[1])
    v[...] = wide(qkv[2])
    do[...] = wide(low(dot_last(da[:, :LANES], wso[0, 0]) + dot_last(da[:, LANES:], wso[1, 0])))
    tokens = da.shape[0]

    def step(r, _):
        rows = pl.ds(pl.multiple_of(r * seq, 8), seq)
        valid = lax.broadcasted_iota(jnp.int32, (4 * seq, seq), 1) < lengths[r]
        asked = [heads_apart(q[rows, c]) for c in quads()]
        came = [heads_apart(do[rows, c]) for c in quads()]
        keys = [low(k[rows, c]) for c in quads()]
        values = [low(v[rows, c]) for c in quads()]
        scores = [dot_last(a, key) for a, key in zip(asked, keys)]
        backs = [dot_last(d, value) for d, value in zip(came, values)]
        weights = [softmax(jnp.where(valid, score, -jnp.inf)) for score in scores]
        backs = [score_back(w, b) for w, b in zip(weights, backs)]
        queries = [heads_joined(dot(b, key)) for b, key in zip(backs, keys)]
        key_parts = [dot_first(b, a) for b, a in zip(backs, asked)]
        value_parts = [dot_first(low(w), d) for w, d in zip(weights, came)]
        for j, c in enumerate(quads()):
            dq[rows, c] = queries[j] * 0.125
            dk[rows, c] = key_parts[j]
            dv[rows, c] = value_parts[j]
        return 0

    lax.fori_loop(0, tokens // seq, step, 0, unroll=2)
    for j, made in enumerate((dq, dk, dv)):
        dqkv[j] = low(made[...])
    rows_out[0:1] = row_sum(wide(dqkv[0]))
    rows_out[1:2] = row_sum(wide(dqkv[2]))
    rows_out[2:8] = jnp.zeros((6, q.shape[1]), F32)


def text_grad_kernel(dz1, dqkv, w_ref, out, total):
    total[...] = dz1[...]
    for j in range(3):
        for c in range(2):
            total[...] += dot_last(dqkv[j, :, c * LANES : (c + 1) * LANES], w_ref[c, j])
    seq = out.shape[1]
    for r in range(out.shape[0]):
        out[r] = low(total[r * seq : (r + 1) * seq, :])


def patch_grad_kernel(dkv, w_ref, kept, sent, rows_out):
    _, slots, images, padded, width = dkv.shape
    rows = images * padded
    total = jnp.zeros((1, width), F32)
    for slot in range(slots):
        made = None
        for j in range(2):
            grad = dkv[j, slot].reshape(rows, width)
            for c in range(2):
                term = dot_last(grad[:, c * LANES : (c + 1) * LANES], w_ref[c, j])
                made = term if made is None else made + term
        out = sent if slot % 2 else kept
        out[slot // 2] = low(made).reshape(images, padded, w_ref.shape[2])
        total = total + row_sum(wide(grad))
    rows_out[0:1] = total
    rows_out[1:8] = jnp.zeros((7, width), F32)


def on_device(
    text_input,
    patch_input,
    text_lengths,
    image_of_row,
    cotangent,
    self_qkv,
    self_out,
    cross_q,
    cross_kv,
    cross_out,
    ffn_in,
    ffn_out,
    biases,
    norm_gains,
    ffn_bias,
):
    dp = lax.axis_size(DP)
    micros, row_count, seq, width = text_input.shape
    patches, patch_width = patch_input.shape[2:]
    rows_all = micros * row_count
    tokens = rows_all * seq
    hidden = ffn_in.shape[1]
    padded = -(-patches // 16) * 16
    images = micros * patch_input.shape[1]

    part = biases.shape[1]
    small = jnp.concatenate((biases, norm_gains, ffn_bias.reshape(-1, part)))
    small_rows = small.shape[0]
    wide_rows = biases.shape[0] + norm_gains.shape[0]
    small = jnp.pad(small, ((0, 2 * PAD_ROWS - small_rows), (0, LANES - part)))
    small = jnp.broadcast_to(small.reshape(2, PAD_ROWS, LANES), (2, 2, PAD_ROWS, LANES))

    half = width // dp // 2
    half_v = cross_kv.shape[1] // 2
    in_units = hidden // (2 * LANES)
    text_group = (
        (small, self_qkv, self_out, cross_q),
        ((1, PAD_ROWS), (3, half), (1, half), (1, half)),
    )
    patch_group = ((cross_kv, cross_out), ((2, half_v), (1, half)))
    hidden_group = ((ffn_in, ffn_out), ((in_units, half), (1, ffn_out.shape[0] // 2)))

    text = text_input.reshape(tokens, width)
    pixels = call(pixel_kernel, shape((images, padded, patch_width)), [VMEM])(
        patch_input.reshape(images, patches, patch_width)
    )
    lengths = text_lengths.reshape(-1)
    slots = image_of_row.reshape(-1) ^ lax.axis_index(STREAM)
    flat = (tokens, width)
    full = pltpu.VMEM(flat, F32)
    flops = 2 * tokens * width * width
    steps = hidden // LANES
    chunks = hidden // width
    kv_shape = (4, 2, images, padded, width)
    in_block = pl.BlockSpec(
        (8, 2, 1, width // 16, LANES), lambda i: (0, 0, i // in_units, i % in_units, 0)
    )
    v = types.SimpleNamespace()

    bf16 = jnp.bfloat16

    def pixel_steps():
        (v.across,) = yield [(pixels, STREAM, ACROSS)]
        v.beside, v.apart = yield [(pixels, STREAM, CORE), (v.across, STREAM, CORE)]

    def run_text(tie, sources, spec=None, small_inputs=()):
        units = text_group[1]
        wholes = [(2, 1, 16 * PAD_ROWS, LANES)]
        wholes += [(2, count, depth * 2 * dp, LANES) for count, depth in units[1:]]
        outs = [
            shape((16, width), F32), shape((steps, LANES), F32), shape(flat), shape(flat, F32),
            shape((tokens, 1), F32), shape(flat), shape(flat), shape((3, *flat)),
            *[shape(dims) for dims in wholes[1:]],
        ]
        (
            v.vec, v.hidden_bias, v.attended, v.n1, v.inverse1, v.h1, v.qc, v.qkv,
            v.w_qkv, v.w_so, v.w_cq,
        ) = call(
            functools.partial(text_kernel, units, len(sources), spec, seq),
            outs,
            [SMEM, VMEM] + [ANY] * len(sources) + [VMEM] * len(small_inputs),
            [
                *[pltpu.VMEM(dims, bf16) for dims in wholes],
                pltpu.VMEM((3, *flat), bf16), full, full, full, full,
                pltpu.SemaphoreType.DMA((32 * len(units),)), pltpu.SemaphoreType.DMA((4,)),
            ],
            out_specs=[VMEM] * 7 + [ANY] * 4,
            mib=60,
            flops=8 * flops,
        )(lengths, tie(text), *sources, *small_inputs)
        return v.qc

    def run_patch(tie, sources, spec=None):
        units = patch_group[1]
        wholes = [(2, count, depth * 2 * dp, LANES) for count, depth in units]
        pixels_shape = (4, images, padded, patch_width)
        outs = [
            shape(flat), shape(flat, F32), shape((tokens, 1), F32), shape(flat),
            shape(kv_shape), shape(pixels_shape), *[shape(dims) for dims in wholes],
        ]
        v.oc, v.n2, v.inverse2, v.h2, v.kv, pixels_all, v.w_kv, v.w_co = call(
            functools.partial(patch_kernel, units, len(sources), spec, seq, patches, row_count),
            outs,
            [SMEM, VMEM, VMEM, VMEM] + [ANY] * (len(sources) + 4),
            [
                *[pltpu.VMEM(dims, bf16) for dims in wholes],
                pltpu.VMEM(kv_shape, bf16), pltpu.VMEM(pixels_shape, bf16), full, full,
                pltpu.SemaphoreType.DMA((32 * len(units),)), pltpu.SemaphoreType.DMA((4,)),
                pltpu.SemaphoreType.DMA((4,)),
            ],
            out_specs=[VMEM] * 4 + [ANY] * 4,
            mib=60,
            flops=18 * flops,
        )(slots, tie(v.qc), v.n1, v.vec, *sources, pixels, v.beside, v.across, v.apart)
        v.pixels_all = pixels_all.reshape(-1, patch_width)
        return v.h2

    def run_ffn(tie, sources, spec=None):
        w_shape = (8, 2, 2, hidden // 8, LANES)
        v.out_rows, v.dz3, v.df, v.sums3, v.active, v.slope, v.w_hidden = call(
            functools.partial(ffn_kernel, len(sources), spec, in_units, seq),
            [
                shape((rows_all, seq, width)), shape(flat, F32), shape(flat),
                shape((8, width), F32), shape((tokens, hidden)), shape((tokens, hidden)),
                shape(w_shape),
            ],
            [SMEM] + [VMEM] * 5 + [ANY] * len(sources),
            [
                pltpu.VMEM(w_shape, bf16), full, pltpu.SemaphoreType.DMA((32,)),
                pltpu.SemaphoreType.DMA((1,)),
            ],
            out_specs=[VMEM] * 6 + [ANY],
            flops=8 * flops,
        )(
            lengths, tie(v.h2), v.hidden_bias, v.n2,
            cotangent.reshape(rows_all, seq, width), v.vec, *sources,
        )
        return v.df

    def run_hidden_back(tie):
        v.du, v.hidden_bias_grad, v.dz2, v.dac, v.sums2 = call(
            functools.partial(hidden_back_kernel, seq),
            [
                shape((tokens, hidden)),
                shape((steps, LANES), F32),
                shape(flat, F32),
                shape(flat),
                shape((8, width), F32),
            ],
            [
                VMEM,
                pl.BlockSpec((1, 2, 2, hidden // 16, LANES), lambda i: (i, 0, 0, 1, 0)),
                in_block,
                pl.BlockSpec((tokens, LANES), lambda i: (0, i)),
                VMEM,
                VMEM,
                VMEM,
                VMEM,
            ],
            [full],
            out_specs=[pl.BlockSpec((tokens, LANES), lambda i: (0, i)), VMEM, VMEM, VMEM, VMEM],
            grid=(steps,),
            flops=8 * flops,
        )(
            tie(v.df), v.w_hidden, v.w_hidden, v.slope, v.dz3, v.n2, v.inverse2,
            v.vec,
        )
        return v.dac

    def run_cross_back(tie):
        v.dqc, v.dkv_all = call(
            functools.partial(cross_back_kernel, seq, patches, row_count),
            [shape(flat), shape((2, 4, images, padded, width))],
            [SMEM, VMEM, VMEM, VMEM, VMEM],
            [pltpu.VMEM((2, 4, images, padded, width), F32), full, full, full],
            flops=4 * flops,
        )(slots, tie(v.dac), v.qc, v.kv, v.w_co)
        return v.dqc

    def patch_steps():
        (came,) = yield [(v.patch_sent, STREAM, CORE)]
        made = wide(v.patch_kept) + wide(came)
        (across,) = yield [(low(made[1]), STREAM, ACROSS)]
        v.patch_rows = low(made[0] + wide(across))[:, :patches].reshape(patch_input.shape)

    def run_first_back(tie):
        v.dz1, v.da, v.sums1 = call(
            functools.partial(first_back_kernel, seq),
            [shape(flat, F32), shape(flat), shape((8, width), F32)],
            [VMEM] * 6,
            [full],
            flops=flops,
        )(tie(v.dqc), v.w_cq, v.dz2, v.n1, v.inverse1, v.vec)
        return v.da

    def run_self_back(tie):
        v.dqkv, v.sums0 = call(
            functools.partial(self_back_kernel, seq),
            [shape((3, *flat)), shape((8, width), F32)],
            [SMEM, VMEM, VMEM, VMEM],
            [full] * 7,
            flops=4 * flops,
        )(lengths, tie(v.da), v.qkv, v.w_so)
        return v.dqkv

    def run_patch_grad(tie):
        v.patch_kept, v.patch_sent, v.sums_kv = call(
            patch_grad_kernel,
            [shape((2, images, padded, patch_width))] * 2 + [shape((8, width), F32)],
            [VMEM] * 2,
            flops=16 * flops,
        )(tie(v.dkv_all), v.w_kv)
        return v.patch_sent

    def run_text_grad(tie):
        v.text_rows = call(
            text_grad_kernel,
            shape((rows_all, seq, width)),
            [VMEM] * 3,
            [full],
            flops=3 * flops,
        )(tie(v.dz1), v.dqkv, v.w_qkv)
        return v.text_rows

    def small_grads():
        sums0, sums1, sums2, sums3, sums_kv = v.sums0, v.sums1, v.sums2, v.sums3, v.sums_kv
        grads = jnp.concatenate(
            (
                sums0[0:2], sums1[2:3], sums1[1:2], sums1[3:4], sums_kv[0:1], sums2[2:3],
                sums2[1:2], sums3[2:3], sums3[1:2], sums1[0:1], sums2[0:1], sums3[0:1],
            )
        )
        return jnp.concatenate(
            (
                grads.reshape(wide_rows, dp, part).transpose(1, 0, 2),
                v.hidden_bias_grad.reshape(dp, -1, part),
            ),
            axis=1,
        )

    def run_all(moves):
        finish(Mover(moves))

    def finish(mover):
        while not mover.done:
            mover.give([lax.ppermute(array, axis, hops) for array, axis, hops in mover.requests])

    if not special_mesh():
        def free(array):
            return array

        w_small, *wholes = gather_plain(*text_group)
        patch_wholes = gather_plain(*patch_group)
        values = wide(w_small[0, 0].reshape(dp, 2 * PAD_ROWS, LANES)[:, :small_rows, :part])
        vec = values[:, :wide_rows].transpose(1, 0, 2).reshape(wide_rows, width)
        vec = jnp.pad(vec, ((0, 16 - wide_rows), (0, 0)))
        hidden_bias = values[:, wide_rows:].reshape(-1, LANES)
        w_small = w_small[:, :, : 16 * PAD_ROWS]
        w_in = lax.all_gather(ffn_in, DP, axis=0, tiled=True)
        w_out = lax.all_gather(ffn_out, DP, axis=0, tiled=True)
        w_in = w_in.reshape(8, 2, width // 16, 2, in_units, LANES).transpose(0, 1, 3, 4, 2, 5)
        w_in = w_in.reshape(8, 2, 2, -1, LANES)
        w_out = w_out.reshape(8, 2, hidden // 16, 2, LANES).transpose(0, 1, 3, 2, 4)
        w_hidden = jnp.concatenate((w_in, w_out), axis=3)
        run_all(pixel_steps())
        run_text(free, (w_small, *wholes), None, (vec, hidden_bias))
        run_patch(free, patch_wholes)
        run_ffn(free, (w_hidden,))
        for work in (run_hidden_back, run_cross_back, run_patch_grad):
            work(free)
        run_all(patch_steps())
        for work in (run_first_back, run_self_back, run_text_grad):
            work(free)
        s_out, s_in, s_co, s_cq, s_so, s_kv, s_qkv = reduce_plain(
            (
                (v.active, v.df), (v.h2, v.du), (v.oc, v.dac), (v.h1, v.dqc),
                (v.attended, v.da), (v.pixels_all, v.dkv_all.reshape(2, -1, width)), (text, v.dqkv),
            )
        )
        s_small = lax.psum_scatter(low(small_grads()), DP, scatter_dimension=0, tiled=True)
        s_small = wide(lax.psum(s_small, STREAM))[0]
        s_biases = s_small[: biases.shape[0]]
        s_gains = s_small[biases.shape[0] : wide_rows]
        s_hidden_bias = s_small[wide_rows:]
    else:
        clock = Clock()
        gather_text, gather_patch, gather_hidden = (
            Mover(gather_steps(*pack_group(*group)), pieces=True)
            for group in (text_group, patch_group, hidden_group)
        )
        move_pixels = Mover(pixel_steps())
        clock.step([gather_text, move_pixels])
        clock.step([gather_text, gather_patch])
        clock.step([gather_hidden, gather_text, gather_patch])
        first_hidden = gather_hidden.given
        clock.step(
            [gather_hidden, gather_patch, move_pixels], [lambda tie: run_text(tie, *piece_sources(gather_text.result, tie))]
        )
        hidden_bases = [piece.base for piece in (*first_hidden, *gather_hidden.given)]

        def early(tie):
            for base in dict.fromkeys(hidden_bases):
                base.exchange(tie)
                clock.bases.append(base)
            return ()

        clock.step([gather_hidden], [early, lambda tie: run_patch(tie, *piece_sources(gather_patch.result, tie))])
        clock.step([gather_hidden], [lambda tie: run_ffn(tie, *piece_sources(gather_hidden.result, tie))])

        out_group, in_group, mid_group, last_group = Group(), Group(), Group(), Group()

        def begin_out(tie):
            return out_group.sibling(tie, (v.active, v.df))

        def begin_in(tie):
            return in_group.sibling(tie, (v.h2, v.du))

        def begin_mid(tie):
            return mid_group.sibling(
                tie,
                (v.oc, v.dac),
                (v.h1, v.dqc),
                (v.attended, v.da),
                (v.pixels_all, v.dkv_all.reshape(2, -1, width)),
            )

        def begin_last(tie):
            return last_group.sibling(tie, (text, v.dqkv))

        def own_last(tie):
            return last_group.own(
                tie, (v.sums0, v.sums1, v.sums2, v.sums3, v.sums_kv, v.hidden_bias_grad)
            )

        clock.step([], [begin_out])
        clock.step([out_group.core_move()], [run_hidden_back, out_group.own], eager=True)
        move_out = out_group.move()
        clock.step([], [begin_in])
        clock.step(
            [move_out, in_group.core_move()],
            [run_cross_back, run_first_back, in_group.own, begin_mid],
            eager=True,
        )
        move_in = in_group.move()
        clock.step(
            [move_out, move_in, mid_group.core_move()],
            [run_self_back, run_patch_grad, mid_group.own, begin_last],
            eager=True,
            last=True,
        )
        move_mid, move_patch = mid_group.move(), Mover(patch_steps())
        clock.step(
            [move_out, move_in, move_mid, last_group.core_move(), move_patch],
            [own_last, run_text_grad],
            eager=True,
        )
        move_last = last_group.move()
        movers = [move_out, move_in, move_mid, move_last, move_patch]
        results = {}

        small_shapes = [
            shape((rows, part), F32)
            for rows in (biases.shape[0], norm_gains.shape[0], small_rows - wide_rows)
        ]

        def unpack(group, mover):
            def work(tie):
                results[mover] = group.unpack(
                    (tie(mover.result[0]), mover.result[1]),
                    small_shapes if group is last_group else (),
                )
                return results[mover]
            return work

        groups = [
            (out_group, move_out), (in_group, move_in), (mid_group, move_mid), (last_group, move_last)
        ]
        def ready():
            return [
                unpack(group, mover)
                for group, mover in groups
                if mover.done and mover not in results
            ]

        for _ in range(3):
            clock.step(movers, ready, eager=True)
        for mover in movers:
            if not mover.done:
                finish(mover)
        for work in ready():
            work(clock.tie)
        (s_out,), (s_in,) = results[move_out], results[move_in]
        s_co, s_cq, s_so, s_kv = results[move_mid]
        s_qkv, s_biases, s_gains, s_hidden_bias = results[move_last]
    return (
        v.out_rows.reshape(text_input.shape),
        v.text_rows.reshape(text_input.shape),
        v.patch_rows,
        s_qkv,
        s_so,
        s_cq,
        s_kv,
        s_co,
        s_in,
        s_out,
        s_biases,
        s_gains,
        s_hidden_bias.reshape(-1),
    )


def solution(mesh):
    placed = (
        P(None, (DP, STREAM), None, None),
        P(None, (DP, STREAM), None, None),
        P(None, (DP, STREAM)),
        P(None, (DP, STREAM)),
        P(None, (DP, STREAM), None, None),
        P(None, DP, None),
        P(DP, None),
        P(DP, None),
        P(None, DP, None),
        P(DP, None),
        P(DP, None),
        P(DP, None),
        P(None, DP),
        P(None, DP),
        P(DP),
    )
    return jax.shard_map(
        on_device,
        mesh=mesh,
        in_specs=placed,
        out_specs=(
            P(None, (DP, STREAM), None, None),
            P(None, (DP, STREAM), None, None),
            P(None, (DP, STREAM), None, None),
            P(None, DP, None),
            P(DP, None),
            P(DP, None),
            P(None, DP, None),
            P(DP, None),
            P(DP, None),
            P(DP, None),
            P(None, DP),
            P(None, DP),
            P(DP),
        ),
        check_vma=False,
    )
```
